32 devices in a mesh: seq: 4 (over x, core), head: 4 (over z), rep: 2 (over y).
Axes of the slice: x: 2, y: 2, z: 4, core: 2. Of those that a mesh axis runs over, the one named last changes fastest.
Arguments:
- token_ids: int32 [2048], P(('rep', 'seq')), parts along dimension 0, may hold values from 0 to 15
- embedding: float32 [16, 256], replicated, may hold values from -6 to 6
- complement: int32 [256], replicated, may hold values from 0 to 255, each once
- prenorm_first: float32 [256], replicated, may hold values from 0.1 to 1.9
- inproj_first: float32 [256, 2, 512], P(None, None, 'head'), may hold values from -0.375 to 0.375
- statemap_first: float32 [256, 2, 128], replicated, may hold values from -0.375 to 0.375
- stepmap_first: float32 [256, 8], P(None, 'head'), may hold values from -0.375 to 0.375
- stepbias_first: float32 [8], P('head'), may hold values from -1 to 1
- rates_first: float32 [8], P('head'), may hold values from 0.000185546875 to 0.11, as said below
- skipgain_first: float32 [8], P('head'), may hold values from 0.5 to 1.5
- outnorm_first: float32 [512], P('head'), may hold values from 0.1 to 1.9
- outproj_first: float32 [512, 256], P('head'), may hold values from -0.25 to 0.25
- prenorm_second: float32 [256], replicated, may hold values from 0.1 to 1.9
- inproj_second: float32 [256, 2, 512], P(None, None, 'head'), may hold values from -0.375 to 0.375
- statemap_second: float32 [256, 2, 128], replicated, may hold values from -0.375 to 0.375
- stepmap_second: float32 [256, 8], P(None, 'head'), may hold values from -0.375 to 0.375
- stepbias_second: float32 [8], P('head'), may hold values from -1 to 1
- rates_second: float32 [8], P('head'), may hold values from 0.000185546875 to 0.11, as said below
- skipgain_second: float32 [8], P('head'), may hold values from 0.5 to 1.5
- outnorm_second: float32 [512], P('head'), may hold values from 0.1 to 1.9
- outproj_second: float32 [512, 256], P('head'), may hold values from -0.25 to 0.25
Outputs:
- strand_out: float32 [2048, 256], P(('rep', 'seq', 'head')), parts along dimension 0
The draws below stay inside these ranges and needn't reach their ends.
There are 2 independent parts, one for each index of `rep`. The reference program is written for one: setup_inputs(seed, part) draws one part's arguments, and reference() takes and returns one part's arrays. A program takes and returns all parts, laid end to end along the dimension named above; an argument that names none is the same for every part. Nothing has to cross between parts.
Inputs may be any that keep to these rules, and one draw needn't show every extreme that they name: `complement`: each channel index appears once. `rates_first`: positive rates. `rates_second`: positive rates.
All inputs are finite; a program needn't handle non-finite values.
Results may differ from the reference program's by a relative error of at most 0.00018.
Values sent between devices are 32-bit elements; how exact they have to be, the bound alone decides.
No kernel may reach another device: no remote copies, remote signals or barrier semaphores. Data moves between devices by JAX's collectives and lax.ppermute only.
A program may use at most 64 MiB of HBM per device.

```python
import jax
import jax.numpy as jnp
from jax import lax

D = 256
HEADS = 8
STATE = 128
VOCAB = 16
BLOCK = 256
INNER = 512
SEQ_LEN = 1024


def rate_values(key, salt_value):
    mixed_key = jax.random.fold_in(key, salt_value)
    first_key, second_key, third_key = jax.random.split(mixed_key, 3)
    slow_log = jax.random.uniform(first_key, (HEADS,), jnp.float32, jnp.log(0.2 / SEQ_LEN), jnp.log(1.0 / SEQ_LEN))
    fast_log = jax.random.uniform(second_key, (HEADS,), jnp.float32, jnp.log(0.03), jnp.log(0.1))
    slow_count = HEADS // 2
    ranking = jax.random.permutation(third_key, HEADS)
    return jnp.exp(jnp.where(ranking < slow_count, slow_log, fast_log)).astype(jnp.float32)


def draw_rates_first(key, part):
    return rate_values(key, 11)


def draw_rates_second(key, part):
    return rate_values(key, 23)


def plant(result, stream_key, least, high):
    longest = result.shape.index(max(result.shape))
    spots = []
    for shift in (0, 1):
        where = [jax.random.randint(jax.random.fold_in(stream_key, axis), (), 0, length) for axis, length in enumerate(result.shape)]
        where[longest] = (where[longest] + shift) % result.shape[longest]
        spots.append(tuple(where))
    return result.at[spots[0]].set(least).at[spots[1]].set(high)


def block_levels(key, shape, cuts, low, top_value):
    def one(axis_at, parts):
        heights = jax.random.uniform(jax.random.fold_in(jax.random.fold_in(key, 6), axis_at), (parts,), jnp.float32, low / len(cuts), top_value / len(cuts))
        return jnp.repeat(jnp.exp(heights), shape[axis_at] // parts).reshape((-1,) + (1,) * (len(shape) - axis_at - 1))

    loudness = one(*cuts[0])
    for cut in cuts[1:]:
        loudness = loudness * one(*cut)
    return loudness


def bell_draw(stream_key, shape, deviation, bound, pieces=(), dtype=jnp.bfloat16):
    gain = block_levels(stream_key, shape, pieces, -0.22, 0.18) if pieces else 1.0
    array = jax.random.normal(stream_key, shape, jnp.float32) * deviation * gain
    return jnp.minimum(jnp.maximum(array, -bound), bound).astype(dtype)


def setup_inputs(seed: int = 0, part: int = 0) -> dict:
    key_of = jax.random.split(jax.random.key(seed), 22)
    part_splits = jax.random.split(jax.random.fold_in(key_of[21], part), 22)
    token_ids = plant(jax.random.randint(part_splits[0], (SEQ_LEN,), 0, VOCAB), jax.random.fold_in(part_splits[0], 1), 0, VOCAB - 1).astype(jnp.int32)
    embedding = bell_draw(key_of[1], (VOCAB, D), 1.0, 6.0, (), jnp.float32)
    complement = jax.random.permutation(key_of[2], D).astype(jnp.int32)
    prenorm_first = jnp.clip(1.0 + 0.18 * jax.random.normal(key_of[3], (D,), jnp.float32), 0.1, 1.9)
    inproj_first = bell_draw(key_of[4], (D, 2, INNER), D ** -0.5, 0.375, ((2, 4),), jnp.float32)
    statemap_first = bell_draw(key_of[5], (D, 2, STATE), D ** -0.5, 0.375, (), jnp.float32)
    stepmap_first = bell_draw(key_of[6], (D, HEADS), D ** -0.5, 0.375, ((1, 4),), jnp.float32)
    stepbias_first = jnp.clip(jax.random.uniform(key_of[7], (HEADS,), jnp.float32, -1.0, 1.0) * block_levels(key_of[7], (HEADS,), ((0, 4),), -0.4, 0.0), -1.0, 1.0)
    rates_first = draw_rates_first(jax.random.fold_in(key_of[21], 71), part)
    skipgain_first = jnp.clip(0.5 + 1.0 * jax.random.uniform(key_of[9], (HEADS,), jnp.float32) ** block_levels(key_of[9], (HEADS,), ((0, 4),), -0.2, 0.2), 0.5, 1.5)
    outnorm_first = jnp.clip(1.0 + 0.18 * jax.random.normal(key_of[10], (INNER,), jnp.float32), 0.1, 1.9)
    outproj_first = bell_draw(key_of[11], (INNER, D), INNER ** -0.5, 0.25, ((0, 4),), jnp.float32)
    prenorm_second = jnp.clip(1.0 + 0.18 * jax.random.normal(key_of[12], (D,), jnp.float32), 0.1, 1.9)
    inproj_second = bell_draw(key_of[13], (D, 2, INNER), D ** -0.5, 0.375, ((2, 4),), jnp.float32)
    statemap_second = bell_draw(key_of[14], (D, 2, STATE), D ** -0.5, 0.375, (), jnp.float32)
    stepmap_second = bell_draw(key_of[15], (D, HEADS), D ** -0.5, 0.375, ((1, 4),), jnp.float32)
    stepbias_second = jnp.clip(jax.random.uniform(key_of[16], (HEADS,), jnp.float32, -1.0, 1.0) * block_levels(key_of[16], (HEADS,), ((0, 4),), -0.4, 0.0), -1.0, 1.0)
    rates_second = draw_rates_second(jax.random.fold_in(key_of[21], 71), part)
    skipgain_second = jnp.clip(0.5 + 1.0 * jax.random.uniform(key_of[18], (HEADS,), jnp.float32) ** block_levels(key_of[18], (HEADS,), ((0, 4),), -0.2, 0.2), 0.5, 1.5)
    outnorm_second = jnp.clip(1.0 + 0.18 * jax.random.normal(key_of[19], (INNER,), jnp.float32), 0.1, 1.9)
    outproj_second = bell_draw(key_of[20], (INNER, D), INNER ** -0.5, 0.25, ((0, 4),), jnp.float32)
    return dict(token_ids=token_ids, embedding=embedding, complement=complement, prenorm_first=prenorm_first, inproj_first=inproj_first, statemap_first=statemap_first, stepmap_first=stepmap_first, stepbias_first=stepbias_first, rates_first=rates_first, skipgain_first=skipgain_first, outnorm_first=outnorm_first, outproj_first=outproj_first, prenorm_second=prenorm_second, inproj_second=inproj_second, statemap_second=statemap_second, stepmap_second=stepmap_second, stepbias_second=stepbias_second, rates_second=rates_second, skipgain_second=skipgain_second, outnorm_second=outnorm_second, outproj_second=outproj_second)


highest = lax.Precision.HIGHEST
epsilon = 1e-05

def matmul(left, right):
    return jnp.dot(left, right, precision=highest, preferred_element_type=jnp.float32)

def rms_scale(values, gain_vec):
    return values * lax.rsqrt(lax.optimization_barrier(jnp.mean(values * values, axis=-1, keepdims=True)) + epsilon) * gain_vec

def running(values, axis_number, reverse):
    if reverse:
        return jnp.flip(jnp.cumsum(jnp.flip(values, axis_number), axis_number), axis_number)
    return jnp.cumsum(values, axis_number)

def project(layer_in, prenorm, inproj, statemap, stepmap, stepbias, rates):
    normed = rms_scale(layer_in, prenorm)
    length = layer_in.shape[0]
    inner_width = inproj.shape[2]
    head_count = stepmap.shape[1]
    both_parts = matmul(normed, inproj.reshape(inproj.shape[0], 2 * inner_width))
    gate_vals = both_parts[:, :inner_width]
    x_heads = both_parts[:, inner_width:].reshape(length, head_count, inner_width // head_count)
    state_width = statemap.shape[2]
    write_read = matmul(normed, statemap.reshape(statemap.shape[0], 2 * state_width))
    write_vecs = write_read[:, :state_width]
    read_vecs = write_read[:, state_width:]
    step_sizes = jax.nn.softplus(matmul(normed, stepmap) + stepbias)
    log_decay = -rates * step_sizes
    return (gate_vals, x_heads, write_vecs, read_vecs, step_sizes, log_decay)

def gated_norm(outputs, gate_vals, outnorm):
    length, head_count, head_dim = outputs.shape
    gated_vals = outputs * jax.nn.silu(gate_vals).reshape(outputs.shape)
    normed = gated_vals * lax.rsqrt(lax.optimization_barrier(jnp.mean(gated_vals * gated_vals, axis=-1, keepdims=True)) + epsilon)
    return normed.reshape(length, head_count * head_dim) * outnorm

def block_scan(x_heads, step_sizes, log_decay, write_vecs, read_vecs, skipgain, reverse):
    length, head_count, head_dim = x_heads.shape
    blocks = length // BLOCK
    block_items = (x_heads.reshape(blocks, BLOCK, head_count, head_dim), step_sizes.reshape(blocks, BLOCK, head_count), log_decay.reshape(blocks, BLOCK, head_count), write_vecs.reshape(blocks, BLOCK, -1), read_vecs.reshape(blocks, BLOCK, -1))
    positions = jnp.arange(BLOCK)
    if reverse:
        allowed = positions[None, :] >= positions[:, None]
    else:
        allowed = positions[None, :] <= positions[:, None]
    allowed = allowed[:, :, None]

    def block_step(carry_state, item_group):
        x_block, step_block, log_block, write_block, read_block = item_group
        cumulative = running(log_block, 0, reverse)
        pair_products = matmul(read_block, write_block.T)
        differ = cumulative[:, None, :] - cumulative[None, :, :]
        weights = jnp.where(allowed, jnp.exp(jnp.where(allowed, differ, 0.0)), 0.0) * pair_products[:, :, None] * step_block[None, :, :]
        outputs = jnp.einsum('qsh,shp->qhp', weights, x_block, precision=highest)
        outputs = outputs + jnp.exp(cumulative)[:, :, None] * jnp.einsum('qn,hpn->qhp', read_block, carry_state, precision=highest)
        outputs = outputs + skipgain[None, :, None] * x_block
        if reverse:
            end_log = cumulative[0]
        else:
            end_log = cumulative[-1]
        scaled = x_block * (jnp.exp(end_log[None, :] - cumulative) * step_block)[:, :, None]
        new_state = jnp.exp(end_log)[:, None, None] * carry_state + jnp.einsum('shp,sn->hpn', scaled, write_block, precision=highest)
        return (new_state, outputs)
    start_state = jnp.zeros((head_count, head_dim, write_vecs.shape[1]), jnp.float32)
    final_state, outputs = lax.scan(block_step, start_state, block_items, reverse=reverse)
    return outputs.reshape(length, head_count, head_dim)

def reference(token_ids, embedding, complement, prenorm_first, inproj_first, statemap_first, stepmap_first, stepbias_first, rates_first, skipgain_first, outnorm_first, outproj_first, prenorm_second, inproj_second, statemap_second, stepmap_second, stepbias_second, rates_second, skipgain_second, outnorm_second, outproj_second):
    embedded = jnp.take(embedding, token_ids, axis=0)
    gate_vals, x_heads, write_vecs, read_vecs, step_sizes, log_decay = project(embedded, prenorm_first, inproj_first, statemap_first, stepmap_first, stepbias_first, rates_first)
    forward_out = block_scan(x_heads, step_sizes, log_decay, write_vecs, read_vecs, skipgain_first, False)
    backward_out = block_scan(x_heads, step_sizes, log_decay, write_vecs, read_vecs, skipgain_first, True)
    mixed = gated_norm(forward_out, gate_vals, outnorm_first) + gated_norm(backward_out, gate_vals, outnorm_first)
    hidden = embedded + matmul(mixed, outproj_first)
    mirrored = jnp.take(hidden[::-1], complement, axis=1)
    gate_two, x_two, write_two, read_two, step_two, log_two = project(mirrored, prenorm_second, inproj_second, statemap_second, stepmap_second, stepbias_second, rates_second)
    forward_two = block_scan(x_two, step_two, log_two, write_two, read_two, skipgain_second, False)
    return mirrored + matmul(gated_norm(forward_two, gate_two, outnorm_second), outproj_second)
```

```python
import functools

import jax
import jax.numpy as jnp
from jax import lax
from jax.experimental import pallas as pl
from jax.experimental.pallas import tpu as pltpu
from jax.sharding import PartitionSpec as P

epsilon = 1e-05
f32 = jnp.float32
bf16 = jnp.bfloat16
LIMIT = 48 * 1024 * 1024

MM = (((1,), (0,)), ((), ()))
NT = (((1,), (1,)), ((), ()))
TN = (((0,), (0,)), ((), ()))


def iota(shape, axis):
    return lax.broadcasted_iota(jnp.int32, shape, axis)


def split2(value):
    high = value.astype(bf16)
    return high, (value - high.astype(f32)).astype(bf16)


def split3(value):
    high = value.astype(bf16)
    rest = value - high.astype(f32)
    middle = rest.astype(bf16)
    return high, middle, (rest - middle.astype(f32)).astype(bf16)


def dot(left, right, dims=MM):
    return lax.dot_general(left, right, dims, preferred_element_type=f32)


def dot_split(left, right, dims=MM):
    return (
        dot(left[0], right[1], dims) + dot(left[1], right[0], dims)
    ) + dot(left[0], right[0], dims)


def dot3(left, right, dims=MM):
    return dot_split(split2(left), split2(right), dims)


def dot_left_exact(left, right, dims=MM):
    high, middle, low = split3(right)
    return (dot(left, low, dims) + dot(left, middle, dims)) + dot(left, high, dims)


def dot_right_exact(left, right, dims=MM):
    high, middle, low = split3(left)
    return (dot(low, right, dims) + dot(middle, right, dims)) + dot(high, right, dims)


def softplus(value):
    return jnp.maximum(value, 0.0) + jnp.log1p(jnp.exp(-jnp.abs(value)))


def silu(value):
    return value / (1.0 + jnp.exp(-value))


def rms(value):
    return value * lax.rsqrt(jnp.mean(value * value, axis=-1, keepdims=True) + epsilon)


def tables_kernel(
    dims, tok, emb, prenorm, inproj, statemap, stepmap, bias, rates, skip, outnorm, packet, pairs
):
    V, D, hl, ch, nh, ns, T, N = dims
    H, LV = nh * hl, nh * hl * V
    normed = split2(rms(emb[...]) * prenorm[...])
    gate = dot_split(normed, split2(inproj[pl.ds(0, D, stride=2), :]))
    inner = dot_split(normed, split2(inproj[pl.ds(1, D, stride=2), :]))
    write = dot_split(normed, split2(statemap[pl.ds(0, D, stride=2), :]))
    read = dot_split(normed, split2(statemap[pl.ds(1, D, stride=2), :]))
    pairs[...] = dot3(read, jnp.concatenate([write] * H, axis=0), NT)
    steps = split2(stepmap[...])
    raw = dot_split(normed, steps, NT)
    raw_t = dot_split(steps, normed, NT)
    lane = iota((V, LV), 1)
    own = (lane % V) == iota((V, LV), 0)
    of_head = (lane // V) % hl
    decay = jnp.zeros((V, LV), f32)
    step = jnp.zeros((V, LV), f32)
    gain = jnp.zeros((V, LV), f32)
    log_t = jnp.zeros((H, V), f32)
    row_head = iota((H, V), 0) % hl
    for head in range(hl):
        column = softplus(raw[:, head : head + 1] + bias[head])
        here = of_head == head
        decay = jnp.where(here, jnp.exp(-rates[head] * column), decay)
        step = jnp.where(here & own, column, step)
        gain = jnp.where(here & own, skip[head], gain)
        line = softplus(raw_t[head : head + 1, :] + bias[head])
        log_t = jnp.where(row_head == head, -rates[head] * line, log_t)
    flip = (iota((T, T), 0) + iota((T, T), 1) == T - 1).astype(f32).astype(bf16)
    tokens = jnp.broadcast_to(tok[...].astype(f32), (8, T)).astype(bf16)
    packet[0:V, 0:ch] = gate
    packet[0:V, ch : 2 * ch] = inner
    start = 2 * ch
    packet[0:V, start : start + LV] = decay
    packet[0:V, start + LV : start + 2 * LV] = step
    packet[0:V, start + 2 * LV : start + 3 * LV] = gain
    packet[V : V + 8, 0:T] = dot(tokens, flip)
    packet[V + 8 : V + 8 + H, 0:V] = log_t
    packet[V + 8 : V + 8 + H, LV : LV + ch] = jnp.broadcast_to(outnorm[...], (H, ch))


def shift_rows(value, amount, fill):
    size = value.shape[0]
    rolled = pltpu.roll(value, amount % size, 0)
    row = iota(value.shape, 0)
    have = (row >= amount) if amount > 0 else (row < size + amount)
    return jnp.where(have, rolled, fill)


def scan_rows(decay, value, sign):
    size = value.shape[0]
    amount = 1
    while amount < size:
        value = value + decay * shift_rows(value, sign * amount, 0.0)
        if 2 * amount < size:
            decay = decay * shift_rows(decay, sign * amount, 1.0)
        amount *= 2
    return value


def first_kernel(dims, *refs):
    V, D, hl, ch, nh, ns, T, N = dims
    H, LV, P = nh * hl, nh * hl * V, ch // hl
    C = nh * ch
    count = max(ns, nh)
    refs = list(refs)

    def take(number):
        taken, refs[:] = refs[:number], refs[number:]
        return taken

    packets = take(count)
    projections = take(nh)
    emb, pairs, complement = take(3)
    prenorm2, inproj2, statemap2, stepmap2, bias2, rates2, skip2 = take(7)
    out_state, out_read, out_base, out_scale, out_gate, out_own = take(6)
    tokens, mirrored_ref = take(2)
    mine = lax.axis_index("seq")

    for k in range(ns):
        block = ns - 1 - lax.rem(mine - k + ns, ns)
        tokens[pl.ds(block, 1), :] = packets[k][V : V + 1, 0:T]

    lane = iota((V, LV), 1) // (V * hl)
    start = 2 * ch

    def table(place):
        low, high = start + place * LV, start + (place + 1) * LV
        result = packets[0][0:V, low:high]
        for k in range(1, nh):
            result = jnp.where(lane == k, packets[k][0:V, low:high], result)
        return result

    decay_table, step_table, gain_table = table(0), table(1), table(2)
    log_t = packets[0][V + 8 : V + 8 + H, 0:V]
    for k in range(1, nh):
        log_t = jnp.where(iota((H, V), 0) // hl == k, packets[k][V + 8 : V + 8 + H, 0:V], log_t)
    gates = jnp.concatenate([packets[k][0:V, 0:ch] for k in range(nh)], axis=1)
    inners = jnp.concatenate([packets[k][0:V, ch : 2 * ch] for k in range(nh)], axis=1)
    gains = jnp.concatenate(
        [packets[k][V + 8 : V + 9, LV : LV + ch] for k in range(nh)], axis=1
    )

    token_row = iota((LV, T), 0) % V
    log_split = jnp.concatenate(split3(log_t), axis=1)
    onehots, logs = [], []
    for block in range(ns):
        onehot = (tokens[block : block + 1, :] == token_row.astype(f32)).astype(f32).astype(bf16)
        onehots.append(onehot)
        logs.append(dot(log_split, onehot[0 : 3 * V, :]))
    logs = jnp.concatenate(logs, axis=0)
    first, second = iota((T, T), 0), iota((T, T), 1)
    later = (first > second).astype(f32).astype(bf16)
    sooner = (first < second).astype(f32).astype(bf16)
    logs3 = split3(logs)
    after = dot(logs3[2], later) + dot(logs3[1], later) + dot(logs3[0], later)
    before = dot(logs3[2], sooner) + dot(logs3[1], sooner) + dot(logs3[0], sooner)
    totals = jnp.sum(logs, axis=1, keepdims=True)
    total_rows = jnp.broadcast_to(totals, (ns * H, 128))
    row, column = iota((ns * H, ns * H), 0), iota((ns * H, ns * H), 1)
    row_block, column_block = row // H, column // H
    between = ((row_block < column_block) & (column_block < mine)) | (
        (row_block > column_block) & (column_block > mine)
    )
    between = (between & (row % H == column % H)).astype(f32).astype(bf16)
    gap = dot_left_exact(between, total_rows)[:, 0:1]
    block_of = iota((ns * H, T), 0) // H
    weight_up = jnp.where(block_of < mine, jnp.exp(after + gap), 0.0)
    weight_down = jnp.where(block_of > mine, jnp.exp(before + gap), 0.0)
    entering = jnp.zeros((2 * H, LV), f32)
    for block in range(ns):
        both = jnp.concatenate(
            [weight_up[block * H : (block + 1) * H], weight_down[block * H : (block + 1) * H]],
            axis=0,
        )
        high, low = split2(both)
        entering = entering + (dot(low, onehots[block], NT) + dot(high, onehots[block], NT))
    diagonal = iota((H, LV), 1) // V == iota((H, LV), 0)
    step_row = jnp.sum(step_table, axis=0, keepdims=True)
    enter_up = step_row * jnp.sum(
        jnp.where(diagonal, entering[0:H], 0.0), axis=0, keepdims=True
    )
    enter_down = step_row * jnp.sum(
        jnp.where(diagonal, entering[H : 2 * H], 0.0), axis=0, keepdims=True
    )

    silus = silu(gates)
    looked = jnp.concatenate(
        [decay_table, step_table, pairs[...], gain_table, silus, emb[...]], axis=1
    )
    looked = jnp.concatenate(split3(looked), axis=0)
    token = tokens[pl.ds(mine, 1), :]
    onehot = (token == (iota((3 * V, T), 0) % V).astype(f32)).astype(f32).astype(bf16)
    rows = dot(onehot, looked, TN)
    decay, step = rows[:, 0:LV], rows[:, LV : 2 * LV]
    pair, gain = rows[:, 2 * LV : 3 * LV], rows[:, 3 * LV : 4 * LV]
    silu_rows = rows[:, 4 * LV : 4 * LV + C]
    embedded = rows[:, 4 * LV + C :]

    position = iota((T, LV), 0)
    up = scan_rows(decay, jnp.where(position == 0, step + decay * enter_up, step), 1)
    down = scan_rows(decay, jnp.where(position == T - 1, step + decay * enter_down, step), -1)

    tiled = jnp.concatenate([inners] * H, axis=0)
    spread = jnp.where(iota((LV, C), 0) // V == iota((LV, C), 1) // P, tiled, 0.0)
    spread_high, spread_low = split2(spread)
    half = (iota((C, C), 0) // P == iota((C, C), 1) // P).astype(f32).astype(bf16)

    def gated(coefficients):
        high, low = split2(coefficients * pair + gain)
        value = dot(high, spread_low) + dot(low, spread_high) + dot(high, spread_high)
        value = value * silu_rows
        high, low = split2(value * value)
        square = dot(low, half) + dot(high, half)
        return value * lax.rsqrt(square * (1.0 / P) + epsilon)

    mixed = split2((gated(up) + gated(down)) * gains)
    hidden = embedded
    for k in range(nh):
        part = (mixed[0][:, k * ch : (k + 1) * ch], mixed[1][:, k * ch : (k + 1) * ch])
        hidden = hidden + dot_split(part, split2(projections[k][...]))
    choose = (complement[...] == iota((D, D), 0)).astype(f32).astype(bf16)
    mirrored = dot_right_exact(hidden, choose)
    mirrored_ref[...] = mirrored
    share = T // nh
    out_own[...] = mirrored_ref[pl.ds(pl.multiple_of(lax.axis_index("head") * share, 8), share), :]

    normed = split2(rms(mirrored) * prenorm2[...])
    gate = dot_split(normed, split2(inproj2[pl.ds(0, D, stride=2), :]))
    inner = dot_split(normed, split2(inproj2[pl.ds(1, D, stride=2), :]))
    write = split2(dot_split(normed, split2(statemap2[pl.ds(0, D, stride=2), :])))
    read = dot_split(normed, split2(statemap2[pl.ds(1, D, stride=2), :]))
    out_read[...] = read
    read = split2(read)
    steps = split2(stepmap2[...])
    raw = dot_split(normed, steps, NT)
    raw_t = dot_split(steps, normed, NT)
    of_head = iota((T, ch), 1) // P
    step = jnp.zeros((T, ch), f32)
    log = jnp.zeros((T, ch), f32)
    skip = jnp.zeros((T, ch), f32)
    logs = []
    for head in range(hl):
        column = softplus(raw[:, head : head + 1] + bias2[head])
        here = of_head == head
        step = jnp.where(here, column, step)
        log = jnp.where(here, -rates2[head] * column, log)
        skip = jnp.where(here, skip2[head], skip)
        logs.append(-rates2[head] * softplus(raw_t[head : head + 1, :] + bias2[head]))
    upto = (first >= second).astype(f32).astype(bf16)
    total = dot_left_exact(upto, log)
    logs = jnp.concatenate(logs, axis=0)
    total_t = dot_right_exact(logs, (first <= second).astype(f32).astype(bf16))
    end = total[T - 1 : T, :]
    stepped = inner * step
    state = dot3(stepped * jnp.exp(end - total), write[0].astype(f32) + write[1].astype(f32), TN)
    out_state[0:ch, :] = state
    for head in range(hl):
        out_state[ch + head : ch + head + 1, :] = jnp.broadcast_to(
            end[:, head * P : head * P + 1], (1, state.shape[1])
        )
    products = dot_split(read, write, NT)
    stepped = split2(stepped)
    base = []
    for head in range(hl):
        differ = total[:, head * P : head * P + 1] - total_t[head : head + 1, :]
        allowed = first >= second
        weights = jnp.where(allowed, jnp.exp(jnp.where(allowed, differ, 0.0)), 0.0) * products
        part = (
            stepped[0][:, head * P : (head + 1) * P],
            stepped[1][:, head * P : (head + 1) * P],
        )
        base.append(dot_split(split2(weights), part))
    out_base[...] = jnp.concatenate(base, axis=1) + skip * inner
    out_scale[...] = jnp.exp(total)
    out_gate[...] = silu(gate)


def second_kernel(dims, *refs):
    V, D, hl, ch, nh, ns, T, N = dims
    P = ch // hl
    refs = list(refs)

    def take(number):
        taken, refs[:] = refs[:number], refs[number:]
        return taken

    states = take(ns - 1)
    read, base, scale, gate, own, outnorm, outproj = take(7)
    outs = take(nh)
    (partial_ref,) = take(1)
    entering = states[0][0:ch, :]
    if ns > 2:
        head_of = iota((ch, N), 0) // P

        def rows(values):
            result = jnp.broadcast_to(values[0:1, :], (ch, N))
            for head in range(1, hl):
                result = jnp.where(head_of == head, values[head : head + 1, :], result)
            return result

        logs = states[0][ch : ch + 8, :]
        for k in range(1, ns - 1):
            entering = entering + rows(jnp.exp(logs)) * states[k][0:ch, :]
            logs = logs + states[k][ch : ch + 8, :]
    value = (base[...] + dot3(read[...], entering, NT) * scale[...]) * gate[...]
    half = (iota((ch, ch), 0) // P == iota((ch, ch), 1) // P).astype(f32).astype(bf16)
    high, low = split2(value * value)
    square = dot(low, half) + dot(high, half)
    value = value * lax.rsqrt(square * (1.0 / P) + epsilon) * outnorm[...]
    partial_ref[...] = dot3(value, outproj[...])
    share = T // nh
    mine = lax.axis_index("head")
    for k in range(nh):
        place = pl.multiple_of(lax.rem(mine + k, nh) * share, 8)
        part = partial_ref[pl.ds(place, share), :]
        outs[k][...] = part + own[...] if k == 0 else part


def per_device(
    token_ids,
    embedding,
    complement,
    prenorm_first,
    inproj_first,
    statemap_first,
    stepmap_first,
    stepbias_first,
    rates_first,
    skipgain_first,
    outnorm_first,
    outproj_first,
    prenorm_second,
    inproj_second,
    statemap_second,
    stepmap_second,
    stepbias_second,
    rates_second,
    skipgain_second,
    outnorm_second,
    outproj_second,
):
    nh, ns = lax.axis_size("head"), lax.axis_size("seq")
    V, D = embedding.shape
    ch = inproj_first.shape[2]
    hl = stepmap_first.shape[1]
    N = statemap_first.shape[2]
    T = token_ids.shape[0]
    H, LV = nh * hl, nh * hl * V
    dims = (V, D, hl, ch, nh, ns, T, N)
    vmem = pl.BlockSpec(memory_space=pltpu.VMEM)
    smem = pl.BlockSpec(memory_space=pltpu.SMEM)
    params = pltpu.CompilerParams(vmem_limit_bytes=LIMIT)

    def line(value):
        return value.reshape(1, -1)

    def flat(value):
        return value.reshape(-1, value.shape[-1])

    projections = [outproj_first]
    for k in range(1, nh):
        pairs = [(source, (source + k) % nh) for source in range(nh)]
        projections.append(lax.ppermute(outproj_first, "head", pairs))

    width = max(2 * ch + 3 * LV, T, LV + ch)
    packet, pair_table = pl.pallas_call(
        functools.partial(tables_kernel, dims),
        out_shape=(
            jax.ShapeDtypeStruct((V + 8 + H, width), f32),
            jax.ShapeDtypeStruct((V, LV), f32),
        ),
        in_specs=[vmem] * 6 + [smem] * 3 + [vmem],
        out_specs=(vmem, vmem),
        compiler_params=params,
        name="tables",
    )(
        line(token_ids),
        embedding,
        line(prenorm_first),
        flat(inproj_first),
        flat(statemap_first),
        stepmap_first.T,
        stepbias_first,
        rates_first,
        skipgain_first,
        line(outnorm_first),
    )
    packets = [packet]
    for k in range(1, max(ns, nh)):
        pairs = [
            (seq * nh + head, ((seq + k) % ns) * nh + (head + k) % nh)
            for seq in range(ns)
            for head in range(nh)
        ]
        packets.append(lax.ppermute(packet, ("seq", "head"), pairs))

    share = T // nh
    state, read, base, scale, gate, own = pl.pallas_call(
        functools.partial(first_kernel, dims),
        out_shape=(
            jax.ShapeDtypeStruct((ch + 8, N), f32),
            jax.ShapeDtypeStruct((T, N), f32),
            jax.ShapeDtypeStruct((T, ch), f32),
            jax.ShapeDtypeStruct((T, ch), f32),
            jax.ShapeDtypeStruct((T, ch), f32),
            jax.ShapeDtypeStruct((share, D), f32),
        ),
        in_specs=[vmem] * (len(packets) + nh + 7) + [smem] * 3,
        out_specs=(vmem,) * 6,
        scratch_shapes=[pltpu.VMEM((max(ns, 8), T), f32), pltpu.VMEM((T, D), f32)],
        compiler_params=params,
        name="first",
    )(
        *packets,
        *projections,
        embedding,
        pair_table,
        line(complement),
        line(prenorm_second),
        flat(inproj_second),
        flat(statemap_second),
        stepmap_second.T,
        stepbias_second,
        rates_second,
        skipgain_second,
    )
    states = []
    for k in range(1, ns):
        states.append(lax.ppermute(state, "seq", [(s, s + k) for s in range(ns - k)]))
    parts = pl.pallas_call(
        functools.partial(second_kernel, dims),
        out_shape=(jax.ShapeDtypeStruct((share, D), f32),) * nh,
        in_specs=[vmem] * (ns - 1 + 7),
        out_specs=(vmem,) * nh,
        scratch_shapes=[pltpu.VMEM((T, D), f32)],
        compiler_params=params,
        name="second",
    )(*states, read, base, scale, gate, own, line(outnorm_second), outproj_second)
    result = parts[0]
    for k in range(1, nh):
        pairs = [(source, (source + k) % nh) for source in range(nh)]
        result = result + lax.ppermute(parts[k], "head", pairs)
    return result


def solution(mesh):
    return jax.shard_map(
        per_device,
        mesh=mesh,
        in_specs=(
            P(("rep", "seq")),
            P(),
            P(),
            P(),
            P(None, None, "head"),
            P(),
            P(None, "head"),
            P("head"),
            P("head"),
            P("head"),
            P("head"),
            P("head", None),
            P(),
            P(None, None, "head"),
            P(),
            P(None, "head"),
            P("head"),
            P("head"),
            P("head"),
            P("head"),
            P("head", None),
        ),
        out_specs=P(("rep", "seq", "head"), None),
        check_vma=False,
    )
```

```python
import functools

import jax
import jax.numpy as jnp
from jax import lax
from jax.experimental import pallas as pl
from jax.experimental.pallas import tpu as pltpu
from jax.sharding import PartitionSpec as P

epsilon = 1e-05
f32 = jnp.float32
bf16 = jnp.bfloat16
LIMIT = 48 * 1024 * 1024

MM = (((1,), (0,)), ((), ()))
NT = (((1,), (1,)), ((), ()))
TN = (((0,), (0,)), ((), ()))


def iota(shape, axis):
    return lax.broadcasted_iota(jnp.int32, shape, axis)


def split2(value):
    high = value.astype(bf16)
    return high, (value - high.astype(f32)).astype(bf16)


def split3(value):
    high = value.astype(bf16)
    rest = value - high.astype(f32)
    middle = rest.astype(bf16)
    return high, middle, (rest - middle.astype(f32)).astype(bf16)


def dot(left, right, dims=MM):
    return lax.dot_general(left, right, dims, preferred_element_type=f32)


def dot_split(left, right, dims=MM):
    return (
        dot(left[0], right[1], dims) + dot(left[1], right[0], dims)
    ) + dot(left[0], right[0], dims)


def dot3(left, right, dims=MM):
    return dot_split(split2(left), split2(right), dims)


def dot_left_exact(left, right, dims=MM):
    high, middle, low = split3(right)
    return (dot(left, low, dims) + dot(left, middle, dims)) + dot(left, high, dims)


def dot_right_exact(left, right, dims=MM):
    high, middle, low = split3(left)
    return (dot(low, right, dims) + dot(middle, right, dims)) + dot(high, right, dims)


def softplus(value):
    return jnp.maximum(value, 0.0) + jnp.log1p(jnp.exp(-jnp.abs(value)))


def silu(value):
    return value / (1.0 + jnp.exp(-value))


def rms(value):
    return value * lax.rsqrt(jnp.mean(value * value, axis=-1, keepdims=True) + epsilon)


def fetch(sources, places, semaphores):
    copies = []
    for number, (source, place) in enumerate(zip(sources, places)):
        copies.append(pltpu.make_async_copy(source, place, semaphores.at[number]))
        copies[-1].start()
    return copies


def tables_kernel(dims, *refs):
    V, D, hl, ch, nh, ns, T, N = dims
    H, LV = nh * hl, nh * hl * V
    refs = list(refs)

    def take(number):
        taken, refs[:] = refs[:number], refs[number:]
        return taken

    sources = take(17)
    outproj_source = take(1)[0]
    message, pairs, small, outproj = take(4)
    places = take(17)
    semaphores = take(1)[0]
    half = ch // 2
    base = V + 2 + 3 * hl
    core = lax.rem(lax.axis_index("seq"), 2)
    copies = fetch(
        sources + [outproj_source],
        places + [outproj],
        semaphores,
    )
    for copy in copies:
        copy.wait()
    message[base : base + half, 0:D] = outproj[pl.ds(pl.multiple_of(core * half, 8), half), :]
    (tok, emb, prenorm, inproj, statemap, stepmap, bias, rates, skip, outnorm) = places[:10]
    (complement, prenorm2, stepmap2, bias2, rates2, skip2, outnorm2) = places[10:]

    normed = split2(rms(emb[...]) * prenorm[...])
    gate = dot_split(normed, split2(inproj[pl.ds(0, D, stride=2), :]))
    inner = dot_split(normed, split2(inproj[pl.ds(1, D, stride=2), :]))
    message[0:V, 0:ch] = gate
    message[0:V, ch : 2 * ch] = inner
    flip = (iota((T, T), 0) + iota((T, T), 1) == T - 1).astype(f32).astype(bf16)
    tokens = jnp.broadcast_to(tok[...].astype(f32), (8, T)).astype(bf16)
    message[V : V + 1, 0:T] = dot(tokens, flip)[0:1]
    message[V + 1 : V + 2, 0:ch] = outnorm[...]
    raw_t = dot_split(split2(stepmap[...]), normed, NT)
    for head in range(hl):
        line = softplus(raw_t[head : head + 1, :] + bias[:, head : head + 1])
        row = V + 2 + head
        message[row : row + 1, 0:V] = line
        message[row + hl : row + hl + 1, 0:V] = -rates[:, head : head + 1] * line
        message[row + 2 * hl : row + 2 * hl + 1, 0:V] = jnp.broadcast_to(
            skip[:, head : head + 1], (1, V)
        )

    write = dot_split(normed, split2(statemap[pl.ds(0, D, stride=2), :]))
    read = dot_split(normed, split2(statemap[pl.ds(1, D, stride=2), :]))
    pairs[...] = dot3(read, jnp.concatenate([write] * H, axis=0), NT)
    small[0:1, 0:D] = complement[...].astype(f32)
    small[1:2, 0:D] = prenorm2[...]
    small[2:3, 0:ch] = outnorm2[...]
    small[8 : 8 + hl, 0:D] = stepmap2[...]
    for place, ref in ((3, bias2), (4, rates2), (5, skip2)):
        small[place : place + 1, 0:hl] = ref[...]


def shift_rows(value, amount, fill):
    size = value.shape[0]
    rolled = pltpu.roll(value, amount % size, 0)
    row = iota(value.shape, 0)
    have = (row >= amount) if amount > 0 else (row < size + amount)
    return jnp.where(have, rolled, fill)


def scan_rows(decay, value, sign):
    size = value.shape[0]
    amount = 1
    while amount < size:
        value = value + decay * shift_rows(value, sign * amount, 0.0)
        if 2 * amount < size:
            decay = decay * shift_rows(decay, sign * amount, 1.0)
        amount *= 2
    return value


def mix_kernel(dims, *refs):
    V, D, hl, ch, nh, ns, T, N = dims
    H, LV, P = nh * hl, nh * hl * V, ch // hl
    C = nh * ch
    refs = list(refs)

    def take(number):
        taken, refs[:] = refs[:number], refs[number:]
        return taken

    packets = take(max(ns, nh))
    emb, pairs = take(2)
    out_high, out_low, out_embedded = take(3)
    tokens = take(1)[0]
    mine = lax.axis_index("seq")

    for k in range(ns):
        block = ns - 1 - lax.rem(mine - k + ns, ns)
        tokens[pl.ds(block, 1), :] = packets[k][V : V + 1, 0:T]

    def rows_of(place):
        low = V + 2 + place * hl
        return jnp.concatenate([packets[k][low : low + hl, 0:V] for k in range(nh)], axis=0)

    step_t, log_t, skip_t = rows_of(0), rows_of(1), rows_of(2)
    spread_heads = (iota((H, LV), 1) // V == iota((H, LV), 0)).astype(f32).astype(bf16)

    def widen(value):
        high, middle, low = split3(value)
        return (dot(low, spread_heads, TN) + dot(middle, spread_heads, TN)) + dot(
            high, spread_heads, TN
        )

    own = iota((V, LV), 1) % V == iota((V, LV), 0)
    decay_table = jnp.exp(widen(log_t))
    step_table = jnp.where(own, widen(step_t), 0.0)
    gain_table = jnp.where(own, widen(skip_t), 0.0)
    gates = jnp.concatenate([packets[k][0:V, 0:ch] for k in range(nh)], axis=1)
    inners = jnp.concatenate([packets[k][0:V, ch : 2 * ch] for k in range(nh)], axis=1)
    gains = jnp.concatenate([packets[k][V + 1 : V + 2, 0:ch] for k in range(nh)], axis=1)

    token_row = (iota((LV, T), 0) % V).astype(f32)
    log_split = jnp.concatenate(split3(log_t), axis=1)
    onehots, logs = [], []
    for block in range(ns):
        onehot = (tokens[block : block + 1, :] == token_row).astype(f32).astype(bf16)
        onehots.append(onehot)
        logs.append(dot(log_split, onehot[0 : 3 * V, :]))
    logs = jnp.concatenate(logs, axis=0)
    first, second = iota((T, T), 0), iota((T, T), 1)
    later = (first > second).astype(f32).astype(bf16)
    sooner = (first < second).astype(f32).astype(bf16)
    logs3 = split3(logs)
    after = dot(logs3[2], later) + dot(logs3[1], later) + dot(logs3[0], later)
    before = dot(logs3[2], sooner) + dot(logs3[1], sooner) + dot(logs3[0], sooner)
    totals = jnp.sum(logs, axis=1, keepdims=True)
    total_rows = jnp.broadcast_to(totals, (ns * H, 128))
    row, column = iota((ns * H, ns * H), 0), iota((ns * H, ns * H), 1)
    row_block, column_block = row // H, column // H
    between = ((row_block < column_block) & (column_block < mine)) | (
        (row_block > column_block) & (column_block > mine)
    )
    between = (between & (row % H == column % H)).astype(f32).astype(bf16)
    gap = dot_left_exact(between, total_rows)[:, 0:1]
    block_of = iota((ns * H, T), 0) // H
    weight_up = jnp.where(block_of < mine, jnp.exp(after + gap), 0.0)
    weight_down = jnp.where(block_of > mine, jnp.exp(before + gap), 0.0)
    entering = jnp.zeros((2 * H, LV), f32)
    for block in range(ns):
        both = jnp.concatenate(
            [weight_up[block * H : (block + 1) * H], weight_down[block * H : (block + 1) * H]],
            axis=0,
        )
        high, low = split2(both)
        entering = entering + (dot(low, onehots[block], NT) + dot(high, onehots[block], NT))
    diagonal = iota((H, LV), 1) // V == iota((H, LV), 0)
    step_row = jnp.sum(step_table, axis=0, keepdims=True)
    enter_up = step_row * jnp.sum(
        jnp.where(diagonal, entering[0:H], 0.0), axis=0, keepdims=True
    )
    enter_down = step_row * jnp.sum(
        jnp.where(diagonal, entering[H : 2 * H], 0.0), axis=0, keepdims=True
    )

    looked = jnp.concatenate(
        [decay_table, step_table, pairs[...], gain_table, silu(gates), emb[...]], axis=1
    )
    looked = jnp.concatenate(split3(looked), axis=0)
    token = tokens[pl.ds(mine, 1), :]
    onehot = (token == (iota((3 * V, T), 0) % V).astype(f32)).astype(f32).astype(bf16)
    rows = dot(onehot, looked, TN)
    decay, step = rows[:, 0:LV], rows[:, LV : 2 * LV]
    pair, gain = rows[:, 2 * LV : 3 * LV], rows[:, 3 * LV : 4 * LV]
    silu_rows = rows[:, 4 * LV : 4 * LV + C]
    out_embedded[...] = rows[:, 4 * LV + C :]

    position = iota((T, LV), 0)
    up = scan_rows(decay, jnp.where(position == 0, step + decay * enter_up, step), 1)
    down = scan_rows(decay, jnp.where(position == T - 1, step + decay * enter_down, step), -1)

    tiled = jnp.concatenate([inners] * H, axis=0)
    spread = jnp.where(iota((LV, C), 0) // V == iota((LV, C), 1) // P, tiled, 0.0)
    spread_high, spread_low = split2(spread)
    group = (iota((C, C), 0) // P == iota((C, C), 1) // P).astype(f32).astype(bf16)

    def gated(coefficients):
        high, low = split2(coefficients * pair + gain)
        value = dot(high, spread_low) + dot(low, spread_high) + dot(high, spread_high)
        value = value * silu_rows
        high, low = split2(value * value)
        square = dot(low, group) + dot(high, group)
        return value * lax.rsqrt(square * (1.0 / P) + epsilon)

    out_high[...], out_low[...] = split2((gated(up) + gated(down)) * gains)


def project_kernel(dims, *refs):
    V, D, hl, ch, nh, ns, T, N = dims
    P = ch // hl
    refs = list(refs)

    def take(number):
        taken, refs[:] = refs[:number], refs[number:]
        return taken

    high, low, embedded, small, outproj = take(5)
    nears = take(nh - 1)
    others = take(nh - 1)
    sources = take(2)
    out_state, out_read, out_write, out_inner, out_stepped, out_gate = take(6)
    out_total, out_total_t, out_own = take(3)
    places = take(2)
    mirrored_ref, semaphores = take(2)
    copies = fetch(sources, places, semaphores)
    inproj2, statemap2 = places
    half = ch // 2
    base = V + 2 + 3 * hl
    mine = lax.axis_index("seq")

    hidden = embedded[...]
    for k in range(1, nh):
        near = nears[k - 1][base : base + half, 0:D]
        other = others[k - 1][base : base + half, 0:D]
        even = lax.rem(mine - k + ns * nh, 2) == 0
        weights = jnp.concatenate(
            [jnp.where(even, near, other), jnp.where(even, other, near)], axis=0
        )
        part = (high[:, k * ch : (k + 1) * ch], low[:, k * ch : (k + 1) * ch])
        hidden = hidden + dot_split(part, split2(weights))
    hidden = hidden + dot_split((high[:, 0:ch], low[:, 0:ch]), split2(outproj[...]))
    choose = (small[0:1, 0:D] == iota((D, D), 0).astype(f32)).astype(f32).astype(bf16)
    mirrored = dot_right_exact(hidden, choose)
    mirrored_ref[...] = mirrored
    share = T // nh
    out_own[...] = mirrored_ref[pl.ds(pl.multiple_of(lax.axis_index("head") * share, 8), share), :]

    normed = split2(rms(mirrored) * small[1:2, 0:D])
    copies[0].wait()
    gate = dot_split(normed, split2(inproj2[pl.ds(0, D, stride=2), :]))
    inner = dot_split(normed, split2(inproj2[pl.ds(1, D, stride=2), :]))
    copies[1].wait()
    write = dot_split(normed, split2(statemap2[pl.ds(0, D, stride=2), :]))
    out_read[...] = dot_split(normed, split2(statemap2[pl.ds(1, D, stride=2), :]))
    out_write[...] = write
    out_inner[...] = inner
    out_gate[...] = silu(gate)
    steps = split2(small[8 : 8 + hl, 0:D])
    raw = dot_split(normed, steps, NT)
    raw_t = dot_split(steps, normed, NT)
    of_head = iota((T, ch), 1) // P
    step = jnp.zeros((T, ch), f32)
    log = jnp.zeros((T, ch), f32)
    logs = []
    for head in range(hl):
        bias2, rates2 = small[3:4, head : head + 1], small[4:5, head : head + 1]
        column = softplus(raw[:, head : head + 1] + bias2)
        here = of_head == head
        step = jnp.where(here, column, step)
        log = jnp.where(here, -rates2 * column, log)
        logs.append(-rates2 * softplus(raw_t[head : head + 1, :] + bias2))
    first, second = iota((T, T), 0), iota((T, T), 1)
    total = dot_left_exact((first >= second).astype(f32).astype(bf16), log)
    logs = jnp.concatenate(logs, axis=0)
    out_total_t[0:hl, :] = dot_right_exact(logs, (first <= second).astype(f32).astype(bf16))
    out_total[...] = total
    end = total[T - 1 : T, :]
    stepped = inner * step
    out_stepped[...] = stepped
    state = dot3(stepped * jnp.exp(end - total), write, TN)
    out_state[0:ch, :] = state
    for head in range(hl):
        out_state[ch + head : ch + head + 1, :] = jnp.broadcast_to(
            end[:, head * P : head * P + 1], (1, N)
        )


def block_kernel(dims, read, write, inner, stepped, total, total_t, small, base):
    V, D, hl, ch, nh, ns, T, N = dims
    P = ch // hl
    products = dot3(read[...], write[...], NT)
    stepped_high, stepped_low = split2(stepped[...])
    allowed = iota((T, T), 0) >= iota((T, T), 1)
    parts = []
    for head in range(hl):
        low, high = head * P, (head + 1) * P
        differ = total[:, low : low + 1] - total_t[head : head + 1, :]
        weights = jnp.where(allowed, jnp.exp(jnp.where(allowed, differ, 0.0)), 0.0) * products
        part = dot_split(split2(weights), (stepped_high[:, low:high], stepped_low[:, low:high]))
        parts.append(part + small[5:6, head : head + 1] * inner[:, low:high])
    base[...] = jnp.concatenate(parts, axis=1)


def state_rows(dims, values):
    V, D, hl, ch, nh, ns, T, N = dims
    head_of = iota((ch, N), 0) // (ch // hl)
    result = jnp.broadcast_to(values[0:1, :], (ch, N))
    for head in range(1, hl):
        result = jnp.where(head_of == head, values[head : head + 1, :], result)
    return result


def join_kernel(dims, bit, total, prefix, came, out_total, out_prefix):
    V, D, hl, ch, nh, ns, T, N = dims
    later = lax.rem(lax.div(lax.axis_index("seq"), 2**bit), 2) == 1
    came_state, came_log = came[0:ch, :], came[ch : ch + hl, :]
    state, log = total[0:ch, :], total[ch : ch + hl, :]
    factor = jnp.exp(state_rows(dims, jnp.where(later, log, came_log)))
    out_total[0:ch, :] = jnp.where(
        later, factor * came_state + state, factor * state + came_state
    )
    out_total[ch : ch + hl, :] = log + came_log
    if prefix is None:
        out_prefix[0:ch, :] = jnp.where(later, came_state, 0.0)
        out_prefix[ch : ch + hl, :] = jnp.where(later, came_log, 0.0)
    else:
        joined = prefix_joined(dims, bit, prefix, came)
        out_prefix[0:ch, :] = joined
        out_prefix[ch : ch + hl, :] = prefix[ch : ch + hl, :] + jnp.where(later, came_log, 0.0)


def prefix_joined(dims, bit, prefix, came):
    V, D, hl, ch, nh, ns, T, N = dims
    later = lax.rem(lax.div(lax.axis_index("seq"), 2**bit), 2) == 1
    factor = jnp.exp(state_rows(dims, prefix[ch : ch + hl, :]))
    return prefix[0:ch, :] + jnp.where(later, factor * came[0:ch, :], 0.0)


def output_kernel(dims, bit, *refs):
    V, D, hl, ch, nh, ns, T, N = dims
    P = ch // hl
    refs = list(refs)

    def take(number):
        taken, refs[:] = refs[:number], refs[number:]
        return taken

    prefix, came, read, base, total, gate, own, small, outproj_source = take(9)
    outs = take(nh)
    partial_ref, outproj, semaphore = take(3)
    copy = pltpu.make_async_copy(outproj_source, outproj, semaphore.at[0])
    copy.start()
    entering = prefix_joined(dims, bit, prefix, came)
    value = (base[...] + dot3(read[...], entering, NT) * jnp.exp(total[...])) * gate[...]
    group = (iota((ch, ch), 0) // P == iota((ch, ch), 1) // P).astype(f32).astype(bf16)
    high, low = split2(value * value)
    square = dot(low, group) + dot(high, group)
    value = value * lax.rsqrt(square * (1.0 / P) + epsilon) * small[2:3, 0:ch]
    copy.wait()
    partial_ref[...] = dot3(value, outproj[...])
    share = T // nh
    mine = lax.axis_index("head")
    for k in range(nh):
        place = pl.multiple_of(lax.rem(mine + k, nh) * share, 8)
        part = partial_ref[pl.ds(place, share), :]
        outs[k][...] = part + own[...] if k == 0 else part


def per_device(
    token_ids,
    embedding,
    complement,
    prenorm_first,
    inproj_first,
    statemap_first,
    stepmap_first,
    stepbias_first,
    rates_first,
    skipgain_first,
    outnorm_first,
    outproj_first,
    prenorm_second,
    inproj_second,
    statemap_second,
    stepmap_second,
    stepbias_second,
    rates_second,
    skipgain_second,
    outnorm_second,
    outproj_second,
):
    nh, ns = lax.axis_size("head"), lax.axis_size("seq")
    V, D = embedding.shape
    ch = inproj_first.shape[2]
    hl = stepmap_first.shape[1]
    N = statemap_first.shape[2]
    T = token_ids.shape[0]
    LV = nh * hl * V
    dims = (V, D, hl, ch, nh, ns, T, N)
    vmem = pl.BlockSpec(memory_space=pltpu.VMEM)
    anywhere = pl.BlockSpec(memory_space=pl.ANY)
    params = pltpu.CompilerParams(vmem_limit_bytes=LIMIT)

    def shape(*sizes, dtype=f32):
        return jax.ShapeDtypeStruct(sizes, dtype)

    def room(value):
        return pltpu.VMEM(value.shape, value.dtype)

    def line(value):
        return value.reshape(1, -1)

    def flat(value):
        return value.reshape(-1, value.shape[-1])

    def cost(flops):
        return pl.CostEstimate(flops=flops, bytes_accessed=4 * T * D, transcendentals=T * D)

    head_rows = V + 2 + 3 * hl
    half = ch // 2
    width = max(2 * ch, T, D)
    fetched = [
        line(token_ids),
        embedding,
        line(prenorm_first),
        flat(inproj_first),
        flat(statemap_first),
        stepmap_first.T,
        line(stepbias_first),
        line(rates_first),
        line(skipgain_first),
        line(outnorm_first),
        line(complement),
        line(prenorm_second),
        stepmap_second.T,
        line(stepbias_second),
        line(rates_second),
        line(skipgain_second),
        line(outnorm_second),
    ]
    message, pair_table, small, own_projection = pl.pallas_call(
        functools.partial(tables_kernel, dims),
        out_shape=(
            shape(head_rows + half, width),
            shape(V, LV),
            shape(16, D),
            shape(ch, D),
        ),
        in_specs=[anywhere] * (len(fetched) + 1),
        out_specs=(vmem,) * 4,
        scratch_shapes=[room(value) for value in fetched]
        + [pltpu.SemaphoreType.DMA((len(fetched) + 1,))],
        name="tables",
    )(*fetched, outproj_first)

    messages = [message]
    for k in range(1, max(ns, nh)):
        pairs = [
            (seq * nh + head, ((seq + k) % ns) * nh + (head + k) % nh)
            for seq in range(ns)
            for head in range(nh)
        ]
        sent = message if k < nh else message[0 : V + 8]
        messages.append(lax.ppermute(sent, ("seq", "head"), pairs))
    swap = [(seq, seq ^ 1) for seq in range(ns)]
    others = [lax.ppermute(messages[k], "seq", swap) for k in range(1, nh)]

    mixed_high, mixed_low, embedded = pl.pallas_call(
        functools.partial(mix_kernel, dims),
        out_shape=(
            shape(T, nh * ch, dtype=bf16),
            shape(T, nh * ch, dtype=bf16),
            shape(T, D),
        ),
        in_specs=[vmem] * (len(messages) + 2),
        out_specs=(vmem,) * 3,
        scratch_shapes=[pltpu.VMEM((max(ns, 8), T), f32)],
        compiler_params=params,
        cost_estimate=cost(6 * T * D * D * 16),
        name="mix",
    )(*messages, embedding, pair_table)

    fetched = [flat(inproj_second), flat(statemap_second)]
    share = T // nh
    state, read, write, inner, stepped, gate, total, total_t, own = pl.pallas_call(
        functools.partial(project_kernel, dims),
        out_shape=(
            shape(ch + 8, N),
            shape(T, N),
            shape(T, N),
            shape(T, ch),
            shape(T, ch),
            shape(T, ch),
            shape(T, ch),
            shape(8, T),
            shape(share, D),
        ),
        in_specs=[vmem] * (5 + 2 * (nh - 1)) + [anywhere] * len(fetched),
        out_specs=(vmem,) * 9,
        scratch_shapes=[room(value) for value in fetched]
        + [pltpu.VMEM((T, D), f32), pltpu.SemaphoreType.DMA((len(fetched),))],
        compiler_params=params,
        name="project",
    )(mixed_high, mixed_low, embedded, small, own_projection, *messages[1:nh], *others, *fetched)

    base = pl.pallas_call(
        functools.partial(block_kernel, dims),
        out_shape=shape(T, ch),
        in_specs=[vmem] * 7,
        out_specs=vmem,
        compiler_params=params,
        cost_estimate=cost(6 * T * D * D * 8),
        name="block",
    )(read, write, inner, stepped, total, total_t, small)

    prefix = None
    bits = ns.bit_length() - 1
    for bit in range(bits):
        came = lax.ppermute(state, "seq", [(seq, seq ^ 2**bit) for seq in range(ns)])
        if bit == bits - 1:
            break
        given = [state] + ([] if prefix is None else [prefix]) + [came]

        def join(bit, known, *refs):
            if known:
                join_kernel(dims, bit, *refs)
            else:
                join_kernel(dims, bit, refs[0], None, *refs[1:])

        state, prefix = pl.pallas_call(
            functools.partial(join, bit, prefix is not None),
            out_shape=(shape(ch + 8, N),) * 2,
            in_specs=[vmem] * len(given),
            out_specs=(vmem,) * 2,
            compiler_params=params,
            name="join",
        )(*given)
    if prefix is None:
        prefix = jnp.zeros_like(state)

    parts = pl.pallas_call(
        functools.partial(output_kernel, dims, bits - 1),
        out_shape=(shape(share, D),) * nh,
        in_specs=[vmem] * 8 + [anywhere],
        out_specs=(vmem,) * nh,
        scratch_shapes=[
            pltpu.VMEM((T, D), f32),
            room(outproj_second),
            pltpu.SemaphoreType.DMA((1,)),
        ],
        compiler_params=params,
        name="output",
    )(prefix, came, read, base, total, gate, own, small, outproj_second)
    result = parts[0]
    for k in range(1, nh):
        pairs = [(source, (source + k) % nh) for source in range(nh)]
        result = result + lax.ppermute(parts[k], "head", pairs)
    return result


def solution(mesh):
    return jax.shard_map(
        per_device,
        mesh=mesh,
        in_specs=(
            P(("rep", "seq")),
            P(),
            P(),
            P(),
            P(None, None, "head"),
            P(),
            P(None, "head"),
            P("head"),
            P("head"),
            P("head"),
            P("head"),
            P("head", None),
            P(),
            P(None, None, "head"),
            P(),
            P(None, "head"),
            P("head"),
            P("head"),
            P("head"),
            P("head"),
            P("head", None),
        ),
        out_specs=P(("rep", "seq", "head"), None),
        check_vma=False,
    )
```

```python
import functools

import jax
import jax.numpy as jnp
from jax import lax
from jax.experimental import pallas as pl
from jax.experimental.pallas import tpu as pltpu
from jax.sharding import PartitionSpec as P

epsilon = 1e-05
f32 = jnp.float32
bf16 = jnp.bfloat16
LIMIT = 48 * 1024 * 1024
TABLES_LIMIT = 60 * 1000 * 1000

MM = (((1,), (0,)), ((), ()))
NT = (((1,), (1,)), ((), ()))
TN = (((0,), (0,)), ((), ()))


def iota(shape, axis):
    return lax.broadcasted_iota(jnp.int32, shape, axis)


def split2(value):
    high = value.astype(bf16)
    return high, (value - high.astype(f32)).astype(bf16)


def split3(value):
    high = value.astype(bf16)
    rest = value - high.astype(f32)
    middle = rest.astype(bf16)
    return high, middle, (rest - middle.astype(f32)).astype(bf16)


def dot(left, right, dims=MM):
    return lax.dot_general(left, right, dims, preferred_element_type=f32)


def dot_split(left, right, dims=MM):
    return (
        dot(left[0], right[1], dims) + dot(left[1], right[0], dims)
    ) + dot(left[0], right[0], dims)


def dot3(left, right, dims=MM):
    return dot_split(split2(left), split2(right), dims)


def dot_left_exact(left, right, dims=MM):
    high, middle, low = split3(right)
    return (dot(left, low, dims) + dot(left, middle, dims)) + dot(left, high, dims)


def dot_right_exact(left, right, dims=MM):
    high, middle, low = split3(left)
    return (dot(low, right, dims) + dot(middle, right, dims)) + dot(high, right, dims)


def softplus(value):
    return jnp.maximum(value, 0.0) + jnp.log1p(jnp.exp(-jnp.abs(value)))


def silu(value):
    return value / (1.0 + jnp.exp(-value))


def rms(value):
    return value * lax.rsqrt(jnp.mean(value * value, axis=-1, keepdims=True) + epsilon)


def fetch(sources, places, semaphores):
    copies = []
    for number, (source, place) in enumerate(zip(sources, places)):
        copies.append(pltpu.make_async_copy(source, place, semaphores.at[number]))
        copies[-1].start()
    return copies


def fetch(sources, places, semaphores):
    copies = []
    for number, (source, place) in enumerate(zip(sources, places)):
        copies.append(pltpu.make_async_copy(source, place, semaphores.at[number]))
        copies[-1].start()
    return copies


def tables_kernel(dims, *refs):
    V, D, hl, ch, nh, ns, T, N = dims
    refs = list(refs)

    def take(number):
        taken, refs[:] = refs[:number], refs[number:]
        return taken

    sources = take(9)
    outproj_source, message = take(2)
    places = take(9)
    semaphores = take(1)[0]
    half = ch // 2
    base = V + 2 + 3 * hl
    core = lax.rem(lax.axis_index("seq"), 2)
    copies = fetch(
        sources + [outproj_source.at[pl.ds(pl.multiple_of(core * half, 8), half), :]],
        places + [message.at[base : base + half, 0:D]],
        semaphores,
    )
    for copy in copies[:9]:
        copy.wait()
    (inproj, tok, emb, prenorm, stepmap, bias, rates, skip, outnorm) = places
    normed = split2(rms(emb[...]) * prenorm[...])
    raw_t = dot_split(split2(stepmap[...]), normed, NT)
    gate = dot_split(normed, split2(inproj[pl.ds(0, D, stride=2), :]))
    inner = dot_split(normed, split2(inproj[pl.ds(1, D, stride=2), :]))
    message[0:V, 0:ch] = gate
    message[0:V, ch : 2 * ch] = inner
    flip = (iota((T, T), 0) + iota((T, T), 1) == T - 1).astype(f32).astype(bf16)
    tokens = jnp.broadcast_to(tok[...].astype(f32), (8, T)).astype(bf16)
    message[V : V + 1, 0:T] = dot(tokens, flip)[0:1]
    message[V + 1 : V + 2, 0:ch] = outnorm[...]
    for head in range(hl):
        line = softplus(raw_t[head : head + 1, :] + bias[:, head : head + 1])
        row = V + 2 + head
        message[row : row + 1, 0:V] = line
        message[row + hl : row + hl + 1, 0:V] = -rates[:, head : head + 1] * line
        message[row + 2 * hl : row + 2 * hl + 1, 0:V] = jnp.broadcast_to(
            skip[:, head : head + 1], (1, V)
        )
    copies[9].wait()


def prepare_kernel(dims, *refs):
    V, D, hl, ch, nh, ns, T, N = dims
    H, P = nh * hl, ch // hl
    refs = list(refs)

    def take(number):
        taken, refs[:] = refs[:number], refs[number:]
        return taken

    emb, prenorm, statemap, complement, outproj = take(5)
    prenorm2, inproj2, statemap2, stepmap2, bias2, rates2, skip2, outnorm2, outproj2 = take(9)
    pairs, small, choose_out, own_high, own_low = take(5)
    state_high, state_low, rest_high, rest_low, out_high, out_low = take(6)
    normed = split2(rms(emb[...]) * prenorm[...])
    write = dot_split(normed, split2(statemap[pl.ds(0, D, stride=2), :]))
    read = dot_split(normed, split2(statemap[pl.ds(1, D, stride=2), :]))
    pairs[...] = dot3(read, jnp.concatenate([write] * H, axis=0), NT)
    own_high[...], own_low[...] = split2(outproj[...])
    choose = (complement[...] == iota((D, D), 0)).astype(f32).astype(bf16)
    choose_out[...] = choose
    gain = jnp.transpose(jnp.broadcast_to(prenorm2[...], (128, D)))

    def weights(values):
        return split2(dot_left_exact(choose, values))

    gain_wide = gain[:, 0:1]
    inner = inproj2[pl.ds(1, D, stride=2), :] * gain_wide
    step = jnp.transpose(
        jnp.concatenate(
            [jnp.broadcast_to(stepmap2[head : head + 1, :], (P, D)) for head in range(hl)], axis=0
        )
    )
    write2 = statemap2[pl.ds(0, D, stride=2), :] * gain_wide
    state_high[...], state_low[...] = weights(
        jnp.concatenate([inner, step * gain_wide, write2], axis=1)
    )
    gate = inproj2[pl.ds(0, D, stride=2), :] * gain_wide
    read2 = statemap2[pl.ds(1, D, stride=2), :] * gain_wide
    rest_high[...], rest_low[...] = weights(jnp.concatenate([gate, read2], axis=1))
    out_gain = jnp.transpose(jnp.broadcast_to(outnorm2[...], (128, ch)))
    out_high[...], out_low[...] = split2(outproj2[...] * out_gain[:, 0:1])
    lane_head = iota((1, ch), 1) // P
    for place, ref in ((0, bias2), (1, rates2), (2, skip2)):
        line = jnp.zeros((1, ch), f32)
        for head in range(hl):
            line = jnp.where(lane_head == head, ref[head], line)
        small[place : place + 1, :] = line


def shift_rows(value, amount, fill):
    size = value.shape[0]
    if amount % 8 == 0:
        empty = jnp.full((abs(amount),) + value.shape[1:], fill, value.dtype)
        if amount > 0:
            return jnp.concatenate([empty, value[: size - amount]], axis=0)
        return jnp.concatenate([value[-amount:], empty], axis=0)
    rolled = pltpu.roll(value, amount % size, 0)
    row = iota(value.shape, 0)
    have = (row >= amount) if amount > 0 else (row < size + amount)
    return jnp.where(have, rolled, fill)


def scan_rows(decay, value, sign):
    size = value.shape[0]
    amount = 1
    while amount < size:
        value = value + decay * shift_rows(value, sign * amount, 0.0)
        if 2 * amount < size:
            decay = decay * shift_rows(decay, sign * amount, 1.0)
        amount *= 2
    return value


def mix_kernel(dims, *refs):
    V, D, hl, ch, nh, ns, T, N = dims
    H, LV, P = nh * hl, nh * hl * V, ch // hl
    C = nh * ch
    refs = list(refs)

    def take(number):
        taken, refs[:] = refs[:number], refs[number:]
        return taken

    packets = take(max(ns, nh))
    emb, pairs = take(2)
    out_high, out_low, out_embedded = take(3)
    tokens = take(1)[0]
    mine = lax.axis_index("seq")

    for k in range(ns):
        block = ns - 1 - lax.rem(mine - k + ns, ns)
        tokens[pl.ds(block, 1), :] = packets[k][V : V + 1, 0:T]

    def rows_of(place):
        low = V + 2 + place * hl
        return jnp.concatenate([packets[k][low : low + hl, 0:V] for k in range(nh)], axis=0)

    step_t, log_t, skip_t = rows_of(0), rows_of(1), rows_of(2)
    spread_heads = (iota((H, LV), 1) // V == iota((H, LV), 0)).astype(f32).astype(bf16)

    def widen(value):
        high, middle, low = split3(value)
        return (dot(low, spread_heads, TN) + dot(middle, spread_heads, TN)) + dot(
            high, spread_heads, TN
        )

    own = iota((V, LV), 1) % V == iota((V, LV), 0)
    decay_table = jnp.exp(widen(log_t))
    step_table = jnp.where(own, widen(step_t), 0.0)
    gain_table = jnp.where(own, widen(skip_t), 0.0)
    gates = jnp.concatenate([packets[k][0:V, 0:ch] for k in range(nh)], axis=1)
    inners = jnp.concatenate([packets[k][0:V, ch : 2 * ch] for k in range(nh)], axis=1)
    gains = jnp.concatenate([packets[k][V + 1 : V + 2, 0:ch] for k in range(nh)], axis=1)

    token_row = (iota((LV, T), 0) % V).astype(f32)
    log_split = jnp.concatenate(split3(log_t), axis=1)
    onehots, logs = [], []
    for block in range(ns):
        onehot = (tokens[block : block + 1, :] == token_row).astype(f32).astype(bf16)
        onehots.append(onehot)
        logs.append(dot(log_split, onehot[0 : 3 * V, :]))
    logs = jnp.concatenate(logs, axis=0)
    first, second = iota((T, T), 0), iota((T, T), 1)
    later = (first > second).astype(f32).astype(bf16)
    sooner = (first < second).astype(f32).astype(bf16)
    logs3 = split3(logs)
    after = dot(logs3[2], later) + dot(logs3[1], later) + dot(logs3[0], later)
    before = dot(logs3[2], sooner) + dot(logs3[1], sooner) + dot(logs3[0], sooner)
    totals = jnp.sum(logs, axis=1, keepdims=True)
    total_rows = jnp.broadcast_to(totals, (ns * H, 128))
    row, column = iota((ns * H, ns * H), 0), iota((ns * H, ns * H), 1)
    row_block, column_block = row // H, column // H
    between = ((row_block < column_block) & (column_block < mine)) | (
        (row_block > column_block) & (column_block > mine)
    )
    between = (between & (row % H == column % H)).astype(f32).astype(bf16)
    gap = dot_left_exact(between, total_rows)[:, 0:1]
    block_of = iota((ns * H, T), 0) // H
    weight_up = jnp.where(block_of < mine, jnp.exp(after + gap), 0.0)
    weight_down = jnp.where(block_of > mine, jnp.exp(before + gap), 0.0)
    entering = jnp.zeros((2 * H, LV), f32)
    for block in range(ns):
        both = jnp.concatenate(
            [weight_up[block * H : (block + 1) * H], weight_down[block * H : (block + 1) * H]],
            axis=0,
        )
        high, low = split2(both)
        entering = entering + (dot(low, onehots[block], NT) + dot(high, onehots[block], NT))
    diagonal = iota((H, LV), 1) // V == iota((H, LV), 0)
    step_row = jnp.sum(step_table, axis=0, keepdims=True)
    enter_up = step_row * jnp.sum(
        jnp.where(diagonal, entering[0:H], 0.0), axis=0, keepdims=True
    )
    enter_down = step_row * jnp.sum(
        jnp.where(diagonal, entering[H : 2 * H], 0.0), axis=0, keepdims=True
    )

    looked = jnp.concatenate(
        [decay_table, step_table, pairs[...], gain_table, silu(gates), emb[...]], axis=1
    )
    looked = jnp.concatenate(split3(looked), axis=0)
    token = tokens[pl.ds(mine, 1), :]
    onehot = (token == (iota((3 * V, T), 0) % V).astype(f32)).astype(f32).astype(bf16)
    rows = dot(onehot, looked, TN)
    decay, step = rows[:, 0:LV], rows[:, LV : 2 * LV]
    pair, gain = rows[:, 2 * LV : 3 * LV], rows[:, 3 * LV : 4 * LV]
    silu_rows = rows[:, 4 * LV : 4 * LV + C]
    out_embedded[...] = rows[:, 4 * LV + C :]

    position = iota((T, LV), 0)
    up = scan_rows(decay, jnp.where(position == 0, step + decay * enter_up, step), 1)
    down = scan_rows(decay, jnp.where(position == T - 1, step + decay * enter_down, step), -1)

    tiled = jnp.concatenate([inners] * H, axis=0)
    spread = jnp.where(iota((LV, C), 0) // V == iota((LV, C), 1) // P, tiled, 0.0)
    spread_high, spread_low = split2(spread)
    both = jnp.concatenate([up * pair + gain, down * pair + gain], axis=0)
    high, low = split2(both)
    value = dot(high, spread_low) + dot(
        jnp.concatenate([low, high], axis=1),
        jnp.concatenate([spread_high, spread_high], axis=0),
    )
    value = value * jnp.concatenate([silu_rows, silu_rows], axis=0)
    wide = max(ch, 256)
    group = (iota((wide, wide), 0) // P == iota((wide, wide), 1) // P).astype(f32).astype(bf16)
    high, low = split2(value * value)
    for start in range(0, C, wide):
        stop = start + wide
        square = dot(low[:, start:stop], group) + dot(high[:, start:stop], group)
        normed = value[:, start:stop] * lax.rsqrt(square * (1.0 / P) + epsilon)
        out_high[:, start:stop], out_low[:, start:stop] = split2(
            (normed[0:T] + normed[T : 2 * T]) * gains[:, start:stop]
        )


def project_kernel(dims, *refs):
    V, D, hl, ch, nh, ns, T, N = dims
    P = ch // hl
    refs = list(refs)

    def take(number):
        taken, refs[:] = refs[:number], refs[number:]
        return taken

    high, low, embedded, small, own_high, own_low, state_high, state_low = take(8)
    nears = take(nh - 1)
    others = take(nh - 1)
    out_state, out_high, out_low, out_scale = take(4)
    out_write, out_inner, out_stepped, out_total = take(4)
    half = ch // 2
    base = V + 2 + 3 * hl
    mine = lax.axis_index("seq")

    pieces = []
    for k in range(1, nh):
        near = nears[k - 1][base : base + half, 0:D]
        other = others[k - 1][base : base + half, 0:D]
        even = lax.rem(mine - k + ns * nh, 2) == 0
        pieces.append(jnp.where(even, near, other))
        pieces.append(jnp.where(even, other, near))
    weights = split2(jnp.concatenate(pieces, axis=0))
    weights = (
        jnp.concatenate([own_high[...], weights[0]], axis=0),
        jnp.concatenate([own_low[...], weights[1]], axis=0),
    )
    hidden = embedded[...] + dot_split((high[...], low[...]), weights)
    split = split2(hidden)
    out_high[...], out_low[...] = split
    scale = lax.rsqrt(jnp.mean(hidden * hidden, axis=-1, keepdims=True) + epsilon)
    out_scale[...] = jnp.broadcast_to(scale, (T, ch))

    rows = dot_split(split, (state_high[...], state_low[...])) * scale
    inner, write = rows[:, 0:ch], rows[:, 2 * ch :]
    step = softplus(rows[:, ch : 2 * ch] + small[0:1, :])
    stepped = inner * step
    upto = (iota((T, T), 0) >= iota((T, T), 1)).astype(f32).astype(bf16)
    total = dot_left_exact(upto, -small[1:2, :] * step)
    end = total[T - 1 : T, :]
    state = dot3(stepped * jnp.exp(end - total), write, TN)
    out_state[0:ch, :] = state
    for head in range(hl):
        out_state[ch + head : ch + head + 1, :] = jnp.broadcast_to(
            end[:, head * P : head * P + 1], (1, N)
        )
    out_write[...] = write
    out_inner[...] = inner
    out_stepped[...] = stepped
    out_total[...] = total


def block_kernel(dims, *refs):
    V, D, hl, ch, nh, ns, T, N = dims
    P = ch // hl
    refs = list(refs)

    def take(number):
        taken, refs[:] = refs[:number], refs[number:]
        return taken

    high, low, scale, write, inner, stepped, total, small, choose = take(9)
    rest_high, rest_low = take(2)
    base, out_read, out_gate, own, hidden_ref = take(5)
    rows = dot_split((high[...], low[...]), (rest_high[...], rest_low[...]))
    out_gate[...] = silu(rows[:, 0:ch] * scale[...])
    read = rows[:, ch:] * scale[...]
    out_read[...] = read
    products = dot3(read, write[...], NT)
    stepped_high, stepped_low = split2(stepped[...])
    select = (iota((8, ch), 1) == iota((8, ch), 0) * P).astype(f32).astype(bf16)
    total_high, total_middle, total_low = split3(total[...])
    total_t = (dot(select, total_low, NT) + dot(select, total_middle, NT)) + dot(
        select, total_high, NT
    )
    allowed = iota((T, T), 0) >= iota((T, T), 1)
    parts = []
    for head in range(hl):
        start, stop = head * P, (head + 1) * P
        differ = total[:, start : start + 1] - total_t[head : head + 1, :]
        weights = jnp.where(allowed, jnp.exp(jnp.where(allowed, differ, 0.0)), 0.0) * products
        part = dot_split(
            split2(weights), (stepped_high[:, start:stop], stepped_low[:, start:stop])
        )
        parts.append(part + small[2:3, start:stop] * inner[:, start:stop])
    base[...] = jnp.concatenate(parts, axis=1)
    share = T // nh
    hidden_ref[...] = high[...].astype(f32) + low[...].astype(f32)
    place = pl.multiple_of(lax.axis_index("head") * share, 8)
    own[...] = dot_right_exact(hidden_ref[pl.ds(place, share), :], choose[...])


def state_rows(dims, values):
    V, D, hl, ch, nh, ns, T, N = dims
    head_of = iota((ch, N), 0) // (ch // hl)
    result = jnp.broadcast_to(values[0:1, :], (ch, N))
    for head in range(1, hl):
        result = jnp.where(head_of == head, values[head : head + 1, :], result)
    return result


def join_kernel(dims, bit, total, prefix, came, out_total, out_prefix):
    V, D, hl, ch, nh, ns, T, N = dims
    later = lax.rem(lax.div(lax.axis_index("seq"), 2**bit), 2) == 1
    came_state, came_log = came[0:ch, :], came[ch : ch + hl, :]
    state, log = total[0:ch, :], total[ch : ch + hl, :]
    factor = jnp.exp(state_rows(dims, jnp.where(later, log, came_log)))
    out_total[0:ch, :] = jnp.where(
        later, factor * came_state + state, factor * state + came_state
    )
    out_total[ch : ch + hl, :] = log + came_log
    if prefix is None:
        out_prefix[0:ch, :] = jnp.where(later, came_state, 0.0)
        out_prefix[ch : ch + hl, :] = jnp.where(later, came_log, 0.0)
    else:
        joined = prefix_joined(dims, bit, prefix, came)
        out_prefix[0:ch, :] = joined
        out_prefix[ch : ch + hl, :] = prefix[ch : ch + hl, :] + jnp.where(later, came_log, 0.0)


def prefix_joined(dims, bit, prefix, came):
    V, D, hl, ch, nh, ns, T, N = dims
    later = lax.rem(lax.div(lax.axis_index("seq"), 2**bit), 2) == 1
    factor = jnp.exp(state_rows(dims, prefix[ch : ch + hl, :]))
    return prefix[0:ch, :] + jnp.where(later, factor * came[0:ch, :], 0.0)


def output_kernel(dims, bit, *refs):
    V, D, hl, ch, nh, ns, T, N = dims
    P = ch // hl
    prefix, came, read, base, total, gate, own, proj_high, proj_low, out = refs
    entering = prefix_joined(dims, bit, prefix, came)
    value = (base[...] + dot3(read[...], entering, NT) * jnp.exp(total[...])) * gate[...]
    group = (iota((ch, ch), 0) // P == iota((ch, ch), 1) // P).astype(f32).astype(bf16)
    high, low = split2(value * value)
    square = dot(low, group) + dot(high, group)
    value = value * lax.rsqrt(square * (1.0 / P) + epsilon)
    share = T // nh
    partial = dot_split(split2(value), (proj_high[...], proj_low[...]))
    out[...] = partial.reshape(nh, share, D)
    mine = lax.axis_index("head")
    out[pl.ds(mine, 1)] = out[pl.ds(mine, 1)] + own[...].reshape(1, share, D)


def per_device(
    token_ids,
    embedding,
    complement,
    prenorm_first,
    inproj_first,
    statemap_first,
    stepmap_first,
    stepbias_first,
    rates_first,
    skipgain_first,
    outnorm_first,
    outproj_first,
    prenorm_second,
    inproj_second,
    statemap_second,
    stepmap_second,
    stepbias_second,
    rates_second,
    skipgain_second,
    outnorm_second,
    outproj_second,
):
    nh, ns = lax.axis_size("head"), lax.axis_size("seq")
    V, D = embedding.shape
    ch = inproj_first.shape[2]
    hl = stepmap_first.shape[1]
    N = statemap_first.shape[2]
    T = token_ids.shape[0]
    LV = nh * hl * V
    dims = (V, D, hl, ch, nh, ns, T, N)
    vmem = pl.BlockSpec(memory_space=pltpu.VMEM)
    smem = pl.BlockSpec(memory_space=pltpu.SMEM)
    anywhere = pl.BlockSpec(memory_space=pl.ANY)
    params = pltpu.CompilerParams(vmem_limit_bytes=LIMIT)

    def shape(*sizes, dtype=f32):
        return jax.ShapeDtypeStruct(sizes, dtype)

    def halves(*sizes):
        return [shape(*sizes, dtype=bf16)] * 2

    def room(value):
        return pltpu.VMEM(value.shape, value.dtype)

    def line(value):
        return value.reshape(1, -1)

    def flat(value):
        return value.reshape(-1, value.shape[-1])

    def cost(flops):
        return pl.CostEstimate(flops=flops, bytes_accessed=4 * T * D, transcendentals=T * D)

    head_rows = V + 2 + 3 * hl
    half = ch // 2
    width = max(2 * ch, T, D)
    share = T // nh
    fetched = [
        flat(inproj_first),
        line(token_ids),
        embedding,
        line(prenorm_first),
        stepmap_first.T,
        line(stepbias_first),
        line(rates_first),
        line(skipgain_first),
        line(outnorm_first),
    ]
    message = pl.pallas_call(
        functools.partial(tables_kernel, dims),
        out_shape=shape(head_rows + half, width),
        in_specs=[anywhere] * (len(fetched) + 1),
        out_specs=vmem,
        scratch_shapes=[room(value) for value in fetched]
        + [pltpu.SemaphoreType.DMA((len(fetched) + 1,))],
        compiler_params=pltpu.CompilerParams(vmem_limit_bytes=TABLES_LIMIT),
        name="tables",
    )(*fetched, outproj_first)

    prepared = [
        embedding,
        line(prenorm_first),
        flat(statemap_first),
        line(complement),
        outproj_first,
        line(prenorm_second),
        flat(inproj_second),
        flat(statemap_second),
        stepmap_second.T,
        stepbias_second,
        rates_second,
        skipgain_second,
        line(outnorm_second),
        outproj_second,
    ]
    (
        pair_table,
        small,
        choose,
        own_high,
        own_low,
        state_high,
        state_low,
        rest_high,
        rest_low,
        proj_high,
        proj_low,
    ) = pl.pallas_call(
        functools.partial(prepare_kernel, dims),
        out_shape=(
            shape(V, LV),
            shape(8, ch),
            shape(D, D, dtype=bf16),
            *halves(ch, D),
            *halves(D, 2 * ch + N),
            *halves(D, ch + N),
            *halves(ch, D),
        ),
        in_specs=[vmem] * 9 + [smem] * 3 + [vmem] * 2,
        out_specs=(vmem,) * 11,
        compiler_params=params,
        cost_estimate=cost(6 * T * D * D * 4),
        name="prepare",
    )(*prepared)

    messages = [message]
    for k in range(1, max(ns, nh)):
        pairs = [
            (seq * nh + head, ((seq + k) % ns) * nh + (head + k) % nh)
            for seq in range(ns)
            for head in range(nh)
        ]
        sent = message if k < nh else message[0:head_rows]
        messages.append(lax.ppermute(sent, ("seq", "head"), pairs))
    swap = [(seq, seq ^ 1) for seq in range(ns)]
    others = [lax.ppermute(messages[k], "seq", swap) for k in range(1, nh)]

    mixed_high, mixed_low, embedded = pl.pallas_call(
        functools.partial(mix_kernel, dims),
        out_shape=(*halves(T, nh * ch), shape(T, D)),
        in_specs=[vmem] * (len(messages) + 2),
        out_specs=(vmem,) * 3,
        scratch_shapes=[pltpu.VMEM((max(ns, 8), T), f32)],
        compiler_params=params,
        cost_estimate=cost(6 * T * D * D * 16),
        name="mix",
    )(*messages, embedding, pair_table)

    state, hidden_high, hidden_low, scale, write, inner, stepped, total = pl.pallas_call(
        functools.partial(project_kernel, dims),
        out_shape=(
            shape(ch + 8, N),
            *halves(T, D),
            shape(T, ch),
            shape(T, N),
            shape(T, ch),
            shape(T, ch),
            shape(T, ch),
        ),
        in_specs=[vmem] * (8 + 2 * (nh - 1)),
        out_specs=(vmem,) * 8,
        compiler_params=params,
        name="project",
    )(
        mixed_high,
        mixed_low,
        embedded,
        small,
        own_high,
        own_low,
        state_high,
        state_low,
        *messages[1:nh],
        *others,
    )

    base, read, gate, own = pl.pallas_call(
        functools.partial(block_kernel, dims),
        out_shape=(shape(T, ch), shape(T, N), shape(T, ch), shape(share, D)),
        in_specs=[vmem] * 11,
        out_specs=(vmem,) * 4,
        scratch_shapes=[pltpu.VMEM((T, D), f32)],
        compiler_params=params,
        cost_estimate=cost(6 * T * D * D * 8),
        name="block",
    )(
        hidden_high,
        hidden_low,
        scale,
        write,
        inner,
        stepped,
        total,
        small,
        choose,
        rest_high,
        rest_low,
    )

    prefix = None
    bits = ns.bit_length() - 1
    for bit in range(bits):
        came = lax.ppermute(state, "seq", [(seq, seq ^ 2**bit) for seq in range(ns)])
        if bit == bits - 1:
            break
        given = [state] + ([] if prefix is None else [prefix]) + [came]

        def join(bit, known, *refs):
            if known:
                join_kernel(dims, bit, *refs)
            else:
                join_kernel(dims, bit, refs[0], None, *refs[1:])

        state, prefix = pl.pallas_call(
            functools.partial(join, bit, prefix is not None),
            out_shape=(shape(ch + 8, N),) * 2,
            in_specs=[vmem] * len(given),
            out_specs=(vmem,) * 2,
            compiler_params=params,
            name="join",
        )(*given)
    if prefix is None:
        prefix = jnp.zeros_like(state)

    parts = pl.pallas_call(
        functools.partial(output_kernel, dims, bits - 1),
        out_shape=shape(nh, share, D),
        in_specs=[vmem] * 9,
        out_specs=vmem,
        compiler_params=params,
        name="output",
    )(prefix, came, read, base, total, gate, own, proj_high, proj_low)
    parts = lax.all_to_all(parts, "head", 0, 0, tiled=True)
    return jnp.sum(parts, axis=0)


def solution(mesh):
    return jax.shard_map(
        per_device,
        mesh=mesh,
        in_specs=(
            P(("rep", "seq")),
            P(),
            P(),
            P(),
            P(None, None, "head"),
            P(),
            P(None, "head"),
            P("head"),
            P("head"),
            P("head"),
            P("head"),
            P("head", None),
            P(),
            P(None, None, "head"),
            P(),
            P(None, "head"),
            P("head"),
            P("head"),
            P("head"),
            P("head"),
            P("head", None),
        ),
        out_specs=P(("rep", "seq", "head"), None),
        check_vma=False,
    )
```

```python
import functools

import jax
import jax.numpy as jnp
from jax import lax
from jax.experimental import pallas as pl
from jax.experimental.pallas import tpu as pltpu
from jax.sharding import PartitionSpec as P

epsilon = 1e-05
f32 = jnp.float32
bf16 = jnp.bfloat16
LIMIT = 48 * 1024 * 1024
TABLES_LIMIT = 60 * 1000 * 1000

MM = (((1,), (0,)), ((), ()))
NT = (((1,), (1,)), ((), ()))
TN = (((0,), (0,)), ((), ()))


def iota(shape, axis):
    return lax.broadcasted_iota(jnp.int32, shape, axis)


def split2(value):
    high = value.astype(bf16)
    return high, (value - high.astype(f32)).astype(bf16)


def split3(value):
    high = value.astype(bf16)
    rest = value - high.astype(f32)
    middle = rest.astype(bf16)
    return high, middle, (rest - middle.astype(f32)).astype(bf16)


def dot(left, right, dims=MM):
    return lax.dot_general(left, right, dims, preferred_element_type=f32)


def dot_split(left, right, dims=MM):
    return (
        dot(left[0], right[1], dims) + dot(left[1], right[0], dims)
    ) + dot(left[0], right[0], dims)


def dot3(left, right, dims=MM):
    return dot_split(split2(left), split2(right), dims)


def dot_left_exact(left, right, dims=MM):
    high, middle, low = split3(right)
    return (dot(left, low, dims) + dot(left, middle, dims)) + dot(left, high, dims)


def dot_right_exact(left, right, dims=MM):
    high, middle, low = split3(left)
    return (dot(low, right, dims) + dot(middle, right, dims)) + dot(high, right, dims)


def softplus(value):
    return jnp.maximum(value, 0.0) + jnp.log1p(jnp.exp(-jnp.abs(value)))


def silu(value):
    return value / (1.0 + jnp.exp(-value))


def rms(value):
    return value * lax.rsqrt(jnp.mean(value * value, axis=-1, keepdims=True) + epsilon)


def fetch(sources, places, semaphores):
    copies = []
    for number, (source, place) in enumerate(zip(sources, places)):
        copies.append(pltpu.make_async_copy(source, place, semaphores.at[number]))
        copies[-1].start()
    return copies


def fetch(sources, places, semaphores):
    copies = []
    for number, (source, place) in enumerate(zip(sources, places)):
        copies.append(pltpu.make_async_copy(source, place, semaphores.at[number]))
        copies[-1].start()
    return copies


def tables_kernel(dims, *refs):
    V, D, hl, ch, nh, ns, T, N = dims
    refs = list(refs)

    def take(number):
        taken, refs[:] = refs[:number], refs[number:]
        return taken

    sources = take(9)
    outproj_source, message = take(2)
    places = take(9)
    semaphores = take(1)[0]
    half = ch // 2
    base = V + 2 + 3 * hl
    core = lax.rem(lax.axis_index("seq"), 2)
    copies = fetch(
        sources + [outproj_source.at[pl.ds(pl.multiple_of(core * half, 8), half), :]],
        places + [message.at[base : base + half, 0:D]],
        semaphores,
    )
    for copy in copies[:9]:
        copy.wait()
    (inproj, tok, emb, prenorm, stepmap, bias, rates, skip, outnorm) = places
    normed = split2(rms(emb[...]) * prenorm[...])
    raw_t = dot_split(split2(stepmap[...]), normed, NT)
    gate = dot_split(normed, split2(inproj[pl.ds(0, D, stride=2), :]))
    inner = dot_split(normed, split2(inproj[pl.ds(1, D, stride=2), :]))
    message[0:V, 0:ch] = gate
    message[0:V, ch : 2 * ch] = inner
    flip = (iota((T, T), 0) + iota((T, T), 1) == T - 1).astype(f32).astype(bf16)
    tokens = jnp.broadcast_to(tok[...].astype(f32), (8, T)).astype(bf16)
    message[V : V + 1, 0:T] = dot(tokens, flip)[0:1]
    message[V + 1 : V + 2, 0:ch] = outnorm[...]
    for head in range(hl):
        line = softplus(raw_t[head : head + 1, :] + bias[:, head : head + 1])
        row = V + 2 + head
        message[row : row + 1, 0:V] = line
        message[row + hl : row + hl + 1, 0:V] = -rates[:, head : head + 1] * line
        message[row + 2 * hl : row + 2 * hl + 1, 0:V] = jnp.broadcast_to(
            skip[:, head : head + 1], (1, V)
        )
    copies[9].wait()


def prepare_kernel(dims, *refs):
    V, D, hl, ch, nh, ns, T, N = dims
    H, P = nh * hl, ch // hl
    refs = list(refs)

    def take(number):
        taken, refs[:] = refs[:number], refs[number:]
        return taken

    emb, prenorm, statemap, complement, outproj = take(5)
    prenorm2, inproj2, statemap2, stepmap2, bias2, rates2, skip2, outnorm2, outproj2 = take(9)
    pairs, small, choose_out, own_high, own_low = take(5)
    state_high, state_low, rest_high, rest_low, out_high, out_low = take(6)
    normed = split2(rms(emb[...]) * prenorm[...])
    write = dot_split(normed, split2(statemap[pl.ds(0, D, stride=2), :]))
    read = dot_split(normed, split2(statemap[pl.ds(1, D, stride=2), :]))
    pairs[...] = dot3(read, jnp.concatenate([write] * H, axis=0), NT)
    own_high[...], own_low[...] = split2(outproj[...])
    choose = (complement[...] == iota((D, D), 0)).astype(f32).astype(bf16)
    choose_out[...] = choose
    gain = jnp.transpose(jnp.broadcast_to(prenorm2[...], (128, D)))

    def weights(values):
        return split2(dot_left_exact(choose, values))

    gain_wide = gain[:, 0:1]
    inner = inproj2[pl.ds(1, D, stride=2), :] * gain_wide
    step = jnp.transpose(
        jnp.concatenate(
            [jnp.broadcast_to(stepmap2[head : head + 1, :], (P, D)) for head in range(hl)], axis=0
        )
    )
    write2 = statemap2[pl.ds(0, D, stride=2), :] * gain_wide
    state_high[...], state_low[...] = weights(
        jnp.concatenate([inner, step * gain_wide, write2], axis=1)
    )
    gate = inproj2[pl.ds(0, D, stride=2), :] * gain_wide
    read2 = statemap2[pl.ds(1, D, stride=2), :] * gain_wide
    rest_high[...], rest_low[...] = weights(jnp.concatenate([gate, read2], axis=1))
    out_gain = jnp.transpose(jnp.broadcast_to(outnorm2[...], (128, ch)))
    out_high[...], out_low[...] = split2(outproj2[...] * out_gain[:, 0:1])
    lane_head = iota((1, ch), 1) // P
    for place, ref in ((0, bias2), (1, rates2), (2, skip2)):
        line = jnp.zeros((1, ch), f32)
        for head in range(hl):
            line = jnp.where(lane_head == head, ref[head], line)
        small[place : place + 1, :] = line


def shift_rows(value, amount, fill):
    size = value.shape[0]
    if amount % 8 == 0:
        empty = jnp.full((abs(amount),) + value.shape[1:], fill, value.dtype)
        if amount > 0:
            return jnp.concatenate([empty, value[: size - amount]], axis=0)
        return jnp.concatenate([value[-amount:], empty], axis=0)
    rolled = pltpu.roll(value, amount % size, 0)
    row = iota(value.shape, 0)
    have = (row >= amount) if amount > 0 else (row < size + amount)
    return jnp.where(have, rolled, fill)


def scan_rows(decay, value, sign):
    size = value.shape[0]
    amount = 1
    while amount < size:
        value = value + decay * shift_rows(value, sign * amount, 0.0)
        if 2 * amount < size:
            decay = decay * shift_rows(decay, sign * amount, 1.0)
        amount *= 2
    return value


def mix_kernel(dims, *refs):
    V, D, hl, ch, nh, ns, T, N = dims
    H, LV, P = nh * hl, nh * hl * V, ch // hl
    C = nh * ch
    refs = list(refs)

    def take(number):
        taken, refs[:] = refs[:number], refs[number:]
        return taken

    packets = take(max(ns, nh))[::-1]
    emb, pairs = take(2)
    out_high, out_low, out_embedded = take(3)
    tokens = take(1)[0]
    mine = lax.axis_index("seq")

    for k in range(ns):
        block = ns - 1 - lax.rem(mine - k + ns, ns)
        tokens[pl.ds(block, 1), :] = packets[k][V : V + 1, 0:T]

    def rows_of(place):
        low = V + 2 + place * hl
        return jnp.concatenate([packets[k][low : low + hl, 0:V] for k in range(nh)], axis=0)

    step_t, log_t, skip_t = rows_of(0), rows_of(1), rows_of(2)
    spread_heads = (iota((H, LV), 1) // V == iota((H, LV), 0)).astype(f32).astype(bf16)

    def widen(value):
        high, middle, low = split3(value)
        return (dot(low, spread_heads, TN) + dot(middle, spread_heads, TN)) + dot(
            high, spread_heads, TN
        )

    own = iota((V, LV), 1) % V == iota((V, LV), 0)
    decay_table = jnp.exp(widen(log_t))
    step_table = jnp.where(own, widen(step_t), 0.0)
    gain_table = jnp.where(own, widen(skip_t), 0.0)
    gates = jnp.concatenate([packets[k][0:V, 0:ch] for k in range(nh)], axis=1)
    inners = jnp.concatenate([packets[k][0:V, ch : 2 * ch] for k in range(nh)], axis=1)
    gains = jnp.concatenate([packets[k][V + 1 : V + 2, 0:ch] for k in range(nh)], axis=1)

    token_row = (iota((LV, T), 0) % V).astype(f32)
    log_split = jnp.concatenate(split3(log_t), axis=1)
    onehots, logs = [], []
    for block in range(ns):
        onehot = (tokens[block : block + 1, :] == token_row).astype(f32).astype(bf16)
        onehots.append(onehot)
        logs.append(dot(log_split, onehot[0 : 3 * V, :]))
    logs = jnp.concatenate(logs, axis=0)
    first, second = iota((T, T), 0), iota((T, T), 1)
    later = (first > second).astype(f32).astype(bf16)
    sooner = (first < second).astype(f32).astype(bf16)
    logs3 = split3(logs)
    after = dot(logs3[2], later) + dot(logs3[1], later) + dot(logs3[0], later)
    before = dot(logs3[2], sooner) + dot(logs3[1], sooner) + dot(logs3[0], sooner)
    totals = jnp.sum(logs, axis=1, keepdims=True)
    total_rows = jnp.broadcast_to(totals, (ns * H, 128))
    row, column = iota((ns * H, ns * H), 0), iota((ns * H, ns * H), 1)
    row_block, column_block = row // H, column // H
    between = ((row_block < column_block) & (column_block < mine)) | (
        (row_block > column_block) & (column_block > mine)
    )
    between = (between & (row % H == column % H)).astype(f32).astype(bf16)
    gap = dot_left_exact(between, total_rows)[:, 0:1]
    block_of = iota((ns * H, T), 0) // H
    weight_up = jnp.where(block_of < mine, jnp.exp(after + gap), 0.0)
    weight_down = jnp.where(block_of > mine, jnp.exp(before + gap), 0.0)
    entering = jnp.zeros((2 * H, LV), f32)
    for block in range(ns):
        both = jnp.concatenate(
            [weight_up[block * H : (block + 1) * H], weight_down[block * H : (block + 1) * H]],
            axis=0,
        )
        high, low = split2(both)
        entering = entering + (dot(low, onehots[block], NT) + dot(high, onehots[block], NT))
    diagonal = iota((H, LV), 1) // V == iota((H, LV), 0)
    step_row = jnp.sum(step_table, axis=0, keepdims=True)
    enter_up = step_row * jnp.sum(
        jnp.where(diagonal, entering[0:H], 0.0), axis=0, keepdims=True
    )
    enter_down = step_row * jnp.sum(
        jnp.where(diagonal, entering[H : 2 * H], 0.0), axis=0, keepdims=True
    )

    looked = jnp.concatenate(
        [decay_table, step_table, pairs[...], gain_table, silu(gates), emb[...]], axis=1
    )
    looked = jnp.concatenate(split3(looked), axis=0)
    token = tokens[pl.ds(mine, 1), :]
    onehot = (token == (iota((3 * V, T), 0) % V).astype(f32)).astype(f32).astype(bf16)
    rows = dot(onehot, looked, TN)
    decay, step = rows[:, 0:LV], rows[:, LV : 2 * LV]
    pair, gain = rows[:, 2 * LV : 3 * LV], rows[:, 3 * LV : 4 * LV]
    silu_rows = rows[:, 4 * LV : 4 * LV + C]
    out_embedded[...] = rows[:, 4 * LV + C :]

    position = iota((T, LV), 0)
    up = scan_rows(decay, jnp.where(position == 0, step + decay * enter_up, step), 1)
    down = scan_rows(decay, jnp.where(position == T - 1, step + decay * enter_down, step), -1)

    tiled = jnp.concatenate([inners] * H, axis=0)
    spread = jnp.where(iota((LV, C), 0) // V == iota((LV, C), 1) // P, tiled, 0.0)
    spread_high, spread_low = split2(spread)
    both = jnp.concatenate([up * pair + gain, down * pair + gain], axis=0)
    high, low = split2(both)
    value = dot(high, spread_low) + dot(
        jnp.concatenate([low, high], axis=1),
        jnp.concatenate([spread_high, spread_high], axis=0),
    )
    value = value * jnp.concatenate([silu_rows, silu_rows], axis=0)
    wide = max(ch, 256)
    group = (iota((wide, wide), 0) // P == iota((wide, wide), 1) // P).astype(f32).astype(bf16)
    high, low = split2(value * value)
    for start in range(0, C, wide):
        stop = start + wide
        square = dot(low[:, start:stop], group) + dot(high[:, start:stop], group)
        normed = value[:, start:stop] * lax.rsqrt(square * (1.0 / P) + epsilon)
        out_high[:, start:stop], out_low[:, start:stop] = split2(
            (normed[0:T] + normed[T : 2 * T]) * gains[:, start:stop]
        )


def project_kernel(dims, *refs):
    V, D, hl, ch, nh, ns, T, N = dims
    P = ch // hl
    refs = list(refs)

    def take(number):
        taken, refs[:] = refs[:number], refs[number:]
        return taken

    high, low, embedded, small, own_high, own_low, state_high, state_low = take(8)
    nears = take(nh - 1)[::-1]
    others = take(nh - 1)[::-1]
    out_state, out_high, out_low, out_scale = take(4)
    out_write, out_inner, out_stepped, out_total = take(4)
    half = ch // 2
    base = V + 2 + 3 * hl
    mine = lax.axis_index("seq")

    pieces = []
    for k in range(1, nh):
        near = nears[k - 1][base : base + half, 0:D]
        other = others[k - 1][base : base + half, 0:D]
        even = lax.rem(mine - k + ns * nh, 2) == 0
        pieces.append(jnp.where(even, near, other))
        pieces.append(jnp.where(even, other, near))
    weights = split2(jnp.concatenate(pieces, axis=0))
    weights = (
        jnp.concatenate([own_high[...], weights[0]], axis=0),
        jnp.concatenate([own_low[...], weights[1]], axis=0),
    )
    hidden = embedded[...] + dot_split((high[...], low[...]), weights)
    split = split2(hidden)
    out_high[...], out_low[...] = split
    scale = lax.rsqrt(jnp.mean(hidden * hidden, axis=-1, keepdims=True) + epsilon)
    out_scale[...] = jnp.broadcast_to(scale, (T, ch))

    rows = dot_split(split, (state_high[...], state_low[...])) * scale
    inner, write = rows[:, 0:ch], rows[:, 2 * ch :]
    step = softplus(rows[:, ch : 2 * ch] + small[0:1, :])
    stepped = inner * step
    upto = (iota((T, T), 0) >= iota((T, T), 1)).astype(f32).astype(bf16)
    total = dot_left_exact(upto, -small[1:2, :] * step)
    end = total[T - 1 : T, :]
    state = dot3(stepped * jnp.exp(end - total), write, TN)
    out_state[0:ch, :] = state
    for head in range(hl):
        out_state[ch + head : ch + head + 1, :] = jnp.broadcast_to(
            end[:, head * P : head * P + 1], (1, N)
        )
    out_write[...] = write
    out_inner[...] = inner
    out_stepped[...] = stepped
    out_total[...] = total


def block_kernel(dims, *refs):
    V, D, hl, ch, nh, ns, T, N = dims
    P = ch // hl
    refs = list(refs)

    def take(number):
        taken, refs[:] = refs[:number], refs[number:]
        return taken

    high, low, scale, write, inner, stepped, total, small, choose = take(9)
    rest_high, rest_low = take(2)
    base, out_read, out_gate, own, hidden_ref = take(5)
    rows = dot_split((high[...], low[...]), (rest_high[...], rest_low[...]))
    out_gate[...] = silu(rows[:, 0:ch] * scale[...])
    read = rows[:, ch:] * scale[...]
    out_read[...] = read
    products = dot3(read, write[...], NT)
    stepped_high, stepped_low = split2(stepped[...])
    select = (iota((8, ch), 1) == iota((8, ch), 0) * P).astype(f32).astype(bf16)
    total_high, total_middle, total_low = split3(total[...])
    total_t = (dot(select, total_low, NT) + dot(select, total_middle, NT)) + dot(
        select, total_high, NT
    )
    allowed = iota((T, T), 0) >= iota((T, T), 1)
    parts = []
    for head in range(hl):
        start, stop = head * P, (head + 1) * P
        differ = total[:, start : start + 1] - total_t[head : head + 1, :]
        weights = jnp.where(allowed, jnp.exp(jnp.where(allowed, differ, 0.0)), 0.0) * products
        part = dot_split(
            split2(weights), (stepped_high[:, start:stop], stepped_low[:, start:stop])
        )
        parts.append(part + small[2:3, start:stop] * inner[:, start:stop])
    base[...] = jnp.concatenate(parts, axis=1)
    share = T // nh
    hidden_ref[...] = high[...].astype(f32) + low[...].astype(f32)
    place = pl.multiple_of(lax.axis_index("head") * share, 8)
    own[...] = dot_right_exact(hidden_ref[pl.ds(place, share), :], choose[...])


def state_rows(dims, values):
    V, D, hl, ch, nh, ns, T, N = dims
    head_of = iota((ch, N), 0) // (ch // hl)
    result = jnp.broadcast_to(values[0:1, :], (ch, N))
    for head in range(1, hl):
        result = jnp.where(head_of == head, values[head : head + 1, :], result)
    return result


def join_kernel(dims, bit, total, prefix, came, out_total, out_prefix):
    V, D, hl, ch, nh, ns, T, N = dims
    later = lax.rem(lax.div(lax.axis_index("seq"), 2**bit), 2) == 1
    came_state, came_log = came[0:ch, :], came[ch : ch + hl, :]
    state, log = total[0:ch, :], total[ch : ch + hl, :]
    factor = jnp.exp(state_rows(dims, jnp.where(later, log, came_log)))
    out_total[0:ch, :] = jnp.where(
        later, factor * came_state + state, factor * state + came_state
    )
    out_total[ch : ch + hl, :] = log + came_log
    if prefix is None:
        out_prefix[0:ch, :] = jnp.where(later, came_state, 0.0)
        out_prefix[ch : ch + hl, :] = jnp.where(later, came_log, 0.0)
    else:
        joined = prefix_joined(dims, bit, prefix, came)
        out_prefix[0:ch, :] = joined
        out_prefix[ch : ch + hl, :] = prefix[ch : ch + hl, :] + jnp.where(later, came_log, 0.0)


def prefix_joined(dims, bit, prefix, came):
    V, D, hl, ch, nh, ns, T, N = dims
    later = lax.rem(lax.div(lax.axis_index("seq"), 2**bit), 2) == 1
    factor = jnp.exp(state_rows(dims, prefix[ch : ch + hl, :]))
    return prefix[0:ch, :] + jnp.where(later, factor * came[0:ch, :], 0.0)


def output_kernel(dims, bit, *refs):
    V, D, hl, ch, nh, ns, T, N = dims
    P = ch // hl
    prefix, came, read, base, total, gate, own, proj_high, proj_low = refs[:9]
    outs, partial_ref = refs[9 : 9 + nh], refs[9 + nh]
    entering = prefix_joined(dims, bit, prefix, came)
    value = (base[...] + dot3(read[...], entering, NT) * jnp.exp(total[...])) * gate[...]
    group = (iota((ch, ch), 0) // P == iota((ch, ch), 1) // P).astype(f32).astype(bf16)
    high, low = split2(value * value)
    square = dot(low, group) + dot(high, group)
    value = value * lax.rsqrt(square * (1.0 / P) + epsilon)
    share = T // nh
    partial_ref[...] = dot_split(split2(value), (proj_high[...], proj_low[...]))
    mine = lax.axis_index("head")
    for k in range(nh):
        place = pl.multiple_of(lax.rem(mine + k, nh) * share, 8)
        part = partial_ref[pl.ds(place, share), :]
        outs[k][...] = part + own[...] if k == 0 else part


def per_device(
    token_ids,
    embedding,
    complement,
    prenorm_first,
    inproj_first,
    statemap_first,
    stepmap_first,
    stepbias_first,
    rates_first,
    skipgain_first,
    outnorm_first,
    outproj_first,
    prenorm_second,
    inproj_second,
    statemap_second,
    stepmap_second,
    stepbias_second,
    rates_second,
    skipgain_second,
    outnorm_second,
    outproj_second,
):
    nh, ns = lax.axis_size("head"), lax.axis_size("seq")
    V, D = embedding.shape
    ch = inproj_first.shape[2]
    hl = stepmap_first.shape[1]
    N = statemap_first.shape[2]
    T = token_ids.shape[0]
    LV = nh * hl * V
    dims = (V, D, hl, ch, nh, ns, T, N)
    vmem = pl.BlockSpec(memory_space=pltpu.VMEM)
    smem = pl.BlockSpec(memory_space=pltpu.SMEM)
    anywhere = pl.BlockSpec(memory_space=pl.ANY)
    params = pltpu.CompilerParams(vmem_limit_bytes=LIMIT)

    def shape(*sizes, dtype=f32):
        return jax.ShapeDtypeStruct(sizes, dtype)

    def halves(*sizes):
        return [shape(*sizes, dtype=bf16)] * 2

    def room(value):
        return pltpu.VMEM(value.shape, value.dtype)

    def line(value):
        return value.reshape(1, -1)

    def flat(value):
        return value.reshape(-1, value.shape[-1])

    def cost(flops):
        return pl.CostEstimate(flops=flops, bytes_accessed=4 * T * D, transcendentals=T * D)

    head_rows = V + 2 + 3 * hl
    half = ch // 2
    width = max(2 * ch, T, D)
    share = T // nh
    fetched = [
        flat(inproj_first),
        line(token_ids),
        embedding,
        line(prenorm_first),
        stepmap_first.T,
        line(stepbias_first),
        line(rates_first),
        line(skipgain_first),
        line(outnorm_first),
    ]
    message = pl.pallas_call(
        functools.partial(tables_kernel, dims),
        out_shape=shape(head_rows + half, width),
        in_specs=[anywhere] * (len(fetched) + 1),
        out_specs=vmem,
        scratch_shapes=[room(value) for value in fetched]
        + [pltpu.SemaphoreType.DMA((len(fetched) + 1,))],
        compiler_params=pltpu.CompilerParams(vmem_limit_bytes=TABLES_LIMIT),
        name="tables",
    )(*fetched, outproj_first)

    prepared = [
        embedding,
        line(prenorm_first),
        flat(statemap_first),
        line(complement),
        outproj_first,
        line(prenorm_second),
        flat(inproj_second),
        flat(statemap_second),
        stepmap_second.T,
        stepbias_second,
        rates_second,
        skipgain_second,
        line(outnorm_second),
        outproj_second,
    ]
    (
        pair_table,
        small,
        choose,
        own_high,
        own_low,
        state_high,
        state_low,
        rest_high,
        rest_low,
        proj_high,
        proj_low,
    ) = pl.pallas_call(
        functools.partial(prepare_kernel, dims),
        out_shape=(
            shape(V, LV),
            shape(8, ch),
            shape(D, D, dtype=bf16),
            *halves(ch, D),
            *halves(D, 2 * ch + N),
            *halves(D, ch + N),
            *halves(ch, D),
        ),
        in_specs=[vmem] * 9 + [smem] * 3 + [vmem] * 2,
        out_specs=(vmem,) * 11,
        compiler_params=params,
        cost_estimate=cost(6 * T * D * D * 4),
        name="prepare",
    )(*prepared)

    messages = [message]
    for k in range(1, max(ns, nh)):
        pairs = [
            (seq * nh + head, ((seq + k) % ns) * nh + (head + k) % nh)
            for seq in range(ns)
            for head in range(nh)
        ]
        sent = message if k < nh else message[0:head_rows]
        messages.append(lax.ppermute(sent, ("seq", "head"), pairs))
    swap = [(seq, seq ^ 1) for seq in range(ns)]
    others = [lax.ppermute(messages[k], "seq", swap) for k in range(1, nh)]

    mixed_high, mixed_low, embedded = pl.pallas_call(
        functools.partial(mix_kernel, dims),
        out_shape=(*halves(T, nh * ch), shape(T, D)),
        in_specs=[vmem] * (len(messages) + 2),
        out_specs=(vmem,) * 3,
        scratch_shapes=[pltpu.VMEM((max(ns, 8), T), f32)],
        compiler_params=params,
        cost_estimate=cost(6 * T * D * D * 16),
        name="mix",
    )(*messages[::-1], embedding, pair_table)

    state, hidden_high, hidden_low, scale, write, inner, stepped, total = pl.pallas_call(
        functools.partial(project_kernel, dims),
        out_shape=(
            shape(ch + 8, N),
            *halves(T, D),
            shape(T, ch),
            shape(T, N),
            shape(T, ch),
            shape(T, ch),
            shape(T, ch),
        ),
        in_specs=[vmem] * (8 + 2 * (nh - 1)),
        out_specs=(vmem,) * 8,
        compiler_params=params,
        name="project",
    )(
        mixed_high,
        mixed_low,
        embedded,
        small,
        own_high,
        own_low,
        state_high,
        state_low,
        *messages[1:nh][::-1],
        *others[::-1],
    )

    base, read, gate, own = pl.pallas_call(
        functools.partial(block_kernel, dims),
        out_shape=(shape(T, ch), shape(T, N), shape(T, ch), shape(share, D)),
        in_specs=[vmem] * 11,
        out_specs=(vmem,) * 4,
        scratch_shapes=[pltpu.VMEM((T, D), f32)],
        compiler_params=params,
        cost_estimate=cost(6 * T * D * D * 8),
        name="block",
    )(
        hidden_high,
        hidden_low,
        scale,
        write,
        inner,
        stepped,
        total,
        small,
        choose,
        rest_high,
        rest_low,
    )

    prefix = None
    bits = ns.bit_length() - 1
    for bit in range(bits):
        came = lax.ppermute(state, "seq", [(seq, seq ^ 2**bit) for seq in range(ns)])
        if bit == bits - 1:
            break
        given = [state] + ([] if prefix is None else [prefix]) + [came]

        def join(bit, known, *refs):
            if known:
                join_kernel(dims, bit, *refs)
            else:
                join_kernel(dims, bit, refs[0], None, *refs[1:])

        state, prefix = pl.pallas_call(
            functools.partial(join, bit, prefix is not None),
            out_shape=(shape(ch + 8, N),) * 2,
            in_specs=[vmem] * len(given),
            out_specs=(vmem,) * 2,
            compiler_params=params,
            name="join",
        )(*given)
    if prefix is None:
        prefix = jnp.zeros_like(state)

    parts = pl.pallas_call(
        functools.partial(output_kernel, dims, bits - 1),
        out_shape=(shape(share, D),) * nh,
        in_specs=[vmem] * 9,
        out_specs=(vmem,) * nh,
        scratch_shapes=[pltpu.VMEM((T, D), f32)],
        compiler_params=params,
        name="output",
    )(prefix, came, read, base, total, gate, own, proj_high, proj_low)
    result = parts[0]
    for k in range(1, nh):
        pairs = [(source, (source + k) % nh) for source in range(nh)]
        result = result + lax.ppermute(parts[k], "head", pairs)
    return result


def solution(mesh):
    return jax.shard_map(
        per_device,
        mesh=mesh,
        in_specs=(
            P(("rep", "seq")),
            P(),
            P(),
            P(),
            P(None, None, "head"),
            P(),
            P(None, "head"),
            P("head"),
            P("head"),
            P("head"),
            P("head"),
            P("head", None),
            P(),
            P(None, None, "head"),
            P(),
            P(None, "head"),
            P("head"),
            P("head"),
            P("head"),
            P("head"),
            P("head", None),
        ),
        out_specs=P(("rep", "seq", "head"), None),
        check_vma=False,
    )
```

```python
import functools

import jax
import jax.numpy as jnp
from jax import lax
from jax.experimental import pallas as pl
from jax.experimental.pallas import tpu as pltpu
from jax.sharding import PartitionSpec as P

epsilon = 1e-05
f32 = jnp.float32
bf16 = jnp.bfloat16
LIMIT = 48 * 1024 * 1024
TABLES_LIMIT = 60 * 1000 * 1000

MM = (((1,), (0,)), ((), ()))
NT = (((1,), (1,)), ((), ()))
TN = (((0,), (0,)), ((), ()))


def iota(shape, axis):
    return lax.broadcasted_iota(jnp.int32, shape, axis)


def split2(value):
    high = value.astype(bf16)
    return high, (value - high.astype(f32)).astype(bf16)


def split3(value):
    high = value.astype(bf16)
    rest = value - high.astype(f32)
    middle = rest.astype(bf16)
    return high, middle, (rest - middle.astype(f32)).astype(bf16)


def dot(left, right, dims=MM):
    return lax.dot_general(left, right, dims, preferred_element_type=f32)


def dot_split(left, right, dims=MM):
    return (
        dot(left[0], right[1], dims) + dot(left[1], right[0], dims)
    ) + dot(left[0], right[0], dims)


def dot3(left, right, dims=MM):
    return dot_split(split2(left), split2(right), dims)


def dot_left_exact(left, right, dims=MM):
    high, middle, low = split3(right)
    return (dot(left, low, dims) + dot(left, middle, dims)) + dot(left, high, dims)


def dot_right_exact(left, right, dims=MM):
    high, middle, low = split3(left)
    return (dot(low, right, dims) + dot(middle, right, dims)) + dot(high, right, dims)


def softplus(value):
    return jnp.maximum(value, 0.0) + jnp.log1p(jnp.exp(-jnp.abs(value)))


def silu(value):
    return value / (1.0 + jnp.exp(-value))


def rms(value):
    return value * lax.rsqrt(jnp.mean(value * value, axis=-1, keepdims=True) + epsilon)


def fetch(sources, places, semaphores):
    copies = []
    for number, (source, place) in enumerate(zip(sources, places)):
        copies.append(pltpu.make_async_copy(source, place, semaphores.at[number]))
        copies[-1].start()
    return copies


def fetch(sources, places, semaphores):
    copies = []
    for number, (source, place) in enumerate(zip(sources, places)):
        copies.append(pltpu.make_async_copy(source, place, semaphores.at[number]))
        copies[-1].start()
    return copies


def tables_kernel(dims, *refs):
    V, D, hl, ch, nh, ns, T, N = dims
    refs = list(refs)

    def take(number):
        taken, refs[:] = refs[:number], refs[number:]
        return taken

    sources = take(9)
    outproj_source, message = take(2)
    places = take(9)
    top, semaphores = take(2)
    half = ch // 2
    base = V + 2 + 3 * hl
    core = lax.rem(lax.axis_index("seq"), 2)
    copies = fetch(
        sources + [outproj_source.at[pl.ds(pl.multiple_of(core * half, 8), half), :]],
        places + [message.at[base : base + half, 0:D]],
        semaphores,
    )
    flip = (iota((T, T), 0) + iota((T, T), 1) == T - 1).astype(f32).astype(bf16)
    for copy in copies[:9]:
        copy.wait()
    (inproj, tok, emb, prenorm, stepmap, bias, rates, skip, outnorm) = places
    normed = split2(rms(emb[...]) * prenorm[...])
    raw_t = dot_split(split2(stepmap[...]), normed, NT)
    gate = dot_split(normed, split2(inproj[pl.ds(0, D, stride=2), :]))
    inner = dot_split(normed, split2(inproj[pl.ds(1, D, stride=2), :]))
    top[0:V, 0:ch] = gate
    top[0:V, ch : 2 * ch] = inner
    tokens = jnp.broadcast_to(tok[...].astype(f32), (8, T)).astype(bf16)
    top[V : V + 1, 0:T] = dot(tokens, flip)[0:1]
    top[V + 1 : V + 2, 0:ch] = outnorm[...]
    for head in range(hl):
        line = softplus(raw_t[head : head + 1, :] + bias[:, head : head + 1])
        row = V + 2 + head
        top[row : row + 1, 0:V] = line
        top[row + hl : row + hl + 1, 0:V] = -rates[:, head : head + 1] * line
        top[row + 2 * hl : row + 2 * hl + 1, 0:V] = jnp.broadcast_to(
            skip[:, head : head + 1], (1, V)
        )
    last = pltpu.make_async_copy(top, message.at[0:base, :], semaphores.at[10])
    last.start()
    copies[9].wait()
    last.wait()


def prepare_kernel(dims, *refs):
    V, D, hl, ch, nh, ns, T, N = dims
    P = ch // hl
    refs = list(refs)

    def take(number):
        taken, refs[:] = refs[:number], refs[number:]
        return taken

    sources = take(11)
    small, choose_out, own_high, own_low = take(4)
    state_high, state_low, rest_high, rest_low, out_high, out_low = take(6)
    places = take(11)
    semaphores = take(1)[0]
    copies = fetch(sources, places, semaphores)
    for copy in copies:
        copy.wait()
    complement, outproj, prenorm2, inproj2, statemap2, stepmap2 = places[:6]
    bias2, rates2, skip2, outnorm2, outproj2 = places[6:]
    out_gain = jnp.transpose(jnp.broadcast_to(outnorm2[...], (128, ch)))
    out_high[...], out_low[...] = split2(outproj2[...] * out_gain[:, 0:1])
    own_high[...], own_low[...] = split2(outproj[...])
    choose = (complement[...] == iota((D, D), 0)).astype(f32).astype(bf16)
    choose_out[...] = choose
    gain = jnp.transpose(jnp.broadcast_to(prenorm2[...], (128, D)))

    def weights(values):
        return split2(dot_left_exact(choose, values))

    gain_wide = gain[:, 0:1]
    inner = inproj2[pl.ds(1, D, stride=2), :] * gain_wide
    step = jnp.transpose(
        jnp.concatenate(
            [jnp.broadcast_to(stepmap2[head : head + 1, :], (P, D)) for head in range(hl)], axis=0
        )
    )
    write2 = statemap2[pl.ds(0, D, stride=2), :] * gain_wide
    state_high[...], state_low[...] = weights(
        jnp.concatenate([inner, step * gain_wide, write2], axis=1)
    )
    gate = inproj2[pl.ds(0, D, stride=2), :] * gain_wide
    read2 = statemap2[pl.ds(1, D, stride=2), :] * gain_wide
    rest_high[...], rest_low[...] = weights(jnp.concatenate([gate, read2], axis=1))
    lane_head = iota((1, ch), 1) // P
    for place, ref in ((0, bias2), (1, rates2), (2, skip2)):
        line = jnp.zeros((1, ch), f32)
        for head in range(hl):
            line = jnp.where(lane_head == head, ref[:, head : head + 1], line)
        small[place : place + 1, :] = line


def pairs_kernel(dims, emb, prenorm, statemap, small, pairs):
    V, D, hl, ch, nh, ns, T, N = dims
    normed = split2(rms(emb[...]) * prenorm[...])
    write = dot_split(normed, split2(statemap[pl.ds(0, D, stride=2), :]))
    read = dot_split(normed, split2(statemap[pl.ds(1, D, stride=2), :]))
    pairs[...] = dot3(read, jnp.concatenate([write] * (nh * hl), axis=0), NT)


def shift_rows(value, amount, fill):
    size = value.shape[0]
    if amount % 8 == 0:
        empty = jnp.full((abs(amount),) + value.shape[1:], fill, value.dtype)
        if amount > 0:
            return jnp.concatenate([empty, value[: size - amount]], axis=0)
        return jnp.concatenate([value[-amount:], empty], axis=0)
    rolled = pltpu.roll(value, amount % size, 0)
    row = iota(value.shape, 0)
    have = (row >= amount) if amount > 0 else (row < size + amount)
    return jnp.where(have, rolled, fill)


def scan_rows(decay, value, sign):
    size = value.shape[0]
    amount = 1
    while amount < size:
        value = value + decay * shift_rows(value, sign * amount, 0.0)
        if 2 * amount < size:
            decay = decay * shift_rows(decay, sign * amount, 1.0)
        amount *= 2
    return value


def mix_kernel(dims, *refs):
    V, D, hl, ch, nh, ns, T, N = dims
    H, LV, P = nh * hl, nh * hl * V, ch // hl
    C = nh * ch
    refs = list(refs)

    def take(number):
        taken, refs[:] = refs[:number], refs[number:]
        return taken

    packets = take(max(ns, nh))[::-1]
    emb, pairs = take(2)
    out_high, out_low, out_embedded = take(3)
    tokens = take(1)[0]
    mine = lax.axis_index("seq")

    for k in range(ns):
        block = ns - 1 - lax.rem(mine - k + ns, ns)
        tokens[pl.ds(block, 1), :] = packets[k][V : V + 1, 0:T]

    def rows_of(place):
        low = V + 2 + place * hl
        return jnp.concatenate([packets[k][low : low + hl, 0:V] for k in range(nh)], axis=0)

    step_t, log_t, skip_t = rows_of(0), rows_of(1), rows_of(2)
    spread_heads = (iota((H, LV), 1) // V == iota((H, LV), 0)).astype(f32).astype(bf16)

    def widen(value):
        high, middle, low = split3(value)
        return (dot(low, spread_heads, TN) + dot(middle, spread_heads, TN)) + dot(
            high, spread_heads, TN
        )

    own = iota((V, LV), 1) % V == iota((V, LV), 0)
    decay_table = jnp.exp(widen(log_t))
    step_table = jnp.where(own, widen(step_t), 0.0)
    gain_table = jnp.where(own, widen(skip_t), 0.0)
    gates = jnp.concatenate([packets[k][0:V, 0:ch] for k in range(nh)], axis=1)
    inners = jnp.concatenate([packets[k][0:V, ch : 2 * ch] for k in range(nh)], axis=1)
    gains = jnp.concatenate([packets[k][V + 1 : V + 2, 0:ch] for k in range(nh)], axis=1)

    token_row = (iota((LV, T), 0) % V).astype(f32)
    log_split = jnp.concatenate(split3(log_t), axis=1)
    onehots, logs = [], []
    for block in range(ns):
        onehot = (tokens[block : block + 1, :] == token_row).astype(f32).astype(bf16)
        onehots.append(onehot)
        logs.append(dot(log_split, onehot[0 : 3 * V, :]))
    logs = jnp.concatenate(logs, axis=0)
    first, second = iota((T, T), 0), iota((T, T), 1)
    later = (first > second).astype(f32).astype(bf16)
    sooner = (first < second).astype(f32).astype(bf16)
    logs3 = split3(logs)
    after = dot(logs3[2], later) + dot(logs3[1], later) + dot(logs3[0], later)
    before = dot(logs3[2], sooner) + dot(logs3[1], sooner) + dot(logs3[0], sooner)
    totals = jnp.sum(logs, axis=1, keepdims=True)
    total_rows = jnp.broadcast_to(totals, (ns * H, 128))
    row, column = iota((ns * H, ns * H), 0), iota((ns * H, ns * H), 1)
    row_block, column_block = row // H, column // H
    between = ((row_block < column_block) & (column_block < mine)) | (
        (row_block > column_block) & (column_block > mine)
    )
    between = (between & (row % H == column % H)).astype(f32).astype(bf16)
    gap = dot_left_exact(between, total_rows)[:, 0:1]
    block_of = iota((ns * H, T), 0) // H
    weight_up = jnp.where(block_of < mine, jnp.exp(after + gap), 0.0)
    weight_down = jnp.where(block_of > mine, jnp.exp(before + gap), 0.0)
    entering = jnp.zeros((2 * H, LV), f32)
    for block in range(ns):
        both = jnp.concatenate(
            [weight_up[block * H : (block + 1) * H], weight_down[block * H : (block + 1) * H]],
            axis=0,
        )
        high, low = split2(both)
        entering = entering + (dot(low, onehots[block], NT) + dot(high, onehots[block], NT))
    diagonal = iota((H, LV), 1) // V == iota((H, LV), 0)
    step_row = jnp.sum(step_table, axis=0, keepdims=True)
    enter_up = step_row * jnp.sum(
        jnp.where(diagonal, entering[0:H], 0.0), axis=0, keepdims=True
    )
    enter_down = step_row * jnp.sum(
        jnp.where(diagonal, entering[H : 2 * H], 0.0), axis=0, keepdims=True
    )

    looked = jnp.concatenate(
        [decay_table, step_table, pairs[...], gain_table, silu(gates), emb[...]], axis=1
    )
    looked = jnp.concatenate(split3(looked), axis=0)
    token = tokens[pl.ds(mine, 1), :]
    onehot = (token == (iota((3 * V, T), 0) % V).astype(f32)).astype(f32).astype(bf16)
    rows = dot(onehot, looked, TN)
    decay, step = rows[:, 0:LV], rows[:, LV : 2 * LV]
    pair, gain = rows[:, 2 * LV : 3 * LV], rows[:, 3 * LV : 4 * LV]
    silu_rows = rows[:, 4 * LV : 4 * LV + C]
    out_embedded[...] = rows[:, 4 * LV + C :]

    position = iota((T, LV), 0)
    up = scan_rows(decay, jnp.where(position == 0, step + decay * enter_up, step), 1)
    down = scan_rows(decay, jnp.where(position == T - 1, step + decay * enter_down, step), -1)

    tiled = jnp.concatenate([inners] * H, axis=0)
    spread = jnp.where(iota((LV, C), 0) // V == iota((LV, C), 1) // P, tiled, 0.0)
    spread_high, spread_low = split2(spread)
    both = jnp.concatenate([up * pair + gain, down * pair + gain], axis=0)
    high, low = split2(both)
    value = dot(high, spread_low) + dot(
        jnp.concatenate([low, high], axis=1),
        jnp.concatenate([spread_high, spread_high], axis=0),
    )
    value = value * jnp.concatenate([silu_rows, silu_rows], axis=0)
    wide = max(ch, 256)
    group = (iota((wide, wide), 0) // P == iota((wide, wide), 1) // P).astype(f32).astype(bf16)
    high, low = split2(value * value)
    for start in range(0, C, wide):
        stop = start + wide
        square = dot(low[:, start:stop], group) + dot(high[:, start:stop], group)
        normed = value[:, start:stop] * lax.rsqrt(square * (1.0 / P) + epsilon)
        out_high[:, start:stop], out_low[:, start:stop] = split2(
            (normed[0:T] + normed[T : 2 * T]) * gains[:, start:stop]
        )


def project_kernel(dims, *refs):
    V, D, hl, ch, nh, ns, T, N = dims
    P = ch // hl
    refs = list(refs)

    def take(number):
        taken, refs[:] = refs[:number], refs[number:]
        return taken

    high, low, embedded, small, own_high, own_low, state_high, state_low = take(8)
    nears = take(nh - 1)[::-1]
    others = take(nh - 1)[::-1]
    out_state, out_high, out_low, out_scale = take(4)
    out_write, out_inner, out_stepped, out_total = take(4)
    half = ch // 2
    base = V + 2 + 3 * hl
    mine = lax.axis_index("seq")

    pieces = []
    for k in range(1, nh):
        near = nears[k - 1][base : base + half, 0:D]
        other = others[k - 1][base : base + half, 0:D]
        even = lax.rem(mine - k + ns * nh, 2) == 0
        pieces.append(jnp.where(even, near, other))
        pieces.append(jnp.where(even, other, near))
    weights = split2(jnp.concatenate(pieces, axis=0))
    weights = (
        jnp.concatenate([own_high[...], weights[0]], axis=0),
        jnp.concatenate([own_low[...], weights[1]], axis=0),
    )
    hidden = embedded[...] + dot_split((high[...], low[...]), weights)
    split = split2(hidden)
    out_high[...], out_low[...] = split
    scale = lax.rsqrt(jnp.mean(hidden * hidden, axis=-1, keepdims=True) + epsilon)
    out_scale[...] = jnp.broadcast_to(scale, (T, ch))

    rows = dot_split(split, (state_high[...], state_low[...])) * scale
    inner, write = rows[:, 0:ch], rows[:, 2 * ch :]
    step = softplus(rows[:, ch : 2 * ch] + small[0:1, :])
    stepped = inner * step
    upto = (iota((T, T), 0) >= iota((T, T), 1)).astype(f32).astype(bf16)
    total = dot_left_exact(upto, -small[1:2, :] * step)
    end = total[T - 1 : T, :]
    state = dot3(stepped * jnp.exp(end - total), write, TN)
    out_state[0:ch, :] = state
    for head in range(hl):
        out_state[ch + head : ch + head + 1, :] = jnp.broadcast_to(
            end[:, head * P : head * P + 1], (1, N)
        )
    out_write[...] = write
    out_inner[...] = inner
    out_stepped[...] = stepped
    out_total[...] = total


def block_kernel(dims, *refs):
    V, D, hl, ch, nh, ns, T, N = dims
    P = ch // hl
    refs = list(refs)

    def take(number):
        taken, refs[:] = refs[:number], refs[number:]
        return taken

    high, low, scale, write, inner, stepped, total, small, choose = take(9)
    rest_high, rest_low = take(2)
    base, out_read, out_gate, own, hidden_ref = take(5)
    rows = dot_split((high[...], low[...]), (rest_high[...], rest_low[...]))
    out_gate[...] = silu(rows[:, 0:ch] * scale[...])
    read = rows[:, ch:] * scale[...]
    out_read[...] = read
    products = dot3(read, write[...], NT)
    stepped_high, stepped_low = split2(stepped[...])
    select = (iota((8, ch), 1) == iota((8, ch), 0) * P).astype(f32).astype(bf16)
    total_high, total_middle, total_low = split3(total[...])
    total_t = (dot(select, total_low, NT) + dot(select, total_middle, NT)) + dot(
        select, total_high, NT
    )
    allowed = iota((T, T), 0) >= iota((T, T), 1)
    parts = []
    for head in range(hl):
        start, stop = head * P, (head + 1) * P
        differ = total[:, start : start + 1] - total_t[head : head + 1, :]
        weights = jnp.where(allowed, jnp.exp(jnp.where(allowed, differ, 0.0)), 0.0) * products
        part = dot_split(
            split2(weights), (stepped_high[:, start:stop], stepped_low[:, start:stop])
        )
        parts.append(part + small[2:3, start:stop] * inner[:, start:stop])
    base[...] = jnp.concatenate(parts, axis=1)
    share = T // nh
    hidden_ref[...] = high[...].astype(f32) + low[...].astype(f32)
    place = pl.multiple_of(lax.axis_index("head") * share, 8)
    own[...] = dot_right_exact(hidden_ref[pl.ds(place, share), :], choose[...])


def state_rows(dims, values):
    V, D, hl, ch, nh, ns, T, N = dims
    head_of = iota((ch, N), 0) // (ch // hl)
    result = jnp.broadcast_to(values[0:1, :], (ch, N))
    for head in range(1, hl):
        result = jnp.where(head_of == head, values[head : head + 1, :], result)
    return result


def join_kernel(dims, bit, total, prefix, came, out_total, out_prefix):
    V, D, hl, ch, nh, ns, T, N = dims
    later = lax.rem(lax.div(lax.axis_index("seq"), 2**bit), 2) == 1
    came_state, came_log = came[0:ch, :], came[ch : ch + hl, :]
    state, log = total[0:ch, :], total[ch : ch + hl, :]
    factor = jnp.exp(state_rows(dims, jnp.where(later, log, came_log)))
    out_total[0:ch, :] = jnp.where(
        later, factor * came_state + state, factor * state + came_state
    )
    out_total[ch : ch + hl, :] = log + came_log
    if prefix is None:
        out_prefix[0:ch, :] = jnp.where(later, came_state, 0.0)
        out_prefix[ch : ch + hl, :] = jnp.where(later, came_log, 0.0)
    else:
        joined = prefix_joined(dims, bit, prefix, came)
        out_prefix[0:ch, :] = joined
        out_prefix[ch : ch + hl, :] = prefix[ch : ch + hl, :] + jnp.where(later, came_log, 0.0)


def prefix_joined(dims, bit, prefix, came):
    V, D, hl, ch, nh, ns, T, N = dims
    later = lax.rem(lax.div(lax.axis_index("seq"), 2**bit), 2) == 1
    factor = jnp.exp(state_rows(dims, prefix[ch : ch + hl, :]))
    return prefix[0:ch, :] + jnp.where(later, factor * came[0:ch, :], 0.0)


def output_kernel(dims, bit, *refs):
    V, D, hl, ch, nh, ns, T, N = dims
    P = ch // hl
    prefix, came, read, base, total, gate, own, proj_high, proj_low = refs[:9]
    outs, partial_ref = refs[9 : 9 + nh], refs[9 + nh]
    entering = prefix_joined(dims, bit, prefix, came)
    value = (base[...] + dot3(read[...], entering, NT) * jnp.exp(total[...])) * gate[...]
    group = (iota((ch, ch), 0) // P == iota((ch, ch), 1) // P).astype(f32).astype(bf16)
    high, low = split2(value * value)
    square = dot(low, group) + dot(high, group)
    value = value * lax.rsqrt(square * (1.0 / P) + epsilon)
    share = T // nh
    partial_ref[...] = dot_split(split2(value), (proj_high[...], proj_low[...]))
    mine = lax.axis_index("head")
    for k in range(nh):
        place = pl.multiple_of(lax.rem(mine + k, nh) * share, 8)
        part = partial_ref[pl.ds(place, share), :]
        outs[k][...] = part + own[...] if k == 0 else part


def per_device(
    token_ids,
    embedding,
    complement,
    prenorm_first,
    inproj_first,
    statemap_first,
    stepmap_first,
    stepbias_first,
    rates_first,
    skipgain_first,
    outnorm_first,
    outproj_first,
    prenorm_second,
    inproj_second,
    statemap_second,
    stepmap_second,
    stepbias_second,
    rates_second,
    skipgain_second,
    outnorm_second,
    outproj_second,
):
    nh, ns = lax.axis_size("head"), lax.axis_size("seq")
    V, D = embedding.shape
    ch = inproj_first.shape[2]
    hl = stepmap_first.shape[1]
    N = statemap_first.shape[2]
    T = token_ids.shape[0]
    LV = nh * hl * V
    dims = (V, D, hl, ch, nh, ns, T, N)
    vmem = pl.BlockSpec(memory_space=pltpu.VMEM)
    smem = pl.BlockSpec(memory_space=pltpu.SMEM)
    anywhere = pl.BlockSpec(memory_space=pl.ANY)
    params = pltpu.CompilerParams(vmem_limit_bytes=LIMIT)

    def shape(*sizes, dtype=f32):
        return jax.ShapeDtypeStruct(sizes, dtype)

    def halves(*sizes):
        return [shape(*sizes, dtype=bf16)] * 2

    def room(value):
        return pltpu.VMEM(value.shape, value.dtype)

    def line(value):
        return value.reshape(1, -1)

    def flat(value):
        return value.reshape(-1, value.shape[-1])

    light = pl.CostEstimate(flops=1000, bytes_accessed=1000, transcendentals=0)
    heavy = pl.CostEstimate(flops=960 * T * D * D, bytes_accessed=4 * T * D, transcendentals=T * D)

    head_rows = V + 2 + 3 * hl
    half = ch // 2
    width = max(2 * ch, T, D)
    share = T // nh
    fetched = [
        flat(inproj_first),
        line(token_ids),
        embedding,
        line(prenorm_first),
        stepmap_first.T,
        line(stepbias_first),
        line(rates_first),
        line(skipgain_first),
        line(outnorm_first),
    ]
    message = pl.pallas_call(
        functools.partial(tables_kernel, dims),
        out_shape=shape(head_rows + half, width),
        in_specs=[anywhere] * (len(fetched) + 1),
        out_specs=anywhere,
        scratch_shapes=[room(value) for value in fetched]
        + [pltpu.VMEM((head_rows, width), f32), pltpu.SemaphoreType.DMA((len(fetched) + 2,))],
        compiler_params=pltpu.CompilerParams(vmem_limit_bytes=TABLES_LIMIT),
        name="tables",
    )(*fetched, outproj_first)

    prepared = [
        line(complement),
        outproj_first,
        line(prenorm_second),
        flat(inproj_second),
        flat(statemap_second),
        stepmap_second.T,
        line(stepbias_second),
        line(rates_second),
        line(skipgain_second),
        line(outnorm_second),
        outproj_second,
    ]
    (
        small,
        choose,
        own_high,
        own_low,
        state_high,
        state_low,
        rest_high,
        rest_low,
        proj_high,
        proj_low,
    ) = pl.pallas_call(
        functools.partial(prepare_kernel, dims),
        out_shape=(
            shape(8, ch),
            shape(D, D, dtype=bf16),
            *halves(ch, D),
            *halves(D, 2 * ch + N),
            *halves(D, ch + N),
            *halves(ch, D),
        ),
        in_specs=[anywhere] * len(prepared),
        out_specs=(vmem,) * 10,
        scratch_shapes=[room(value) for value in prepared]
        + [pltpu.SemaphoreType.DMA((len(prepared),))],
        compiler_params=pltpu.CompilerParams(vmem_limit_bytes=TABLES_LIMIT),
        cost_estimate=heavy,
        name="prepare",
    )(*prepared)
    pair_table = pl.pallas_call(
        functools.partial(pairs_kernel, dims),
        out_shape=shape(V, LV),
        in_specs=[vmem] * 4,
        out_specs=vmem,
        compiler_params=params,
        cost_estimate=light,
        name="pairs",
    )(embedding, line(prenorm_first), flat(statemap_first), small)

    messages = [message]
    for k in range(1, max(ns, nh)):
        pairs = [
            (seq * nh + head, ((seq + k) % ns) * nh + (head + k) % nh)
            for seq in range(ns)
            for head in range(nh)
        ]
        sent = message if k < nh else message[0:head_rows]
        messages.append(lax.ppermute(sent, ("seq", "head"), pairs))
    swap = [(seq, seq ^ 1) for seq in range(ns)]
    others = [lax.ppermute(messages[k], "seq", swap) for k in range(1, nh)]

    mixed_high, mixed_low, embedded = pl.pallas_call(
        functools.partial(mix_kernel, dims),
        out_shape=(*halves(T, nh * ch), shape(T, D)),
        in_specs=[vmem] * (len(messages) + 2),
        out_specs=(vmem,) * 3,
        scratch_shapes=[pltpu.VMEM((max(ns, 8), T), f32)],
        compiler_params=params,
        cost_estimate=heavy,
        name="mix",
    )(*messages[::-1], embedding, pair_table)

    state, hidden_high, hidden_low, scale, write, inner, stepped, total = pl.pallas_call(
        functools.partial(project_kernel, dims),
        out_shape=(
            shape(ch + 8, N),
            *halves(T, D),
            shape(T, ch),
            shape(T, N),
            shape(T, ch),
            shape(T, ch),
            shape(T, ch),
        ),
        in_specs=[vmem] * (8 + 2 * (nh - 1)),
        out_specs=(vmem,) * 8,
        compiler_params=params,
        name="project",
    )(
        mixed_high,
        mixed_low,
        embedded,
        small,
        own_high,
        own_low,
        state_high,
        state_low,
        *messages[1:nh][::-1],
        *others[::-1],
    )

    base, read, gate, own = pl.pallas_call(
        functools.partial(block_kernel, dims),
        out_shape=(shape(T, ch), shape(T, N), shape(T, ch), shape(share, D)),
        in_specs=[vmem] * 11,
        out_specs=(vmem,) * 4,
        scratch_shapes=[pltpu.VMEM((T, D), f32)],
        compiler_params=params,
        cost_estimate=heavy,
        name="block",
    )(
        hidden_high,
        hidden_low,
        scale,
        write,
        inner,
        stepped,
        total,
        small,
        choose,
        rest_high,
        rest_low,
    )

    prefix = None
    bits = ns.bit_length() - 1
    for bit in range(bits):
        came = lax.ppermute(state, "seq", [(seq, seq ^ 2**bit) for seq in range(ns)])
        if bit == bits - 1:
            break
        given = [state] + ([] if prefix is None else [prefix]) + [came]

        def join(bit, known, *refs):
            if known:
                join_kernel(dims, bit, *refs)
            else:
                join_kernel(dims, bit, refs[0], None, *refs[1:])

        state, prefix = pl.pallas_call(
            functools.partial(join, bit, prefix is not None),
            out_shape=(shape(ch + 8, N),) * 2,
            in_specs=[vmem] * len(given),
            out_specs=(vmem,) * 2,
            compiler_params=params,
            name="join",
        )(*given)
    if prefix is None:
        prefix = jnp.zeros_like(state)

    parts = pl.pallas_call(
        functools.partial(output_kernel, dims, bits - 1),
        out_shape=(shape(share, D),) * nh,
        in_specs=[vmem] * 9,
        out_specs=(vmem,) * nh,
        scratch_shapes=[pltpu.VMEM((T, D), f32)],
        compiler_params=params,
        name="output",
    )(prefix, came, read, base, total, gate, own, proj_high, proj_low)
    result = parts[0]
    for k in range(1, nh):
        pairs = [(source, (source + k) % nh) for source in range(nh)]
        result = result + lax.ppermute(parts[k], "head", pairs)
    return result


def solution(mesh):
    return jax.shard_map(
        per_device,
        mesh=mesh,
        in_specs=(
            P(("rep", "seq")),
            P(),
            P(),
            P(),
            P(None, None, "head"),
            P(),
            P(None, "head"),
            P("head"),
            P("head"),
            P("head"),
            P("head"),
            P("head", None),
            P(),
            P(None, None, "head"),
            P(),
            P(None, "head"),
            P("head"),
            P("head"),
            P("head"),
            P("head"),
            P("head", None),
        ),
        out_specs=P(("rep", "seq", "head"), None),
        check_vma=False,
    )
```

```python
import functools

import jax
import jax.numpy as jnp
from jax import lax
from jax.experimental import pallas as pl
from jax.experimental.pallas import tpu as pltpu
from jax.sharding import PartitionSpec as P

epsilon = 1e-05
f32 = jnp.float32
bf16 = jnp.bfloat16
LIMIT = 48 * 1024 * 1024
TABLES_LIMIT = 60 * 1000 * 1000

MM = (((1,), (0,)), ((), ()))
NT = (((1,), (1,)), ((), ()))
TN = (((0,), (0,)), ((), ()))


def iota(shape, axis):
    return lax.broadcasted_iota(jnp.int32, shape, axis)


def split2(value):
    high = value.astype(bf16)
    return high, (value - high.astype(f32)).astype(bf16)


def split3(value):
    high = value.astype(bf16)
    rest = value - high.astype(f32)
    middle = rest.astype(bf16)
    return high, middle, (rest - middle.astype(f32)).astype(bf16)


def dot(left, right, dims=MM):
    return lax.dot_general(left, right, dims, preferred_element_type=f32)


def dot_split(left, right, dims=MM):
    return (
        dot(left[0], right[1], dims) + dot(left[1], right[0], dims)
    ) + dot(left[0], right[0], dims)


def dot3(left, right, dims=MM):
    return dot_split(split2(left), split2(right), dims)


def dot_left_exact(left, right, dims=MM):
    high, middle, low = split3(right)
    return (dot(left, low, dims) + dot(left, middle, dims)) + dot(left, high, dims)


def dot_right_exact(left, right, dims=MM):
    high, middle, low = split3(left)
    return (dot(low, right, dims) + dot(middle, right, dims)) + dot(high, right, dims)


def softplus(value):
    return jnp.maximum(value, 0.0) + jnp.log1p(jnp.exp(-jnp.abs(value)))


def silu(value):
    return value / (1.0 + jnp.exp(-value))


def rms(value):
    return value * lax.rsqrt(jnp.mean(value * value, axis=-1, keepdims=True) + epsilon)


def fetch(sources, places, semaphores):
    copies = []
    for number, (source, place) in enumerate(zip(sources, places)):
        copies.append(pltpu.make_async_copy(source, place, semaphores.at[number]))
        copies[-1].start()
    return copies


def fetch(sources, places, semaphores):
    copies = []
    for number, (source, place) in enumerate(zip(sources, places)):
        copies.append(pltpu.make_async_copy(source, place, semaphores.at[number]))
        copies[-1].start()
    return copies


def tables_kernel(dims, *refs):
    V, D, hl, ch, nh, ns, T, N = dims
    refs = list(refs)

    def take(number):
        taken, refs[:] = refs[:number], refs[number:]
        return taken

    sources = take(9)
    outproj_source, message = take(2)
    places = take(9)
    semaphores = take(1)[0]
    half = ch // 2
    base = V + 2 + 3 * hl
    core = lax.rem(lax.axis_index("seq"), 2)
    copies = fetch(
        sources + [outproj_source.at[pl.ds(pl.multiple_of(core * half, 8), half), :]],
        places + [message.at[base : base + half, 0:D]],
        semaphores,
    )
    flip = (iota((T, T), 0) + iota((T, T), 1) == T - 1).astype(f32).astype(bf16)
    for copy in copies[:9]:
        copy.wait()
    (inproj, tok, emb, prenorm, stepmap, bias, rates, skip, outnorm) = places
    normed = split2(rms(emb[...]) * prenorm[...])
    raw_t = dot_split(split2(stepmap[...]), normed, NT)
    gate = dot_split(normed, split2(inproj[pl.ds(0, D, stride=2), :]))
    inner = dot_split(normed, split2(inproj[pl.ds(1, D, stride=2), :]))
    message[0:V, 0:ch] = gate
    message[0:V, ch : 2 * ch] = inner
    tokens = jnp.broadcast_to(tok[...].astype(f32), (8, T)).astype(bf16)
    message[V : V + 1, 0:T] = dot(tokens, flip)[0:1]
    message[V + 1 : V + 2, 0:ch] = outnorm[...]
    for head in range(hl):
        line = softplus(raw_t[head : head + 1, :] + bias[:, head : head + 1])
        row = V + 2 + head
        message[row : row + 1, 0:V] = line
        message[row + hl : row + hl + 1, 0:V] = -rates[:, head : head + 1] * line
        message[row + 2 * hl : row + 2 * hl + 1, 0:V] = jnp.broadcast_to(
            skip[:, head : head + 1], (1, V)
        )
    copies[9].wait()


def head_line(dims, values):
    V, D, hl, ch, nh, ns, T, N = dims
    head_of = iota((1, ch), 1) // (ch // hl)
    line = jnp.zeros((1, ch), f32)
    for head in range(hl):
        line = jnp.where(head_of == head, values[head], line)
    return line


def prepare_kernel(dims, *refs):
    V, D, hl, ch, nh, ns, T, N = dims
    H, P = nh * hl, ch // hl
    refs = list(refs)

    def take(number):
        taken, refs[:] = refs[:number], refs[number:]
        return taken

    emb, prenorm, statemap, complement, outproj = take(5)
    prenorm2, inproj2, statemap2, stepmap2 = take(4)
    bias2, rates2, skip2, outnorm2 = take(4)
    pairs, small, choose_out, own_high, own_low = take(5)
    state_high, state_low, rest_high, rest_low = take(4)
    normed = split2(rms(emb[...]) * prenorm[...])
    write = dot_split(normed, split2(statemap[pl.ds(0, D, stride=2), :]))
    read = dot_split(normed, split2(statemap[pl.ds(1, D, stride=2), :]))
    pairs[...] = dot3(read, jnp.concatenate([write] * H, axis=0), NT)
    own_high[...], own_low[...] = split2(outproj[...])
    choose = (complement[...] == iota((D, D), 0)).astype(f32).astype(bf16)
    choose_out[...] = choose
    gain = jnp.transpose(jnp.broadcast_to(prenorm2[...], (128, D)))

    def weights(values):
        return split2(dot_left_exact(choose, values))

    gain_wide = gain[:, 0:1]
    inner = inproj2[pl.ds(1, D, stride=2), :] * gain_wide
    step = jnp.transpose(
        jnp.concatenate(
            [jnp.broadcast_to(stepmap2[head : head + 1, :], (P, D)) for head in range(hl)], axis=0
        )
    )
    write2 = statemap2[pl.ds(0, D, stride=2), :] * gain_wide
    state_high[...], state_low[...] = weights(
        jnp.concatenate([inner, step * gain_wide, write2], axis=1)
    )
    gate = inproj2[pl.ds(0, D, stride=2), :] * gain_wide
    read2 = statemap2[pl.ds(1, D, stride=2), :] * gain_wide
    rest_high[...], rest_low[...] = weights(jnp.concatenate([gate, read2], axis=1))
    small[0:1, :] = head_line(dims, bias2)
    small[1:2, :] = head_line(dims, rates2)
    small[2:3, :] = head_line(dims, skip2)
    small[3:4, :] = outnorm2[...]


def shift_rows(value, amount, fill):
    size = value.shape[0]
    if amount % 8 == 0:
        empty = jnp.full((abs(amount),) + value.shape[1:], fill, value.dtype)
        if amount > 0:
            return jnp.concatenate([empty, value[: size - amount]], axis=0)
        return jnp.concatenate([value[-amount:], empty], axis=0)
    rolled = pltpu.roll(value, amount % size, 0)
    row = iota(value.shape, 0)
    have = (row >= amount) if amount > 0 else (row < size + amount)
    return jnp.where(have, rolled, fill)


def scan_rows(decay, value, sign):
    size = value.shape[0]
    amount = 1
    while amount < size:
        value = value + decay * shift_rows(value, sign * amount, 0.0)
        if 2 * amount < size:
            decay = decay * shift_rows(decay, sign * amount, 1.0)
        amount *= 2
    return value


def mix_kernel(dims, *refs):
    V, D, hl, ch, nh, ns, T, N = dims
    H, LV, P = nh * hl, nh * hl * V, ch // hl
    C = nh * ch
    refs = list(refs)

    def take(number):
        taken, refs[:] = refs[:number], refs[number:]
        return taken

    packets = take(max(ns, nh))[::-1]
    emb, pairs = take(2)
    out_high, out_low, out_embedded = take(3)
    tokens = take(1)[0]
    mine = lax.axis_index("seq")

    for k in range(ns):
        block = ns - 1 - lax.rem(mine - k + ns, ns)
        tokens[pl.ds(block, 1), :] = packets[k][V : V + 1, 0:T]

    def rows_of(place):
        low = V + 2 + place * hl
        return jnp.concatenate([packets[k][low : low + hl, 0:V] for k in range(nh)], axis=0)

    step_t, log_t, skip_t = rows_of(0), rows_of(1), rows_of(2)
    spread_heads = (iota((H, LV), 1) // V == iota((H, LV), 0)).astype(f32).astype(bf16)

    def widen(value):
        high, middle, low = split3(value)
        return (dot(low, spread_heads, TN) + dot(middle, spread_heads, TN)) + dot(
            high, spread_heads, TN
        )

    own = iota((V, LV), 1) % V == iota((V, LV), 0)
    decay_table = jnp.exp(widen(log_t))
    step_table = jnp.where(own, widen(step_t), 0.0)
    gain_table = jnp.where(own, widen(skip_t), 0.0)
    gates = jnp.concatenate([packets[k][0:V, 0:ch] for k in range(nh)], axis=1)
    inners = jnp.concatenate([packets[k][0:V, ch : 2 * ch] for k in range(nh)], axis=1)
    gains = jnp.concatenate([packets[k][V + 1 : V + 2, 0:ch] for k in range(nh)], axis=1)

    token_row = (iota((LV, T), 0) % V).astype(f32)
    log_split = jnp.concatenate(split3(log_t), axis=1)
    onehots, logs = [], []
    for block in range(ns):
        onehot = (tokens[block : block + 1, :] == token_row).astype(f32).astype(bf16)
        onehots.append(onehot)
        logs.append(dot(log_split, onehot[0 : 3 * V, :]))
    logs = jnp.concatenate(logs, axis=0)
    first, second = iota((T, T), 0), iota((T, T), 1)
    later = (first > second).astype(f32).astype(bf16)
    sooner = (first < second).astype(f32).astype(bf16)
    logs3 = split3(logs)
    after = dot(logs3[2], later) + dot(logs3[1], later) + dot(logs3[0], later)
    before = dot(logs3[2], sooner) + dot(logs3[1], sooner) + dot(logs3[0], sooner)
    totals = jnp.sum(logs, axis=1, keepdims=True)
    total_rows = jnp.broadcast_to(totals, (ns * H, 128))
    row, column = iota((ns * H, ns * H), 0), iota((ns * H, ns * H), 1)
    row_block, column_block = row // H, column // H
    between = ((row_block < column_block) & (column_block < mine)) | (
        (row_block > column_block) & (column_block > mine)
    )
    between = (between & (row % H == column % H)).astype(f32).astype(bf16)
    gap = dot_left_exact(between, total_rows)[:, 0:1]
    block_of = iota((ns * H, T), 0) // H
    weight_up = jnp.where(block_of < mine, jnp.exp(after + gap), 0.0)
    weight_down = jnp.where(block_of > mine, jnp.exp(before + gap), 0.0)
    entering = jnp.zeros((2 * H, LV), f32)
    for block in range(ns):
        both = jnp.concatenate(
            [weight_up[block * H : (block + 1) * H], weight_down[block * H : (block + 1) * H]],
            axis=0,
        )
        high, low = split2(both)
        entering = entering + (dot(low, onehots[block], NT) + dot(high, onehots[block], NT))
    diagonal = iota((H, LV), 1) // V == iota((H, LV), 0)
    step_row = jnp.sum(step_table, axis=0, keepdims=True)
    enter_up = step_row * jnp.sum(
        jnp.where(diagonal, entering[0:H], 0.0), axis=0, keepdims=True
    )
    enter_down = step_row * jnp.sum(
        jnp.where(diagonal, entering[H : 2 * H], 0.0), axis=0, keepdims=True
    )

    looked = jnp.concatenate(
        [decay_table, step_table, pairs[...], gain_table, silu(gates), emb[...]], axis=1
    )
    looked = jnp.concatenate(split3(looked), axis=0)
    token = tokens[pl.ds(mine, 1), :]
    onehot = (token == (iota((3 * V, T), 0) % V).astype(f32)).astype(f32).astype(bf16)
    rows = dot(onehot, looked, TN)
    decay, step = rows[:, 0:LV], rows[:, LV : 2 * LV]
    pair, gain = rows[:, 2 * LV : 3 * LV], rows[:, 3 * LV : 4 * LV]
    silu_rows = rows[:, 4 * LV : 4 * LV + C]
    out_embedded[...] = rows[:, 4 * LV + C :]

    position = iota((T, LV), 0)
    up = scan_rows(decay, jnp.where(position == 0, step + decay * enter_up, step), 1)
    down = scan_rows(decay, jnp.where(position == T - 1, step + decay * enter_down, step), -1)

    tiled = jnp.concatenate([inners] * H, axis=0)
    spread = jnp.where(iota((LV, C), 0) // V == iota((LV, C), 1) // P, tiled, 0.0)
    spread_high, spread_low = split2(spread)
    both = jnp.concatenate([up * pair + gain, down * pair + gain], axis=0)
    high, low = split2(both)
    value = dot(high, spread_low) + dot(
        jnp.concatenate([low, high], axis=1),
        jnp.concatenate([spread_high, spread_high], axis=0),
    )
    value = value * jnp.concatenate([silu_rows, silu_rows], axis=0)
    wide = max(ch, 256)
    group = (iota((wide, wide), 0) // P == iota((wide, wide), 1) // P).astype(f32).astype(bf16)
    high, low = split2(value * value)
    for start in range(0, C, wide):
        stop = start + wide
        square = dot(low[:, start:stop], group) + dot(high[:, start:stop], group)
        normed = value[:, start:stop] * lax.rsqrt(square * (1.0 / P) + epsilon)
        out_high[:, start:stop], out_low[:, start:stop] = split2(
            (normed[0:T] + normed[T : 2 * T]) * gains[:, start:stop]
        )


def project_kernel(dims, *refs):
    V, D, hl, ch, nh, ns, T, N = dims
    P = ch // hl
    refs = list(refs)

    def take(number):
        taken, refs[:] = refs[:number], refs[number:]
        return taken

    high, low, embedded, small, own_high, own_low, state_high, state_low = take(8)
    nears = take(nh - 1)[::-1]
    others = take(nh - 1)[::-1]
    out_state, out_high, out_low, out_scale = take(4)
    out_write, out_inner, out_stepped, out_total = take(4)
    half = ch // 2
    base = V + 2 + 3 * hl
    mine = lax.axis_index("seq")

    pieces = []
    for k in range(1, nh):
        near = nears[k - 1][base : base + half, 0:D]
        other = others[k - 1][base : base + half, 0:D]
        even = lax.rem(mine - k + ns * nh, 2) == 0
        pieces.append(jnp.where(even, near, other))
        pieces.append(jnp.where(even, other, near))
    weights = split2(jnp.concatenate(pieces, axis=0))
    weights = (
        jnp.concatenate([own_high[...], weights[0]], axis=0),
        jnp.concatenate([own_low[...], weights[1]], axis=0),
    )
    hidden = embedded[...] + dot_split((high[...], low[...]), weights)
    split = split2(hidden)
    out_high[...], out_low[...] = split
    scale = lax.rsqrt(jnp.mean(hidden * hidden, axis=-1, keepdims=True) + epsilon)
    out_scale[...] = jnp.broadcast_to(scale, (T, ch))

    rows = dot_split(split, (state_high[...], state_low[...])) * scale
    inner, write = rows[:, 0:ch], rows[:, 2 * ch :]
    step = softplus(rows[:, ch : 2 * ch] + small[0:1, :])
    stepped = inner * step
    upto = (iota((T, T), 0) >= iota((T, T), 1)).astype(f32).astype(bf16)
    total = dot_left_exact(upto, -small[1:2, :] * step)
    end = total[T - 1 : T, :]
    state = dot3(stepped * jnp.exp(end - total), write, TN)
    out_state[0:ch, :] = state
    for head in range(hl):
        out_state[ch + head : ch + head + 1, :] = jnp.broadcast_to(
            end[:, head * P : head * P + 1], (1, N)
        )
    out_write[...] = write
    out_inner[...] = inner
    out_stepped[...] = stepped
    out_total[...] = total


def block_kernel(dims, *refs):
    V, D, hl, ch, nh, ns, T, N = dims
    P = ch // hl
    refs = list(refs)

    def take(number):
        taken, refs[:] = refs[:number], refs[number:]
        return taken

    high, low, scale, write, inner, stepped, total, choose = take(8)
    rest_high, rest_low, small, outproj2 = take(4)
    base, out_read, out_gate, own, out_high, out_low, hidden_ref = take(7)
    rows = dot_split((high[...], low[...]), (rest_high[...], rest_low[...]))
    out_gate[...] = silu(rows[:, 0:ch] * scale[...])
    read = rows[:, ch:] * scale[...]
    out_read[...] = read
    products = dot3(read, write[...], NT)
    stepped_high, stepped_low = split2(stepped[...])
    select = (iota((8, ch), 1) == iota((8, ch), 0) * P).astype(f32).astype(bf16)
    total_high, total_middle, total_low = split3(total[...])
    total_t = (dot(select, total_low, NT) + dot(select, total_middle, NT)) + dot(
        select, total_high, NT
    )
    allowed = iota((T, T), 0) >= iota((T, T), 1)
    parts = []
    for head in range(hl):
        start, stop = head * P, (head + 1) * P
        differ = total[:, start : start + 1] - total_t[head : head + 1, :]
        weights = jnp.where(allowed, jnp.exp(jnp.where(allowed, differ, 0.0)), 0.0) * products
        part = dot_split(
            split2(weights), (stepped_high[:, start:stop], stepped_low[:, start:stop])
        )
        parts.append(part + small[2:3, start:stop] * inner[:, start:stop])
    base[...] = jnp.concatenate(parts, axis=1)
    share = T // nh
    hidden_ref[...] = high[...].astype(f32) + low[...].astype(f32)
    place = pl.multiple_of(lax.axis_index("head") * share, 8)
    out_gain = jnp.transpose(jnp.broadcast_to(small[3:4, :], (128, ch)))
    out_high[...], out_low[...] = split2(outproj2[...] * out_gain[:, 0:1])
    own[...] = dot_right_exact(hidden_ref[pl.ds(place, share), :], choose[...])


def state_rows(dims, values):
    V, D, hl, ch, nh, ns, T, N = dims
    head_of = iota((ch, N), 0) // (ch // hl)
    result = jnp.broadcast_to(values[0:1, :], (ch, N))
    for head in range(1, hl):
        result = jnp.where(head_of == head, values[head : head + 1, :], result)
    return result


def join_kernel(dims, bit, total, prefix, came, out_total, out_prefix):
    V, D, hl, ch, nh, ns, T, N = dims
    later = lax.rem(lax.div(lax.axis_index("seq"), 2**bit), 2) == 1
    came_state, came_log = came[0:ch, :], came[ch : ch + hl, :]
    state, log = total[0:ch, :], total[ch : ch + hl, :]
    factor = jnp.exp(state_rows(dims, jnp.where(later, log, came_log)))
    out_total[0:ch, :] = jnp.where(
        later, factor * came_state + state, factor * state + came_state
    )
    out_total[ch : ch + hl, :] = log + came_log
    if prefix is None:
        out_prefix[0:ch, :] = jnp.where(later, came_state, 0.0)
        out_prefix[ch : ch + hl, :] = jnp.where(later, came_log, 0.0)
    else:
        joined = prefix_joined(dims, bit, prefix, came)
        out_prefix[0:ch, :] = joined
        out_prefix[ch : ch + hl, :] = prefix[ch : ch + hl, :] + jnp.where(later, came_log, 0.0)


def prefix_joined(dims, bit, prefix, came):
    V, D, hl, ch, nh, ns, T, N = dims
    later = lax.rem(lax.div(lax.axis_index("seq"), 2**bit), 2) == 1
    factor = jnp.exp(state_rows(dims, prefix[ch : ch + hl, :]))
    return prefix[0:ch, :] + jnp.where(later, factor * came[0:ch, :], 0.0)


def output_kernel(dims, bit, *refs):
    V, D, hl, ch, nh, ns, T, N = dims
    P = ch // hl
    prefix, came, read, base, total, gate, own, proj_high, proj_low = refs[:9]
    outs, partial_ref = refs[9 : 9 + nh], refs[9 + nh]
    entering = prefix_joined(dims, bit, prefix, came)
    value = (base[...] + dot3(read[...], entering, NT) * jnp.exp(total[...])) * gate[...]
    group = (iota((ch, ch), 0) // P == iota((ch, ch), 1) // P).astype(f32).astype(bf16)
    high, low = split2(value * value)
    square = dot(low, group) + dot(high, group)
    value = value * lax.rsqrt(square * (1.0 / P) + epsilon)
    share = T // nh
    partial_ref[...] = dot_split(split2(value), (proj_high[...], proj_low[...]))
    mine = lax.axis_index("head")
    for k in range(nh):
        place = pl.multiple_of(lax.rem(mine + k, nh) * share, 8)
        part = partial_ref[pl.ds(place, share), :]
        outs[k][...] = part + own[...] if k == 0 else part


def per_device(
    token_ids,
    embedding,
    complement,
    prenorm_first,
    inproj_first,
    statemap_first,
    stepmap_first,
    stepbias_first,
    rates_first,
    skipgain_first,
    outnorm_first,
    outproj_first,
    prenorm_second,
    inproj_second,
    statemap_second,
    stepmap_second,
    stepbias_second,
    rates_second,
    skipgain_second,
    outnorm_second,
    outproj_second,
):
    nh, ns = lax.axis_size("head"), lax.axis_size("seq")
    V, D = embedding.shape
    ch = inproj_first.shape[2]
    hl = stepmap_first.shape[1]
    N = statemap_first.shape[2]
    T = token_ids.shape[0]
    LV = nh * hl * V
    dims = (V, D, hl, ch, nh, ns, T, N)
    vmem = pl.BlockSpec(memory_space=pltpu.VMEM)
    smem = pl.BlockSpec(memory_space=pltpu.SMEM)
    anywhere = pl.BlockSpec(memory_space=pl.ANY)
    params = pltpu.CompilerParams(vmem_limit_bytes=LIMIT)

    def shape(*sizes, dtype=f32):
        return jax.ShapeDtypeStruct(sizes, dtype)

    def halves(*sizes):
        return [shape(*sizes, dtype=bf16)] * 2

    def room(value):
        return pltpu.VMEM(value.shape, value.dtype)

    def line(value):
        return value.reshape(1, -1)

    def flat(value):
        return value.reshape(-1, value.shape[-1])

    heavy = pl.CostEstimate(flops=960 * T * D * D, bytes_accessed=4 * T * D, transcendentals=T * D)

    head_rows = V + 2 + 3 * hl
    half = ch // 2
    width = max(2 * ch, T, D)
    share = T // nh
    fetched = [
        flat(inproj_first),
        line(token_ids),
        embedding,
        line(prenorm_first),
        stepmap_first.T,
        line(stepbias_first),
        line(rates_first),
        line(skipgain_first),
        line(outnorm_first),
    ]
    message = pl.pallas_call(
        functools.partial(tables_kernel, dims),
        out_shape=shape(head_rows + half, width),
        in_specs=[anywhere] * (len(fetched) + 1),
        out_specs=vmem,
        scratch_shapes=[room(value) for value in fetched]
        + [pltpu.SemaphoreType.DMA((len(fetched) + 1,))],
        compiler_params=pltpu.CompilerParams(vmem_limit_bytes=TABLES_LIMIT),
        cost_estimate=heavy,
        name="tables",
    )(*fetched, outproj_first)

    prepared = [
        embedding,
        line(prenorm_first),
        flat(statemap_first),
        line(complement),
        outproj_first,
        line(prenorm_second),
        flat(inproj_second),
        flat(statemap_second),
        stepmap_second.T,
        stepbias_second,
        rates_second,
        skipgain_second,
        line(outnorm_second),
    ]
    (
        pair_table,
        small,
        choose,
        own_high,
        own_low,
        state_high,
        state_low,
        rest_high,
        rest_low,
    ) = pl.pallas_call(
        functools.partial(prepare_kernel, dims),
        out_shape=(
            shape(V, LV),
            shape(8, ch),
            shape(D, D, dtype=bf16),
            *halves(ch, D),
            *halves(D, 2 * ch + N),
            *halves(D, ch + N),
        ),
        in_specs=[vmem] * 9 + [smem] * 3 + [vmem],
        out_specs=(vmem,) * 9,
        compiler_params=params,
        cost_estimate=heavy,
        name="prepare",
    )(*prepared)

    messages = [message]
    for k in range(1, max(ns, nh)):
        pairs = [
            (seq * nh + head, ((seq + k) % ns) * nh + (head + k) % nh)
            for seq in range(ns)
            for head in range(nh)
        ]
        sent = message if k < nh else message[0:head_rows]
        messages.append(lax.ppermute(sent, ("seq", "head"), pairs))
    swap = [(seq, seq ^ 1) for seq in range(ns)]
    others = [lax.ppermute(messages[k], "seq", swap) for k in range(1, nh)]

    mixed_high, mixed_low, embedded = pl.pallas_call(
        functools.partial(mix_kernel, dims),
        out_shape=(*halves(T, nh * ch), shape(T, D)),
        in_specs=[vmem] * (len(messages) + 2),
        out_specs=(vmem,) * 3,
        scratch_shapes=[pltpu.VMEM((max(ns, 8), T), f32)],
        compiler_params=params,
        cost_estimate=heavy,
        name="mix",
    )(*messages[::-1], embedding, pair_table)

    state, hidden_high, hidden_low, scale, write, inner, stepped, total = pl.pallas_call(
        functools.partial(project_kernel, dims),
        out_shape=(
            shape(ch + 8, N),
            *halves(T, D),
            shape(T, ch),
            shape(T, N),
            shape(T, ch),
            shape(T, ch),
            shape(T, ch),
        ),
        in_specs=[vmem] * (8 + 2 * (nh - 1)),
        out_specs=(vmem,) * 8,
        compiler_params=params,
        name="project",
    )(
        mixed_high,
        mixed_low,
        embedded,
        small,
        own_high,
        own_low,
        state_high,
        state_low,
        *messages[1:nh][::-1],
        *others[::-1],
    )

    base, read, gate, own, proj_high, proj_low = pl.pallas_call(
        functools.partial(block_kernel, dims),
        out_shape=(shape(T, ch), shape(T, N), shape(T, ch), shape(share, D), *halves(ch, D)),
        in_specs=[vmem] * 12,
        out_specs=(vmem,) * 6,
        scratch_shapes=[pltpu.VMEM((T, D), f32)],
        compiler_params=params,
        cost_estimate=heavy,
        name="block",
    )(
        hidden_high,
        hidden_low,
        scale,
        write,
        inner,
        stepped,
        total,
        choose,
        rest_high,
        rest_low,
        small,
        outproj_second,
    )

    prefix = None
    bits = ns.bit_length() - 1
    for bit in range(bits):
        came = lax.ppermute(state, "seq", [(seq, seq ^ 2**bit) for seq in range(ns)])
        if bit == bits - 1:
            break
        given = [state] + ([] if prefix is None else [prefix]) + [came]

        def join(bit, known, *refs):
            if known:
                join_kernel(dims, bit, *refs)
            else:
                join_kernel(dims, bit, refs[0], None, *refs[1:])

        state, prefix = pl.pallas_call(
            functools.partial(join, bit, prefix is not None),
            out_shape=(shape(ch + 8, N),) * 2,
            in_specs=[vmem] * len(given),
            out_specs=(vmem,) * 2,
            compiler_params=params,
            name="join",
        )(*given)
    if prefix is None:
        prefix = jnp.zeros_like(state)

    parts = pl.pallas_call(
        functools.partial(output_kernel, dims, bits - 1),
        out_shape=(shape(share, D),) * nh,
        in_specs=[vmem] * 9,
        out_specs=(vmem,) * nh,
        scratch_shapes=[pltpu.VMEM((T, D), f32)],
        compiler_params=params,
        name="output",
    )(prefix, came, read, base, total, gate, own, proj_high, proj_low)
    result = parts[0]
    for k in range(1, nh):
        pairs = [(source, (source + k) % nh) for source in range(nh)]
        result = result + lax.ppermute(parts[k], "head", pairs)
    return result


def solution(mesh):
    return jax.shard_map(
        per_device,
        mesh=mesh,
        in_specs=(
            P(("rep", "seq")),
            P(),
            P(),
            P(),
            P(None, None, "head"),
            P(),
            P(None, "head"),
            P("head"),
            P("head"),
            P("head"),
            P("head"),
            P("head", None),
            P(),
            P(None, None, "head"),
            P(),
            P(None, "head"),
            P("head"),
            P("head"),
            P("head"),
            P("head"),
            P("head", None),
        ),
        out_specs=P(("rep", "seq", "head"), None),
        check_vma=False,
    )
```

```python
import functools

import jax
import jax.numpy as jnp
from jax import lax
from jax.experimental import pallas as pl
from jax.experimental.pallas import tpu as pltpu
from jax.sharding import PartitionSpec as P

epsilon = 1e-05
f32 = jnp.float32
bf16 = jnp.bfloat16
LIMIT = 48 * 1024 * 1024
TABLES_LIMIT = 60 * 1000 * 1000

MM = (((1,), (0,)), ((), ()))
NT = (((1,), (1,)), ((), ()))
TN = (((0,), (0,)), ((), ()))


def partners(ns, nh):
    count = max(ns, nh)
    return [((ns - k) if 0 < k < ns else 0, k if k < nh else 0) for k in range(count)]


def in_turn(count):
    return sorted(range(1, count), key=lambda k: (-k.bit_length(), k))


def iota(shape, axis):
    return lax.broadcasted_iota(jnp.int32, shape, axis)


def split2(value):
    high = value.astype(bf16)
    return high, (value - high.astype(f32)).astype(bf16)


def split3(value):
    high = value.astype(bf16)
    rest = value - high.astype(f32)
    middle = rest.astype(bf16)
    return high, middle, (rest - middle.astype(f32)).astype(bf16)


def dot(left, right, dims=MM):
    return lax.dot_general(left, right, dims, preferred_element_type=f32)


def dot_split(left, right, dims=MM):
    return (
        dot(left[0], right[1], dims) + dot(left[1], right[0], dims)
    ) + dot(left[0], right[0], dims)


def dot3(left, right, dims=MM):
    return dot_split(split2(left), split2(right), dims)


def dot_left_exact(left, right, dims=MM):
    high, middle, low = split3(right)
    return (dot(left, low, dims) + dot(left, middle, dims)) + dot(left, high, dims)


def dot_right_exact(left, right, dims=MM):
    high, middle, low = split3(left)
    return (dot(low, right, dims) + dot(middle, right, dims)) + dot(high, right, dims)


def softplus(value):
    return jnp.maximum(value, 0.0) + jnp.log1p(jnp.exp(-jnp.abs(value)))


def silu(value):
    return value / (1.0 + jnp.exp(-value))


def rms(value):
    return value * lax.rsqrt(jnp.mean(value * value, axis=-1, keepdims=True) + epsilon)


def fetch(sources, places, semaphores):
    copies = []
    for number, (source, place) in enumerate(zip(sources, places)):
        copies.append(pltpu.make_async_copy(source, place, semaphores.at[number]))
        copies[-1].start()
    return copies


def fetch(sources, places, semaphores):
    copies = []
    for number, (source, place) in enumerate(zip(sources, places)):
        copies.append(pltpu.make_async_copy(source, place, semaphores.at[number]))
        copies[-1].start()
    return copies


def tables_kernel(dims, *refs):
    V, D, hl, ch, nh, ns, T, N = dims
    refs = list(refs)

    def take(number):
        taken, refs[:] = refs[:number], refs[number:]
        return taken

    sources = take(9)
    outproj_source, message = take(2)
    places = take(9)
    semaphores = take(1)[0]
    half = ch // 2
    base = V + 2 + 3 * hl
    core = lax.rem(lax.axis_index("seq"), 2)
    copies = fetch(
        sources + [outproj_source.at[pl.ds(pl.multiple_of(core * half, 8), half), :]],
        places + [message.at[base : base + half, 0:D]],
        semaphores,
    )
    flip = (iota((T, T), 0) + iota((T, T), 1) == T - 1).astype(f32).astype(bf16)
    for copy in copies[:9]:
        copy.wait()
    (inproj, tok, emb, prenorm, stepmap, bias, rates, skip, outnorm) = places
    normed = split2(rms(emb[...]) * prenorm[...])
    raw_t = dot_split(split2(stepmap[...]), normed, NT)
    gate = dot_split(normed, split2(inproj[pl.ds(0, D, stride=2), :]))
    inner = dot_split(normed, split2(inproj[pl.ds(1, D, stride=2), :]))
    message[0:V, 0:ch] = gate
    message[0:V, ch : 2 * ch] = inner
    tokens = jnp.broadcast_to(tok[...].astype(f32), (8, T)).astype(bf16)
    message[V : V + 1, 0:T] = dot(tokens, flip)[0:1]
    message[V + 1 : V + 2, 0:ch] = outnorm[...]
    for head in range(hl):
        line = softplus(raw_t[head : head + 1, :] + bias[:, head : head + 1])
        row = V + 2 + head
        message[row : row + 1, 0:V] = line
        message[row + hl : row + hl + 1, 0:V] = -rates[:, head : head + 1] * line
        message[row + 2 * hl : row + 2 * hl + 1, 0:V] = jnp.broadcast_to(
            skip[:, head : head + 1], (1, V)
        )
    copies[9].wait()


def head_line(dims, values):
    V, D, hl, ch, nh, ns, T, N = dims
    head_of = iota((1, ch), 1) // (ch // hl)
    line = jnp.zeros((1, ch), f32)
    for head in range(hl):
        line = jnp.where(head_of == head, values[head], line)
    return line


def prepare_kernel(dims, *refs):
    V, D, hl, ch, nh, ns, T, N = dims
    H, P = nh * hl, ch // hl
    refs = list(refs)

    def take(number):
        taken, refs[:] = refs[:number], refs[number:]
        return taken

    emb, prenorm, statemap, complement, outproj = take(5)
    prenorm2, inproj2, statemap2, stepmap2 = take(4)
    bias2, rates2, skip2, outnorm2 = take(4)
    pairs, small, choose_out, own_high, own_low = take(5)
    state_high, state_low, rest_high, rest_low = take(4)
    normed = split2(rms(emb[...]) * prenorm[...])
    write = dot_split(normed, split2(statemap[pl.ds(0, D, stride=2), :]))
    read = dot_split(normed, split2(statemap[pl.ds(1, D, stride=2), :]))
    pairs[...] = dot3(read, jnp.concatenate([write] * H, axis=0), NT)
    own_high[...], own_low[...] = split2(outproj[...])
    choose = (complement[...] == iota((D, D), 0)).astype(f32).astype(bf16)
    choose_out[...] = choose
    gain = jnp.transpose(jnp.broadcast_to(prenorm2[...], (128, D)))

    def weights(values):
        return split2(dot_left_exact(choose, values))

    gain_wide = gain[:, 0:1]
    inner = inproj2[pl.ds(1, D, stride=2), :] * gain_wide
    step = jnp.transpose(
        jnp.concatenate(
            [jnp.broadcast_to(stepmap2[head : head + 1, :], (P, D)) for head in range(hl)], axis=0
        )
    )
    write2 = statemap2[pl.ds(0, D, stride=2), :] * gain_wide
    state_high[...], state_low[...] = weights(
        jnp.concatenate([inner, step * gain_wide, write2], axis=1)
    )
    gate = inproj2[pl.ds(0, D, stride=2), :] * gain_wide
    read2 = statemap2[pl.ds(1, D, stride=2), :] * gain_wide
    rest_high[...], rest_low[...] = weights(jnp.concatenate([gate, read2], axis=1))
    small[0:1, :] = head_line(dims, bias2)
    small[1:2, :] = head_line(dims, rates2)
    small[2:3, :] = head_line(dims, skip2)
    small[3:4, :] = outnorm2[...]


def shift_rows(value, amount, fill):
    size = value.shape[0]
    if amount % 8 == 0:
        empty = jnp.full((abs(amount),) + value.shape[1:], fill, value.dtype)
        if amount > 0:
            return jnp.concatenate([empty, value[: size - amount]], axis=0)
        return jnp.concatenate([value[-amount:], empty], axis=0)
    rolled = pltpu.roll(value, amount % size, 0)
    row = iota(value.shape, 0)
    have = (row >= amount) if amount > 0 else (row < size + amount)
    return jnp.where(have, rolled, fill)


def scan_rows(decay, value, sign):
    size = value.shape[0]
    amount = 1
    while amount < size:
        value = value + decay * shift_rows(value, sign * amount, 0.0)
        if 2 * amount < size:
            decay = decay * shift_rows(decay, sign * amount, 1.0)
        amount *= 2
    return value


def mix_kernel(dims, *refs):
    V, D, hl, ch, nh, ns, T, N = dims
    H, LV, P = nh * hl, nh * hl * V, ch // hl
    C = nh * ch
    refs = list(refs)

    def take(number):
        taken, refs[:] = refs[:number], refs[number:]
        return taken

    count = max(ns, nh)
    packets = dict(zip(in_turn(count)[::-1] + [0], take(count)))
    emb, pairs = take(2)
    out_high, out_low, out_embedded = take(3)
    tokens = take(1)[0]
    mine = lax.axis_index("seq")

    for k in range(ns):
        block = ns - 1 - lax.bitwise_xor(mine, partners(ns, nh)[k][0])
        tokens[pl.ds(block, 1), :] = packets[k][V : V + 1, 0:T]

    def rows_of(place):
        low = V + 2 + place * hl
        return jnp.concatenate([packets[k][low : low + hl, 0:V] for k in range(nh)], axis=0)

    step_t, log_t, skip_t = rows_of(0), rows_of(1), rows_of(2)
    spread_heads = (iota((H, LV), 1) // V == iota((H, LV), 0)).astype(f32).astype(bf16)

    def widen(value):
        high, middle, low = split3(value)
        return (dot(low, spread_heads, TN) + dot(middle, spread_heads, TN)) + dot(
            high, spread_heads, TN
        )

    own = iota((V, LV), 1) % V == iota((V, LV), 0)
    decay_table = jnp.exp(widen(log_t))
    step_table = jnp.where(own, widen(step_t), 0.0)
    gain_table = jnp.where(own, widen(skip_t), 0.0)
    gates = jnp.concatenate([packets[k][0:V, 0:ch] for k in range(nh)], axis=1)
    inners = jnp.concatenate([packets[k][0:V, ch : 2 * ch] for k in range(nh)], axis=1)
    gains = jnp.concatenate([packets[k][V + 1 : V + 2, 0:ch] for k in range(nh)], axis=1)

    token_row = (iota((LV, T), 0) % V).astype(f32)
    log_split = jnp.concatenate(split3(log_t), axis=1)
    onehots, logs = [], []
    for block in range(ns):
        onehot = (tokens[block : block + 1, :] == token_row).astype(f32).astype(bf16)
        onehots.append(onehot)
        logs.append(dot(log_split, onehot[0 : 3 * V, :]))
    logs = jnp.concatenate(logs, axis=0)
    first, second = iota((T, T), 0), iota((T, T), 1)
    later = (first > second).astype(f32).astype(bf16)
    sooner = (first < second).astype(f32).astype(bf16)
    logs3 = split3(logs)
    after = dot(logs3[2], later) + dot(logs3[1], later) + dot(logs3[0], later)
    before = dot(logs3[2], sooner) + dot(logs3[1], sooner) + dot(logs3[0], sooner)
    totals = jnp.sum(logs, axis=1, keepdims=True)
    total_rows = jnp.broadcast_to(totals, (ns * H, 128))
    row, column = iota((ns * H, ns * H), 0), iota((ns * H, ns * H), 1)
    row_block, column_block = row // H, column // H
    between = ((row_block < column_block) & (column_block < mine)) | (
        (row_block > column_block) & (column_block > mine)
    )
    between = (between & (row % H == column % H)).astype(f32).astype(bf16)
    gap = dot_left_exact(between, total_rows)[:, 0:1]
    block_of = iota((ns * H, T), 0) // H
    weight_up = jnp.where(block_of < mine, jnp.exp(after + gap), 0.0)
    weight_down = jnp.where(block_of > mine, jnp.exp(before + gap), 0.0)
    entering = jnp.zeros((2 * H, LV), f32)
    for block in range(ns):
        both = jnp.concatenate(
            [weight_up[block * H : (block + 1) * H], weight_down[block * H : (block + 1) * H]],
            axis=0,
        )
        high, low = split2(both)
        entering = entering + (dot(low, onehots[block], NT) + dot(high, onehots[block], NT))
    diagonal = iota((H, LV), 1) // V == iota((H, LV), 0)
    step_row = jnp.sum(step_table, axis=0, keepdims=True)
    enter_up = step_row * jnp.sum(
        jnp.where(diagonal, entering[0:H], 0.0), axis=0, keepdims=True
    )
    enter_down = step_row * jnp.sum(
        jnp.where(diagonal, entering[H : 2 * H], 0.0), axis=0, keepdims=True
    )

    looked = jnp.concatenate(
        [decay_table, step_table, pairs[...], gain_table, silu(gates), emb[...]], axis=1
    )
    looked = jnp.concatenate(split3(looked), axis=0)
    token = tokens[pl.ds(mine, 1), :]
    onehot = (token == (iota((3 * V, T), 0) % V).astype(f32)).astype(f32).astype(bf16)
    rows = dot(onehot, looked, TN)
    decay, step = rows[:, 0:LV], rows[:, LV : 2 * LV]
    pair, gain = rows[:, 2 * LV : 3 * LV], rows[:, 3 * LV : 4 * LV]
    silu_rows = rows[:, 4 * LV : 4 * LV + C]
    out_embedded[...] = rows[:, 4 * LV + C :]

    position = iota((T, LV), 0)
    up = scan_rows(decay, jnp.where(position == 0, step + decay * enter_up, step), 1)
    down = scan_rows(decay, jnp.where(position == T - 1, step + decay * enter_down, step), -1)

    tiled = jnp.concatenate([inners] * H, axis=0)
    spread = jnp.where(iota((LV, C), 0) // V == iota((LV, C), 1) // P, tiled, 0.0)
    spread_high, spread_low = split2(spread)
    both = jnp.concatenate([up * pair + gain, down * pair + gain], axis=0)
    high, low = split2(both)
    value = dot(high, spread_low) + dot(
        jnp.concatenate([low, high], axis=1),
        jnp.concatenate([spread_high, spread_high], axis=0),
    )
    value = value * jnp.concatenate([silu_rows, silu_rows], axis=0)
    wide = max(ch, 256)
    group = (iota((wide, wide), 0) // P == iota((wide, wide), 1) // P).astype(f32).astype(bf16)
    high, low = split2(value * value)
    for start in range(0, C, wide):
        stop = start + wide
        square = dot(low[:, start:stop], group) + dot(high[:, start:stop], group)
        normed = value[:, start:stop] * lax.rsqrt(square * (1.0 / P) + epsilon)
        out_high[:, start:stop], out_low[:, start:stop] = split2(
            (normed[0:T] + normed[T : 2 * T]) * gains[:, start:stop]
        )


def project_kernel(dims, *refs):
    V, D, hl, ch, nh, ns, T, N = dims
    P = ch // hl
    refs = list(refs)

    def take(number):
        taken, refs[:] = refs[:number], refs[number:]
        return taken

    high, low, embedded, small, own_high, own_low, state_high, state_low = take(8)
    order = in_turn(nh)[::-1]
    nears = dict(zip(order, take(nh - 1)))
    others = dict(zip(order, take(nh - 1)))
    out_state, out_high, out_low, out_scale = take(4)
    out_write, out_inner, out_stepped, out_total = take(4)
    half = ch // 2
    base = V + 2 + 3 * hl
    mine = lax.axis_index("seq")

    pieces = []
    for k in range(1, nh):
        near = nears[k][base : base + half, 0:D]
        other = others[k][base : base + half, 0:D]
        even = lax.rem(lax.bitwise_xor(mine, partners(ns, nh)[k][0]), 2) == 0
        pieces.append(jnp.where(even, near, other))
        pieces.append(jnp.where(even, other, near))
    weights = split2(jnp.concatenate(pieces, axis=0))
    weights = (
        jnp.concatenate([own_high[...], weights[0]], axis=0),
        jnp.concatenate([own_low[...], weights[1]], axis=0),
    )
    hidden = embedded[...] + dot_split((high[...], low[...]), weights)
    split = split2(hidden)
    out_high[...], out_low[...] = split
    scale = lax.rsqrt(jnp.mean(hidden * hidden, axis=-1, keepdims=True) + epsilon)
    out_scale[...] = jnp.broadcast_to(scale, (T, ch))

    rows = dot_split(split, (state_high[...], state_low[...])) * scale
    inner, write = rows[:, 0:ch], rows[:, 2 * ch :]
    step = softplus(rows[:, ch : 2 * ch] + small[0:1, :])
    stepped = inner * step
    upto = (iota((T, T), 0) >= iota((T, T), 1)).astype(f32).astype(bf16)
    total = dot_left_exact(upto, -small[1:2, :] * step)
    end = total[T - 1 : T, :]
    state = dot3(stepped * jnp.exp(end - total), write, TN)
    out_state[0:ch, :] = state
    for head in range(hl):
        out_state[ch + head : ch + head + 1, :] = jnp.broadcast_to(
            end[:, head * P : head * P + 1], (1, N)
        )
    out_write[...] = write
    out_inner[...] = inner
    out_stepped[...] = stepped
    out_total[...] = total


def block_kernel(dims, *refs):
    V, D, hl, ch, nh, ns, T, N = dims
    P = ch // hl
    refs = list(refs)

    def take(number):
        taken, refs[:] = refs[:number], refs[number:]
        return taken

    high, low, scale, write, inner, stepped, total, choose = take(8)
    rest_high, rest_low, small, outproj2 = take(4)
    base, out_read, out_gate, own, out_high, out_low, hidden_ref = take(7)
    rows = dot_split((high[...], low[...]), (rest_high[...], rest_low[...]))
    out_gate[...] = silu(rows[:, 0:ch] * scale[...])
    read = rows[:, ch:] * scale[...]
    out_read[...] = read
    products = dot3(read, write[...], NT)
    stepped_high, stepped_low = split2(stepped[...])
    select = (iota((8, ch), 1) == iota((8, ch), 0) * P).astype(f32).astype(bf16)
    total_high, total_middle, total_low = split3(total[...])
    total_t = (dot(select, total_low, NT) + dot(select, total_middle, NT)) + dot(
        select, total_high, NT
    )
    allowed = iota((T, T), 0) >= iota((T, T), 1)
    parts = []
    for head in range(hl):
        start, stop = head * P, (head + 1) * P
        differ = total[:, start : start + 1] - total_t[head : head + 1, :]
        weights = jnp.where(allowed, jnp.exp(jnp.where(allowed, differ, 0.0)), 0.0) * products
        part = dot_split(
            split2(weights), (stepped_high[:, start:stop], stepped_low[:, start:stop])
        )
        parts.append(part + small[2:3, start:stop] * inner[:, start:stop])
    base[...] = jnp.concatenate(parts, axis=1)
    share = T // nh
    hidden_ref[...] = high[...].astype(f32) + low[...].astype(f32)
    place = pl.multiple_of(lax.axis_index("head") * share, 8)
    out_gain = jnp.transpose(jnp.broadcast_to(small[3:4, :], (128, ch)))
    out_high[...], out_low[...] = split2(outproj2[...] * out_gain[:, 0:1])
    own[...] = dot_right_exact(hidden_ref[pl.ds(place, share), :], choose[...])


def state_rows(dims, values):
    V, D, hl, ch, nh, ns, T, N = dims
    head_of = iota((ch, N), 0) // (ch // hl)
    result = jnp.broadcast_to(values[0:1, :], (ch, N))
    for head in range(1, hl):
        result = jnp.where(head_of == head, values[head : head + 1, :], result)
    return result


def join_kernel(dims, bit, total, prefix, came, out_total, out_prefix):
    V, D, hl, ch, nh, ns, T, N = dims
    later = lax.rem(lax.div(lax.axis_index("seq"), 2**bit), 2) == 1
    came_state, came_log = came[0:ch, :], came[ch : ch + hl, :]
    state, log = total[0:ch, :], total[ch : ch + hl, :]
    factor = jnp.exp(state_rows(dims, jnp.where(later, log, came_log)))
    out_total[0:ch, :] = jnp.where(
        later, factor * came_state + state, factor * state + came_state
    )
    out_total[ch : ch + hl, :] = log + came_log
    if prefix is None:
        out_prefix[0:ch, :] = jnp.where(later, came_state, 0.0)
        out_prefix[ch : ch + hl, :] = jnp.where(later, came_log, 0.0)
    else:
        joined = prefix_joined(dims, bit, prefix, came)
        out_prefix[0:ch, :] = joined
        out_prefix[ch : ch + hl, :] = prefix[ch : ch + hl, :] + jnp.where(later, came_log, 0.0)


def prefix_joined(dims, bit, prefix, came):
    V, D, hl, ch, nh, ns, T, N = dims
    later = lax.rem(lax.div(lax.axis_index("seq"), 2**bit), 2) == 1
    factor = jnp.exp(state_rows(dims, prefix[ch : ch + hl, :]))
    return prefix[0:ch, :] + jnp.where(later, factor * came[0:ch, :], 0.0)


def output_kernel(dims, bit, *refs):
    V, D, hl, ch, nh, ns, T, N = dims
    P = ch // hl
    prefix, came, read, base, total, gate, own, proj_high, proj_low = refs[:9]
    outs, partial_ref = refs[9 : 9 + nh], refs[9 + nh]
    entering = prefix_joined(dims, bit, prefix, came)
    value = (base[...] + dot3(read[...], entering, NT) * jnp.exp(total[...])) * gate[...]
    group = (iota((ch, ch), 0) // P == iota((ch, ch), 1) // P).astype(f32).astype(bf16)
    high, low = split2(value * value)
    square = dot(low, group) + dot(high, group)
    value = value * lax.rsqrt(square * (1.0 / P) + epsilon)
    share = T // nh
    partial_ref[...] = dot_split(split2(value), (proj_high[...], proj_low[...]))
    mine = lax.axis_index("head")
    for k in range(nh):
        place = pl.multiple_of(lax.bitwise_xor(mine, k) * share, 8)
        part = partial_ref[pl.ds(place, share), :]
        outs[k][...] = part + own[...] if k == 0 else part


def per_device(
    token_ids,
    embedding,
    complement,
    prenorm_first,
    inproj_first,
    statemap_first,
    stepmap_first,
    stepbias_first,
    rates_first,
    skipgain_first,
    outnorm_first,
    outproj_first,
    prenorm_second,
    inproj_second,
    statemap_second,
    stepmap_second,
    stepbias_second,
    rates_second,
    skipgain_second,
    outnorm_second,
    outproj_second,
):
    nh, ns = lax.axis_size("head"), lax.axis_size("seq")
    V, D = embedding.shape
    ch = inproj_first.shape[2]
    hl = stepmap_first.shape[1]
    N = statemap_first.shape[2]
    T = token_ids.shape[0]
    LV = nh * hl * V
    dims = (V, D, hl, ch, nh, ns, T, N)
    vmem = pl.BlockSpec(memory_space=pltpu.VMEM)
    smem = pl.BlockSpec(memory_space=pltpu.SMEM)
    anywhere = pl.BlockSpec(memory_space=pl.ANY)
    params = pltpu.CompilerParams(vmem_limit_bytes=LIMIT)

    def shape(*sizes, dtype=f32):
        return jax.ShapeDtypeStruct(sizes, dtype)

    def halves(*sizes):
        return [shape(*sizes, dtype=bf16)] * 2

    def room(value):
        return pltpu.VMEM(value.shape, value.dtype)

    def line(value):
        return value.reshape(1, -1)

    def flat(value):
        return value.reshape(-1, value.shape[-1])

    heavy = pl.CostEstimate(flops=960 * T * D * D, bytes_accessed=4 * T * D, transcendentals=T * D)

    head_rows = V + 2 + 3 * hl
    half = ch // 2
    width = max(2 * ch, T, D)
    share = T // nh
    fetched = [
        flat(inproj_first),
        line(token_ids),
        embedding,
        line(prenorm_first),
        stepmap_first.T,
        line(stepbias_first),
        line(rates_first),
        line(skipgain_first),
        line(outnorm_first),
    ]
    message = pl.pallas_call(
        functools.partial(tables_kernel, dims),
        out_shape=shape(head_rows + half, width),
        in_specs=[anywhere] * (len(fetched) + 1),
        out_specs=vmem,
        scratch_shapes=[room(value) for value in fetched]
        + [pltpu.SemaphoreType.DMA((len(fetched) + 1,))],
        compiler_params=pltpu.CompilerParams(vmem_limit_bytes=TABLES_LIMIT),
        cost_estimate=heavy,
        name="tables",
    )(*fetched, outproj_first)

    prepared = [
        embedding,
        line(prenorm_first),
        flat(statemap_first),
        line(complement),
        outproj_first,
        line(prenorm_second),
        flat(inproj_second),
        flat(statemap_second),
        stepmap_second.T,
        stepbias_second,
        rates_second,
        skipgain_second,
        line(outnorm_second),
    ]
    (
        pair_table,
        small,
        choose,
        own_high,
        own_low,
        state_high,
        state_low,
        rest_high,
        rest_low,
    ) = pl.pallas_call(
        functools.partial(prepare_kernel, dims),
        out_shape=(
            shape(V, LV),
            shape(8, ch),
            shape(D, D, dtype=bf16),
            *halves(ch, D),
            *halves(D, 2 * ch + N),
            *halves(D, ch + N),
        ),
        in_specs=[vmem] * 9 + [smem] * 3 + [vmem],
        out_specs=(vmem,) * 9,
        compiler_params=params,
        cost_estimate=heavy,
        name="prepare",
    )(*prepared)

    count = max(ns, nh)
    messages = {0: message}
    for k in in_turn(count):
        seq_bits, head_bits = partners(ns, nh)[k]
        pairs = [
            (seq * nh + head, (seq ^ seq_bits) * nh + (head ^ head_bits))
            for seq in range(ns)
            for head in range(nh)
        ]
        sent = message if k < nh else message[0:head_rows]
        messages[k] = lax.ppermute(sent, ("seq", "head"), pairs)
    swap = [(seq, seq ^ 1) for seq in range(ns)]
    order = in_turn(nh)[::-1]
    others = [lax.ppermute(messages[k], "seq", swap) for k in order]

    mixed_high, mixed_low, embedded = pl.pallas_call(
        functools.partial(mix_kernel, dims),
        out_shape=(*halves(T, nh * ch), shape(T, D)),
        in_specs=[vmem] * (count + 2),
        out_specs=(vmem,) * 3,
        scratch_shapes=[pltpu.VMEM((max(ns, 8), T), f32)],
        compiler_params=params,
        cost_estimate=heavy,
        name="mix",
    )(*[messages[k] for k in in_turn(count)[::-1] + [0]], embedding, pair_table)

    state, hidden_high, hidden_low, scale, write, inner, stepped, total = pl.pallas_call(
        functools.partial(project_kernel, dims),
        out_shape=(
            shape(ch + 8, N),
            *halves(T, D),
            shape(T, ch),
            shape(T, N),
            shape(T, ch),
            shape(T, ch),
            shape(T, ch),
        ),
        in_specs=[vmem] * (8 + 2 * (nh - 1)),
        out_specs=(vmem,) * 8,
        compiler_params=params,
        name="project",
    )(
        mixed_high,
        mixed_low,
        embedded,
        small,
        own_high,
        own_low,
        state_high,
        state_low,
        *[messages[k] for k in order],
        *others,
    )

    base, read, gate, own, proj_high, proj_low = pl.pallas_call(
        functools.partial(block_kernel, dims),
        out_shape=(shape(T, ch), shape(T, N), shape(T, ch), shape(share, D), *halves(ch, D)),
        in_specs=[vmem] * 12,
        out_specs=(vmem,) * 6,
        scratch_shapes=[pltpu.VMEM((T, D), f32)],
        compiler_params=params,
        cost_estimate=heavy,
        name="block",
    )(
        hidden_high,
        hidden_low,
        scale,
        write,
        inner,
        stepped,
        total,
        choose,
        rest_high,
        rest_low,
        small,
        outproj_second,
    )

    prefix = None
    bits = ns.bit_length() - 1
    for bit in range(bits):
        came = lax.ppermute(state, "seq", [(seq, seq ^ 2**bit) for seq in range(ns)])
        if bit == bits - 1:
            break
        given = [state] + ([] if prefix is None else [prefix]) + [came]

        def join(bit, known, *refs):
            if known:
                join_kernel(dims, bit, *refs)
            else:
                join_kernel(dims, bit, refs[0], None, *refs[1:])

        state, prefix = pl.pallas_call(
            functools.partial(join, bit, prefix is not None),
            out_shape=(shape(ch + 8, N),) * 2,
            in_specs=[vmem] * len(given),
            out_specs=(vmem,) * 2,
            compiler_params=params,
            name="join",
        )(*given)
    if prefix is None:
        prefix = jnp.zeros_like(state)

    parts = pl.pallas_call(
        functools.partial(output_kernel, dims, bits - 1),
        out_shape=(shape(share, D),) * nh,
        in_specs=[vmem] * 9,
        out_specs=(vmem,) * nh,
        scratch_shapes=[pltpu.VMEM((T, D), f32)],
        compiler_params=params,
        name="output",
    )(prefix, came, read, base, total, gate, own, proj_high, proj_low)
    result = parts[0]
    for k in in_turn(nh):
        pairs = [(source, source ^ k) for source in range(nh)]
        result = result + lax.ppermute(parts[k], "head", pairs)
    return result


def solution(mesh):
    return jax.shard_map(
        per_device,
        mesh=mesh,
        in_specs=(
            P(("rep", "seq")),
            P(),
            P(),
            P(),
            P(None, None, "head"),
            P(),
            P(None, "head"),
            P("head"),
            P("head"),
            P("head"),
            P("head"),
            P("head", None),
            P(),
            P(None, None, "head"),
            P(),
            P(None, "head"),
            P("head"),
            P("head"),
            P("head"),
            P("head"),
            P("head", None),
        ),
        out_specs=P(("rep", "seq", "head"), None),
        check_vma=False,
    )
```

```python
import functools

import jax
import jax.numpy as jnp
from jax import lax
from jax.experimental import pallas as pl
from jax.experimental.pallas import tpu as pltpu
from jax.sharding import PartitionSpec as P

epsilon = 1e-05
f32 = jnp.float32
bf16 = jnp.bfloat16
LIMIT = 48 * 1024 * 1024
TABLES_LIMIT = 60 * 1000 * 1000

MM = (((1,), (0,)), ((), ()))
NT = (((1,), (1,)), ((), ()))
TN = (((0,), (0,)), ((), ()))


def partners(ns, nh):
    count = max(ns, nh)
    return [((ns - k) if 0 < k < ns else 0, k if k < nh else 0) for k in range(count)]


def in_turn(count):
    return sorted(range(1, count), key=lambda k: (-k.bit_length(), k))


def iota(shape, axis):
    return lax.broadcasted_iota(jnp.int32, shape, axis)


def split2(value):
    high = value.astype(bf16)
    return high, (value - high.astype(f32)).astype(bf16)


def split3(value):
    high = value.astype(bf16)
    rest = value - high.astype(f32)
    middle = rest.astype(bf16)
    return high, middle, (rest - middle.astype(f32)).astype(bf16)


def dot(left, right, dims=MM):
    return lax.dot_general(left, right, dims, preferred_element_type=f32)


def dot_split(left, right, dims=MM):
    return (
        dot(left[0], right[1], dims) + dot(left[1], right[0], dims)
    ) + dot(left[0], right[0], dims)


def dot3(left, right, dims=MM):
    return dot_split(split2(left), split2(right), dims)


def dot_left_exact(left, right, dims=MM):
    high, middle, low = split3(right)
    return (dot(left, low, dims) + dot(left, middle, dims)) + dot(left, high, dims)


def dot_right_exact(left, right, dims=MM):
    high, middle, low = split3(left)
    return (dot(low, right, dims) + dot(middle, right, dims)) + dot(high, right, dims)


def softplus(value):
    return jnp.maximum(value, 0.0) + jnp.log1p(jnp.exp(-jnp.abs(value)))


def silu(value):
    return value / (1.0 + jnp.exp(-value))


def rms(value):
    return value * lax.rsqrt(jnp.mean(value * value, axis=-1, keepdims=True) + epsilon)


def fetch(sources, places, semaphores):
    copies = []
    for number, (source, place) in enumerate(zip(sources, places)):
        copies.append(pltpu.make_async_copy(source, place, semaphores.at[number]))
        copies[-1].start()
    return copies


def fetch(sources, places, semaphores):
    copies = []
    for number, (source, place) in enumerate(zip(sources, places)):
        copies.append(pltpu.make_async_copy(source, place, semaphores.at[number]))
        copies[-1].start()
    return copies


def tables_kernel(dims, *refs):
    V, D, hl, ch, nh, ns, T, N = dims
    refs = list(refs)

    def take(number):
        taken, refs[:] = refs[:number], refs[number:]
        return taken

    sources = take(9)
    outproj_source, message, part = take(3)
    places = take(9)
    semaphores = take(1)[0]
    half = ch // 2
    core = lax.rem(lax.axis_index("seq"), 2)
    copies = fetch(
        sources + [outproj_source.at[pl.ds(pl.multiple_of(core * half, 8), half), :]],
        places + [part],
        semaphores,
    )
    flip = (iota((T, T), 0) + iota((T, T), 1) == T - 1).astype(f32).astype(bf16)
    for copy in copies[:9]:
        copy.wait()
    (inproj, tok, emb, prenorm, stepmap, bias, rates, skip, outnorm) = places
    normed = split2(rms(emb[...]) * prenorm[...])
    raw_t = dot_split(split2(stepmap[...]), normed, NT)
    gate = dot_split(normed, split2(inproj[pl.ds(0, D, stride=2), :]))
    inner = dot_split(normed, split2(inproj[pl.ds(1, D, stride=2), :]))
    message[0:V, 0:ch] = gate
    message[0:V, ch : 2 * ch] = inner
    tokens = jnp.broadcast_to(tok[...].astype(f32), (8, T)).astype(bf16)
    message[V : V + 1, 0:T] = dot(tokens, flip)[0:1]
    message[V + 1 : V + 2, 0:ch] = outnorm[...]
    for head in range(hl):
        line = softplus(raw_t[head : head + 1, :] + bias[:, head : head + 1])
        row = V + 2 + head
        message[row : row + 1, 0:V] = line
        message[row + hl : row + hl + 1, 0:V] = -rates[:, head : head + 1] * line
        message[row + 2 * hl : row + 2 * hl + 1, 0:V] = jnp.broadcast_to(
            skip[:, head : head + 1], (1, V)
        )
    copies[9].wait()


def head_line(dims, values):
    V, D, hl, ch, nh, ns, T, N = dims
    head_of = iota((1, ch), 1) // (ch // hl)
    line = jnp.zeros((1, ch), f32)
    for head in range(hl):
        line = jnp.where(head_of == head, values[head], line)
    return line


def prepare_kernel(dims, *refs):
    V, D, hl, ch, nh, ns, T, N = dims
    H, P = nh * hl, ch // hl
    refs = list(refs)

    def take(number):
        taken, refs[:] = refs[:number], refs[number:]
        return taken

    emb, prenorm, statemap, complement, outproj = take(5)
    prenorm2, inproj2, statemap2, stepmap2 = take(4)
    bias2, rates2, skip2, outnorm2 = take(4)
    pairs, small, choose_out, own_high, own_low = take(5)
    state_high, state_low, rest_high, rest_low = take(4)
    normed = split2(rms(emb[...]) * prenorm[...])
    write = dot_split(normed, split2(statemap[pl.ds(0, D, stride=2), :]))
    read = dot_split(normed, split2(statemap[pl.ds(1, D, stride=2), :]))
    pairs[...] = dot3(read, jnp.concatenate([write] * H, axis=0), NT)
    own_high[...], own_low[...] = split2(outproj[...])
    choose = (complement[...] == iota((D, D), 0)).astype(f32).astype(bf16)
    choose_out[...] = choose
    gain = jnp.transpose(jnp.broadcast_to(prenorm2[...], (128, D)))

    def weights(values):
        return split2(dot_left_exact(choose, values))

    gain_wide = gain[:, 0:1]
    inner = inproj2[pl.ds(1, D, stride=2), :] * gain_wide
    step = jnp.transpose(
        jnp.concatenate(
            [jnp.broadcast_to(stepmap2[head : head + 1, :], (P, D)) for head in range(hl)], axis=0
        )
    )
    write2 = statemap2[pl.ds(0, D, stride=2), :] * gain_wide
    state_high[...], state_low[...] = weights(
        jnp.concatenate([inner, step * gain_wide, write2], axis=1)
    )
    gate = inproj2[pl.ds(0, D, stride=2), :] * gain_wide
    read2 = statemap2[pl.ds(1, D, stride=2), :] * gain_wide
    rest_high[...], rest_low[...] = weights(jnp.concatenate([gate, read2], axis=1))
    small[0:1, :] = head_line(dims, bias2)
    small[1:2, :] = head_line(dims, rates2)
    small[2:3, :] = head_line(dims, skip2)
    small[3:4, :] = outnorm2[...]


def shift_rows(value, amount, fill):
    size = value.shape[0]
    if amount % 8 == 0:
        empty = jnp.full((abs(amount),) + value.shape[1:], fill, value.dtype)
        if amount > 0:
            return jnp.concatenate([empty, value[: size - amount]], axis=0)
        return jnp.concatenate([value[-amount:], empty], axis=0)
    rolled = pltpu.roll(value, amount % size, 0)
    row = iota(value.shape, 0)
    have = (row >= amount) if amount > 0 else (row < size + amount)
    return jnp.where(have, rolled, fill)


def scan_rows(decay, value, sign):
    size = value.shape[0]
    amount = 1
    while amount < size:
        value = value + decay * shift_rows(value, sign * amount, 0.0)
        if 2 * amount < size:
            decay = decay * shift_rows(decay, sign * amount, 1.0)
        amount *= 2
    return value


def mix_kernel(dims, *refs):
    V, D, hl, ch, nh, ns, T, N = dims
    H, LV, P = nh * hl, nh * hl * V, ch // hl
    C = nh * ch
    refs = list(refs)

    def take(number):
        taken, refs[:] = refs[:number], refs[number:]
        return taken

    count = max(ns, nh)
    packets = dict(zip(in_turn(count)[::-1] + [0], take(count)))
    emb, pairs = take(2)
    out_high, out_low, out_embedded = take(3)
    tokens = take(1)[0]
    mine = lax.axis_index("seq")

    for k in range(ns):
        block = ns - 1 - lax.bitwise_xor(mine, partners(ns, nh)[k][0])
        tokens[pl.ds(block, 1), :] = packets[k][V : V + 1, 0:T]

    def rows_of(place):
        low = V + 2 + place * hl
        return jnp.concatenate([packets[k][low : low + hl, 0:V] for k in range(nh)], axis=0)

    step_t, log_t, skip_t = rows_of(0), rows_of(1), rows_of(2)
    spread_heads = (iota((H, LV), 1) // V == iota((H, LV), 0)).astype(f32).astype(bf16)

    def widen(value):
        high, middle, low = split3(value)
        return (dot(low, spread_heads, TN) + dot(middle, spread_heads, TN)) + dot(
            high, spread_heads, TN
        )

    own = iota((V, LV), 1) % V == iota((V, LV), 0)
    decay_table = jnp.exp(widen(log_t))
    step_table = jnp.where(own, widen(step_t), 0.0)
    gain_table = jnp.where(own, widen(skip_t), 0.0)
    gates = jnp.concatenate([packets[k][0:V, 0:ch] for k in range(nh)], axis=1)
    inners = jnp.concatenate([packets[k][0:V, ch : 2 * ch] for k in range(nh)], axis=1)
    gains = jnp.concatenate([packets[k][V + 1 : V + 2, 0:ch] for k in range(nh)], axis=1)

    token_row = (iota((LV, T), 0) % V).astype(f32)
    log_split = jnp.concatenate(split3(log_t), axis=1)
    onehots, logs = [], []
    for block in range(ns):
        onehot = (tokens[block : block + 1, :] == token_row).astype(f32).astype(bf16)
        onehots.append(onehot)
        logs.append(dot(log_split, onehot[0 : 3 * V, :]))
    logs = jnp.concatenate(logs, axis=0)
    first, second = iota((T, T), 0), iota((T, T), 1)
    later = (first > second).astype(f32).astype(bf16)
    sooner = (first < second).astype(f32).astype(bf16)
    logs3 = split3(logs)
    after = dot(logs3[2], later) + dot(logs3[1], later) + dot(logs3[0], later)
    before = dot(logs3[2], sooner) + dot(logs3[1], sooner) + dot(logs3[0], sooner)
    totals = jnp.sum(logs, axis=1, keepdims=True)
    total_rows = jnp.broadcast_to(totals, (ns * H, 128))
    row, column = iota((ns * H, ns * H), 0), iota((ns * H, ns * H), 1)
    row_block, column_block = row // H, column // H
    between = ((row_block < column_block) & (column_block < mine)) | (
        (row_block > column_block) & (column_block > mine)
    )
    between = (between & (row % H == column % H)).astype(f32).astype(bf16)
    gap = dot_left_exact(between, total_rows)[:, 0:1]
    block_of = iota((ns * H, T), 0) // H
    weight_up = jnp.where(block_of < mine, jnp.exp(after + gap), 0.0)
    weight_down = jnp.where(block_of > mine, jnp.exp(before + gap), 0.0)
    entering = jnp.zeros((2 * H, LV), f32)
    for block in range(ns):
        both = jnp.concatenate(
            [weight_up[block * H : (block + 1) * H], weight_down[block * H : (block + 1) * H]],
            axis=0,
        )
        high, low = split2(both)
        entering = entering + (dot(low, onehots[block], NT) + dot(high, onehots[block], NT))
    diagonal = iota((H, LV), 1) // V == iota((H, LV), 0)
    step_row = jnp.sum(step_table, axis=0, keepdims=True)
    enter_up = step_row * jnp.sum(
        jnp.where(diagonal, entering[0:H], 0.0), axis=0, keepdims=True
    )
    enter_down = step_row * jnp.sum(
        jnp.where(diagonal, entering[H : 2 * H], 0.0), axis=0, keepdims=True
    )

    looked = jnp.concatenate(
        [decay_table, step_table, pairs[...], gain_table, silu(gates), emb[...]], axis=1
    )
    looked = jnp.concatenate(split3(looked), axis=0)
    token = tokens[pl.ds(mine, 1), :]
    onehot = (token == (iota((3 * V, T), 0) % V).astype(f32)).astype(f32).astype(bf16)
    rows = dot(onehot, looked, TN)
    decay, step = rows[:, 0:LV], rows[:, LV : 2 * LV]
    pair, gain = rows[:, 2 * LV : 3 * LV], rows[:, 3 * LV : 4 * LV]
    silu_rows = rows[:, 4 * LV : 4 * LV + C]
    out_embedded[...] = rows[:, 4 * LV + C :]

    position = iota((T, LV), 0)
    up = scan_rows(decay, jnp.where(position == 0, step + decay * enter_up, step), 1)
    down = scan_rows(decay, jnp.where(position == T - 1, step + decay * enter_down, step), -1)

    tiled = jnp.concatenate([inners] * H, axis=0)
    spread = jnp.where(iota((LV, C), 0) // V == iota((LV, C), 1) // P, tiled, 0.0)
    spread_high, spread_low = split2(spread)
    both = jnp.concatenate([up * pair + gain, down * pair + gain], axis=0)
    high, low = split2(both)
    value = dot(high, spread_low) + dot(
        jnp.concatenate([low, high], axis=1),
        jnp.concatenate([spread_high, spread_high], axis=0),
    )
    value = value * jnp.concatenate([silu_rows, silu_rows], axis=0)
    wide = max(ch, 256)
    group = (iota((wide, wide), 0) // P == iota((wide, wide), 1) // P).astype(f32).astype(bf16)
    high, low = split2(value * value)
    for start in range(0, C, wide):
        stop = start + wide
        square = dot(low[:, start:stop], group) + dot(high[:, start:stop], group)
        normed = value[:, start:stop] * lax.rsqrt(square * (1.0 / P) + epsilon)
        out_high[:, start:stop], out_low[:, start:stop] = split2(
            (normed[0:T] + normed[T : 2 * T]) * gains[:, start:stop]
        )


def project_kernel(dims, *refs):
    V, D, hl, ch, nh, ns, T, N = dims
    P = ch // hl
    refs = list(refs)

    def take(number):
        taken, refs[:] = refs[:number], refs[number:]
        return taken

    high, low, embedded, small, own_high, own_low, state_high, state_low = take(8)
    order = in_turn(nh)[::-1]
    nears = dict(zip(order, take(nh - 1)))
    others = dict(zip(order, take(nh - 1)))
    out_state, out_high, out_low, out_scale = take(4)
    out_write, out_inner, out_stepped, out_total = take(4)
    mine = lax.axis_index("seq")

    even = lax.rem(mine, 2) == 0
    pieces = []
    for k in range(1, nh):
        near, other = nears[k][...], others[k][...]
        pieces.append(jnp.where(even, near, other))
        pieces.append(jnp.where(even, other, near))
    weights = split2(jnp.concatenate(pieces, axis=0))
    weights = (
        jnp.concatenate([own_high[...], weights[0]], axis=0),
        jnp.concatenate([own_low[...], weights[1]], axis=0),
    )
    hidden = embedded[...] + dot_split((high[...], low[...]), weights)
    split = split2(hidden)
    out_high[...], out_low[...] = split
    scale = lax.rsqrt(jnp.mean(hidden * hidden, axis=-1, keepdims=True) + epsilon)
    out_scale[...] = jnp.broadcast_to(scale, (T, ch))

    rows = dot_split(split, (state_high[...], state_low[...])) * scale
    inner, write = rows[:, 0:ch], rows[:, 2 * ch :]
    step = softplus(rows[:, ch : 2 * ch] + small[0:1, :])
    stepped = inner * step
    upto = (iota((T, T), 0) >= iota((T, T), 1)).astype(f32).astype(bf16)
    total = dot_left_exact(upto, -small[1:2, :] * step)
    end = total[T - 1 : T, :]
    state = dot3(stepped * jnp.exp(end - total), write, TN)
    out_state[0:ch, :] = state
    for head in range(hl):
        out_state[ch + head : ch + head + 1, :] = jnp.broadcast_to(
            end[:, head * P : head * P + 1], (1, N)
        )
    out_write[...] = write
    out_inner[...] = inner
    out_stepped[...] = stepped
    out_total[...] = total


def block_kernel(dims, *refs):
    V, D, hl, ch, nh, ns, T, N = dims
    P = ch // hl
    refs = list(refs)

    def take(number):
        taken, refs[:] = refs[:number], refs[number:]
        return taken

    high, low, scale, write, inner, stepped, total, choose = take(8)
    rest_high, rest_low, small, outproj2 = take(4)
    base, out_read, out_gate, own, out_high, out_low, hidden_ref = take(7)
    rows = dot_split((high[...], low[...]), (rest_high[...], rest_low[...]))
    out_gate[...] = silu(rows[:, 0:ch] * scale[...])
    read = rows[:, ch:] * scale[...]
    out_read[...] = read
    products = dot3(read, write[...], NT)
    stepped_high, stepped_low = split2(stepped[...])
    select = (iota((8, ch), 1) == iota((8, ch), 0) * P).astype(f32).astype(bf16)
    total_high, total_middle, total_low = split3(total[...])
    total_t = (dot(select, total_low, NT) + dot(select, total_middle, NT)) + dot(
        select, total_high, NT
    )
    allowed = iota((T, T), 0) >= iota((T, T), 1)
    parts = []
    for head in range(hl):
        start, stop = head * P, (head + 1) * P
        differ = total[:, start : start + 1] - total_t[head : head + 1, :]
        weights = jnp.where(allowed, jnp.exp(jnp.where(allowed, differ, 0.0)), 0.0) * products
        part = dot_split(
            split2(weights), (stepped_high[:, start:stop], stepped_low[:, start:stop])
        )
        parts.append(part + small[2:3, start:stop] * inner[:, start:stop])
    base[...] = jnp.concatenate(parts, axis=1)
    share = T // nh
    hidden_ref[...] = high[...].astype(f32) + low[...].astype(f32)
    place = pl.multiple_of(lax.axis_index("head") * share, 8)
    out_gain = jnp.transpose(jnp.broadcast_to(small[3:4, :], (128, ch)))
    out_high[...], out_low[...] = split2(outproj2[...] * out_gain[:, 0:1])
    own[...] = dot_right_exact(hidden_ref[pl.ds(place, share), :], choose[...])


def state_rows(dims, values):
    V, D, hl, ch, nh, ns, T, N = dims
    head_of = iota((ch, N), 0) // (ch // hl)
    result = jnp.broadcast_to(values[0:1, :], (ch, N))
    for head in range(1, hl):
        result = jnp.where(head_of == head, values[head : head + 1, :], result)
    return result


def join_kernel(dims, bit, total, prefix, came, out_total, out_prefix):
    V, D, hl, ch, nh, ns, T, N = dims
    later = lax.rem(lax.div(lax.axis_index("seq"), 2**bit), 2) == 1
    came_state, came_log = came[0:ch, :], came[ch : ch + hl, :]
    state, log = total[0:ch, :], total[ch : ch + hl, :]
    factor = jnp.exp(state_rows(dims, jnp.where(later, log, came_log)))
    out_total[0:ch, :] = jnp.where(
        later, factor * came_state + state, factor * state + came_state
    )
    out_total[ch : ch + hl, :] = log + came_log
    if prefix is None:
        out_prefix[0:ch, :] = jnp.where(later, came_state, 0.0)
        out_prefix[ch : ch + hl, :] = jnp.where(later, came_log, 0.0)
    else:
        joined = prefix_joined(dims, bit, prefix, came)
        out_prefix[0:ch, :] = joined
        out_prefix[ch : ch + hl, :] = prefix[ch : ch + hl, :] + jnp.where(later, came_log, 0.0)


def prefix_joined(dims, bit, prefix, came):
    V, D, hl, ch, nh, ns, T, N = dims
    later = lax.rem(lax.div(lax.axis_index("seq"), 2**bit), 2) == 1
    factor = jnp.exp(state_rows(dims, prefix[ch : ch + hl, :]))
    return prefix[0:ch, :] + jnp.where(later, factor * came[0:ch, :], 0.0)


def output_kernel(dims, bit, *refs):
    V, D, hl, ch, nh, ns, T, N = dims
    P = ch // hl
    prefix, came, read, base, total, gate, own, proj_high, proj_low = refs[:9]
    outs, partial_ref = refs[9 : 9 + nh], refs[9 + nh]
    entering = prefix_joined(dims, bit, prefix, came)
    value = (base[...] + dot3(read[...], entering, NT) * jnp.exp(total[...])) * gate[...]
    group = (iota((ch, ch), 0) // P == iota((ch, ch), 1) // P).astype(f32).astype(bf16)
    high, low = split2(value * value)
    square = dot(low, group) + dot(high, group)
    value = value * lax.rsqrt(square * (1.0 / P) + epsilon)
    share = T // nh
    partial_ref[...] = dot_split(split2(value), (proj_high[...], proj_low[...]))
    mine = lax.axis_index("head")
    for k in range(nh):
        place = pl.multiple_of(lax.bitwise_xor(mine, k) * share, 8)
        part = partial_ref[pl.ds(place, share), :]
        outs[k][...] = part + own[...] if k == 0 else part


def per_device(
    token_ids,
    embedding,
    complement,
    prenorm_first,
    inproj_first,
    statemap_first,
    stepmap_first,
    stepbias_first,
    rates_first,
    skipgain_first,
    outnorm_first,
    outproj_first,
    prenorm_second,
    inproj_second,
    statemap_second,
    stepmap_second,
    stepbias_second,
    rates_second,
    skipgain_second,
    outnorm_second,
    outproj_second,
):
    nh, ns = lax.axis_size("head"), lax.axis_size("seq")
    V, D = embedding.shape
    ch = inproj_first.shape[2]
    hl = stepmap_first.shape[1]
    N = statemap_first.shape[2]
    T = token_ids.shape[0]
    LV = nh * hl * V
    dims = (V, D, hl, ch, nh, ns, T, N)
    vmem = pl.BlockSpec(memory_space=pltpu.VMEM)
    smem = pl.BlockSpec(memory_space=pltpu.SMEM)
    anywhere = pl.BlockSpec(memory_space=pl.ANY)
    params = pltpu.CompilerParams(vmem_limit_bytes=LIMIT)

    def shape(*sizes, dtype=f32):
        return jax.ShapeDtypeStruct(sizes, dtype)

    def halves(*sizes):
        return [shape(*sizes, dtype=bf16)] * 2

    def room(value):
        return pltpu.VMEM(value.shape, value.dtype)

    def line(value):
        return value.reshape(1, -1)

    def flat(value):
        return value.reshape(-1, value.shape[-1])

    heavy = pl.CostEstimate(flops=960 * T * D * D, bytes_accessed=4 * T * D, transcendentals=T * D)

    head_rows = V + 2 + 3 * hl
    half = ch // 2
    width = max(2 * ch, T)
    share = T // nh
    fetched = [
        flat(inproj_first),
        line(token_ids),
        embedding,
        line(prenorm_first),
        stepmap_first.T,
        line(stepbias_first),
        line(rates_first),
        line(skipgain_first),
        line(outnorm_first),
    ]
    message, part = pl.pallas_call(
        functools.partial(tables_kernel, dims),
        out_shape=(shape(head_rows, width), shape(half, D)),
        in_specs=[anywhere] * (len(fetched) + 1),
        out_specs=(vmem, vmem),
        scratch_shapes=[room(value) for value in fetched]
        + [pltpu.SemaphoreType.DMA((len(fetched) + 1,))],
        compiler_params=pltpu.CompilerParams(vmem_limit_bytes=TABLES_LIMIT),
        cost_estimate=heavy,
        name="tables",
    )(*fetched, outproj_first)

    prepared = [
        embedding,
        line(prenorm_first),
        flat(statemap_first),
        line(complement),
        outproj_first,
        line(prenorm_second),
        flat(inproj_second),
        flat(statemap_second),
        stepmap_second.T,
        stepbias_second,
        rates_second,
        skipgain_second,
        line(outnorm_second),
    ]
    (
        pair_table,
        small,
        choose,
        own_high,
        own_low,
        state_high,
        state_low,
        rest_high,
        rest_low,
    ) = pl.pallas_call(
        functools.partial(prepare_kernel, dims),
        out_shape=(
            shape(V, LV),
            shape(8, ch),
            shape(D, D, dtype=bf16),
            *halves(ch, D),
            *halves(D, 2 * ch + N),
            *halves(D, ch + N),
        ),
        in_specs=[vmem] * 9 + [smem] * 3 + [vmem],
        out_specs=(vmem,) * 9,
        compiler_params=params,
        cost_estimate=heavy,
        name="prepare",
    )(*prepared)

    count = max(ns, nh)
    messages = {0: message}
    for k in in_turn(count):
        seq_bits, head_bits = partners(ns, nh)[k]
        pairs = [
            (seq * nh + head, (seq ^ seq_bits) * nh + (head ^ head_bits))
            for seq in range(ns)
            for head in range(nh)
        ]
        messages[k] = lax.ppermute(message, ("seq", "head"), pairs)
    swap = [(seq, seq ^ 1) for seq in range(ns)]
    order = in_turn(nh)[::-1]
    nears = {
        k: lax.ppermute(part, "head", [(head, head ^ k) for head in range(nh)])
        for k in in_turn(nh)
    }
    mixed_high, mixed_low, embedded = pl.pallas_call(
        functools.partial(mix_kernel, dims),
        out_shape=(*halves(T, nh * ch), shape(T, D)),
        in_specs=[vmem] * (count + 2),
        out_specs=(vmem,) * 3,
        scratch_shapes=[pltpu.VMEM((max(ns, 8), T), f32)],
        compiler_params=params,
        cost_estimate=heavy,
        name="mix",
    )(*[messages[k] for k in in_turn(count)[::-1] + [0]], embedding, pair_table)

    mixed = [mixed_high, mixed_low, embedded]
    for place, k in enumerate(order):
        place = place % len(mixed)
        mixed[place], nears[k] = lax.optimization_barrier((mixed[place], nears[k]))
    mixed_high, mixed_low, embedded = mixed
    others = [lax.ppermute(nears[k], "seq", swap) for k in order]

    state, hidden_high, hidden_low, scale, write, inner, stepped, total = pl.pallas_call(
        functools.partial(project_kernel, dims),
        out_shape=(
            shape(ch + 8, N),
            *halves(T, D),
            shape(T, ch),
            shape(T, N),
            shape(T, ch),
            shape(T, ch),
            shape(T, ch),
        ),
        in_specs=[vmem] * (8 + 2 * (nh - 1)),
        out_specs=(vmem,) * 8,
        compiler_params=params,
        name="project",
    )(
        mixed_high,
        mixed_low,
        embedded,
        small,
        own_high,
        own_low,
        state_high,
        state_low,
        *[nears[k] for k in order],
        *others,
    )

    base, read, gate, own, proj_high, proj_low = pl.pallas_call(
        functools.partial(block_kernel, dims),
        out_shape=(shape(T, ch), shape(T, N), shape(T, ch), shape(share, D), *halves(ch, D)),
        in_specs=[vmem] * 12,
        out_specs=(vmem,) * 6,
        scratch_shapes=[pltpu.VMEM((T, D), f32)],
        compiler_params=params,
        cost_estimate=heavy,
        name="block",
    )(
        hidden_high,
        hidden_low,
        scale,
        write,
        inner,
        stepped,
        total,
        choose,
        rest_high,
        rest_low,
        small,
        outproj_second,
    )

    prefix = None
    bits = ns.bit_length() - 1
    for bit in range(bits):
        came = lax.ppermute(state, "seq", [(seq, seq ^ 2**bit) for seq in range(ns)])
        if bit == bits - 1:
            break
        given = [state] + ([] if prefix is None else [prefix]) + [came]

        def join(bit, known, *refs):
            if known:
                join_kernel(dims, bit, *refs)
            else:
                join_kernel(dims, bit, refs[0], None, *refs[1:])

        state, prefix = pl.pallas_call(
            functools.partial(join, bit, prefix is not None),
            out_shape=(shape(ch + 8, N),) * 2,
            in_specs=[vmem] * len(given),
            out_specs=(vmem,) * 2,
            compiler_params=params,
            name="join",
        )(*given)
    if prefix is None:
        prefix = jnp.zeros_like(state)

    parts = pl.pallas_call(
        functools.partial(output_kernel, dims, bits - 1),
        out_shape=(shape(share, D),) * nh,
        in_specs=[vmem] * 9,
        out_specs=(vmem,) * nh,
        scratch_shapes=[pltpu.VMEM((T, D), f32)],
        compiler_params=params,
        name="output",
    )(prefix, came, read, base, total, gate, own, proj_high, proj_low)
    result = parts[0]
    for k in in_turn(nh):
        pairs = [(source, source ^ k) for source in range(nh)]
        result = result + lax.ppermute(parts[k], "head", pairs)
    return result


def solution(mesh):
    return jax.shard_map(
        per_device,
        mesh=mesh,
        in_specs=(
            P(("rep", "seq")),
            P(),
            P(),
            P(),
            P(None, None, "head"),
            P(),
            P(None, "head"),
            P("head"),
            P("head"),
            P("head"),
            P("head"),
            P("head", None),
            P(),
            P(None, None, "head"),
            P(),
            P(None, "head"),
            P("head"),
            P("head"),
            P("head"),
            P("head"),
            P("head", None),
        ),
        out_specs=P(("rep", "seq", "head"), None),
        check_vma=False,
    )
```

```python
import functools

import jax
import jax.numpy as jnp
from jax import lax
from jax.experimental import pallas as pl
from jax.experimental.pallas import tpu as pltpu
from jax.sharding import PartitionSpec as P

epsilon = 1e-05
f32 = jnp.float32
bf16 = jnp.bfloat16
LIMIT = 48 * 1024 * 1024
TABLES_LIMIT = 60 * 1000 * 1000

MM = (((1,), (0,)), ((), ()))
NT = (((1,), (1,)), ((), ()))
TN = (((0,), (0,)), ((), ()))


def partners(ns, nh):
    count = max(ns, nh)
    return [((ns - k) if 0 < k < ns else 0, k if k < nh else 0) for k in range(count)]


def in_turn(count):
    return sorted(range(1, count), key=lambda k: (-k.bit_length(), k))


def iota(shape, axis):
    return lax.broadcasted_iota(jnp.int32, shape, axis)


def split2(value):
    high = value.astype(bf16)
    return high, (value - high.astype(f32)).astype(bf16)


def split3(value):
    high = value.astype(bf16)
    rest = value - high.astype(f32)
    middle = rest.astype(bf16)
    return high, middle, (rest - middle.astype(f32)).astype(bf16)


def dot(left, right, dims=MM):
    return lax.dot_general(left, right, dims, preferred_element_type=f32)


def dot_split(left, right, dims=MM):
    axis = 1 if dims == TN else 0
    size = left[0].shape[axis]
    if size % 16:
        return (dot(left[0], right[1], dims) + dot(left[1], right[0], dims)) + dot(
            left[0], right[0], dims
        )
    both = dot(jnp.concatenate([left[1], left[0]], axis=axis), right[0], dims)
    return (dot(left[0], right[1], dims) + both[0:size]) + both[size:]


def dot3(left, right, dims=MM):
    return dot_split(split2(left), split2(right), dims)


def dot_left_exact(left, right, dims=MM):
    high, middle, low = split3(right)
    return (dot(left, low, dims) + dot(left, middle, dims)) + dot(left, high, dims)


def dot_right_exact(left, right, dims=MM):
    high, middle, low = split3(left)
    return (dot(low, right, dims) + dot(middle, right, dims)) + dot(high, right, dims)


def softplus(value):
    return jnp.maximum(value, 0.0) + jnp.log1p(jnp.exp(-jnp.abs(value)))


def silu(value):
    return value / (1.0 + jnp.exp(-value))


def rms(value):
    return value * lax.rsqrt(jnp.mean(value * value, axis=-1, keepdims=True) + epsilon)


def fetch(sources, places, semaphores):
    copies = []
    for number, (source, place) in enumerate(zip(sources, places)):
        copies.append(pltpu.make_async_copy(source, place, semaphores.at[number]))
        copies[-1].start()
    return copies


def fetch(sources, places, semaphores):
    copies = []
    for number, (source, place) in enumerate(zip(sources, places)):
        copies.append(pltpu.make_async_copy(source, place, semaphores.at[number]))
        copies[-1].start()
    return copies


def tables_kernel(dims, *refs):
    V, D, hl, ch, nh, ns, T, N = dims
    refs = list(refs)

    def take(number):
        taken, refs[:] = refs[:number], refs[number:]
        return taken

    sources = take(9)
    outproj_source, message = take(2)
    places = take(9)
    semaphores = take(1)[0]
    half = ch // 2
    base = V + 2 + 3 * hl
    core = lax.rem(lax.axis_index("seq"), 2)
    copies = fetch(
        sources + [outproj_source.at[pl.ds(pl.multiple_of(core * half, 8), half), :]],
        places + [message.at[base : base + half, 0:D]],
        semaphores,
    )
    flip = (iota((T, T), 0) + iota((T, T), 1) == T - 1).astype(f32).astype(bf16)
    for copy in copies[:9]:
        copy.wait()
    (inproj, tok, emb, prenorm, stepmap, bias, rates, skip, outnorm) = places
    normed = split2(rms(emb[...]) * prenorm[...])
    raw_t = dot_split(split2(stepmap[...]), normed, NT)
    weights = jnp.concatenate(
        [inproj[pl.ds(0, D, stride=2), :], inproj[pl.ds(1, D, stride=2), :]], axis=1
    )
    message[0:V, 0 : 2 * ch] = dot_split(normed, split2(weights))
    tokens = jnp.broadcast_to(tok[...].astype(f32), (8, T)).astype(bf16)
    message[V : V + 1, 0:T] = dot(tokens, flip)[0:1]
    message[V + 1 : V + 2, 0:ch] = outnorm[...]
    for head in range(hl):
        line = softplus(raw_t[head : head + 1, :] + bias[:, head : head + 1])
        row = V + 2 + head
        message[row : row + 1, 0:V] = line
        message[row + hl : row + hl + 1, 0:V] = -rates[:, head : head + 1] * line
        message[row + 2 * hl : row + 2 * hl + 1, 0:V] = jnp.broadcast_to(
            skip[:, head : head + 1], (1, V)
        )
    copies[9].wait()


def head_line(dims, values):
    V, D, hl, ch, nh, ns, T, N = dims
    head_of = iota((1, ch), 1) // (ch // hl)
    line = jnp.zeros((1, ch), f32)
    for head in range(hl):
        line = jnp.where(head_of == head, values[head], line)
    return line


def prepare_kernel(dims, *refs):
    V, D, hl, ch, nh, ns, T, N = dims
    H, P = nh * hl, ch // hl
    refs = list(refs)

    def take(number):
        taken, refs[:] = refs[:number], refs[number:]
        return taken

    emb, prenorm, statemap, complement, outproj = take(5)
    prenorm2, inproj2, statemap2, stepmap2 = take(4)
    bias2, rates2, skip2, outnorm2 = take(4)
    pairs, small, choose_out, own_high, own_low = take(5)
    state_high, state_low, rest_high, rest_low = take(4)
    normed = split2(rms(emb[...]) * prenorm[...])
    write = dot_split(normed, split2(statemap[pl.ds(0, D, stride=2), :]))
    read = dot_split(normed, split2(statemap[pl.ds(1, D, stride=2), :]))
    pairs[...] = dot3(read, jnp.concatenate([write] * H, axis=0), NT)
    own_high[...], own_low[...] = split2(outproj[...])
    choose = (complement[...] == iota((D, D), 0)).astype(f32).astype(bf16)
    choose_out[...] = choose
    gain = jnp.transpose(jnp.broadcast_to(prenorm2[...], (128, D)))

    def weights(values):
        return split2(dot_left_exact(choose, values))

    gain_wide = gain[:, 0:1]
    inner = inproj2[pl.ds(1, D, stride=2), :] * gain_wide
    step = jnp.transpose(
        jnp.concatenate(
            [jnp.broadcast_to(stepmap2[head : head + 1, :], (P, D)) for head in range(hl)], axis=0
        )
    )
    write2 = statemap2[pl.ds(0, D, stride=2), :] * gain_wide
    state_high[...], state_low[...] = weights(
        jnp.concatenate([inner, step * gain_wide, write2], axis=1)
    )
    gate = inproj2[pl.ds(0, D, stride=2), :] * gain_wide
    read2 = statemap2[pl.ds(1, D, stride=2), :] * gain_wide
    rest_high[...], rest_low[...] = weights(jnp.concatenate([gate, read2], axis=1))
    small[0:1, :] = head_line(dims, bias2)
    small[1:2, :] = head_line(dims, rates2)
    small[2:3, :] = head_line(dims, skip2)
    small[3:4, :] = outnorm2[...]


def shift_rows(value, amount, fill):
    size = value.shape[0]
    if amount % 8 == 0:
        empty = jnp.full((abs(amount),) + value.shape[1:], fill, value.dtype)
        if amount > 0:
            return jnp.concatenate([empty, value[: size - amount]], axis=0)
        return jnp.concatenate([value[-amount:], empty], axis=0)
    rolled = pltpu.roll(value, amount % size, 0)
    row = iota(value.shape, 0)
    have = (row >= amount) if amount > 0 else (row < size + amount)
    return jnp.where(have, rolled, fill)


def scan_rows(decay, value, sign):
    size = value.shape[0]
    amount = 1
    while amount < size:
        value = value + decay * shift_rows(value, sign * amount, 0.0)
        if 2 * amount < size:
            decay = decay * shift_rows(decay, sign * amount, 1.0)
        amount *= 2
    return value


def mix_kernel(dims, *refs):
    V, D, hl, ch, nh, ns, T, N = dims
    H, LV, P = nh * hl, nh * hl * V, ch // hl
    C = nh * ch
    refs = list(refs)

    def take(number):
        taken, refs[:] = refs[:number], refs[number:]
        return taken

    count = max(ns, nh)
    packets = dict(zip(in_turn(count)[::-1] + [0], take(count)))
    emb, pairs = take(2)
    out_high, out_low, out_embedded = take(3)
    tokens = take(1)[0]
    mine = lax.axis_index("seq")

    for k in range(ns):
        block = ns - 1 - lax.bitwise_xor(mine, partners(ns, nh)[k][0])
        tokens[pl.ds(block, 1), :] = packets[k][V : V + 1, 0:T]

    def rows_of(place):
        low = V + 2 + place * hl
        return jnp.concatenate([packets[k][low : low + hl, 0:V] for k in range(nh)], axis=0)

    step_t, log_t, skip_t = rows_of(0), rows_of(1), rows_of(2)
    narrow = split3(jnp.concatenate([step_t, log_t, skip_t], axis=1))
    narrow = jnp.concatenate([part.astype(f32) for part in narrow], axis=0).astype(bf16)
    spread_heads = (iota((3 * H, LV), 1) // V == iota((3 * H, LV), 0) % H).astype(f32).astype(bf16)
    wide = dot(narrow, spread_heads, TN)
    own = iota((V, LV), 1) % V == iota((V, LV), 0)
    decay_table = jnp.exp(wide[V : 2 * V])
    step_table = jnp.where(own, wide[0:V], 0.0)
    gain_table = jnp.where(own, wide[2 * V : 3 * V], 0.0)
    gates = jnp.concatenate([packets[k][0:V, 0:ch] for k in range(nh)], axis=1)
    inners = jnp.concatenate([packets[k][0:V, ch : 2 * ch] for k in range(nh)], axis=1)
    gains = jnp.concatenate([packets[k][V + 1 : V + 2, 0:ch] for k in range(nh)], axis=1)

    token_row = (iota((LV, T), 0) % V).astype(f32)
    log_split = jnp.concatenate(split3(log_t), axis=1)
    onehots, logs = [], []
    for block in range(ns):
        onehot = (tokens[block : block + 1, :] == token_row).astype(f32).astype(bf16)
        onehots.append(onehot)
        logs.append(dot(log_split, onehot[0 : 3 * V, :]))
    logs = jnp.concatenate(logs, axis=0)
    first, second = iota((T, T), 0), iota((T, T), 1)
    later = (first > second).astype(f32).astype(bf16)
    sooner = (first < second).astype(f32).astype(bf16)
    size = ns * H
    sums = dot(
        jnp.concatenate(split3(logs)[::-1], axis=0), jnp.concatenate([later, sooner], axis=1)
    )
    sums = (sums[0:size] + sums[size : 2 * size]) + sums[2 * size :]
    after, before = sums[:, 0:T], sums[:, T:]
    totals = jnp.broadcast_to(jnp.sum(logs, axis=1, keepdims=True), (size, 128))
    piece = iota((size, 128), 1)
    high, middle, low = [part.astype(f32) for part in split3(totals)]
    totals = jnp.where(
        piece == 0, high, jnp.where(piece == 1, middle, jnp.where(piece == 2, low, 0.0))
    )
    row, column = iota((ns * H, ns * H), 0), iota((ns * H, ns * H), 1)
    row_block, column_block = row // H, column // H
    between = ((row_block < column_block) & (column_block < mine)) | (
        (row_block > column_block) & (column_block > mine)
    )
    between = (between & (row % H == column % H)).astype(f32).astype(bf16)
    gap = jnp.sum(dot(between, totals.astype(bf16)), axis=1, keepdims=True)
    block_of = iota((ns * H, T), 0) // H
    weight_up = jnp.where(block_of < mine, jnp.exp(after + gap), 0.0)
    weight_down = jnp.where(block_of > mine, jnp.exp(before + gap), 0.0)
    entering = jnp.zeros((4 * H, LV), f32)
    for block in range(ns):
        rows = slice(block * H, (block + 1) * H)
        both = jnp.concatenate([weight_up[rows], weight_down[rows]], axis=0)
        entering = entering + dot(
            jnp.concatenate(split2(both), axis=0), onehots[block], NT
        )
    entering = entering[2 * H :] + entering[0 : 2 * H]
    diagonal = iota((H, LV), 1) // V == iota((H, LV), 0)
    step_row = jnp.sum(step_table, axis=0, keepdims=True)
    enter_up = step_row * jnp.sum(
        jnp.where(diagonal, entering[0:H], 0.0), axis=0, keepdims=True
    )
    enter_down = step_row * jnp.sum(
        jnp.where(diagonal, entering[H : 2 * H], 0.0), axis=0, keepdims=True
    )

    looked = jnp.concatenate(
        [decay_table, step_table, pairs[...], gain_table, silu(gates), emb[...]], axis=1
    )
    looked = jnp.concatenate(split3(looked), axis=0)
    token = tokens[pl.ds(mine, 1), :]
    onehot = (token == (iota((3 * V, T), 0) % V).astype(f32)).astype(f32).astype(bf16)
    rows = dot(onehot, looked, TN)
    decay, step = rows[:, 0:LV], rows[:, LV : 2 * LV]
    pair, gain = rows[:, 2 * LV : 3 * LV], rows[:, 3 * LV : 4 * LV]
    silu_rows = rows[:, 4 * LV : 4 * LV + C]
    out_embedded[...] = rows[:, 4 * LV + C :]

    position = iota((T, LV), 0)
    up = scan_rows(decay, jnp.where(position == 0, step + decay * enter_up, step), 1)
    down = scan_rows(decay, jnp.where(position == T - 1, step + decay * enter_down, step), -1)

    tiled = jnp.concatenate([inners] * H, axis=0)
    spread = jnp.where(iota((LV, C), 0) // V == iota((LV, C), 1) // P, tiled, 0.0)
    spread_high, spread_low = split2(spread)
    both = jnp.concatenate([up * pair + gain, down * pair + gain], axis=0)
    high, low = split2(both)
    value = dot(high, spread_low) + dot(
        jnp.concatenate([low, high], axis=1),
        jnp.concatenate([spread_high, spread_high], axis=0),
    )
    value = value * jnp.concatenate([silu_rows, silu_rows], axis=0)
    wide = max(ch, 256)
    group = (iota((wide, wide), 0) // P == iota((wide, wide), 1) // P).astype(f32).astype(bf16)
    high, low = split2(value * value)
    starts = list(range(0, C, wide))
    rows = 2 * T
    stacked = [half[:, start : start + wide] for start in starts for half in (low, high)]
    squares = dot(jnp.concatenate(stacked, axis=0), group)
    for number, start in enumerate(starts):
        place = 2 * number * rows
        square = squares[place : place + rows] + squares[place + rows : place + 2 * rows]
        stop = start + wide
        normed = value[:, start:stop] * lax.rsqrt(square * (1.0 / P) + epsilon)
        out_high[:, start:stop], out_low[:, start:stop] = split2(
            (normed[0:T] + normed[T : 2 * T]) * gains[:, start:stop]
        )


def project_kernel(dims, *refs):
    V, D, hl, ch, nh, ns, T, N = dims
    P = ch // hl
    refs = list(refs)

    def take(number):
        taken, refs[:] = refs[:number], refs[number:]
        return taken

    high, low, embedded, small, own_high, own_low, state_high, state_low = take(8)
    order = in_turn(nh)[::-1]
    nears = dict(zip(order, take(nh - 1)))
    others = dict(zip(order, take(nh - 1)))
    out_state, out_high, out_low, out_scale = take(4)
    out_write, out_inner, out_stepped, out_total = take(4)
    half = ch // 2
    base = V + 2 + 3 * hl
    mine = lax.axis_index("seq")

    pieces = []
    for k in range(1, nh):
        near = nears[k][base : base + half, 0:D]
        other = others[k][base : base + half, 0:D]
        even = lax.rem(lax.bitwise_xor(mine, partners(ns, nh)[k][0]), 2) == 0
        pieces.append(jnp.where(even, near, other))
        pieces.append(jnp.where(even, other, near))
    weights = split2(jnp.concatenate(pieces, axis=0))
    weights = (
        jnp.concatenate([own_high[...], weights[0]], axis=0),
        jnp.concatenate([own_low[...], weights[1]], axis=0),
    )
    hidden = embedded[...] + dot_split((high[...], low[...]), weights)
    split = split2(hidden)
    out_high[...], out_low[...] = split
    scale = lax.rsqrt(jnp.mean(hidden * hidden, axis=-1, keepdims=True) + epsilon)
    out_scale[...] = jnp.broadcast_to(scale, (T, ch))

    rows = dot_split(split, (state_high[...], state_low[...])) * scale
    inner, write = rows[:, 0:ch], rows[:, 2 * ch :]
    step = softplus(rows[:, ch : 2 * ch] + small[0:1, :])
    stepped = inner * step
    upto = (iota((T, T), 0) >= iota((T, T), 1)).astype(f32).astype(bf16)
    log_high, log_middle, log_low = split3(-small[1:2, :] * step)
    total = dot(upto, jnp.concatenate([log_low, log_middle], axis=1))
    total = (total[:, 0:ch] + total[:, ch:]) + dot(upto, log_high)
    end = total[T - 1 : T, :]
    state = dot3(stepped * jnp.exp(end - total), write, TN)
    out_state[0:ch, :] = state
    for head in range(hl):
        out_state[ch + head : ch + head + 1, :] = jnp.broadcast_to(
            end[:, head * P : head * P + 1], (1, N)
        )
    out_write[...] = write
    out_inner[...] = inner
    out_stepped[...] = stepped
    out_total[...] = total


def block_kernel(dims, *refs):
    V, D, hl, ch, nh, ns, T, N = dims
    P = ch // hl
    refs = list(refs)

    def take(number):
        taken, refs[:] = refs[:number], refs[number:]
        return taken

    high, low, scale, write, inner, stepped, total, choose = take(8)
    rest_high, rest_low, small, outproj2 = take(4)
    base, read_high, read_low, out_fade, out_gate, own, out_high, out_low, hidden_ref = take(9)
    rows = dot_split((high[...], low[...]), (rest_high[...], rest_low[...]))
    out_gate[...] = silu(rows[:, 0:ch] * scale[...])
    read = rows[:, ch:] * scale[...]
    read = split2(read)
    read_high[...], read_low[...] = read
    out_fade[...] = jnp.exp(total[...])
    products = dot_split(read, split2(write[...]), NT)
    stepped_high, stepped_low = split2(stepped[...])
    select = (iota((8, ch), 1) == iota((8, ch), 0) * P).astype(f32).astype(bf16)
    total_high, total_middle, total_low = split3(total[...])
    total_t = (dot(select, total_low, NT) + dot(select, total_middle, NT)) + dot(
        select, total_high, NT
    )
    allowed = iota((T, T), 0) >= iota((T, T), 1)
    parts = []
    for head in range(hl):
        start, stop = head * P, (head + 1) * P
        differ = total[:, start : start + 1] - total_t[head : head + 1, :]
        weights = jnp.where(allowed, jnp.exp(jnp.where(allowed, differ, 0.0)), 0.0) * products
        part = dot_split(
            split2(weights), (stepped_high[:, start:stop], stepped_low[:, start:stop])
        )
        parts.append(part + small[2:3, start:stop] * inner[:, start:stop])
    base[...] = jnp.concatenate(parts, axis=1)
    share = T // nh
    hidden_ref[...] = high[...].astype(f32) + low[...].astype(f32)
    place = pl.multiple_of(lax.axis_index("head") * share, 8)
    out_gain = jnp.transpose(jnp.broadcast_to(small[3:4, :], (128, ch)))
    out_high[...], out_low[...] = split2(outproj2[...] * out_gain[:, 0:1])
    own[...] = dot_right_exact(hidden_ref[pl.ds(place, share), :], choose[...])


def state_rows(dims, values):
    V, D, hl, ch, nh, ns, T, N = dims
    head_of = iota((ch, N), 0) // (ch // hl)
    result = jnp.broadcast_to(values[0:1, :], (ch, N))
    for head in range(1, hl):
        result = jnp.where(head_of == head, values[head : head + 1, :], result)
    return result


def join_kernel(dims, bit, total, prefix, came, out_total, out_prefix):
    V, D, hl, ch, nh, ns, T, N = dims
    later = lax.rem(lax.div(lax.axis_index("seq"), 2**bit), 2) == 1
    came_state, came_log = came[0:ch, :], came[ch : ch + hl, :]
    state, log = total[0:ch, :], total[ch : ch + hl, :]
    factor = jnp.exp(state_rows(dims, jnp.where(later, log, came_log)))
    out_total[0:ch, :] = jnp.where(
        later, factor * came_state + state, factor * state + came_state
    )
    out_total[ch : ch + hl, :] = log + came_log
    if prefix is None:
        out_prefix[0:ch, :] = jnp.where(later, came_state, 0.0)
        out_prefix[ch : ch + hl, :] = jnp.where(later, came_log, 0.0)
    else:
        joined = prefix_joined(dims, bit, prefix, came)
        out_prefix[0:ch, :] = joined
        out_prefix[ch : ch + hl, :] = prefix[ch : ch + hl, :] + jnp.where(later, came_log, 0.0)


def prefix_joined(dims, bit, prefix, came):
    V, D, hl, ch, nh, ns, T, N = dims
    later = lax.rem(lax.div(lax.axis_index("seq"), 2**bit), 2) == 1
    factor = jnp.exp(state_rows(dims, prefix[ch : ch + hl, :]))
    return prefix[0:ch, :] + jnp.where(later, factor * came[0:ch, :], 0.0)


def output_kernel(dims, bit, *refs):
    V, D, hl, ch, nh, ns, T, N = dims
    P = ch // hl
    prefix, came, read_high, read_low, base, fade, gate, own, proj_high, proj_low = refs[:10]
    outs, partial_ref = refs[10 : 10 + nh], refs[10 + nh]
    entering = prefix_joined(dims, bit, prefix, came)
    value = (base[...] + dot_split((read_high[...], read_low[...]), split2(entering), NT) * fade[...]) * gate[...]
    group = (iota((ch, ch), 0) // P == iota((ch, ch), 1) // P).astype(f32).astype(bf16)
    square = dot(jnp.concatenate(split2(value * value), axis=0), group)
    square = square[T:] + square[0:T]
    value = value * lax.rsqrt(square * (1.0 / P) + epsilon)
    share = T // nh
    partial_ref[...] = dot_split(split2(value), (proj_high[...], proj_low[...]))
    mine = lax.axis_index("head")
    for k in range(nh):
        place = pl.multiple_of(lax.bitwise_xor(mine, k) * share, 8)
        part = partial_ref[pl.ds(place, share), :]
        outs[k][...] = part + own[...] if k == 0 else part


def per_device(
    token_ids,
    embedding,
    complement,
    prenorm_first,
    inproj_first,
    statemap_first,
    stepmap_first,
    stepbias_first,
    rates_first,
    skipgain_first,
    outnorm_first,
    outproj_first,
    prenorm_second,
    inproj_second,
    statemap_second,
    stepmap_second,
    stepbias_second,
    rates_second,
    skipgain_second,
    outnorm_second,
    outproj_second,
):
    nh, ns = lax.axis_size("head"), lax.axis_size("seq")
    V, D = embedding.shape
    ch = inproj_first.shape[2]
    hl = stepmap_first.shape[1]
    N = statemap_first.shape[2]
    T = token_ids.shape[0]
    LV = nh * hl * V
    dims = (V, D, hl, ch, nh, ns, T, N)
    vmem = pl.BlockSpec(memory_space=pltpu.VMEM)
    smem = pl.BlockSpec(memory_space=pltpu.SMEM)
    anywhere = pl.BlockSpec(memory_space=pl.ANY)
    params = pltpu.CompilerParams(vmem_limit_bytes=LIMIT)

    def shape(*sizes, dtype=f32):
        return jax.ShapeDtypeStruct(sizes, dtype)

    def halves(*sizes):
        return [shape(*sizes, dtype=bf16)] * 2

    def room(value):
        return pltpu.VMEM(value.shape, value.dtype)

    def line(value):
        return value.reshape(1, -1)

    def flat(value):
        return value.reshape(-1, value.shape[-1])

    heavy = pl.CostEstimate(flops=960 * T * D * D, bytes_accessed=4 * T * D, transcendentals=T * D)

    head_rows = V + 2 + 3 * hl
    half = ch // 2
    width = max(2 * ch, T, D)
    share = T // nh
    fetched = [
        flat(inproj_first),
        line(token_ids),
        embedding,
        line(prenorm_first),
        stepmap_first.T,
        line(stepbias_first),
        line(rates_first),
        line(skipgain_first),
        line(outnorm_first),
    ]
    message = pl.pallas_call(
        functools.partial(tables_kernel, dims),
        out_shape=shape(head_rows + half, width),
        in_specs=[anywhere] * (len(fetched) + 1),
        out_specs=vmem,
        scratch_shapes=[room(value) for value in fetched]
        + [pltpu.SemaphoreType.DMA((len(fetched) + 1,))],
        compiler_params=pltpu.CompilerParams(vmem_limit_bytes=TABLES_LIMIT),
        cost_estimate=heavy,
        name="tables",
    )(*fetched, outproj_first)

    prepared = [
        embedding,
        line(prenorm_first),
        flat(statemap_first),
        line(complement),
        outproj_first,
        line(prenorm_second),
        flat(inproj_second),
        flat(statemap_second),
        stepmap_second.T,
        stepbias_second,
        rates_second,
        skipgain_second,
        line(outnorm_second),
    ]
    (
        pair_table,
        small,
        choose,
        own_high,
        own_low,
        state_high,
        state_low,
        rest_high,
        rest_low,
    ) = pl.pallas_call(
        functools.partial(prepare_kernel, dims),
        out_shape=(
            shape(V, LV),
            shape(8, ch),
            shape(D, D, dtype=bf16),
            *halves(ch, D),
            *halves(D, 2 * ch + N),
            *halves(D, ch + N),
        ),
        in_specs=[vmem] * 9 + [smem] * 3 + [vmem],
        out_specs=(vmem,) * 9,
        compiler_params=params,
        cost_estimate=heavy,
        name="prepare",
    )(*prepared)

    count = max(ns, nh)
    messages = {0: message}
    for k in in_turn(count):
        seq_bits, head_bits = partners(ns, nh)[k]
        pairs = [
            (seq * nh + head, (seq ^ seq_bits) * nh + (head ^ head_bits))
            for seq in range(ns)
            for head in range(nh)
        ]
        sent = message if k < nh else message[0:head_rows]
        messages[k] = lax.ppermute(sent, ("seq", "head"), pairs)
    swap = [(seq, seq ^ 1) for seq in range(ns)]
    order = in_turn(nh)[::-1]
    others = [lax.ppermute(messages[k], "seq", swap) for k in order]

    mixed_high, mixed_low, embedded = pl.pallas_call(
        functools.partial(mix_kernel, dims),
        out_shape=(*halves(T, nh * ch), shape(T, D)),
        in_specs=[vmem] * (count + 2),
        out_specs=(vmem,) * 3,
        scratch_shapes=[pltpu.VMEM((max(ns, 8), T), f32)],
        compiler_params=params,
        cost_estimate=heavy,
        name="mix",
    )(*[messages[k] for k in in_turn(count)[::-1] + [0]], embedding, pair_table)

    state, hidden_high, hidden_low, scale, write, inner, stepped, total = pl.pallas_call(
        functools.partial(project_kernel, dims),
        out_shape=(
            shape(ch + 8, N),
            *halves(T, D),
            shape(T, ch),
            shape(T, N),
            shape(T, ch),
            shape(T, ch),
            shape(T, ch),
        ),
        in_specs=[vmem] * (8 + 2 * (nh - 1)),
        out_specs=(vmem,) * 8,
        compiler_params=params,
        name="project",
    )(
        mixed_high,
        mixed_low,
        embedded,
        small,
        own_high,
        own_low,
        state_high,
        state_low,
        *[messages[k] for k in order],
        *others,
    )

    base, read_high, read_low, fade, gate, own, proj_high, proj_low = pl.pallas_call(
        functools.partial(block_kernel, dims),
        out_shape=(
            shape(T, ch),
            *halves(T, N),
            shape(T, ch),
            shape(T, ch),
            shape(share, D),
            *halves(ch, D),
        ),
        in_specs=[vmem] * 12,
        out_specs=(vmem,) * 8,
        scratch_shapes=[pltpu.VMEM((T, D), f32)],
        compiler_params=params,
        cost_estimate=heavy,
        name="block",
    )(
        hidden_high,
        hidden_low,
        scale,
        write,
        inner,
        stepped,
        total,
        choose,
        rest_high,
        rest_low,
        small,
        outproj_second,
    )

    prefix = None
    bits = ns.bit_length() - 1
    for bit in range(bits):
        came = lax.ppermute(state, "seq", [(seq, seq ^ 2**bit) for seq in range(ns)])
        if bit == bits - 1:
            break
        given = [state] + ([] if prefix is None else [prefix]) + [came]

        def join(bit, known, *refs):
            if known:
                join_kernel(dims, bit, *refs)
            else:
                join_kernel(dims, bit, refs[0], None, *refs[1:])

        state, prefix = pl.pallas_call(
            functools.partial(join, bit, prefix is not None),
            out_shape=(shape(ch + 8, N),) * 2,
            in_specs=[vmem] * len(given),
            out_specs=(vmem,) * 2,
            compiler_params=params,
            name="join",
        )(*given)
    if prefix is None:
        prefix = jnp.zeros_like(state)

    parts = pl.pallas_call(
        functools.partial(output_kernel, dims, bits - 1),
        out_shape=(shape(share, D),) * nh,
        in_specs=[vmem] * 10,
        out_specs=(vmem,) * nh,
        scratch_shapes=[pltpu.VMEM((T, D), f32)],
        compiler_params=params,
        name="output",
    )(prefix, came, read_high, read_low, base, fade, gate, own, proj_high, proj_low)
    result = parts[0]
    for k in in_turn(nh):
        pairs = [(source, source ^ k) for source in range(nh)]
        result = result + lax.ppermute(parts[k], "head", pairs)
    return result


def solution(mesh):
    return jax.shard_map(
        per_device,
        mesh=mesh,
        in_specs=(
            P(("rep", "seq")),
            P(),
            P(),
            P(),
            P(None, None, "head"),
            P(),
            P(None, "head"),
            P("head"),
            P("head"),
            P("head"),
            P("head"),
            P("head", None),
            P(),
            P(None, None, "head"),
            P(),
            P(None, "head"),
            P("head"),
            P("head"),
            P("head"),
            P("head"),
            P("head", None),
        ),
        out_specs=P(("rep", "seq", "head"), None),
        check_vma=False,
    )
```

```python
import functools

import jax
import jax.numpy as jnp
from jax import lax
from jax.experimental import pallas as pl
from jax.experimental.pallas import tpu as pltpu
from jax.sharding import PartitionSpec as P

epsilon = 1e-05
f32 = jnp.float32
bf16 = jnp.bfloat16
LIMIT = 48 * 1024 * 1024
TABLES_LIMIT = 60 * 1000 * 1000

MM = (((1,), (0,)), ((), ()))
NT = (((1,), (1,)), ((), ()))
TN = (((0,), (0,)), ((), ()))


def partners(ns, nh):
    count = max(ns, nh)
    return [((ns - k) if 0 < k < ns else 0, k if k < nh else 0) for k in range(count)]


def in_turn(count):
    return sorted(range(1, count), key=lambda k: (-k.bit_length(), k))


def iota(shape, axis):
    return lax.broadcasted_iota(jnp.int32, shape, axis)


def split2(value):
    high = value.astype(bf16)
    return high, (value - high.astype(f32)).astype(bf16)


def split3(value):
    high = value.astype(bf16)
    rest = value - high.astype(f32)
    middle = rest.astype(bf16)
    return high, middle, (rest - middle.astype(f32)).astype(bf16)


def dot(left, right, dims=MM):
    return lax.dot_general(left, right, dims, preferred_element_type=f32)


def dot_split(left, right, dims=MM):
    axis = 1 if dims == TN else 0
    size = left[0].shape[axis]
    if size % 16:
        return (dot(left[0], right[1], dims) + dot(left[1], right[0], dims)) + dot(
            left[0], right[0], dims
        )
    both = dot(jnp.concatenate([left[1], left[0]], axis=axis), right[0], dims)
    return (dot(left[0], right[1], dims) + both[0:size]) + both[size:]


def dot3(left, right, dims=MM):
    return dot_split(split2(left), split2(right), dims)


def dot_left_exact(left, right, dims=MM):
    high, middle, low = split3(right)
    return (dot(left, low, dims) + dot(left, middle, dims)) + dot(left, high, dims)


def dot_right_exact(left, right, dims=MM):
    high, middle, low = split3(left)
    return (dot(low, right, dims) + dot(middle, right, dims)) + dot(high, right, dims)


def softplus(value):
    return jnp.maximum(value, 0.0) + jnp.log1p(jnp.exp(-jnp.abs(value)))


def silu(value):
    return value / (1.0 + jnp.exp(-value))


def rms(value):
    return value * lax.rsqrt(jnp.mean(value * value, axis=-1, keepdims=True) + epsilon)


def fetch(sources, places, semaphores):
    copies = []
    for number, (source, place) in enumerate(zip(sources, places)):
        copies.append(pltpu.make_async_copy(source, place, semaphores.at[number]))
        copies[-1].start()
    return copies


def fetch(sources, places, semaphores):
    copies = []
    for number, (source, place) in enumerate(zip(sources, places)):
        copies.append(pltpu.make_async_copy(source, place, semaphores.at[number]))
        copies[-1].start()
    return copies


PIECES = 4


def tables_kernel(dims, *refs):
    V, D, hl, ch, nh, ns, T, N = dims
    refs = list(refs)

    def take(number):
        taken, refs[:] = refs[:number], refs[number:]
        return taken

    sources = take(9)
    outproj_source, message = take(2)
    places = take(9)
    semaphores = take(1)[0]
    half = ch // 2
    top = top_rows(dims)
    core = lax.rem(lax.axis_index("seq"), 2)
    (inproj, tok, emb, prenorm, stepmap, bias, rates, skip, outnorm) = places
    size = inproj.shape[0] // PIECES
    pieces = [pl.ds(number * size, size) for number in range(PIECES)]
    rows = pl.ds(pl.multiple_of(core * half, 8), half)
    wide = [(place, pl.ds(place * ch, ch)) for place in range(D // ch)]
    copies = fetch(
        [sources[0].at[piece, :] for piece in pieces]
        + sources[1:]
        + [outproj_source.at[rows, columns] for _, columns in wide],
        [inproj.at[piece, :] for piece in pieces]
        + places[1:]
        + [message.at[pl.ds(top + place * half, half), :] for place, _ in wide],
        semaphores,
    )
    flip = (iota((T, 1), 0) + iota((1, T), 1) == T - 1).astype(f32).astype(bf16)
    for copy in copies[PIECES : PIECES + 8]:
        copy.wait()
    normed = split2(rms(emb[...]) * prenorm[...])
    raw_t = dot_split(split2(stepmap[...]), normed, NT)
    tokens = jnp.broadcast_to(tok[...].astype(f32), (8, T)).astype(bf16)
    tokens = dot(tokens, flip)
    for place in range(T // ch):
        message[2 * V + place : 2 * V + place + 1, :] = tokens[0:1, place * ch : (place + 1) * ch]
    row = 2 * V + T // ch
    message[row : row + 1, :] = outnorm[...]
    for head in range(hl):
        line = softplus(raw_t[head : head + 1, :] + bias[:, head : head + 1])
        row = row + 1
        message[row : row + 1, 0:V] = line
        message[row : row + 1, V : 2 * V] = -rates[:, head : head + 1] * line
        message[row : row + 1, 2 * V : 3 * V] = jnp.broadcast_to(skip[:, head : head + 1], (1, V))
    for copy in copies[:PIECES]:
        copy.wait()
    weights = jnp.concatenate(
        [inproj[pl.ds(0, D, stride=2), :], inproj[pl.ds(1, D, stride=2), :]], axis=1
    )
    both = dot_split(normed, split2(weights))
    message[0:V, :] = both[:, 0:ch]
    message[V : 2 * V, :] = both[:, ch:]
    for copy in copies[PIECES + 8 :]:
        copy.wait()


def top_rows(dims):
    V, D, hl, ch, nh, ns, T, N = dims
    return 2 * V + -(-(T // ch + 1 + hl) // 8) * 8


def head_line(dims, values):
    V, D, hl, ch, nh, ns, T, N = dims
    head_of = iota((1, ch), 1) // (ch // hl)
    line = jnp.zeros((1, ch), f32)
    for head in range(hl):
        line = jnp.where(head_of == head, values[head], line)
    return line


def prepare_kernel(dims, *refs):
    V, D, hl, ch, nh, ns, T, N = dims
    H, P = nh * hl, ch // hl
    refs = list(refs)

    def take(number):
        taken, refs[:] = refs[:number], refs[number:]
        return taken

    emb, prenorm, statemap, complement, outproj = take(5)
    prenorm2, inproj2, statemap2, stepmap2 = take(4)
    bias2, rates2, skip2, outnorm2 = take(4)
    pairs, small, choose_out, own_high, own_low = take(5)
    state_high, state_low, rest_high, rest_low = take(4)
    triangles, upto, groups, blocks = take(4)
    normed = split2(rms(emb[...]) * prenorm[...])
    write = dot_split(normed, split2(statemap[pl.ds(0, D, stride=2), :]))
    read = dot_split(normed, split2(statemap[pl.ds(1, D, stride=2), :]))
    pairs[...] = dot3(read, jnp.concatenate([write] * H, axis=0), NT)
    own_high[...], own_low[...] = split2(outproj[...])
    choose = (complement[...] == iota((D, 1), 0)).astype(f32).astype(bf16)
    choose_out[...] = choose
    gain = jnp.transpose(jnp.broadcast_to(prenorm2[...], (128, D)))

    def weights(values):
        return split2(dot_left_exact(choose, values))

    gain_wide = gain[:, 0:1]
    inner = inproj2[pl.ds(1, D, stride=2), :] * gain_wide
    step = jnp.transpose(
        jnp.concatenate(
            [jnp.broadcast_to(stepmap2[head : head + 1, :], (P, D)) for head in range(hl)], axis=0
        )
    )
    write2 = statemap2[pl.ds(0, D, stride=2), :] * gain_wide
    state_high[...], state_low[...] = weights(
        jnp.concatenate([inner, step * gain_wide, write2], axis=1)
    )
    gate = inproj2[pl.ds(0, D, stride=2), :] * gain_wide
    read2 = statemap2[pl.ds(1, D, stride=2), :] * gain_wide
    rest_high[...], rest_low[...] = weights(jnp.concatenate([gate, read2], axis=1))
    small[0:1, :] = head_line(dims, bias2)
    small[1:2, :] = head_line(dims, rates2)
    small[2:3, :] = head_line(dims, skip2)
    small[3:4, :] = outnorm2[...]
    row, column = iota((T, 1), 0), iota((1, T), 1)
    triangles[:, 0:T] = (row > column).astype(f32).astype(bf16)
    triangles[:, T:] = (row < column).astype(f32).astype(bf16)
    upto[...] = (row >= column).astype(f32).astype(bf16)
    size = groups.shape[0]
    groups[...] = (iota((size, 1), 0) // P == iota((1, size), 1) // P).astype(f32).astype(bf16)
    rows, columns = blocks.shape
    blocks[...] = (iota((rows, 1), 0) // V == iota((1, columns), 1) // P).astype(f32).astype(bf16)


def shift_rows(value, amount, fill):
    size = value.shape[0]
    if amount % 8 == 0:
        empty = jnp.full((abs(amount),) + value.shape[1:], fill, value.dtype)
        if amount > 0:
            return jnp.concatenate([empty, value[: size - amount]], axis=0)
        return jnp.concatenate([value[-amount:], empty], axis=0)
    rolled = pltpu.roll(value, amount % size, 0)
    row = iota((8,) + value.shape[1:], 0)
    if amount > 0:
        edge = jnp.where(row >= amount, rolled[0:8], fill)
        return jnp.concatenate([edge, rolled[8:]], axis=0)
    edge = jnp.where(row < 8 + amount, rolled[size - 8 :], fill)
    return jnp.concatenate([rolled[: size - 8], edge], axis=0)


def scan_rows(decay, value, sign):
    size = value.shape[0]
    amount = 1
    while amount < size:
        value = value + decay * shift_rows(value, sign * amount, 0.0)
        if 2 * amount < size:
            decay = decay * shift_rows(decay, sign * amount, 1.0)
        amount *= 2
    return value


def mix_kernel(dims, *refs):
    V, D, hl, ch, nh, ns, T, N = dims
    H, LV, P = nh * hl, nh * hl * V, ch // hl
    C = nh * ch
    refs = list(refs)

    def take(number):
        taken, refs[:] = refs[:number], refs[number:]
        return taken

    count = max(ns, nh)
    packets = dict(zip(in_turn(count)[::-1] + [0], take(count)))
    emb, pairs, triangles, groups, blocks = take(5)
    out_high, out_low, out_embedded = take(3)
    tokens = take(1)[0]
    mine = lax.axis_index("seq")

    for k in range(ns):
        block = ns - 1 - lax.bitwise_xor(mine, partners(ns, nh)[k][0])
        row = 2 * V
        pieces = [packets[k][row + place : row + place + 1, :] for place in range(T // ch)]
        tokens[pl.ds(block, 1), :] = jnp.concatenate(pieces, axis=1)

    first = 2 * V + T // ch + 1
    steps = jnp.concatenate(
        [packets[k][first : first + hl, 0 : 3 * V] for k in range(nh)], axis=0
    )
    log_t = steps[:, V : 2 * V]
    narrow = jnp.concatenate([part.astype(f32) for part in split3(steps)], axis=0).astype(bf16)
    spread_heads = (iota((1, LV), 1) // V == iota((3 * H, 1), 0) % H).astype(f32).astype(bf16)
    wide = dot(narrow, spread_heads, TN)
    own = iota((1, LV), 1) % V == iota((V, 1), 0)
    decay_table = jnp.exp(wide[V : 2 * V])
    step_table = jnp.where(own, wide[0:V], 0.0)
    gain_table = jnp.where(own, wide[2 * V : 3 * V], 0.0)
    gates = jnp.concatenate([packets[k][0:V, :] for k in range(nh)], axis=1)
    inners = jnp.concatenate([packets[k][V : 2 * V, :] for k in range(nh)], axis=1)
    gains = jnp.concatenate([packets[k][first - 1 : first, :] for k in range(nh)], axis=1)

    token_row = (iota((LV, 1), 0) % V).astype(f32)
    log_split = jnp.concatenate(split3(log_t), axis=1)
    onehots, logs = [], []
    for block in range(ns):
        onehot = (tokens[block : block + 1, :] == token_row).astype(f32).astype(bf16)
        onehots.append(onehot)
        logs.append(dot(log_split, onehot[0 : 3 * V, :]))
    logs = jnp.concatenate(logs, axis=0)
    size = ns * H
    sums = dot(jnp.concatenate(split3(logs)[::-1], axis=0), triangles[...])
    sums = (sums[0:size] + sums[size : 2 * size]) + sums[2 * size :]
    after, before = sums[:, 0:T], sums[:, T:]
    totals = jnp.broadcast_to(jnp.sum(logs, axis=1, keepdims=True), (size, 128))
    piece = iota((1, 128), 1)
    high, middle, low = [part.astype(f32) for part in split3(totals)]
    totals = jnp.where(
        piece == 0, high, jnp.where(piece == 1, middle, jnp.where(piece == 2, low, 0.0))
    )
    row, column = iota((ns * H, 1), 0), iota((1, ns * H), 1)
    row_block, column_block = row // H, column // H
    between = ((row_block < column_block) & (column_block < mine)) | (
        (row_block > column_block) & (column_block > mine)
    )
    between = (between & (row % H == column % H)).astype(f32).astype(bf16)
    gap = jnp.sum(dot(between, totals.astype(bf16)), axis=1, keepdims=True)
    block_of = iota((ns * H, 1), 0) // H
    weight_up = jnp.where(block_of < mine, jnp.exp(after + gap), 0.0)
    weight_down = jnp.where(block_of > mine, jnp.exp(before + gap), 0.0)
    entering = jnp.zeros((4 * H, LV), f32)
    for block in range(ns):
        rows = slice(block * H, (block + 1) * H)
        both = jnp.concatenate([weight_up[rows], weight_down[rows]], axis=0)
        entering = entering + dot(
            jnp.concatenate(split2(both), axis=0), onehots[block], NT
        )
    entering = entering[2 * H :] + entering[0 : 2 * H]
    diagonal = iota((1, LV), 1) // V == iota((H, 1), 0)
    step_row = jnp.sum(step_table, axis=0, keepdims=True)
    enter_up = step_row * jnp.sum(
        jnp.where(diagonal, entering[0:H], 0.0), axis=0, keepdims=True
    )
    enter_down = step_row * jnp.sum(
        jnp.where(diagonal, entering[H : 2 * H], 0.0), axis=0, keepdims=True
    )

    looked = jnp.concatenate(
        [decay_table, step_table, pairs[...], gain_table, silu(gates), emb[...]], axis=1
    )
    looked = jnp.concatenate(split3(looked), axis=0)
    token = tokens[pl.ds(mine, 1), :]
    onehot = (token == token_row[0 : 3 * V]).astype(f32).astype(bf16)
    rows = dot(onehot, looked, TN)
    decay, step = rows[:, 0:LV], rows[:, LV : 2 * LV]
    pair, gain = rows[:, 2 * LV : 3 * LV], rows[:, 3 * LV : 4 * LV]
    silu_rows = rows[:, 4 * LV : 4 * LV + C]
    out_embedded[...] = rows[:, 4 * LV + C :]

    edge = iota((8, 1), 0)
    begin = jnp.where(edge == 0, decay[0:8] * enter_up, 0.0)
    up = scan_rows(decay, jnp.concatenate([step[0:8] + begin, step[8:]], axis=0), 1)
    begin = jnp.where(edge == 7, decay[T - 8 :] * enter_down, 0.0)
    down = scan_rows(
        decay, jnp.concatenate([step[: T - 8], step[T - 8 :] + begin], axis=0), -1
    )

    spread_high, spread_low = [
        jnp.concatenate([part] * H, axis=0) * blocks[...] for part in split2(inners)
    ]
    both = jnp.concatenate([up * pair + gain, down * pair + gain], axis=0)
    high, low = split2(both)
    value = dot(high, spread_low) + dot(
        jnp.concatenate([low, high], axis=1),
        jnp.concatenate([spread_high, spread_high], axis=0),
    )
    value = value * jnp.concatenate([silu_rows, silu_rows], axis=0)
    wide = groups.shape[0]
    high, low = split2(value * value)
    starts = list(range(0, C, wide))
    rows = 2 * T
    stacked = [half[:, start : start + wide] for start in starts for half in (low, high)]
    squares = dot(jnp.concatenate(stacked, axis=0), groups[...])
    for number, start in enumerate(starts):
        place = 2 * number * rows
        square = squares[place : place + rows] + squares[place + rows : place + 2 * rows]
        stop = start + wide
        normed = value[:, start:stop] * lax.rsqrt(square * (1.0 / P) + epsilon)
        out_high[:, start:stop], out_low[:, start:stop] = split2(
            (normed[0:T] + normed[T : 2 * T]) * gains[:, start:stop]
        )


def project_kernel(dims, *refs):
    V, D, hl, ch, nh, ns, T, N = dims
    P = ch // hl
    refs = list(refs)

    def take(number):
        taken, refs[:] = refs[:number], refs[number:]
        return taken

    high, low, embedded, small, own_high, own_low, state_high, state_low, upto = take(9)
    order = in_turn(nh)[::-1]
    nears = dict(zip(order, take(nh - 1)))
    others = dict(zip(order, take(nh - 1)))
    out_state, out_high, out_low, out_scale = take(4)
    out_write, out_inner, out_stepped, out_total = take(4)
    half = ch // 2
    base = top_rows(dims)
    mine = lax.axis_index("seq")

    pieces = []
    for k in range(1, nh):
        near, other = [
            jnp.concatenate(
                [
                    ref[base + place * half : base + (place + 1) * half, :]
                    for place in range(D // ch)
                ],
                axis=1,
            )
            for ref in (nears[k], others[k])
        ]
        even = lax.rem(lax.bitwise_xor(mine, partners(ns, nh)[k][0]), 2) == 0
        pieces.append(jnp.where(even, near, other))
        pieces.append(jnp.where(even, other, near))
    weights = split2(jnp.concatenate(pieces, axis=0))
    weights = (
        jnp.concatenate([own_high[...], weights[0]], axis=0),
        jnp.concatenate([own_low[...], weights[1]], axis=0),
    )
    hidden = embedded[...] + dot_split((high[...], low[...]), weights)
    split = split2(hidden)
    out_high[...], out_low[...] = split
    scale = lax.rsqrt(jnp.mean(hidden * hidden, axis=-1, keepdims=True) + epsilon)
    out_scale[...] = jnp.broadcast_to(scale, (T, ch))

    rows = dot_split(split, (state_high[...], state_low[...])) * scale
    inner, write = rows[:, 0:ch], rows[:, 2 * ch :]
    step = softplus(rows[:, ch : 2 * ch] + small[0:1, :])
    stepped = inner * step
    log_high, log_middle, log_low = split3(-small[1:2, :] * step)
    total = dot(upto[...], jnp.concatenate([log_low, log_middle], axis=1))
    total = (total[:, 0:ch] + total[:, ch:]) + dot(upto[...], log_high)
    end = total[T - 1 : T, :]
    state = dot3(stepped * jnp.exp(end - total), write, TN)
    out_state[0:ch, :] = state
    for head in range(hl):
        out_state[ch + head : ch + head + 1, :] = jnp.broadcast_to(
            end[:, head * P : head * P + 1], (1, N)
        )
    out_write[...] = write
    out_inner[...] = inner
    out_stepped[...] = stepped
    out_total[...] = total


def block_kernel(dims, *refs):
    V, D, hl, ch, nh, ns, T, N = dims
    P = ch // hl
    refs = list(refs)

    def take(number):
        taken, refs[:] = refs[:number], refs[number:]
        return taken

    high, low, scale, write, inner, stepped, total, choose = take(8)
    rest_high, rest_low, small, outproj2 = take(4)
    base, read_high, read_low, out_fade, out_gate, own, out_high, out_low, hidden_ref = take(9)
    rows = dot_split((high[...], low[...]), (rest_high[...], rest_low[...]))
    out_gate[...] = silu(rows[:, 0:ch] * scale[...])
    read = rows[:, ch:] * scale[...]
    read = split2(read)
    read_high[...], read_low[...] = read
    out_fade[...] = jnp.exp(total[...])
    products = dot_split(read, split2(write[...]), NT)
    stepped_high, stepped_low = split2(stepped[...])
    select = (iota((8, ch), 1) == iota((8, ch), 0) * P).astype(f32).astype(bf16)
    total_high, total_middle, total_low = split3(total[...])
    total_t = (dot(select, total_low, NT) + dot(select, total_middle, NT)) + dot(
        select, total_high, NT
    )
    allowed = iota((T, 1), 0) >= iota((1, T), 1)
    parts = []
    for head in range(hl):
        start, stop = head * P, (head + 1) * P
        differ = total[:, start : start + 1] - total_t[head : head + 1, :]
        weights = jnp.where(allowed, jnp.exp(jnp.where(allowed, differ, 0.0)), 0.0) * products
        part = dot_split(
            split2(weights), (stepped_high[:, start:stop], stepped_low[:, start:stop])
        )
        parts.append(part + small[2:3, start:stop] * inner[:, start:stop])
    base[...] = jnp.concatenate(parts, axis=1)
    share = T // nh
    hidden_ref[...] = high[...].astype(f32) + low[...].astype(f32)
    place = pl.multiple_of(lax.axis_index("head") * share, 8)
    out_gain = jnp.transpose(jnp.broadcast_to(small[3:4, :], (128, ch)))
    out_high[...], out_low[...] = split2(outproj2[...] * out_gain[:, 0:1])
    own[...] = dot_right_exact(hidden_ref[pl.ds(place, share), :], choose[...])


def state_rows(dims, values):
    V, D, hl, ch, nh, ns, T, N = dims
    head_of = iota((ch, N), 0) // (ch // hl)
    result = jnp.broadcast_to(values[0:1, :], (ch, N))
    for head in range(1, hl):
        result = jnp.where(head_of == head, values[head : head + 1, :], result)
    return result


def join_kernel(dims, bit, total, prefix, came, out_total, out_prefix):
    V, D, hl, ch, nh, ns, T, N = dims
    later = lax.rem(lax.div(lax.axis_index("seq"), 2**bit), 2) == 1
    came_state, came_log = came[0:ch, :], came[ch : ch + hl, :]
    state, log = total[0:ch, :], total[ch : ch + hl, :]
    factor = jnp.exp(state_rows(dims, jnp.where(later, log, came_log)))
    out_total[0:ch, :] = jnp.where(
        later, factor * came_state + state, factor * state + came_state
    )
    out_total[ch : ch + hl, :] = log + came_log
    if prefix is None:
        out_prefix[0:ch, :] = jnp.where(later, came_state, 0.0)
        out_prefix[ch : ch + hl, :] = jnp.where(later, came_log, 0.0)
    else:
        joined = prefix_joined(dims, bit, prefix, came)
        out_prefix[0:ch, :] = joined
        out_prefix[ch : ch + hl, :] = prefix[ch : ch + hl, :] + jnp.where(later, came_log, 0.0)


def prefix_joined(dims, bit, prefix, came):
    V, D, hl, ch, nh, ns, T, N = dims
    later = lax.rem(lax.div(lax.axis_index("seq"), 2**bit), 2) == 1
    factor = jnp.exp(state_rows(dims, prefix[ch : ch + hl, :]))
    return prefix[0:ch, :] + jnp.where(later, factor * came[0:ch, :], 0.0)


def output_kernel(dims, bit, *refs):
    V, D, hl, ch, nh, ns, T, N = dims
    P = ch // hl
    prefix, came, read_high, read_low, base, fade, gate, own, proj_high, proj_low = refs[:10]
    groups, outs, partial_ref = refs[10], refs[11 : 11 + nh], refs[11 + nh]
    entering = prefix_joined(dims, bit, prefix, came)
    carried = dot_split((read_high[...], read_low[...]), split2(entering), NT)
    value = (base[...] + carried * fade[...]) * gate[...]
    square = dot(jnp.concatenate(split2(value * value), axis=0), groups[0:ch, 0:ch])
    square = square[T:] + square[0:T]
    value = value * lax.rsqrt(square * (1.0 / P) + epsilon)
    share = T // nh
    partial_ref[...] = dot_split(split2(value), (proj_high[...], proj_low[...]))
    mine = lax.axis_index("head")
    for k in range(nh):
        place = pl.multiple_of(lax.bitwise_xor(mine, k) * share, 8)
        part = partial_ref[pl.ds(place, share), :]
        outs[k][...] = part + own[...] if k == 0 else part


def per_device(
    token_ids,
    embedding,
    complement,
    prenorm_first,
    inproj_first,
    statemap_first,
    stepmap_first,
    stepbias_first,
    rates_first,
    skipgain_first,
    outnorm_first,
    outproj_first,
    prenorm_second,
    inproj_second,
    statemap_second,
    stepmap_second,
    stepbias_second,
    rates_second,
    skipgain_second,
    outnorm_second,
    outproj_second,
):
    nh, ns = lax.axis_size("head"), lax.axis_size("seq")
    V, D = embedding.shape
    ch = inproj_first.shape[2]
    hl = stepmap_first.shape[1]
    N = statemap_first.shape[2]
    T = token_ids.shape[0]
    LV = nh * hl * V
    dims = (V, D, hl, ch, nh, ns, T, N)
    vmem = pl.BlockSpec(memory_space=pltpu.VMEM)
    smem = pl.BlockSpec(memory_space=pltpu.SMEM)
    anywhere = pl.BlockSpec(memory_space=pl.ANY)
    params = pltpu.CompilerParams(vmem_limit_bytes=LIMIT)

    def shape(*sizes, dtype=f32):
        return jax.ShapeDtypeStruct(sizes, dtype)

    def halves(*sizes):
        return [shape(*sizes, dtype=bf16)] * 2

    def room(value):
        return pltpu.VMEM(value.shape, value.dtype)

    def line(value):
        return value.reshape(1, -1)

    def flat(value):
        return value.reshape(-1, value.shape[-1])

    heavy = pl.CostEstimate(flops=960 * T * D * D, bytes_accessed=4 * T * D, transcendentals=T * D)

    half = ch // 2
    share = T // nh
    fetched = [
        flat(inproj_first),
        line(token_ids),
        embedding,
        line(prenorm_first),
        stepmap_first.T,
        line(stepbias_first),
        line(rates_first),
        line(skipgain_first),
        line(outnorm_first),
    ]
    message = pl.pallas_call(
        functools.partial(tables_kernel, dims),
        out_shape=shape(top_rows(dims) + half * (D // ch), ch),
        in_specs=[anywhere] * (len(fetched) + 1),
        out_specs=vmem,
        scratch_shapes=[room(value) for value in fetched]
        + [pltpu.SemaphoreType.DMA((len(fetched) - 1 + PIECES + D // ch,))],
        compiler_params=pltpu.CompilerParams(vmem_limit_bytes=TABLES_LIMIT),
        cost_estimate=heavy,
        name="tables",
    )(*fetched, outproj_first)

    prepared = [
        embedding,
        line(prenorm_first),
        flat(statemap_first),
        line(complement),
        outproj_first,
        line(prenorm_second),
        flat(inproj_second),
        flat(statemap_second),
        stepmap_second.T,
        stepbias_second,
        rates_second,
        skipgain_second,
        line(outnorm_second),
    ]
    (
        pair_table,
        small,
        choose,
        own_high,
        own_low,
        state_high,
        state_low,
        rest_high,
        rest_low,
        triangles,
        upto,
        groups,
        blocks,
    ) = pl.pallas_call(
        functools.partial(prepare_kernel, dims),
        out_shape=(
            shape(V, LV),
            shape(8, ch),
            shape(D, D, dtype=bf16),
            *halves(ch, D),
            *halves(D, 2 * ch + N),
            *halves(D, ch + N),
            shape(T, 2 * T, dtype=bf16),
            shape(T, T, dtype=bf16),
            shape(2 * ch, 2 * ch, dtype=bf16),
            shape(LV, nh * ch, dtype=bf16),
        ),
        in_specs=[vmem] * 9 + [smem] * 3 + [vmem],
        out_specs=(vmem,) * 13,
        compiler_params=params,
        cost_estimate=heavy,
        name="prepare",
    )(*prepared)

    count = max(ns, nh)
    messages = {0: message}
    for k in in_turn(count):
        seq_bits, head_bits = partners(ns, nh)[k]
        pairs = [
            (seq * nh + head, (seq ^ seq_bits) * nh + (head ^ head_bits))
            for seq in range(ns)
            for head in range(nh)
        ]
        sent = message if k < nh else message[0 : top_rows(dims)]
        messages[k] = lax.ppermute(sent, ("seq", "head"), pairs)
    swap = [(seq, seq ^ 1) for seq in range(ns)]
    order = in_turn(nh)[::-1]
    others = [lax.ppermute(messages[k], "seq", swap) for k in order]

    mixed_high, mixed_low, embedded = pl.pallas_call(
        functools.partial(mix_kernel, dims),
        out_shape=(*halves(T, nh * ch), shape(T, D)),
        in_specs=[vmem] * (count + 5),
        out_specs=(vmem,) * 3,
        scratch_shapes=[pltpu.VMEM((max(ns, 8), T), f32)],
        compiler_params=params,
        cost_estimate=heavy,
        name="mix",
    )(
        *[messages[k] for k in in_turn(count)[::-1] + [0]],
        embedding,
        pair_table,
        triangles,
        groups,
        blocks,
    )

    state, hidden_high, hidden_low, scale, write, inner, stepped, total = pl.pallas_call(
        functools.partial(project_kernel, dims),
        out_shape=(
            shape(ch + 8, N),
            *halves(T, D),
            shape(T, ch),
            shape(T, N),
            shape(T, ch),
            shape(T, ch),
            shape(T, ch),
        ),
        in_specs=[vmem] * (9 + 2 * (nh - 1)),
        out_specs=(vmem,) * 8,
        compiler_params=params,
        name="project",
    )(
        mixed_high,
        mixed_low,
        embedded,
        small,
        own_high,
        own_low,
        state_high,
        state_low,
        upto,
        *[messages[k] for k in order],
        *others,
    )

    base, read_high, read_low, fade, gate, own, proj_high, proj_low = pl.pallas_call(
        functools.partial(block_kernel, dims),
        out_shape=(
            shape(T, ch),
            *halves(T, N),
            shape(T, ch),
            shape(T, ch),
            shape(share, D),
            *halves(ch, D),
        ),
        in_specs=[vmem] * 12,
        out_specs=(vmem,) * 8,
        scratch_shapes=[pltpu.VMEM((T, D), f32)],
        compiler_params=params,
        cost_estimate=heavy,
        name="block",
    )(
        hidden_high,
        hidden_low,
        scale,
        write,
        inner,
        stepped,
        total,
        choose,
        rest_high,
        rest_low,
        small,
        outproj_second,
    )

    prefix = None
    bits = ns.bit_length() - 1
    for bit in range(bits):
        came = lax.ppermute(state, "seq", [(seq, seq ^ 2**bit) for seq in range(ns)])
        if bit == bits - 1:
            break
        given = [state] + ([] if prefix is None else [prefix]) + [came]

        def join(bit, known, *refs):
            if known:
                join_kernel(dims, bit, *refs)
            else:
                join_kernel(dims, bit, refs[0], None, *refs[1:])

        state, prefix = pl.pallas_call(
            functools.partial(join, bit, prefix is not None),
            out_shape=(shape(ch + 8, N),) * 2,
            in_specs=[vmem] * len(given),
            out_specs=(vmem,) * 2,
            compiler_params=params,
            name="join",
        )(*given)
    if prefix is None:
        prefix = jnp.zeros_like(state)

    parts = pl.pallas_call(
        functools.partial(output_kernel, dims, bits - 1),
        out_shape=(shape(share, D),) * nh,
        in_specs=[vmem] * 11,
        out_specs=(vmem,) * nh,
        scratch_shapes=[pltpu.VMEM((T, D), f32)],
        compiler_params=params,
        name="output",
    )(
        prefix,
        came,
        read_high,
        read_low,
        base,
        fade,
        gate,
        own,
        proj_high,
        proj_low,
        groups,
    )
    result = parts[0]
    for k in in_turn(nh):
        pairs = [(source, source ^ k) for source in range(nh)]
        result = result + lax.ppermute(parts[k], "head", pairs)
    return result


def solution(mesh):
    return jax.shard_map(
        per_device,
        mesh=mesh,
        in_specs=(
            P(("rep", "seq")),
            P(),
            P(),
            P(),
            P(None, None, "head"),
            P(),
            P(None, "head"),
            P("head"),
            P("head"),
            P("head"),
            P("head"),
            P("head", None),
            P(),
            P(None, None, "head"),
            P(),
            P(None, "head"),
            P("head"),
            P("head"),
            P("head"),
            P("head"),
            P("head", None),
        ),
        out_specs=P(("rep", "seq", "head"), None),
        check_vma=False,
    )
```

```python
import functools

import jax
import jax.numpy as jnp
from jax import lax
from jax.experimental import pallas as pl
from jax.experimental.pallas import tpu as pltpu
from jax.sharding import PartitionSpec as P

epsilon = 1e-05
f32 = jnp.float32
bf16 = jnp.bfloat16
LIMIT = 48 * 1024 * 1024
TABLES_LIMIT = 60 * 1000 * 1000

MM = (((1,), (0,)), ((), ()))
NT = (((1,), (1,)), ((), ()))
TN = (((0,), (0,)), ((), ()))


def partners(ns, nh):
    count = max(ns, nh)
    return [((ns - k) if 0 < k < ns else 0, k if k < nh else 0) for k in range(count)]


def in_turn(count):
    return sorted(range(1, count), key=lambda k: (-k.bit_length(), k))


def iota(shape, axis):
    return lax.broadcasted_iota(jnp.int32, shape, axis)


def split2(value):
    high = value.astype(bf16)
    return high, (value - high.astype(f32)).astype(bf16)


def split3(value):
    high = value.astype(bf16)
    rest = value - high.astype(f32)
    middle = rest.astype(bf16)
    return high, middle, (rest - middle.astype(f32)).astype(bf16)


def dot(left, right, dims=MM):
    return lax.dot_general(left, right, dims, preferred_element_type=f32)


def dot_split(left, right, dims=MM):
    axis = 1 if dims == TN else 0
    size = left[0].shape[axis]
    if size % 16:
        return (dot(left[0], right[1], dims) + dot(left[1], right[0], dims)) + dot(
            left[0], right[0], dims
        )
    both = dot(jnp.concatenate([left[1], left[0]], axis=axis), right[0], dims)
    return (dot(left[0], right[1], dims) + both[0:size]) + both[size:]


def dot3(left, right, dims=MM):
    return dot_split(split2(left), split2(right), dims)


def dot_left_exact(left, right, dims=MM):
    high, middle, low = split3(right)
    return (dot(left, low, dims) + dot(left, middle, dims)) + dot(left, high, dims)


def dot_right_exact(left, right, dims=MM):
    high, middle, low = split3(left)
    return (dot(low, right, dims) + dot(middle, right, dims)) + dot(high, right, dims)


def softplus(value):
    return jnp.maximum(value, 0.0) + jnp.log1p(jnp.exp(-jnp.abs(value)))


def silu(value):
    return value / (1.0 + jnp.exp(-value))


def rms(value):
    return value * lax.rsqrt(jnp.mean(value * value, axis=-1, keepdims=True) + epsilon)


def fetch(sources, places, semaphores):
    copies = []
    for number, (source, place) in enumerate(zip(sources, places)):
        copies.append(pltpu.make_async_copy(source, place, semaphores.at[number]))
        copies[-1].start()
    return copies


def fetch(sources, places, semaphores):
    copies = []
    for number, (source, place) in enumerate(zip(sources, places)):
        copies.append(pltpu.make_async_copy(source, place, semaphores.at[number]))
        copies[-1].start()
    return copies


PIECES = 1


def tables_kernel(dims, *refs):
    V, D, hl, ch, nh, ns, T, N = dims
    refs = list(refs)

    def take(number):
        taken, refs[:] = refs[:number], refs[number:]
        return taken

    sources = take(9)
    outproj_source, message = take(2)
    places = take(9)
    semaphores = take(1)[0]
    half = ch // 2
    top = top_rows(dims)
    core = lax.rem(lax.axis_index("seq"), 2)
    (inproj, tok, emb, prenorm, stepmap, bias, rates, skip, outnorm) = places
    size = inproj.shape[0] // PIECES
    pieces = [pl.ds(number * size, size) for number in range(PIECES)]
    rows = pl.ds(pl.multiple_of(core * half, 8), half)
    wide = [(place, pl.ds(place * ch, ch)) for place in range(D // ch)]
    copies = fetch(
        [sources[0].at[piece, :] for piece in pieces]
        + sources[1:]
        + [outproj_source.at[rows, columns] for _, columns in wide],
        [inproj.at[piece, :] for piece in pieces]
        + places[1:]
        + [message.at[pl.ds(top + place * half, half), :] for place, _ in wide],
        semaphores,
    )
    flip = (iota((T, 1), 0) + iota((1, T), 1) == T - 1).astype(f32).astype(bf16)
    for copy in copies[PIECES : PIECES + 8]:
        copy.wait()
    normed = split2(rms(emb[...]) * prenorm[...])
    raw_t = dot_split(split2(stepmap[...]), normed, NT)
    tokens = jnp.broadcast_to(tok[...].astype(f32), (8, T)).astype(bf16)
    tokens = dot(tokens, flip)
    for place in range(T // ch):
        message[2 * V + place : 2 * V + place + 1, :] = tokens[0:1, place * ch : (place + 1) * ch]
    row = 2 * V + T // ch
    message[row : row + 1, :] = outnorm[...]
    for head in range(hl):
        line = softplus(raw_t[head : head + 1, :] + bias[:, head : head + 1])
        row = row + 1
        message[row : row + 1, 0:V] = line
        message[row : row + 1, V : 2 * V] = -rates[:, head : head + 1] * line
        message[row : row + 1, 2 * V : 3 * V] = jnp.broadcast_to(skip[:, head : head + 1], (1, V))
    for copy in copies[:PIECES]:
        copy.wait()
    weights = jnp.concatenate(
        [inproj[pl.ds(0, D, stride=2), :], inproj[pl.ds(1, D, stride=2), :]], axis=1
    )
    both = dot_split(normed, split2(weights))
    message[0:V, :] = both[:, 0:ch]
    message[V : 2 * V, :] = both[:, ch:]
    for copy in copies[PIECES + 8 :]:
        copy.wait()


def top_rows(dims):
    V, D, hl, ch, nh, ns, T, N = dims
    return 2 * V + -(-(T // ch + 1 + hl) // 8) * 8


def head_line(dims, values):
    V, D, hl, ch, nh, ns, T, N = dims
    head_of = iota((1, ch), 1) // (ch // hl)
    line = jnp.zeros((1, ch), f32)
    for head in range(hl):
        line = jnp.where(head_of == head, values[head], line)
    return line


def prepare_kernel(dims, *refs):
    V, D, hl, ch, nh, ns, T, N = dims
    H, P = nh * hl, ch // hl
    refs = list(refs)

    def take(number):
        taken, refs[:] = refs[:number], refs[number:]
        return taken

    emb, prenorm, statemap, complement, outproj = take(5)
    prenorm2, inproj2, statemap2, stepmap2 = take(4)
    bias2, rates2, skip2, outnorm2 = take(4)
    pairs, small, choose_out, own_high, own_low = take(5)
    state_high, state_low, rest_high, rest_low = take(4)
    triangles, upto, groups, blocks = take(4)
    normed = split2(rms(emb[...]) * prenorm[...])
    write = dot_split(normed, split2(statemap[pl.ds(0, D, stride=2), :]))
    read = dot_split(normed, split2(statemap[pl.ds(1, D, stride=2), :]))
    pairs[...] = dot3(read, jnp.concatenate([write] * H, axis=0), NT)
    own_high[...], own_low[...] = split2(outproj[...])
    choose = (complement[...] == iota((D, 1), 0)).astype(f32).astype(bf16)
    choose_out[...] = choose
    gain = jnp.transpose(jnp.broadcast_to(prenorm2[...], (128, D)))

    def weights(values):
        return split2(dot_left_exact(choose, values))

    gain_wide = gain[:, 0:1]
    inner = inproj2[pl.ds(1, D, stride=2), :] * gain_wide
    step = jnp.transpose(
        jnp.concatenate(
            [jnp.broadcast_to(stepmap2[head : head + 1, :], (P, D)) for head in range(hl)], axis=0
        )
    )
    write2 = statemap2[pl.ds(0, D, stride=2), :] * gain_wide
    state_high[...], state_low[...] = weights(
        jnp.concatenate([inner, step * gain_wide, write2], axis=1)
    )
    gate = inproj2[pl.ds(0, D, stride=2), :] * gain_wide
    read2 = statemap2[pl.ds(1, D, stride=2), :] * gain_wide
    rest_high[...], rest_low[...] = weights(jnp.concatenate([gate, read2], axis=1))
    small[0:1, :] = head_line(dims, bias2)
    small[1:2, :] = head_line(dims, rates2)
    small[2:3, :] = head_line(dims, skip2)
    small[3:4, :] = outnorm2[...]
    row, column = iota((T, 1), 0), iota((1, T), 1)
    triangles[:, 0:T] = (row > column).astype(f32).astype(bf16)
    triangles[:, T : 2 * T] = (row < column).astype(f32).astype(bf16)
    triangles[:, 2 * T :] = jnp.ones((T, 128), bf16)
    upto[...] = (row >= column).astype(f32).astype(bf16)
    size = groups.shape[0]
    groups[...] = (iota((size, 1), 0) // P == iota((1, size), 1) // P).astype(f32).astype(bf16)
    rows, columns = blocks.shape
    blocks[...] = (iota((rows, 1), 0) // V == iota((1, columns), 1) // P).astype(f32).astype(bf16)


def shift_rows(value, amount, fill):
    size = value.shape[0]
    if amount % 8 == 0:
        empty = jnp.full((abs(amount),) + value.shape[1:], fill, value.dtype)
        if amount > 0:
            return jnp.concatenate([empty, value[: size - amount]], axis=0)
        return jnp.concatenate([value[-amount:], empty], axis=0)
    rolled = pltpu.roll(value, amount % size, 0)
    row = iota((8,) + value.shape[1:], 0)
    if amount > 0:
        edge = jnp.where(row >= amount, rolled[0:8], fill)
        return jnp.concatenate([edge, rolled[8:]], axis=0)
    edge = jnp.where(row < 8 + amount, rolled[size - 8 :], fill)
    return jnp.concatenate([rolled[: size - 8], edge], axis=0)


def scan_rows(decay, value, sign):
    size = value.shape[0]
    amount = 1
    while amount < size:
        value = value + decay * shift_rows(value, sign * amount, 0.0)
        decay = decay * shift_rows(decay, sign * amount, 1.0)
        amount *= 2
    return value, decay


def mix_kernel(dims, *refs):
    V, D, hl, ch, nh, ns, T, N = dims
    H, LV, P = nh * hl, nh * hl * V, ch // hl
    C = nh * ch
    refs = list(refs)

    def take(number):
        taken, refs[:] = refs[:number], refs[number:]
        return taken

    count = max(ns, nh)
    packets = dict(zip(in_turn(count)[::-1] + [0], take(count)))
    emb, pairs, triangles, groups, blocks = take(5)
    out_high, out_low, out_embedded = take(3)
    tokens = take(1)[0]
    mine = lax.axis_index("seq")

    for k in range(ns):
        block = ns - 1 - lax.bitwise_xor(mine, partners(ns, nh)[k][0])
        row = 2 * V
        pieces = [packets[k][row + place : row + place + 1, :] for place in range(T // ch)]
        tokens[pl.ds(block, 1), :] = jnp.concatenate(pieces, axis=1)

    first = 2 * V + T // ch + 1
    steps = jnp.concatenate(
        [packets[k][first : first + hl, 0 : 3 * V] for k in range(nh)], axis=0
    )
    log_t = steps[:, V : 2 * V]
    narrow = jnp.concatenate([part.astype(f32) for part in split3(steps)], axis=0).astype(bf16)
    spread_heads = (iota((1, LV), 1) // V == iota((3 * H, 1), 0) % H).astype(f32).astype(bf16)
    wide = dot(narrow, spread_heads, TN)
    own = iota((1, LV), 1) % V == iota((V, 1), 0)
    decay_table = jnp.exp(wide[V : 2 * V])
    step_table = jnp.where(own, wide[0:V], 0.0)
    gain_table = jnp.where(own, wide[2 * V : 3 * V], 0.0)
    gates = jnp.concatenate([packets[k][0:V, :] for k in range(nh)], axis=1)
    inners = jnp.concatenate([packets[k][V : 2 * V, :] for k in range(nh)], axis=1)
    gains = jnp.concatenate([packets[k][first - 1 : first, :] for k in range(nh)], axis=1)

    token_row = (iota((LV, 1), 0) % V).astype(f32)
    log_split = jnp.concatenate(split3(log_t), axis=1)
    onehots, logs = [], []
    for block in range(ns):
        onehot = (tokens[block : block + 1, :] == token_row).astype(f32).astype(bf16)
        onehots.append(onehot)
        logs.append(dot(log_split, onehot[0 : 3 * V, :]))
    logs = jnp.concatenate(logs, axis=0)
    size = ns * H
    sums = dot(jnp.concatenate(split3(logs)[::-1], axis=0), triangles[...])
    sums = (sums[0:size] + sums[size : 2 * size]) + sums[2 * size :]
    blocks_of = [sums[block * H : (block + 1) * H] for block in range(ns)]
    weight_up, weight_down = [None] * ns, [None] * ns
    gap = jnp.zeros((H, 128), f32)
    for block in reversed(range(ns)):
        wide = jnp.concatenate([gap] * (T // 128), axis=1)
        weight_up[block] = jnp.where(
            block < mine, jnp.exp(blocks_of[block][:, 0:T] + wide), 0.0
        )
        gap = jnp.where(block < mine, gap + blocks_of[block][:, 2 * T :], gap)
    gap = jnp.zeros((H, 128), f32)
    for block in range(ns):
        wide = jnp.concatenate([gap] * (T // 128), axis=1)
        weight_down[block] = jnp.where(
            block > mine, jnp.exp(blocks_of[block][:, T : 2 * T] + wide), 0.0
        )
        gap = jnp.where(block > mine, gap + blocks_of[block][:, 2 * T :], gap)
    entering = jnp.zeros((4 * H, LV), f32)
    for block in range(ns):
        both = jnp.concatenate([weight_up[block], weight_down[block]], axis=0)
        entering = entering + dot(
            jnp.concatenate(split2(both), axis=0), onehots[block], NT
        )
    entering = entering[2 * H :] + entering[0 : 2 * H]
    diagonal = iota((1, LV), 1) // V == iota((H, 1), 0)
    step_row = jnp.sum(step_table, axis=0, keepdims=True)
    enter_up = step_row * jnp.sum(
        jnp.where(diagonal, entering[0:H], 0.0), axis=0, keepdims=True
    )
    enter_down = step_row * jnp.sum(
        jnp.where(diagonal, entering[H : 2 * H], 0.0), axis=0, keepdims=True
    )

    looked = jnp.concatenate(
        [decay_table, step_table, pairs[...], gain_table, silu(gates), emb[...]], axis=1
    )
    looked = jnp.concatenate(split3(looked), axis=0)
    token = tokens[pl.ds(mine, 1), :]
    onehot = (token == token_row[0 : 3 * V]).astype(f32).astype(bf16)
    rows = dot(onehot, looked, TN)
    decay, step = rows[:, 0:LV], rows[:, LV : 2 * LV]
    pair, gain = rows[:, 2 * LV : 3 * LV], rows[:, 3 * LV : 4 * LV]
    silu_rows = rows[:, 4 * LV : 4 * LV + C]
    out_embedded[...] = rows[:, 4 * LV + C :]

    up, fade = scan_rows(decay, step, 1)
    up = up + fade * enter_up
    down, fade = scan_rows(decay, step, -1)
    down = down + fade * enter_down

    spread_high, spread_low = [
        jnp.concatenate([part] * H, axis=0) * blocks[...] for part in split2(inners)
    ]
    both = jnp.concatenate([up * pair + gain, down * pair + gain], axis=0)
    high = both.astype(bf16)
    high_wide = high.astype(f32)
    low_turned = pltpu.roll(both - high_wide, LV // 2, 1)
    lower = iota((1, LV), 1) < LV // 2
    value = []
    for side in (0, 1):
        mixed = jnp.where(lower == (side == 0), high_wide, low_turned).astype(bf16)
        rows = slice(side * LV // 2, (side + 1) * LV // 2)
        columns = slice(side * C // 2, (side + 1) * C // 2)
        weight, rest = spread_high[rows, columns], spread_low[:, columns]
        value.append(
            dot(
                jnp.concatenate([mixed, high], axis=1),
                jnp.concatenate([weight, weight, rest], axis=0),
            )
        )
    value = jnp.concatenate(value, axis=1)
    value = value * jnp.concatenate([silu_rows, silu_rows], axis=0)
    wide = groups.shape[0]
    high, low = split2(value * value)
    starts = list(range(0, C, wide))
    rows = 2 * T
    stacked = [half[:, start : start + wide] for start in starts for half in (low, high)]
    squares = dot(jnp.concatenate(stacked, axis=0), groups[...])
    for number, start in enumerate(starts):
        place = 2 * number * rows
        square = squares[place : place + rows] + squares[place + rows : place + 2 * rows]
        stop = start + wide
        normed = value[:, start:stop] * lax.rsqrt(square * (1.0 / P) + epsilon)
        out_high[:, start:stop], out_low[:, start:stop] = split2(
            (normed[0:T] + normed[T : 2 * T]) * gains[:, start:stop]
        )


def project_kernel(dims, *refs):
    V, D, hl, ch, nh, ns, T, N = dims
    P = ch // hl
    refs = list(refs)

    def take(number):
        taken, refs[:] = refs[:number], refs[number:]
        return taken

    high, low, embedded, small, own_high, own_low, state_high, state_low, upto = take(9)
    order = in_turn(nh)[::-1]
    nears = dict(zip(order, take(nh - 1)))
    others = dict(zip(order, take(nh - 1)))
    out_state, out_high, out_low, out_scale = take(4)
    out_write, out_inner, out_stepped, out_total = take(4)
    half = ch // 2
    base = top_rows(dims)
    mine = lax.axis_index("seq")

    pieces = []
    for k in range(1, nh):
        near, other = [
            jnp.concatenate(
                [
                    ref[base + place * half : base + (place + 1) * half, :]
                    for place in range(D // ch)
                ],
                axis=1,
            )
            for ref in (nears[k], others[k])
        ]
        even = lax.rem(lax.bitwise_xor(mine, partners(ns, nh)[k][0]), 2) == 0
        pieces.append(jnp.where(even, near, other))
        pieces.append(jnp.where(even, other, near))
    weights = split2(jnp.concatenate(pieces, axis=0))
    weights = (
        jnp.concatenate([own_high[...], weights[0]], axis=0),
        jnp.concatenate([own_low[...], weights[1]], axis=0),
    )
    hidden = embedded[...] + dot_split((high[...], low[...]), weights)
    split = split2(hidden)
    out_high[...], out_low[...] = split
    scale = lax.rsqrt(jnp.mean(hidden * hidden, axis=-1, keepdims=True) + epsilon)
    out_scale[...] = jnp.broadcast_to(scale, (T, ch))

    rows = dot_split(split, (state_high[...], state_low[...])) * scale
    inner, write = rows[:, 0:ch], rows[:, 2 * ch :]
    step = softplus(rows[:, ch : 2 * ch] + small[0:1, :])
    stepped = inner * step
    log_high, log_middle, log_low = split3(-small[1:2, :] * step)
    total = dot(upto[...], jnp.concatenate([log_low, log_middle], axis=1))
    total = (total[:, 0:ch] + total[:, ch:]) + dot(upto[...], log_high)
    end = total[T - 1 : T, :]
    state = dot3(stepped * jnp.exp(end - total), write, TN)
    out_state[0:ch, :] = state
    for head in range(hl):
        out_state[ch + head : ch + head + 1, :] = jnp.broadcast_to(
            end[:, head * P : head * P + 1], (1, N)
        )
    out_write[...] = write
    out_inner[...] = inner
    out_stepped[...] = stepped
    out_total[...] = total


def block_kernel(dims, *refs):
    V, D, hl, ch, nh, ns, T, N = dims
    P = ch // hl
    refs = list(refs)

    def take(number):
        taken, refs[:] = refs[:number], refs[number:]
        return taken

    high, low, scale, write, inner, stepped, total, choose = take(8)
    rest_high, rest_low, small, outproj2 = take(4)
    base, read_high, read_low, out_fade, out_gate, own, out_high, out_low, hidden_ref = take(9)
    rows = dot_split((high[...], low[...]), (rest_high[...], rest_low[...]))
    out_gate[...] = silu(rows[:, 0:ch] * scale[...])
    read = rows[:, ch:] * scale[...]
    read = split2(read)
    read_high[...], read_low[...] = read
    out_fade[...] = jnp.exp(total[...])
    products = dot_split(read, split2(write[...]), NT)
    stepped_high, stepped_low = split2(stepped[...])
    select = (iota((8, ch), 1) == iota((8, ch), 0) * P).astype(f32).astype(bf16)
    total_high, total_middle, total_low = split3(total[...])
    total_t = (dot(select, total_low, NT) + dot(select, total_middle, NT)) + dot(
        select, total_high, NT
    )
    allowed = iota((T, 1), 0) >= iota((1, T), 1)
    parts = []
    for head in range(hl):
        start, stop = head * P, (head + 1) * P
        differ = total[:, start : start + 1] - total_t[head : head + 1, :]
        weights = jnp.where(allowed, jnp.exp(jnp.where(allowed, differ, 0.0)), 0.0) * products
        part = dot_split(
            split2(weights), (stepped_high[:, start:stop], stepped_low[:, start:stop])
        )
        parts.append(part + small[2:3, start:stop] * inner[:, start:stop])
    base[...] = jnp.concatenate(parts, axis=1)
    share = T // nh
    hidden_ref[...] = high[...].astype(f32) + low[...].astype(f32)
    place = pl.multiple_of(lax.axis_index("head") * share, 8)
    out_gain = jnp.transpose(jnp.broadcast_to(small[3:4, :], (128, ch)))
    out_high[...], out_low[...] = split2(outproj2[...] * out_gain[:, 0:1])
    own[...] = dot_right_exact(hidden_ref[pl.ds(place, share), :], choose[...])


def state_rows(dims, values):
    V, D, hl, ch, nh, ns, T, N = dims
    head_of = iota((ch, N), 0) // (ch // hl)
    result = jnp.broadcast_to(values[0:1, :], (ch, N))
    for head in range(1, hl):
        result = jnp.where(head_of == head, values[head : head + 1, :], result)
    return result


def join_kernel(dims, bit, total, prefix, came, out_total, out_prefix):
    V, D, hl, ch, nh, ns, T, N = dims
    later = lax.rem(lax.div(lax.axis_index("seq"), 2**bit), 2) == 1
    came_state, came_log = came[0:ch, :], came[ch : ch + hl, :]
    state, log = total[0:ch, :], total[ch : ch + hl, :]
    factor = jnp.exp(state_rows(dims, jnp.where(later, log, came_log)))
    out_total[0:ch, :] = jnp.where(
        later, factor * came_state + state, factor * state + came_state
    )
    out_total[ch : ch + hl, :] = log + came_log
    if prefix is None:
        out_prefix[0:ch, :] = jnp.where(later, came_state, 0.0)
        out_prefix[ch : ch + hl, :] = jnp.where(later, came_log, 0.0)
    else:
        joined = prefix_joined(dims, bit, prefix, came)
        out_prefix[0:ch, :] = joined
        out_prefix[ch : ch + hl, :] = prefix[ch : ch + hl, :] + jnp.where(later, came_log, 0.0)


def prefix_joined(dims, bit, prefix, came):
    V, D, hl, ch, nh, ns, T, N = dims
    later = lax.rem(lax.div(lax.axis_index("seq"), 2**bit), 2) == 1
    factor = jnp.exp(state_rows(dims, prefix[ch : ch + hl, :]))
    return prefix[0:ch, :] + jnp.where(later, factor * came[0:ch, :], 0.0)


def output_kernel(dims, bit, *refs):
    V, D, hl, ch, nh, ns, T, N = dims
    P = ch // hl
    prefix, came, read_high, read_low, base, fade, gate, own, proj_high, proj_low = refs[:10]
    groups, outs, partial_ref = refs[10], refs[11 : 11 + nh], refs[11 + nh]
    entering = prefix_joined(dims, bit, prefix, came)
    carried = dot_split((read_high[...], read_low[...]), split2(entering), NT)
    value = (base[...] + carried * fade[...]) * gate[...]
    square = dot(jnp.concatenate(split2(value * value), axis=0), groups[0:ch, 0:ch])
    square = square[T:] + square[0:T]
    value = value * lax.rsqrt(square * (1.0 / P) + epsilon)
    share = T // nh
    partial_ref[...] = dot_split(split2(value), (proj_high[...], proj_low[...]))
    mine = lax.axis_index("head")
    for k in range(nh):
        place = pl.multiple_of(lax.bitwise_xor(mine, k) * share, 8)
        part = partial_ref[pl.ds(place, share), :]
        outs[k][...] = part + own[...] if k == 0 else part


def per_device(
    token_ids,
    embedding,
    complement,
    prenorm_first,
    inproj_first,
    statemap_first,
    stepmap_first,
    stepbias_first,
    rates_first,
    skipgain_first,
    outnorm_first,
    outproj_first,
    prenorm_second,
    inproj_second,
    statemap_second,
    stepmap_second,
    stepbias_second,
    rates_second,
    skipgain_second,
    outnorm_second,
    outproj_second,
):
    nh, ns = lax.axis_size("head"), lax.axis_size("seq")
    V, D = embedding.shape
    ch = inproj_first.shape[2]
    hl = stepmap_first.shape[1]
    N = statemap_first.shape[2]
    T = token_ids.shape[0]
    LV = nh * hl * V
    dims = (V, D, hl, ch, nh, ns, T, N)
    vmem = pl.BlockSpec(memory_space=pltpu.VMEM)
    smem = pl.BlockSpec(memory_space=pltpu.SMEM)
    anywhere = pl.BlockSpec(memory_space=pl.ANY)
    params = pltpu.CompilerParams(vmem_limit_bytes=LIMIT)

    def shape(*sizes, dtype=f32):
        return jax.ShapeDtypeStruct(sizes, dtype)

    def halves(*sizes):
        return [shape(*sizes, dtype=bf16)] * 2

    def room(value):
        return pltpu.VMEM(value.shape, value.dtype)

    def line(value):
        return value.reshape(1, -1)

    def flat(value):
        return value.reshape(-1, value.shape[-1])

    heavy = pl.CostEstimate(flops=960 * T * D * D, bytes_accessed=4 * T * D, transcendentals=T * D)

    half = ch // 2
    share = T // nh
    fetched = [
        flat(inproj_first),
        line(token_ids),
        embedding,
        line(prenorm_first),
        stepmap_first.T,
        line(stepbias_first),
        line(rates_first),
        line(skipgain_first),
        line(outnorm_first),
    ]
    message = pl.pallas_call(
        functools.partial(tables_kernel, dims),
        out_shape=shape(top_rows(dims) + half * (D // ch), ch),
        in_specs=[anywhere] * (len(fetched) + 1),
        out_specs=vmem,
        scratch_shapes=[room(value) for value in fetched]
        + [pltpu.SemaphoreType.DMA((len(fetched) - 1 + PIECES + D // ch,))],
        compiler_params=pltpu.CompilerParams(vmem_limit_bytes=TABLES_LIMIT),
        cost_estimate=heavy,
        name="tables",
    )(*fetched, outproj_first)

    prepared = [
        embedding,
        line(prenorm_first),
        flat(statemap_first),
        line(complement),
        outproj_first,
        line(prenorm_second),
        flat(inproj_second),
        flat(statemap_second),
        stepmap_second.T,
        stepbias_second,
        rates_second,
        skipgain_second,
        line(outnorm_second),
    ]
    (
        pair_table,
        small,
        choose,
        own_high,
        own_low,
        state_high,
        state_low,
        rest_high,
        rest_low,
        triangles,
        upto,
        groups,
        blocks,
    ) = pl.pallas_call(
        functools.partial(prepare_kernel, dims),
        out_shape=(
            shape(V, LV),
            shape(8, ch),
            shape(D, D, dtype=bf16),
            *halves(ch, D),
            *halves(D, 2 * ch + N),
            *halves(D, ch + N),
            shape(T, 2 * T + 128, dtype=bf16),
            shape(T, T, dtype=bf16),
            shape(2 * ch, 2 * ch, dtype=bf16),
            shape(LV, nh * ch, dtype=bf16),
        ),
        in_specs=[vmem] * 9 + [smem] * 3 + [vmem],
        out_specs=(vmem,) * 13,
        compiler_params=params,
        cost_estimate=heavy,
        name="prepare",
    )(*prepared)

    count = max(ns, nh)
    messages = {0: message}
    for k in in_turn(count):
        seq_bits, head_bits = partners(ns, nh)[k]
        pairs = [
            (seq * nh + head, (seq ^ seq_bits) * nh + (head ^ head_bits))
            for seq in range(ns)
            for head in range(nh)
        ]
        sent = message if k < nh else message[0 : top_rows(dims)]
        messages[k] = lax.ppermute(sent, ("seq", "head"), pairs)
    swap = [(seq, seq ^ 1) for seq in range(ns)]
    order = in_turn(nh)[::-1]
    others = [lax.ppermute(messages[k], "seq", swap) for k in order]

    mixed_high, mixed_low, embedded = pl.pallas_call(
        functools.partial(mix_kernel, dims),
        out_shape=(*halves(T, nh * ch), shape(T, D)),
        in_specs=[vmem] * (count + 5),
        out_specs=(vmem,) * 3,
        scratch_shapes=[pltpu.VMEM((max(ns, 8), T), f32)],
        compiler_params=params,
        cost_estimate=heavy,
        name="mix",
    )(
        *[messages[k] for k in in_turn(count)[::-1] + [0]],
        embedding,
        pair_table,
        triangles,
        groups,
        blocks,
    )

    state, hidden_high, hidden_low, scale, write, inner, stepped, total = pl.pallas_call(
        functools.partial(project_kernel, dims),
        out_shape=(
            shape(ch + 8, N),
            *halves(T, D),
            shape(T, ch),
            shape(T, N),
            shape(T, ch),
            shape(T, ch),
            shape(T, ch),
        ),
        in_specs=[vmem] * (9 + 2 * (nh - 1)),
        out_specs=(vmem,) * 8,
        compiler_params=params,
        name="project",
    )(
        mixed_high,
        mixed_low,
        embedded,
        small,
        own_high,
        own_low,
        state_high,
        state_low,
        upto,
        *[messages[k] for k in order],
        *others,
    )

    base, read_high, read_low, fade, gate, own, proj_high, proj_low = pl.pallas_call(
        functools.partial(block_kernel, dims),
        out_shape=(
            shape(T, ch),
            *halves(T, N),
            shape(T, ch),
            shape(T, ch),
            shape(share, D),
            *halves(ch, D),
        ),
        in_specs=[vmem] * 12,
        out_specs=(vmem,) * 8,
        scratch_shapes=[pltpu.VMEM((T, D), f32)],
        compiler_params=params,
        cost_estimate=heavy,
        name="block",
    )(
        hidden_high,
        hidden_low,
        scale,
        write,
        inner,
        stepped,
        total,
        choose,
        rest_high,
        rest_low,
        small,
        outproj_second,
    )

    prefix = None
    bits = ns.bit_length() - 1
    for bit in range(bits):
        came = lax.ppermute(state, "seq", [(seq, seq ^ 2**bit) for seq in range(ns)])
        if bit == bits - 1:
            break
        given = [state] + ([] if prefix is None else [prefix]) + [came]

        def join(bit, known, *refs):
            if known:
                join_kernel(dims, bit, *refs)
            else:
                join_kernel(dims, bit, refs[0], None, *refs[1:])

        state, prefix = pl.pallas_call(
            functools.partial(join, bit, prefix is not None),
            out_shape=(shape(ch + 8, N),) * 2,
            in_specs=[vmem] * len(given),
            out_specs=(vmem,) * 2,
            compiler_params=params,
            name="join",
        )(*given)
    if prefix is None:
        prefix = jnp.zeros_like(state)

    parts = pl.pallas_call(
        functools.partial(output_kernel, dims, bits - 1),
        out_shape=(shape(share, D),) * nh,
        in_specs=[vmem] * 11,
        out_specs=(vmem,) * nh,
        scratch_shapes=[pltpu.VMEM((T, D), f32)],
        compiler_params=params,
        name="output",
    )(
        prefix,
        came,
        read_high,
        read_low,
        base,
        fade,
        gate,
        own,
        proj_high,
        proj_low,
        groups,
    )
    result = parts[0]
    for k in in_turn(nh):
        pairs = [(source, source ^ k) for source in range(nh)]
        result = result + lax.ppermute(parts[k], "head", pairs)
    return result


def solution(mesh):
    return jax.shard_map(
        per_device,
        mesh=mesh,
        in_specs=(
            P(("rep", "seq")),
            P(),
            P(),
            P(),
            P(None, None, "head"),
            P(),
            P(None, "head"),
            P("head"),
            P("head"),
            P("head"),
            P("head"),
            P("head", None),
            P(),
            P(None, None, "head"),
            P(),
            P(None, "head"),
            P("head"),
            P("head"),
            P("head"),
            P("head"),
            P("head", None),
        ),
        out_specs=P(("rep", "seq", "head"), None),
        check_vma=False,
    )
```

```python
import functools

import jax
import jax.numpy as jnp
from jax import lax
from jax.experimental import pallas as pl
from jax.experimental.pallas import tpu as pltpu
from jax.sharding import PartitionSpec as P

epsilon = 1e-05
f32 = jnp.float32
bf16 = jnp.bfloat16
LIMIT = 48 * 1024 * 1024

MM = (((1,), (0,)), ((), ()))
NT = (((1,), (1,)), ((), ()))
TN = (((0,), (0,)), ((), ()))


def partners(ns, nh):
    count = max(ns, nh)
    return [((ns - k) if 0 < k < ns else 0, k if k < nh else 0) for k in range(count)]


def in_turn(count):
    return sorted(range(1, count), key=lambda k: (-k.bit_length(), k))


def iota(shape, axis):
    return lax.broadcasted_iota(jnp.int32, shape, axis)


def split2(value):
    high = value.astype(bf16)
    return high, (value - high.astype(f32)).astype(bf16)


def split3(value):
    high = value.astype(bf16)
    rest = value - high.astype(f32)
    middle = rest.astype(bf16)
    return high, middle, (rest - middle.astype(f32)).astype(bf16)


def dot(left, right, dims=MM):
    return lax.dot_general(left, right, dims, preferred_element_type=f32)


def dot_split(left, right, dims=MM):
    axis = 1 if dims == TN else 0
    size = left[0].shape[axis]
    if size % 16:
        return (dot(left[0], right[1], dims) + dot(left[1], right[0], dims)) + dot(
            left[0], right[0], dims
        )
    both = dot(jnp.concatenate([left[1], left[0]], axis=axis), right[0], dims)
    return (dot(left[0], right[1], dims) + both[0:size]) + both[size:]


def dot3(left, right, dims=MM):
    return dot_split(split2(left), split2(right), dims)


def dot_left_exact(left, right, dims=MM):
    high, middle, low = split3(right)
    return (dot(left, low, dims) + dot(left, middle, dims)) + dot(left, high, dims)


def dot_right_exact(left, right, dims=MM):
    high, middle, low = split3(left)
    return (dot(low, right, dims) + dot(middle, right, dims)) + dot(high, right, dims)


def softplus(value):
    return jnp.maximum(value, 0.0) + jnp.log1p(jnp.exp(-jnp.abs(value)))


def silu(value):
    return value / (1.0 + jnp.exp(-value))


def rms(value):
    return value * lax.rsqrt(jnp.mean(value * value, axis=-1, keepdims=True) + epsilon)


def fetch(sources, places, semaphores):
    copies = []
    for number, (source, place) in enumerate(zip(sources, places)):
        copies.append(pltpu.make_async_copy(source, place, semaphores.at[number]))
        copies[-1].start()
    return copies


def fetch(sources, places, semaphores):
    copies = []
    for number, (source, place) in enumerate(zip(sources, places)):
        copies.append(pltpu.make_async_copy(source, place, semaphores.at[number]))
        copies[-1].start()
    return copies


PIECES = 1


def tables_kernel(dims, *refs):
    V, D, hl, ch, nh, ns, T, N = dims
    refs = list(refs)

    def take(number):
        taken, refs[:] = refs[:number], refs[number:]
        return taken

    sources = take(9)
    outproj_source, message = take(2)
    places = take(9)
    semaphores = take(1)[0]
    half = ch // 2
    top = top_rows(dims)
    core = lax.rem(lax.axis_index("seq"), 2)
    (inproj, tok, emb, prenorm, stepmap, bias, rates, skip, outnorm) = places
    size = inproj.shape[0] // PIECES
    pieces = [pl.ds(number * size, size) for number in range(PIECES)]
    rows = pl.ds(pl.multiple_of(core * half, 8), half)
    wide = [(place, pl.ds(place * ch, ch)) for place in range(D // ch)]
    copies = fetch(
        [sources[0].at[piece, :] for piece in pieces]
        + sources[1:]
        + [outproj_source.at[rows, columns] for _, columns in wide],
        [inproj.at[piece, :] for piece in pieces]
        + places[1:]
        + [message.at[pl.ds(top + place * half, half), :] for place, _ in wide],
        semaphores,
    )
    flip = (iota((T, 1), 0) + iota((1, T), 1) == T - 1).astype(f32).astype(bf16)
    for copy in copies[PIECES : PIECES + 8]:
        copy.wait()
    normed = split2(rms(emb[...]) * prenorm[...])
    raw_t = dot_split(split2(stepmap[...]), normed, NT)
    tokens = jnp.broadcast_to(tok[...].astype(f32), (8, T)).astype(bf16)
    tokens = dot(tokens, flip)
    for place in range(T // ch):
        message[2 * V + place : 2 * V + place + 1, :] = tokens[0:1, place * ch : (place + 1) * ch]
    row = 2 * V + T // ch
    message[row : row + 1, :] = outnorm[...]
    for head in range(hl):
        line = softplus(raw_t[head : head + 1, :] + bias[:, head : head + 1])
        row = row + 1
        message[row : row + 1, 0:V] = line
        message[row : row + 1, V : 2 * V] = -rates[:, head : head + 1] * line
        message[row : row + 1, 2 * V : 3 * V] = jnp.broadcast_to(skip[:, head : head + 1], (1, V))
    for copy in copies[:PIECES]:
        copy.wait()
    weights = jnp.concatenate(
        [inproj[pl.ds(0, D, stride=2), :], inproj[pl.ds(1, D, stride=2), :]], axis=1
    )
    both = dot_split(normed, split2(weights))
    message[0:V, :] = both[:, 0:ch]
    message[V : 2 * V, :] = both[:, ch:]
    for copy in copies[PIECES + 8 :]:
        copy.wait()


def top_rows(dims):
    V, D, hl, ch, nh, ns, T, N = dims
    return 2 * V + -(-(T // ch + 1 + hl) // 8) * 8


def head_line(dims, values):
    V, D, hl, ch, nh, ns, T, N = dims
    head_of = iota((1, ch), 1) // (ch // hl)
    line = jnp.zeros((1, ch), f32)
    for head in range(hl):
        line = jnp.where(head_of == head, values[:, head : head + 1], line)
    return line


def prepare_kernel(dims, *refs):
    V, D, hl, ch, nh, ns, T, N = dims
    H, P = nh * hl, ch // hl
    refs = list(refs)

    def take(number):
        taken, refs[:] = refs[:number], refs[number:]
        return taken

    sources = take(14)
    pairs, small, choose_out, own_high, own_low = take(5)
    state_high, state_low, rest_high, rest_low, out_high, out_low = take(6)
    triangles, upto, groups, blocks = take(4)
    places = take(14)
    semaphores = take(1)[0]
    copies = fetch(sources, places, semaphores)
    inproj2, statemap2, statemap, outproj, outproj2, emb, prenorm, complement = places[:8]
    prenorm2, stepmap2, bias2, rates2, skip2, outnorm2 = places[8:]
    row, column = iota((T, 1), 0), iota((1, T), 1)
    triangles[:, 0:T] = (row > column).astype(f32).astype(bf16)
    triangles[:, T : 2 * T] = (row < column).astype(f32).astype(bf16)
    triangles[:, 2 * T :] = jnp.ones((T, 128), bf16)
    upto[...] = (row >= column).astype(f32).astype(bf16)
    size = groups.shape[0]
    groups[...] = (iota((size, 1), 0) // P == iota((1, size), 1) // P).astype(f32).astype(bf16)
    rows, columns = blocks.shape
    blocks[...] = (iota((rows, 1), 0) // V == iota((1, columns), 1) // P).astype(f32).astype(bf16)
    for copy in copies:
        copy.wait()
    normed = split2(rms(emb[...]) * prenorm[...])
    write = dot_split(normed, split2(statemap[pl.ds(0, D, stride=2), :]))
    read = dot_split(normed, split2(statemap[pl.ds(1, D, stride=2), :]))
    pairs[...] = dot3(read, jnp.concatenate([write] * H, axis=0), NT)
    own_high[...], own_low[...] = split2(outproj[...])
    choose = (complement[...] == iota((D, 1), 0)).astype(f32).astype(bf16)
    choose_out[...] = choose
    gain = jnp.transpose(jnp.broadcast_to(prenorm2[...], (128, D)))

    def weights(values):
        return split2(dot_left_exact(choose, values))

    gain_wide = gain[:, 0:1]
    inner = inproj2[pl.ds(1, D, stride=2), :] * gain_wide
    step = jnp.transpose(
        jnp.concatenate(
            [jnp.broadcast_to(stepmap2[head : head + 1, :], (P, D)) for head in range(hl)], axis=0
        )
    )
    write2 = statemap2[pl.ds(0, D, stride=2), :] * gain_wide
    state_high[...], state_low[...] = weights(
        jnp.concatenate([inner, step * gain_wide, write2], axis=1)
    )
    gate = inproj2[pl.ds(0, D, stride=2), :] * gain_wide
    read2 = statemap2[pl.ds(1, D, stride=2), :] * gain_wide
    rest_high[...], rest_low[...] = weights(jnp.concatenate([gate, read2], axis=1))
    small[0:1, :] = head_line(dims, bias2)
    small[1:2, :] = head_line(dims, rates2)
    small[2:3, :] = head_line(dims, skip2)
    out_gain = jnp.transpose(jnp.broadcast_to(outnorm2[...], (128, ch)))
    out_high[...], out_low[...] = split2(outproj2[...] * out_gain[:, 0:1])


def shift_rows(value, amount, fill):
    size = value.shape[0]
    if amount % 8 == 0:
        empty = jnp.full((abs(amount),) + value.shape[1:], fill, value.dtype)
        if amount > 0:
            return jnp.concatenate([empty, value[: size - amount]], axis=0)
        return jnp.concatenate([value[-amount:], empty], axis=0)
    rolled = pltpu.roll(value, amount % size, 0)
    row = iota((8,) + value.shape[1:], 0)
    if amount > 0:
        edge = jnp.where(row >= amount, rolled[0:8], fill)
        return jnp.concatenate([edge, rolled[8:]], axis=0)
    edge = jnp.where(row < 8 + amount, rolled[size - 8 :], fill)
    return jnp.concatenate([rolled[: size - 8], edge], axis=0)


def scan_rows(decay, value, sign):
    size = value.shape[0]
    amount = 1
    while amount < size:
        value = value + decay * shift_rows(value, sign * amount, 0.0)
        decay = decay * shift_rows(decay, sign * amount, 1.0)
        amount *= 2
    return value, decay


def mix_kernel(dims, *refs):
    V, D, hl, ch, nh, ns, T, N = dims
    H, LV, P = nh * hl, nh * hl * V, ch // hl
    C = nh * ch
    refs = list(refs)

    def take(number):
        taken, refs[:] = refs[:number], refs[number:]
        return taken

    count = max(ns, nh)
    packets = dict(zip(in_turn(count)[::-1] + [0], take(count)))
    emb, pairs, triangles, groups, blocks = take(5)
    out_high, out_low, out_embedded = take(3)
    tokens = take(1)[0]
    mine = lax.axis_index("seq")

    for k in range(ns):
        block = ns - 1 - lax.bitwise_xor(mine, partners(ns, nh)[k][0])
        row = 2 * V
        pieces = [packets[k][row + place : row + place + 1, :] for place in range(T // ch)]
        tokens[pl.ds(block, 1), :] = jnp.concatenate(pieces, axis=1)

    first = 2 * V + T // ch + 1
    steps = jnp.concatenate(
        [packets[k][first : first + hl, 0 : 3 * V] for k in range(nh)], axis=0
    )
    log_t = steps[:, V : 2 * V]
    narrow = jnp.concatenate([part.astype(f32) for part in split3(steps)], axis=0).astype(bf16)
    spread_heads = (iota((1, LV), 1) // V == iota((3 * H, 1), 0) % H).astype(f32).astype(bf16)
    wide = dot(narrow, spread_heads, TN)
    own = iota((1, LV), 1) % V == iota((V, 1), 0)
    decay_table = jnp.exp(wide[V : 2 * V])
    step_table = jnp.where(own, wide[0:V], 0.0)
    gain_table = jnp.where(own, wide[2 * V : 3 * V], 0.0)
    gates = jnp.concatenate([packets[k][0:V, :] for k in range(nh)], axis=1)
    inners = jnp.concatenate([packets[k][V : 2 * V, :] for k in range(nh)], axis=1)
    gains = jnp.concatenate([packets[k][first - 1 : first, :] for k in range(nh)], axis=1)

    token_row = (iota((LV, 1), 0) % V).astype(f32)
    log_split = jnp.concatenate(split3(log_t), axis=1)
    onehots, logs = [], []
    for block in range(ns):
        onehot = (tokens[block : block + 1, :] == token_row).astype(f32).astype(bf16)
        onehots.append(onehot)
        logs.append(dot(log_split, onehot[0 : 3 * V, :]))
    logs = jnp.concatenate(logs, axis=0)
    size = ns * H
    sums = dot(jnp.concatenate(split3(logs)[::-1], axis=0), triangles[...])
    sums = (sums[0:size] + sums[size : 2 * size]) + sums[2 * size :]
    blocks_of = [sums[block * H : (block + 1) * H] for block in range(ns)]
    weight_up, weight_down = [None] * ns, [None] * ns
    gap = jnp.zeros((H, 128), f32)
    for block in reversed(range(ns)):
        wide = jnp.concatenate([gap] * (T // 128), axis=1)
        weight_up[block] = jnp.where(
            block < mine, jnp.exp(blocks_of[block][:, 0:T] + wide), 0.0
        )
        gap = jnp.where(block < mine, gap + blocks_of[block][:, 2 * T :], gap)
    gap = jnp.zeros((H, 128), f32)
    for block in range(ns):
        wide = jnp.concatenate([gap] * (T // 128), axis=1)
        weight_down[block] = jnp.where(
            block > mine, jnp.exp(blocks_of[block][:, T : 2 * T] + wide), 0.0
        )
        gap = jnp.where(block > mine, gap + blocks_of[block][:, 2 * T :], gap)
    entering = jnp.zeros((4 * H, LV), f32)
    for block in range(ns):
        both = jnp.concatenate([weight_up[block], weight_down[block]], axis=0)
        entering = entering + dot(
            jnp.concatenate(split2(both), axis=0), onehots[block], NT
        )
    entering = entering[2 * H :] + entering[0 : 2 * H]
    diagonal = iota((1, LV), 1) // V == iota((H, 1), 0)
    step_row = jnp.sum(step_table, axis=0, keepdims=True)
    enter_up = step_row * jnp.sum(
        jnp.where(diagonal, entering[0:H], 0.0), axis=0, keepdims=True
    )
    enter_down = step_row * jnp.sum(
        jnp.where(diagonal, entering[H : 2 * H], 0.0), axis=0, keepdims=True
    )

    looked = jnp.concatenate(
        [decay_table, step_table, pairs[...], gain_table, silu(gates), emb[...]], axis=1
    )
    looked = jnp.concatenate(split3(looked), axis=0)
    token = tokens[pl.ds(mine, 1), :]
    onehot = (token == token_row[0 : 3 * V]).astype(f32).astype(bf16)
    rows = dot(onehot, looked, TN)
    decay, step = rows[:, 0:LV], rows[:, LV : 2 * LV]
    pair, gain = rows[:, 2 * LV : 3 * LV], rows[:, 3 * LV : 4 * LV]
    silu_rows = rows[:, 4 * LV : 4 * LV + C]
    out_embedded[...] = rows[:, 4 * LV + C :]

    up, fade = scan_rows(decay, step, 1)
    up = up + fade * enter_up
    down, fade = scan_rows(decay, step, -1)
    down = down + fade * enter_down

    spread_high, spread_low = [
        jnp.concatenate([part] * H, axis=0) * blocks[...] for part in split2(inners)
    ]
    both = jnp.concatenate([up * pair + gain, down * pair + gain], axis=0)
    high = both.astype(bf16)
    high_wide = high.astype(f32)
    low_turned = pltpu.roll(both - high_wide, LV // 2, 1)
    lower = iota((1, LV), 1) < LV // 2
    value = []
    for side in (0, 1):
        mixed = jnp.where(lower == (side == 0), high_wide, low_turned).astype(bf16)
        rows = slice(side * LV // 2, (side + 1) * LV // 2)
        columns = slice(side * C // 2, (side + 1) * C // 2)
        weight, rest = spread_high[rows, columns], spread_low[:, columns]
        value.append(
            dot(
                jnp.concatenate([mixed, high], axis=1),
                jnp.concatenate([weight, weight, rest], axis=0),
            )
        )
    value = jnp.concatenate(value, axis=1)
    value = value * jnp.concatenate([silu_rows, silu_rows], axis=0)
    wide = groups.shape[0]
    high, low = split2(value * value)
    starts = list(range(0, C, wide))
    rows = 2 * T
    stacked = [half[:, start : start + wide] for start in starts for half in (low, high)]
    squares = dot(jnp.concatenate(stacked, axis=0), groups[...])
    for number, start in enumerate(starts):
        place = 2 * number * rows
        square = squares[place : place + rows] + squares[place + rows : place + 2 * rows]
        stop = start + wide
        normed = value[:, start:stop] * lax.rsqrt(square * (1.0 / P) + epsilon)
        out_high[:, start:stop], out_low[:, start:stop] = split2(
            (normed[0:T] + normed[T : 2 * T]) * gains[:, start:stop]
        )


def project_kernel(dims, *refs):
    V, D, hl, ch, nh, ns, T, N = dims
    P = ch // hl
    refs = list(refs)

    def take(number):
        taken, refs[:] = refs[:number], refs[number:]
        return taken

    high, low, embedded, small, own_high, own_low, state_high, state_low, upto = take(9)
    order = in_turn(nh)[::-1]
    nears = dict(zip(order, take(nh - 1)))
    others = dict(zip(order, take(nh - 1)))
    out_state, out_high, out_low, out_scale = take(4)
    out_write, out_inner, out_stepped, out_total = take(4)
    half = ch // 2
    base = top_rows(dims)
    mine = lax.axis_index("seq")

    pieces = []
    for k in range(1, nh):
        near, other = [
            jnp.concatenate(
                [
                    ref[base + place * half : base + (place + 1) * half, :]
                    for place in range(D // ch)
                ],
                axis=1,
            )
            for ref in (nears[k], others[k])
        ]
        even = lax.rem(lax.bitwise_xor(mine, partners(ns, nh)[k][0]), 2) == 0
        pieces.append(jnp.where(even, near, other))
        pieces.append(jnp.where(even, other, near))
    weights = split2(jnp.concatenate(pieces, axis=0))
    weights = (
        jnp.concatenate([own_high[...], weights[0]], axis=0),
        jnp.concatenate([own_low[...], weights[1]], axis=0),
    )
    hidden = embedded[...] + dot_split((high[...], low[...]), weights)
    split = split2(hidden)
    out_high[...], out_low[...] = split
    scale = lax.rsqrt(jnp.mean(hidden * hidden, axis=-1, keepdims=True) + epsilon)
    out_scale[...] = jnp.broadcast_to(scale, (T, ch))

    rows = dot_split(split, (state_high[...], state_low[...])) * scale
    inner, write = rows[:, 0:ch], rows[:, 2 * ch :]
    step = softplus(rows[:, ch : 2 * ch] + small[0:1, :])
    stepped = inner * step
    log_high, log_middle, log_low = split3(-small[1:2, :] * step)
    total = dot(upto[...], jnp.concatenate([log_low, log_middle], axis=1))
    total = (total[:, 0:ch] + total[:, ch:]) + dot(upto[...], log_high)
    end = total[T - 1 : T, :]
    state = dot3(stepped * jnp.exp(end - total), write, TN)
    out_state[0:ch, :] = state
    for head in range(hl):
        out_state[ch + head : ch + head + 1, :] = jnp.broadcast_to(
            end[:, head * P : head * P + 1], (1, N)
        )
    out_write[...] = write
    out_inner[...] = inner
    out_stepped[...] = stepped
    out_total[...] = total


def block_kernel(dims, *refs):
    V, D, hl, ch, nh, ns, T, N = dims
    P = ch // hl
    refs = list(refs)

    def take(number):
        taken, refs[:] = refs[:number], refs[number:]
        return taken

    high, low, scale, write, inner, stepped, total, choose = take(8)
    rest_high, rest_low, small = take(3)
    base, read_high, read_low, out_fade, out_gate, own, hidden_ref = take(7)
    rows = dot_split((high[...], low[...]), (rest_high[...], rest_low[...]))
    out_gate[...] = silu(rows[:, 0:ch] * scale[...])
    read = rows[:, ch:] * scale[...]
    read = split2(read)
    read_high[...], read_low[...] = read
    out_fade[...] = jnp.exp(total[...])
    products = dot_split(read, split2(write[...]), NT)
    stepped_high, stepped_low = split2(stepped[...])
    select = (iota((8, ch), 1) == iota((8, ch), 0) * P).astype(f32).astype(bf16)
    total_high, total_middle, total_low = split3(total[...])
    total_t = (dot(select, total_low, NT) + dot(select, total_middle, NT)) + dot(
        select, total_high, NT
    )
    allowed = iota((T, 1), 0) >= iota((1, T), 1)
    parts = []
    for head in range(hl):
        start, stop = head * P, (head + 1) * P
        differ = total[:, start : start + 1] - total_t[head : head + 1, :]
        weights = jnp.where(allowed, jnp.exp(jnp.where(allowed, differ, 0.0)), 0.0) * products
        part = dot_split(
            split2(weights), (stepped_high[:, start:stop], stepped_low[:, start:stop])
        )
        parts.append(part + small[2:3, start:stop] * inner[:, start:stop])
    base[...] = jnp.concatenate(parts, axis=1)
    share = T // nh
    hidden_ref[...] = high[...].astype(f32) + low[...].astype(f32)
    place = pl.multiple_of(lax.axis_index("head") * share, 8)
    own[...] = dot_right_exact(hidden_ref[pl.ds(place, share), :], choose[...])


def state_rows(dims, values):
    V, D, hl, ch, nh, ns, T, N = dims
    head_of = iota((ch, N), 0) // (ch // hl)
    result = jnp.broadcast_to(values[0:1, :], (ch, N))
    for head in range(1, hl):
        result = jnp.where(head_of == head, values[head : head + 1, :], result)
    return result


def join_kernel(dims, bit, total, prefix, came, out_total, out_prefix):
    V, D, hl, ch, nh, ns, T, N = dims
    later = lax.rem(lax.div(lax.axis_index("seq"), 2**bit), 2) == 1
    came_state, came_log = came[0:ch, :], came[ch : ch + hl, :]
    state, log = total[0:ch, :], total[ch : ch + hl, :]
    factor = jnp.exp(state_rows(dims, jnp.where(later, log, came_log)))
    out_total[0:ch, :] = jnp.where(
        later, factor * came_state + state, factor * state + came_state
    )
    out_total[ch : ch + hl, :] = log + came_log
    if prefix is None:
        out_prefix[0:ch, :] = jnp.where(later, came_state, 0.0)
        out_prefix[ch : ch + hl, :] = jnp.where(later, came_log, 0.0)
    else:
        joined = prefix_joined(dims, bit, prefix, came)
        out_prefix[0:ch, :] = joined
        out_prefix[ch : ch + hl, :] = prefix[ch : ch + hl, :] + jnp.where(later, came_log, 0.0)


def prefix_joined(dims, bit, prefix, came):
    V, D, hl, ch, nh, ns, T, N = dims
    later = lax.rem(lax.div(lax.axis_index("seq"), 2**bit), 2) == 1
    factor = jnp.exp(state_rows(dims, prefix[ch : ch + hl, :]))
    return prefix[0:ch, :] + jnp.where(later, factor * came[0:ch, :], 0.0)


def output_kernel(dims, bit, *refs):
    V, D, hl, ch, nh, ns, T, N = dims
    P = ch // hl
    prefix, came, read_high, read_low, base, fade, gate, own, proj_high, proj_low = refs[:10]
    groups, outs, partial_ref = refs[10], refs[11 : 11 + nh], refs[11 + nh]
    entering = prefix_joined(dims, bit, prefix, came)
    carried = dot_split((read_high[...], read_low[...]), split2(entering), NT)
    value = (base[...] + carried * fade[...]) * gate[...]
    square = dot(jnp.concatenate(split2(value * value), axis=0), groups[0:ch, 0:ch])
    square = square[T:] + square[0:T]
    value = value * lax.rsqrt(square * (1.0 / P) + epsilon)
    share = T // nh
    partial_ref[...] = dot_split(split2(value), (proj_high[...], proj_low[...]))
    mine = lax.axis_index("head")
    for k in range(nh):
        place = pl.multiple_of(lax.bitwise_xor(mine, k) * share, 8)
        part = partial_ref[pl.ds(place, share), :]
        outs[k][...] = part + own[...] if k == 0 else part


def per_device(
    token_ids,
    embedding,
    complement,
    prenorm_first,
    inproj_first,
    statemap_first,
    stepmap_first,
    stepbias_first,
    rates_first,
    skipgain_first,
    outnorm_first,
    outproj_first,
    prenorm_second,
    inproj_second,
    statemap_second,
    stepmap_second,
    stepbias_second,
    rates_second,
    skipgain_second,
    outnorm_second,
    outproj_second,
):
    nh, ns = lax.axis_size("head"), lax.axis_size("seq")
    V, D = embedding.shape
    ch = inproj_first.shape[2]
    hl = stepmap_first.shape[1]
    N = statemap_first.shape[2]
    T = token_ids.shape[0]
    LV = nh * hl * V
    dims = (V, D, hl, ch, nh, ns, T, N)
    vmem = pl.BlockSpec(memory_space=pltpu.VMEM)
    anywhere = pl.BlockSpec(memory_space=pl.ANY)
    params = pltpu.CompilerParams(vmem_limit_bytes=LIMIT)

    def shape(*sizes, dtype=f32):
        return jax.ShapeDtypeStruct(sizes, dtype)

    def halves(*sizes):
        return [shape(*sizes, dtype=bf16)] * 2

    def room(value):
        return pltpu.VMEM(value.shape, value.dtype)

    def kept(values):
        return [pltpu.with_memory_space_constraint(value, pltpu.HBM) for value in values]

    def line(value):
        return value.reshape(1, -1)

    def flat(value):
        return value.reshape(-1, value.shape[-1])

    heavy = pl.CostEstimate(flops=960 * T * D * D, bytes_accessed=4 * T * D, transcendentals=T * D)

    half = ch // 2
    share = T // nh
    fetched = [
        flat(inproj_first),
        line(token_ids),
        embedding,
        line(prenorm_first),
        stepmap_first.T,
        line(stepbias_first),
        line(rates_first),
        line(skipgain_first),
        line(outnorm_first),
    ]
    message = pl.pallas_call(
        functools.partial(tables_kernel, dims),
        out_shape=pltpu.VMEM((top_rows(dims) + half * (D // ch), ch), f32),
        in_specs=[anywhere] * (len(fetched) + 1),
        out_specs=vmem,
        scratch_shapes=[room(value) for value in fetched]
        + [pltpu.SemaphoreType.DMA((len(fetched) - 1 + PIECES + D // ch,))],
        compiler_params=params,
        name="tables",
    )(*kept([*fetched, outproj_first]))

    prepared = [
        flat(inproj_second),
        flat(statemap_second),
        flat(statemap_first),
        outproj_first,
        outproj_second,
        embedding,
        line(prenorm_first),
        line(complement),
        line(prenorm_second),
        stepmap_second.T,
        line(stepbias_second),
        line(rates_second),
        line(skipgain_second),
        line(outnorm_second),
    ]
    (
        pair_table,
        small,
        choose,
        own_high,
        own_low,
        state_high,
        state_low,
        rest_high,
        rest_low,
        proj_high,
        proj_low,
        triangles,
        upto,
        groups,
        blocks,
    ) = pl.pallas_call(
        functools.partial(prepare_kernel, dims),
        out_shape=(
            shape(V, LV),
            shape(8, ch),
            shape(D, D, dtype=bf16),
            *halves(ch, D),
            *halves(D, 2 * ch + N),
            *halves(D, ch + N),
            *halves(ch, D),
            shape(T, 2 * T + 128, dtype=bf16),
            shape(T, T, dtype=bf16),
            shape(2 * ch, 2 * ch, dtype=bf16),
            shape(LV, nh * ch, dtype=bf16),
        ),
        in_specs=[anywhere] * len(prepared),
        out_specs=(vmem,) * 15,
        scratch_shapes=[room(value) for value in prepared]
        + [pltpu.SemaphoreType.DMA((len(prepared),))],
        compiler_params=params,
        cost_estimate=heavy,
        name="prepare",
    )(*kept(prepared))

    count = max(ns, nh)
    messages = {0: message}
    for k in in_turn(count):
        seq_bits, head_bits = partners(ns, nh)[k]
        pairs = [
            (seq * nh + head, (seq ^ seq_bits) * nh + (head ^ head_bits))
            for seq in range(ns)
            for head in range(nh)
        ]
        sent = message if k < nh else message[0 : top_rows(dims)]
        messages[k] = lax.ppermute(sent, ("seq", "head"), pairs)
    swap = [(seq, seq ^ 1) for seq in range(ns)]
    order = in_turn(nh)[::-1]
    others = [lax.ppermute(messages[k], "seq", swap) for k in order]

    mixed_high, mixed_low, embedded = pl.pallas_call(
        functools.partial(mix_kernel, dims),
        out_shape=(*halves(T, nh * ch), shape(T, D)),
        in_specs=[vmem] * (count + 5),
        out_specs=(vmem,) * 3,
        scratch_shapes=[pltpu.VMEM((max(ns, 8), T), f32)],
        compiler_params=params,
        cost_estimate=heavy,
        name="mix",
    )(
        *[messages[k] for k in in_turn(count)[::-1] + [0]],
        embedding,
        pair_table,
        triangles,
        groups,
        blocks,
    )

    state, hidden_high, hidden_low, scale, write, inner, stepped, total = pl.pallas_call(
        functools.partial(project_kernel, dims),
        out_shape=(
            shape(ch + 8, N),
            *halves(T, D),
            shape(T, ch),
            shape(T, N),
            shape(T, ch),
            shape(T, ch),
            shape(T, ch),
        ),
        in_specs=[vmem] * (9 + 2 * (nh - 1)),
        out_specs=(vmem,) * 8,
        compiler_params=params,
        name="project",
    )(
        mixed_high,
        mixed_low,
        embedded,
        small,
        own_high,
        own_low,
        state_high,
        state_low,
        upto,
        *[messages[k] for k in order],
        *others,
    )

    base, read_high, read_low, fade, gate, own = pl.pallas_call(
        functools.partial(block_kernel, dims),
        out_shape=(
            shape(T, ch),
            *halves(T, N),
            shape(T, ch),
            shape(T, ch),
            shape(share, D),
        ),
        in_specs=[vmem] * 11,
        out_specs=(vmem,) * 6,
        scratch_shapes=[pltpu.VMEM((T, D), f32)],
        compiler_params=params,
        cost_estimate=heavy,
        name="block",
    )(
        hidden_high,
        hidden_low,
        scale,
        write,
        inner,
        stepped,
        total,
        choose,
        rest_high,
        rest_low,
        small,
    )

    prefix = None
    bits = ns.bit_length() - 1
    for bit in range(bits):
        came = lax.ppermute(state, "seq", [(seq, seq ^ 2**bit) for seq in range(ns)])
        if bit == bits - 1:
            break
        given = [state] + ([] if prefix is None else [prefix]) + [came]

        def join(bit, known, *refs):
            if known:
                join_kernel(dims, bit, *refs)
            else:
                join_kernel(dims, bit, refs[0], None, *refs[1:])

        state, prefix = pl.pallas_call(
            functools.partial(join, bit, prefix is not None),
            out_shape=(shape(ch + 8, N),) * 2,
            in_specs=[vmem] * len(given),
            out_specs=(vmem,) * 2,
            compiler_params=params,
            name="join",
        )(*given)
    if prefix is None:
        prefix = jnp.zeros_like(state)

    parts = pl.pallas_call(
        functools.partial(output_kernel, dims, bits - 1),
        out_shape=(shape(share, D),) * nh,
        in_specs=[vmem] * 11,
        out_specs=(vmem,) * nh,
        scratch_shapes=[pltpu.VMEM((T, D), f32)],
        compiler_params=params,
        name="output",
    )(
        prefix,
        came,
        read_high,
        read_low,
        base,
        fade,
        gate,
        own,
        proj_high,
        proj_low,
        groups,
    )
    result = parts[0]
    for k in in_turn(nh):
        pairs = [(source, source ^ k) for source in range(nh)]
        result = result + lax.ppermute(parts[k], "head", pairs)
    return result


def solution(mesh):
    return jax.shard_map(
        per_device,
        mesh=mesh,
        in_specs=(
            P(("rep", "seq")),
            P(),
            P(),
            P(),
            P(None, None, "head"),
            P(),
            P(None, "head"),
            P("head"),
            P("head"),
            P("head"),
            P("head"),
            P("head", None),
            P(),
            P(None, None, "head"),
            P(),
            P(None, "head"),
            P("head"),
            P("head"),
            P("head"),
            P("head"),
            P("head", None),
        ),
        out_specs=P(("rep", "seq", "head"), None),
        check_vma=False,
    )
```

```python
import functools

import jax
import jax.numpy as jnp
from jax import lax
from jax.experimental import pallas as pl
from jax.experimental.pallas import tpu as pltpu
from jax.sharding import PartitionSpec as P

epsilon = 1e-05
f32 = jnp.float32
bf16 = jnp.bfloat16
LIMIT = 48 * 1024 * 1024

MM = (((1,), (0,)), ((), ()))
NT = (((1,), (1,)), ((), ()))
TN = (((0,), (0,)), ((), ()))


def partners(ns, nh):
    count = max(ns, nh)
    return [((ns - k) if 0 < k < ns else 0, k if k < nh else 0) for k in range(count)]


def in_turn(count):
    return sorted(range(1, count), key=lambda k: (-k.bit_length(), k))


def iota(shape, axis):
    return lax.broadcasted_iota(jnp.int32, shape, axis)


def split2(value):
    high = value.astype(bf16)
    return high, (value - high.astype(f32)).astype(bf16)


def split3(value):
    high = value.astype(bf16)
    rest = value - high.astype(f32)
    middle = rest.astype(bf16)
    return high, middle, (rest - middle.astype(f32)).astype(bf16)


def dot(left, right, dims=MM):
    rows = left.shape[0]
    if dims != TN and rows >= 256:
        parts = [left[: rows // 2], left[rows // 2 :]]
        return jnp.concatenate(
            [lax.dot_general(part, right, dims, preferred_element_type=f32) for part in parts],
            axis=0,
        )
    return lax.dot_general(left, right, dims, preferred_element_type=f32)


def dot_split(left, right, dims=MM):
    axis = 1 if dims == TN else 0
    size = left[0].shape[axis]
    if size % 16:
        return (dot(left[0], right[1], dims) + dot(left[1], right[0], dims)) + dot(
            left[0], right[0], dims
        )
    both = dot(jnp.concatenate([left[1], left[0]], axis=axis), right[0], dims)
    return (dot(left[0], right[1], dims) + both[0:size]) + both[size:]


def dot3(left, right, dims=MM):
    return dot_split(split2(left), split2(right), dims)


def dot_left_exact(left, right, dims=MM):
    high, middle, low = split3(right)
    return (dot(left, low, dims) + dot(left, middle, dims)) + dot(left, high, dims)


def dot_right_exact(left, right, dims=MM):
    high, middle, low = split3(left)
    return (dot(low, right, dims) + dot(middle, right, dims)) + dot(high, right, dims)


def softplus(value):
    return jnp.maximum(value, 0.0) + jnp.log1p(jnp.exp(-jnp.abs(value)))


def silu(value):
    return value / (1.0 + jnp.exp(-value))


def rms(value):
    return value * lax.rsqrt(jnp.mean(value * value, axis=-1, keepdims=True) + epsilon)


def fetch(sources, places, semaphores):
    copies = []
    for number, (source, place) in enumerate(zip(sources, places)):
        copies.append(pltpu.make_async_copy(source, place, semaphores.at[number]))
        copies[-1].start()
    return copies


def fetch(sources, places, semaphores):
    copies = []
    for number, (source, place) in enumerate(zip(sources, places)):
        copies.append(pltpu.make_async_copy(source, place, semaphores.at[number]))
        copies[-1].start()
    return copies


PIECES = 1


def tables_kernel(dims, *refs):
    V, D, hl, ch, nh, ns, T, N = dims
    refs = list(refs)

    def take(number):
        taken, refs[:] = refs[:number], refs[number:]
        return taken

    sources = take(9)
    outproj_source, message = take(2)
    places = take(9)
    semaphores = take(1)[0]
    half = ch // 2
    top = top_rows(dims)
    core = lax.rem(lax.axis_index("seq"), 2)
    (inproj, tok, emb, prenorm, stepmap, bias, rates, skip, outnorm) = places
    size = inproj.shape[0] // PIECES
    pieces = [pl.ds(number * size, size) for number in range(PIECES)]
    rows = pl.ds(pl.multiple_of(core * half, 8), half)
    wide = [(place, pl.ds(place * ch, ch)) for place in range(D // ch)]
    copies = fetch(
        [sources[0].at[piece, :] for piece in pieces]
        + sources[1:]
        + [outproj_source.at[rows, columns] for _, columns in wide],
        [inproj.at[piece, :] for piece in pieces]
        + places[1:]
        + [message.at[pl.ds(top + place * half, half), :] for place, _ in wide],
        semaphores,
    )
    flip = (iota((T, 1), 0) + iota((1, T), 1) == T - 1).astype(f32).astype(bf16)
    for copy in copies[PIECES : PIECES + 8]:
        copy.wait()
    normed = split2(rms(emb[...]) * prenorm[...])
    raw_t = dot_split(split2(stepmap[...]), normed, NT)
    tokens = jnp.broadcast_to(tok[...].astype(f32), (8, T)).astype(bf16)
    tokens = dot(tokens, flip)
    for place in range(T // ch):
        message[2 * V + place : 2 * V + place + 1, :] = tokens[0:1, place * ch : (place + 1) * ch]
    row = 2 * V + T // ch
    message[row : row + 1, :] = outnorm[...]
    for head in range(hl):
        line = softplus(raw_t[head : head + 1, :] + bias[:, head : head + 1])
        row = row + 1
        message[row : row + 1, 0:V] = line
        message[row : row + 1, V : 2 * V] = -rates[:, head : head + 1] * line
        message[row : row + 1, 2 * V : 3 * V] = jnp.broadcast_to(skip[:, head : head + 1], (1, V))
    for copy in copies[:PIECES]:
        copy.wait()
    weights = jnp.concatenate(
        [inproj[pl.ds(0, D, stride=2), :], inproj[pl.ds(1, D, stride=2), :]], axis=1
    )
    both = dot_split(normed, split2(weights))
    message[0:V, :] = both[:, 0:ch]
    message[V : 2 * V, :] = both[:, ch:]
    for copy in copies[PIECES + 8 :]:
        copy.wait()


def top_rows(dims):
    V, D, hl, ch, nh, ns, T, N = dims
    return 2 * V + -(-(T // ch + 1 + hl) // 8) * 8


def head_line(dims, values):
    V, D, hl, ch, nh, ns, T, N = dims
    head_of = iota((1, ch), 1) // (ch // hl)
    line = jnp.zeros((1, ch), f32)
    for head in range(hl):
        line = jnp.where(head_of == head, values[:, head : head + 1], line)
    return line


def prepare_kernel(dims, *refs):
    V, D, hl, ch, nh, ns, T, N = dims
    H, P = nh * hl, ch // hl
    refs = list(refs)

    def take(number):
        taken, refs[:] = refs[:number], refs[number:]
        return taken

    sources = take(14)
    pairs, small, choose_out, own_high, own_low = take(5)
    state_high, state_low, rest_high, rest_low, out_high, out_low = take(6)
    triangles, upto, groups, blocks = take(4)
    places = take(14)
    semaphores = take(1)[0]
    copies = fetch(sources, places, semaphores)
    inproj2, statemap2, statemap, outproj, outproj2, emb, prenorm, complement = places[:8]
    prenorm2, stepmap2, bias2, rates2, skip2, outnorm2 = places[8:]
    row, column = iota((T, 1), 0), iota((1, T), 1)
    triangles[:, 0:T] = (row > column).astype(f32).astype(bf16)
    triangles[:, T : 2 * T] = (row < column).astype(f32).astype(bf16)
    triangles[:, 2 * T :] = jnp.ones((T, 128), bf16)
    upto[...] = (row >= column).astype(f32).astype(bf16)
    size = groups.shape[0]
    groups[...] = (iota((size, 1), 0) // P == iota((1, size), 1) // P).astype(f32).astype(bf16)
    rows, columns = blocks.shape
    blocks[...] = (iota((rows, 1), 0) // V == iota((1, columns), 1) // P).astype(f32).astype(bf16)
    for copy in copies:
        copy.wait()
    normed = split2(rms(emb[...]) * prenorm[...])
    write = dot_split(normed, split2(statemap[pl.ds(0, D, stride=2), :]))
    read = dot_split(normed, split2(statemap[pl.ds(1, D, stride=2), :]))
    pairs[...] = dot3(read, jnp.concatenate([write] * H, axis=0), NT)
    own_high[...], own_low[...] = split2(outproj[...])
    choose = (complement[...] == iota((D, 1), 0)).astype(f32).astype(bf16)
    choose_out[...] = choose
    gain = jnp.transpose(jnp.broadcast_to(prenorm2[...], (128, D)))

    def weights(values):
        return split2(dot_left_exact(choose, values))

    gain_wide = gain[:, 0:1]
    inner = inproj2[pl.ds(1, D, stride=2), :] * gain_wide
    step = jnp.transpose(
        jnp.concatenate(
            [jnp.broadcast_to(stepmap2[head : head + 1, :], (P, D)) for head in range(hl)], axis=0
        )
    )
    write2 = statemap2[pl.ds(0, D, stride=2), :] * gain_wide
    state_high[...], state_low[...] = weights(
        jnp.concatenate([inner, step * gain_wide, write2], axis=1)
    )
    gate = inproj2[pl.ds(0, D, stride=2), :] * gain_wide
    read2 = statemap2[pl.ds(1, D, stride=2), :] * gain_wide
    rest_high[...], rest_low[...] = weights(jnp.concatenate([gate, read2], axis=1))
    small[0:1, :] = head_line(dims, bias2)
    small[1:2, :] = head_line(dims, rates2)
    small[2:3, :] = head_line(dims, skip2)
    out_gain = jnp.transpose(jnp.broadcast_to(outnorm2[...], (128, ch)))
    out_high[...], out_low[...] = split2(outproj2[...] * out_gain[:, 0:1])


def shift_rows(value, amount, fill):
    size = value.shape[0]
    if amount % 8 == 0:
        empty = jnp.full((abs(amount),) + value.shape[1:], fill, value.dtype)
        if amount > 0:
            return jnp.concatenate([empty, value[: size - amount]], axis=0)
        return jnp.concatenate([value[-amount:], empty], axis=0)
    rolled = pltpu.roll(value, amount % size, 0)
    row = iota((8,) + value.shape[1:], 0)
    if amount > 0:
        edge = jnp.where(row >= amount, rolled[0:8], fill)
        return jnp.concatenate([edge, rolled[8:]], axis=0)
    edge = jnp.where(row < 8 + amount, rolled[size - 8 :], fill)
    return jnp.concatenate([rolled[: size - 8], edge], axis=0)


def scan_rows(decay, value, sign):
    size = value.shape[0]
    amount = 1
    while amount < size:
        value = value + decay * shift_rows(value, sign * amount, 0.0)
        decay = decay * shift_rows(decay, sign * amount, 1.0)
        amount *= 2
    return value, decay


def mix_kernel(dims, *refs):
    V, D, hl, ch, nh, ns, T, N = dims
    H, LV, P = nh * hl, nh * hl * V, ch // hl
    C = nh * ch
    refs = list(refs)

    def take(number):
        taken, refs[:] = refs[:number], refs[number:]
        return taken

    count = max(ns, nh)
    packets = dict(zip(in_turn(count)[::-1] + [0], take(count)))
    emb, pairs, triangles, groups, blocks = take(5)
    out_high, out_low, out_embedded = take(3)
    tokens = take(1)[0]
    mine = lax.axis_index("seq")

    for k in range(ns):
        block = ns - 1 - lax.bitwise_xor(mine, partners(ns, nh)[k][0])
        row = 2 * V
        pieces = [packets[k][row + place : row + place + 1, :] for place in range(T // ch)]
        tokens[pl.ds(block, 1), :] = jnp.concatenate(pieces, axis=1)

    first = 2 * V + T // ch + 1
    steps = jnp.concatenate(
        [packets[k][first : first + hl, 0 : 3 * V] for k in range(nh)], axis=0
    )
    log_t = steps[:, V : 2 * V]
    narrow = jnp.concatenate([part.astype(f32) for part in split3(steps)], axis=0).astype(bf16)
    spread_heads = (iota((1, LV), 1) // V == iota((3 * H, 1), 0) % H).astype(f32).astype(bf16)
    wide = dot(narrow, spread_heads, TN)
    own = iota((1, LV), 1) % V == iota((V, 1), 0)
    decay_table = jnp.exp(wide[V : 2 * V])
    step_table = jnp.where(own, wide[0:V], 0.0)
    gain_table = jnp.where(own, wide[2 * V : 3 * V], 0.0)
    gates = jnp.concatenate([packets[k][0:V, :] for k in range(nh)], axis=1)
    inners = jnp.concatenate([packets[k][V : 2 * V, :] for k in range(nh)], axis=1)
    gains = jnp.concatenate([packets[k][first - 1 : first, :] for k in range(nh)], axis=1)

    token_row = (iota((LV, 1), 0) % V).astype(f32)
    log_split = jnp.concatenate(split3(log_t), axis=1)
    onehots, logs = [], []
    for block in range(ns):
        onehot = (tokens[block : block + 1, :] == token_row).astype(f32).astype(bf16)
        onehots.append(onehot)
        logs.append(dot(log_split, onehot[0 : 3 * V, :]))
    logs = jnp.concatenate(logs, axis=0)
    size = ns * H
    sums = dot(jnp.concatenate(split3(logs)[::-1], axis=0), triangles[...])
    sums = (sums[0:size] + sums[size : 2 * size]) + sums[2 * size :]
    blocks_of = [sums[block * H : (block + 1) * H] for block in range(ns)]
    weight_up, weight_down = [None] * ns, [None] * ns
    gap = jnp.zeros((H, 128), f32)
    for block in reversed(range(ns)):
        wide = jnp.concatenate([gap] * (T // 128), axis=1)
        weight_up[block] = jnp.where(
            block < mine, jnp.exp(blocks_of[block][:, 0:T] + wide), 0.0
        )
        gap = jnp.where(block < mine, gap + blocks_of[block][:, 2 * T :], gap)
    gap = jnp.zeros((H, 128), f32)
    for block in range(ns):
        wide = jnp.concatenate([gap] * (T // 128), axis=1)
        weight_down[block] = jnp.where(
            block > mine, jnp.exp(blocks_of[block][:, T : 2 * T] + wide), 0.0
        )
        gap = jnp.where(block > mine, gap + blocks_of[block][:, 2 * T :], gap)
    entering = jnp.zeros((4 * H, LV), f32)
    for block in range(ns):
        both = jnp.concatenate([weight_up[block], weight_down[block]], axis=0)
        entering = entering + dot(
            jnp.concatenate(split2(both), axis=0), onehots[block], NT
        )
    entering = entering[2 * H :] + entering[0 : 2 * H]
    diagonal = iota((1, LV), 1) // V == iota((H, 1), 0)
    step_row = jnp.sum(step_table, axis=0, keepdims=True)
    enter_up = step_row * jnp.sum(
        jnp.where(diagonal, entering[0:H], 0.0), axis=0, keepdims=True
    )
    enter_down = step_row * jnp.sum(
        jnp.where(diagonal, entering[H : 2 * H], 0.0), axis=0, keepdims=True
    )

    looked = jnp.concatenate(
        [decay_table, step_table, pairs[...], gain_table, silu(gates), emb[...]], axis=1
    )
    looked = jnp.concatenate(split3(looked), axis=0)
    token = tokens[pl.ds(mine, 1), :]
    onehot = (token == token_row[0 : 3 * V]).astype(f32).astype(bf16)
    rows = dot(onehot, looked, TN)
    decay, step = rows[:, 0:LV], rows[:, LV : 2 * LV]
    pair, gain = rows[:, 2 * LV : 3 * LV], rows[:, 3 * LV : 4 * LV]
    silu_rows = rows[:, 4 * LV : 4 * LV + C]
    out_embedded[...] = rows[:, 4 * LV + C :]

    up, fade = scan_rows(decay, step, 1)
    up = up + fade * enter_up
    down, fade = scan_rows(decay, step, -1)
    down = down + fade * enter_down

    spread_high, spread_low = [
        jnp.concatenate([part] * H, axis=0) * blocks[...] for part in split2(inners)
    ]
    both = jnp.concatenate([up * pair + gain, down * pair + gain], axis=0)
    high = both.astype(bf16)
    high_wide = high.astype(f32)
    low_turned = pltpu.roll(both - high_wide, LV // 2, 1)
    lower = iota((1, LV), 1) < LV // 2
    value = []
    for side in (0, 1):
        mixed = jnp.where(lower == (side == 0), high_wide, low_turned).astype(bf16)
        rows = slice(side * LV // 2, (side + 1) * LV // 2)
        columns = slice(side * C // 2, (side + 1) * C // 2)
        weight, rest = spread_high[rows, columns], spread_low[:, columns]
        value.append(
            dot(
                jnp.concatenate([mixed, high], axis=1),
                jnp.concatenate([weight, weight, rest], axis=0),
            )
        )
    value = jnp.concatenate(value, axis=1)
    value = value * jnp.concatenate([silu_rows, silu_rows], axis=0)
    wide = groups.shape[0]
    high, low = split2(value * value)
    starts = list(range(0, C, wide))
    rows = 2 * T
    stacked = [half[:, start : start + wide] for start in starts for half in (low, high)]
    squares = dot(jnp.concatenate(stacked, axis=0), groups[...])
    for number, start in enumerate(starts):
        place = 2 * number * rows
        square = squares[place : place + rows] + squares[place + rows : place + 2 * rows]
        stop = start + wide
        normed = value[:, start:stop] * lax.rsqrt(square * (1.0 / P) + epsilon)
        out_high[:, start:stop], out_low[:, start:stop] = split2(
            (normed[0:T] + normed[T : 2 * T]) * gains[:, start:stop]
        )


def project_kernel(dims, *refs):
    V, D, hl, ch, nh, ns, T, N = dims
    P = ch // hl
    refs = list(refs)

    def take(number):
        taken, refs[:] = refs[:number], refs[number:]
        return taken

    high, low, embedded, small, own_high, own_low, state_high, state_low, upto = take(9)
    order = in_turn(nh)[::-1]
    nears = dict(zip(order, take(nh - 1)))
    others = dict(zip(order, take(nh - 1)))
    out_state, out_high, out_low, out_scale = take(4)
    out_write, out_inner, out_stepped, out_total = take(4)
    half = ch // 2
    base = top_rows(dims)
    mine = lax.axis_index("seq")

    pieces = []
    for k in range(1, nh):
        near, other = [
            jnp.concatenate(
                [
                    ref[base + place * half : base + (place + 1) * half, :]
                    for place in range(D // ch)
                ],
                axis=1,
            )
            for ref in (nears[k], others[k])
        ]
        even = lax.rem(lax.bitwise_xor(mine, partners(ns, nh)[k][0]), 2) == 0
        pieces.append(jnp.where(even, near, other))
        pieces.append(jnp.where(even, other, near))
    weights = split2(jnp.concatenate(pieces, axis=0))
    weights = (
        jnp.concatenate([own_high[...], weights[0]], axis=0),
        jnp.concatenate([own_low[...], weights[1]], axis=0),
    )
    hidden = embedded[...] + dot_split((high[...], low[...]), weights)
    split = split2(hidden)
    out_high[...], out_low[...] = split
    scale = lax.rsqrt(jnp.mean(hidden * hidden, axis=-1, keepdims=True) + epsilon)
    out_scale[...] = jnp.broadcast_to(scale, (T, ch))

    rows = dot_split(split, (state_high[...], state_low[...])) * scale
    inner, write = rows[:, 0:ch], rows[:, 2 * ch :]
    step = softplus(rows[:, ch : 2 * ch] + small[0:1, :])
    stepped = inner * step
    log_high, log_middle, log_low = split3(-small[1:2, :] * step)
    total = dot(upto[...], jnp.concatenate([log_low, log_middle], axis=1))
    total = (total[:, 0:ch] + total[:, ch:]) + dot(upto[...], log_high)
    end = total[T - 1 : T, :]
    state = dot3(stepped * jnp.exp(end - total), write, TN)
    out_state[0:ch, :] = state
    for head in range(hl):
        out_state[ch + head : ch + head + 1, :] = jnp.broadcast_to(
            end[:, head * P : head * P + 1], (1, N)
        )
    out_write[...] = write
    out_inner[...] = inner
    out_stepped[...] = stepped
    out_total[...] = total


def block_kernel(dims, *refs):
    V, D, hl, ch, nh, ns, T, N = dims
    P = ch // hl
    refs = list(refs)

    def take(number):
        taken, refs[:] = refs[:number], refs[number:]
        return taken

    high, low, scale, write, inner, stepped, total, choose = take(8)
    rest_high, rest_low, small = take(3)
    base, read_high, read_low, out_fade, out_gate, own, hidden_ref = take(7)
    rows = dot_split((high[...], low[...]), (rest_high[...], rest_low[...]))
    out_gate[...] = silu(rows[:, 0:ch] * scale[...])
    read = rows[:, ch:] * scale[...]
    read = split2(read)
    read_high[...], read_low[...] = read
    out_fade[...] = jnp.exp(total[...])
    products = dot_split(read, split2(write[...]), NT)
    stepped_high, stepped_low = split2(stepped[...])
    select = (iota((8, ch), 1) == iota((8, ch), 0) * P).astype(f32).astype(bf16)
    total_high, total_middle, total_low = split3(total[...])
    total_t = (dot(select, total_low, NT) + dot(select, total_middle, NT)) + dot(
        select, total_high, NT
    )
    allowed = iota((T, 1), 0) >= iota((1, T), 1)
    parts = []
    for head in range(hl):
        start, stop = head * P, (head + 1) * P
        differ = total[:, start : start + 1] - total_t[head : head + 1, :]
        weights = jnp.where(allowed, jnp.exp(jnp.where(allowed, differ, 0.0)), 0.0) * products
        part = dot_split(
            split2(weights), (stepped_high[:, start:stop], stepped_low[:, start:stop])
        )
        parts.append(part + small[2:3, start:stop] * inner[:, start:stop])
    base[...] = jnp.concatenate(parts, axis=1)
    share = T // nh
    hidden_ref[...] = high[...].astype(f32) + low[...].astype(f32)
    place = pl.multiple_of(lax.axis_index("head") * share, 8)
    own[...] = dot_right_exact(hidden_ref[pl.ds(place, share), :], choose[...])


def state_rows(dims, values):
    V, D, hl, ch, nh, ns, T, N = dims
    head_of = iota((ch, N), 0) // (ch // hl)
    result = jnp.broadcast_to(values[0:1, :], (ch, N))
    for head in range(1, hl):
        result = jnp.where(head_of == head, values[head : head + 1, :], result)
    return result


def join_kernel(dims, bit, total, prefix, came, out_total, out_prefix):
    V, D, hl, ch, nh, ns, T, N = dims
    later = lax.rem(lax.div(lax.axis_index("seq"), 2**bit), 2) == 1
    came_state, came_log = came[0:ch, :], came[ch : ch + hl, :]
    state, log = total[0:ch, :], total[ch : ch + hl, :]
    factor = jnp.exp(state_rows(dims, jnp.where(later, log, came_log)))
    out_total[0:ch, :] = jnp.where(
        later, factor * came_state + state, factor * state + came_state
    )
    out_total[ch : ch + hl, :] = log + came_log
    if prefix is None:
        out_prefix[0:ch, :] = jnp.where(later, came_state, 0.0)
        out_prefix[ch : ch + hl, :] = jnp.where(later, came_log, 0.0)
    else:
        joined = prefix_joined(dims, bit, prefix, came)
        out_prefix[0:ch, :] = joined
        out_prefix[ch : ch + hl, :] = prefix[ch : ch + hl, :] + jnp.where(later, came_log, 0.0)


def prefix_joined(dims, bit, prefix, came):
    V, D, hl, ch, nh, ns, T, N = dims
    later = lax.rem(lax.div(lax.axis_index("seq"), 2**bit), 2) == 1
    factor = jnp.exp(state_rows(dims, prefix[ch : ch + hl, :]))
    return prefix[0:ch, :] + jnp.where(later, factor * came[0:ch, :], 0.0)


def output_kernel(dims, bit, *refs):
    V, D, hl, ch, nh, ns, T, N = dims
    P = ch // hl
    prefix, came, read_high, read_low, base, fade, gate, own, proj_high, proj_low = refs[:10]
    groups, outs, partial_ref = refs[10], refs[11 : 11 + nh], refs[11 + nh]
    entering = prefix_joined(dims, bit, prefix, came)
    carried = dot_split((read_high[...], read_low[...]), split2(entering), NT)
    value = (base[...] + carried * fade[...]) * gate[...]
    square = dot(jnp.concatenate(split2(value * value), axis=0), groups[0:ch, 0:ch])
    square = square[T:] + square[0:T]
    value = value * lax.rsqrt(square * (1.0 / P) + epsilon)
    share = T // nh
    partial_ref[...] = dot_split(split2(value), (proj_high[...], proj_low[...]))
    mine = lax.axis_index("head")
    for k in range(nh):
        place = pl.multiple_of(lax.bitwise_xor(mine, k) * share, 8)
        part = partial_ref[pl.ds(place, share), :]
        outs[k][...] = part + own[...] if k == 0 else part


QUARTERS = 4


def finish_kernel(dims, *refs):
    V, D, hl, ch, nh, ns, T, N = dims
    parts, (out, total, semaphores) = refs[:nh][::-1], refs[nh:]
    size = out.shape[0] // QUARTERS
    copies = []
    for quarter in range(QUARTERS):
        rows = pl.ds(quarter * size, size)
        value = parts[0][rows, :]
        for part in parts[1:]:
            value = value + part[rows, :]
        total[rows, :] = value
        copies.append(
            pltpu.make_async_copy(total.at[rows, :], out.at[rows, :], semaphores.at[quarter])
        )
        copies[-1].start()
    for copy in copies:
        copy.wait()


def per_device(
    token_ids,
    embedding,
    complement,
    prenorm_first,
    inproj_first,
    statemap_first,
    stepmap_first,
    stepbias_first,
    rates_first,
    skipgain_first,
    outnorm_first,
    outproj_first,
    prenorm_second,
    inproj_second,
    statemap_second,
    stepmap_second,
    stepbias_second,
    rates_second,
    skipgain_second,
    outnorm_second,
    outproj_second,
):
    nh, ns = lax.axis_size("head"), lax.axis_size("seq")
    V, D = embedding.shape
    ch = inproj_first.shape[2]
    hl = stepmap_first.shape[1]
    N = statemap_first.shape[2]
    T = token_ids.shape[0]
    LV = nh * hl * V
    dims = (V, D, hl, ch, nh, ns, T, N)
    vmem = pl.BlockSpec(memory_space=pltpu.VMEM)
    anywhere = pl.BlockSpec(memory_space=pl.ANY)
    params = pltpu.CompilerParams(vmem_limit_bytes=LIMIT)

    def shape(*sizes, dtype=f32):
        return jax.ShapeDtypeStruct(sizes, dtype)

    def halves(*sizes):
        return [shape(*sizes, dtype=bf16)] * 2

    def room(value):
        return pltpu.VMEM(value.shape, value.dtype)

    def kept(values):
        return [pltpu.with_memory_space_constraint(value, pltpu.HBM) for value in values]

    def line(value):
        return value.reshape(1, -1)

    def flat(value):
        return value.reshape(-1, value.shape[-1])

    heavy = pl.CostEstimate(flops=960 * T * D * D, bytes_accessed=4 * T * D, transcendentals=T * D)

    half = ch // 2
    share = T // nh
    fetched = [
        flat(inproj_first),
        line(token_ids),
        embedding,
        line(prenorm_first),
        stepmap_first.T,
        line(stepbias_first),
        line(rates_first),
        line(skipgain_first),
        line(outnorm_first),
    ]
    message = pl.pallas_call(
        functools.partial(tables_kernel, dims),
        out_shape=pltpu.VMEM((top_rows(dims) + half * (D // ch), ch), f32),
        in_specs=[anywhere] * (len(fetched) + 1),
        out_specs=vmem,
        scratch_shapes=[room(value) for value in fetched]
        + [pltpu.SemaphoreType.DMA((len(fetched) - 1 + PIECES + D // ch,))],
        compiler_params=params,
        name="tables",
    )(*kept([*fetched, outproj_first]))

    prepared = [
        flat(inproj_second),
        flat(statemap_second),
        flat(statemap_first),
        outproj_first,
        outproj_second,
        embedding,
        line(prenorm_first),
        line(complement),
        line(prenorm_second),
        stepmap_second.T,
        line(stepbias_second),
        line(rates_second),
        line(skipgain_second),
        line(outnorm_second),
    ]
    (
        pair_table,
        small,
        choose,
        own_high,
        own_low,
        state_high,
        state_low,
        rest_high,
        rest_low,
        proj_high,
        proj_low,
        triangles,
        upto,
        groups,
        blocks,
    ) = pl.pallas_call(
        functools.partial(prepare_kernel, dims),
        out_shape=(
            shape(V, LV),
            shape(8, ch),
            shape(D, D, dtype=bf16),
            *halves(ch, D),
            *halves(D, 2 * ch + N),
            *halves(D, ch + N),
            *halves(ch, D),
            shape(T, 2 * T + 128, dtype=bf16),
            shape(T, T, dtype=bf16),
            shape(2 * ch, 2 * ch, dtype=bf16),
            shape(LV, nh * ch, dtype=bf16),
        ),
        in_specs=[anywhere] * len(prepared),
        out_specs=(vmem,) * 15,
        scratch_shapes=[room(value) for value in prepared]
        + [pltpu.SemaphoreType.DMA((len(prepared),))],
        compiler_params=params,
        cost_estimate=heavy,
        name="prepare",
    )(*kept(prepared))

    count = max(ns, nh)
    messages = {0: message}
    for k in in_turn(count):
        seq_bits, head_bits = partners(ns, nh)[k]
        pairs = [
            (seq * nh + head, (seq ^ seq_bits) * nh + (head ^ head_bits))
            for seq in range(ns)
            for head in range(nh)
        ]
        sent = message if k < nh else message[0 : top_rows(dims)]
        messages[k] = lax.ppermute(sent, ("seq", "head"), pairs)
    swap = [(seq, seq ^ 1) for seq in range(ns)]
    order = in_turn(nh)[::-1]
    others = [lax.ppermute(messages[k], "seq", swap) for k in order]

    mixed_high, mixed_low, embedded = pl.pallas_call(
        functools.partial(mix_kernel, dims),
        out_shape=(*halves(T, nh * ch), shape(T, D)),
        in_specs=[vmem] * (count + 5),
        out_specs=(vmem,) * 3,
        scratch_shapes=[pltpu.VMEM((max(ns, 8), T), f32)],
        compiler_params=params,
        cost_estimate=heavy,
        name="mix",
    )(
        *[messages[k] for k in in_turn(count)[::-1] + [0]],
        embedding,
        pair_table,
        triangles,
        groups,
        blocks,
    )

    state, hidden_high, hidden_low, scale, write, inner, stepped, total = pl.pallas_call(
        functools.partial(project_kernel, dims),
        out_shape=(
            shape(ch + 8, N),
            *halves(T, D),
            shape(T, ch),
            shape(T, N),
            shape(T, ch),
            shape(T, ch),
            shape(T, ch),
        ),
        in_specs=[vmem] * (9 + 2 * (nh - 1)),
        out_specs=(vmem,) * 8,
        compiler_params=params,
        name="project",
    )(
        mixed_high,
        mixed_low,
        embedded,
        small,
        own_high,
        own_low,
        state_high,
        state_low,
        upto,
        *[messages[k] for k in order],
        *others,
    )

    base, read_high, read_low, fade, gate, own = pl.pallas_call(
        functools.partial(block_kernel, dims),
        out_shape=(
            shape(T, ch),
            *halves(T, N),
            shape(T, ch),
            shape(T, ch),
            shape(share, D),
        ),
        in_specs=[vmem] * 11,
        out_specs=(vmem,) * 6,
        scratch_shapes=[pltpu.VMEM((T, D), f32)],
        compiler_params=params,
        cost_estimate=heavy,
        name="block",
    )(
        hidden_high,
        hidden_low,
        scale,
        write,
        inner,
        stepped,
        total,
        choose,
        rest_high,
        rest_low,
        small,
    )

    prefix = None
    bits = ns.bit_length() - 1
    for bit in range(bits):
        came = lax.ppermute(state, "seq", [(seq, seq ^ 2**bit) for seq in range(ns)])
        if bit == bits - 1:
            break
        given = [state] + ([] if prefix is None else [prefix]) + [came]

        def join(bit, known, *refs):
            if known:
                join_kernel(dims, bit, *refs)
            else:
                join_kernel(dims, bit, refs[0], None, *refs[1:])

        state, prefix = pl.pallas_call(
            functools.partial(join, bit, prefix is not None),
            out_shape=(shape(ch + 8, N),) * 2,
            in_specs=[vmem] * len(given),
            out_specs=(vmem,) * 2,
            compiler_params=params,
            name="join",
        )(*given)
    if prefix is None:
        prefix = jnp.zeros_like(state)

    parts = pl.pallas_call(
        functools.partial(output_kernel, dims, bits - 1),
        out_shape=(shape(share, D),) * nh,
        in_specs=[vmem] * 11,
        out_specs=(vmem,) * nh,
        scratch_shapes=[pltpu.VMEM((T, D), f32)],
        compiler_params=params,
        name="output",
    )(
        prefix,
        came,
        read_high,
        read_low,
        base,
        fade,
        gate,
        own,
        proj_high,
        proj_low,
        groups,
    )
    arrived = [
        lax.ppermute(parts[k], "head", [(source, source ^ k) for source in range(nh)])
        for k in in_turn(nh)
    ]
    return pl.pallas_call(
        functools.partial(finish_kernel, dims),
        out_shape=shape(share, D),
        in_specs=[vmem] * nh,
        out_specs=anywhere,
        scratch_shapes=[pltpu.VMEM((share, D), f32), pltpu.SemaphoreType.DMA((QUARTERS,))],
        compiler_params=params,
        name="finish",
    )(*arrived, parts[0])


def solution(mesh):
    return jax.shard_map(
        per_device,
        mesh=mesh,
        in_specs=(
            P(("rep", "seq")),
            P(),
            P(),
            P(),
            P(None, None, "head"),
            P(),
            P(None, "head"),
            P("head"),
            P("head"),
            P("head"),
            P("head"),
            P("head", None),
            P(),
            P(None, None, "head"),
            P(),
            P(None, "head"),
            P("head"),
            P("head"),
            P("head"),
            P("head"),
            P("head", None),
        ),
        out_specs=P(("rep", "seq", "head"), None),
        check_vma=False,
    )
```

```python
import functools

import jax
import jax.numpy as jnp
from jax import lax
from jax.experimental import pallas as pl
from jax.experimental.pallas import tpu as pltpu
from jax.sharding import PartitionSpec as P

epsilon = 1e-05
f32 = jnp.float32
bf16 = jnp.bfloat16
LIMIT = 48 * 1024 * 1024

MM = (((1,), (0,)), ((), ()))
NT = (((1,), (1,)), ((), ()))
TN = (((0,), (0,)), ((), ()))


def partners(ns, nh):
    count = max(ns, nh)
    return [
        (k % (ns - 1) + 1 if 0 < k < ns else 0, k if k < nh else 0) for k in range(count)
    ]


def in_turn(count):
    return list(range(1, count))[::-1]


def iota(shape, axis):
    return lax.broadcasted_iota(jnp.int32, shape, axis)


def split2(value):
    high = value.astype(bf16)
    return high, (value - high.astype(f32)).astype(bf16)


def split3(value):
    high = value.astype(bf16)
    rest = value - high.astype(f32)
    middle = rest.astype(bf16)
    return high, middle, (rest - middle.astype(f32)).astype(bf16)


def dot(left, right, dims=MM):
    return lax.dot_general(left, right, dims, preferred_element_type=f32)


def dot_split(left, right, dims=MM):
    axis = 1 if dims == TN else 0
    size = left[0].shape[axis]
    if size % 16:
        return (dot(left[0], right[1], dims) + dot(left[1], right[0], dims)) + dot(
            left[0], right[0], dims
        )
    both = dot(jnp.concatenate([left[1], left[0]], axis=axis), right[0], dims)
    return (dot(left[0], right[1], dims) + both[0:size]) + both[size:]


def dot3(left, right, dims=MM):
    return dot_split(split2(left), split2(right), dims)


def dot_left_exact(left, right, dims=MM):
    high, middle, low = split3(right)
    return (dot(left, low, dims) + dot(left, middle, dims)) + dot(left, high, dims)


def dot_right_exact(left, right, dims=MM):
    high, middle, low = split3(left)
    return (dot(low, right, dims) + dot(middle, right, dims)) + dot(high, right, dims)


def softplus(value):
    return jnp.maximum(value, 0.0) + jnp.log1p(jnp.exp(-jnp.abs(value)))


def silu(value):
    return value / (1.0 + jnp.exp(-value))


def rms(value):
    return value * lax.rsqrt(jnp.mean(value * value, axis=-1, keepdims=True) + epsilon)


def fetch(sources, places, semaphores):
    copies = []
    for number, (source, place) in enumerate(zip(sources, places)):
        copies.append(pltpu.make_async_copy(source, place, semaphores.at[number]))
        copies[-1].start()
    return copies


def fetch(sources, places, semaphores):
    copies = []
    for number, (source, place) in enumerate(zip(sources, places)):
        copies.append(pltpu.make_async_copy(source, place, semaphores.at[number]))
        copies[-1].start()
    return copies


PIECES = 1


def tables_kernel(dims, *refs):
    V, D, hl, ch, nh, ns, T, N = dims
    refs = list(refs)

    def take(number):
        taken, refs[:] = refs[:number], refs[number:]
        return taken

    sources = take(9)
    outproj_source, message = take(2)
    places = take(9)
    semaphores = take(1)[0]
    half = ch // 2
    top = top_rows(dims)
    core = lax.rem(lax.axis_index("seq"), 2)
    (inproj, tok, emb, prenorm, stepmap, bias, rates, skip, outnorm) = places
    size = inproj.shape[0] // PIECES
    pieces = [pl.ds(number * size, size) for number in range(PIECES)]
    rows = pl.ds(pl.multiple_of(core * half, 8), half)
    wide = [(place, pl.ds(place * ch, ch)) for place in range(D // ch)]
    copies = fetch(
        [sources[0].at[piece, :] for piece in pieces]
        + sources[1:]
        + [outproj_source.at[rows, columns] for _, columns in wide],
        [inproj.at[piece, :] for piece in pieces]
        + places[1:]
        + [message.at[pl.ds(top + place * half, half), :] for place, _ in wide],
        semaphores,
    )
    flip = (iota((T, 1), 0) + iota((1, T), 1) == T - 1).astype(f32).astype(bf16)
    for copy in copies[PIECES : PIECES + 8]:
        copy.wait()
    normed = split2(rms(emb[...]) * prenorm[...])
    raw_t = dot_split(split2(stepmap[...]), normed, NT)
    tokens = jnp.broadcast_to(tok[...].astype(f32), (8, T)).astype(bf16)
    tokens = dot(tokens, flip)
    for place in range(T // ch):
        message[2 * V + place : 2 * V + place + 1, :] = tokens[0:1, place * ch : (place + 1) * ch]
    row = 2 * V + T // ch
    message[row : row + 1, :] = outnorm[...]
    for head in range(hl):
        line = softplus(raw_t[head : head + 1, :] + bias[:, head : head + 1])
        row = row + 1
        message[row : row + 1, 0:V] = line
        message[row : row + 1, V : 2 * V] = -rates[:, head : head + 1] * line
        message[row : row + 1, 2 * V : 3 * V] = jnp.broadcast_to(skip[:, head : head + 1], (1, V))
    for copy in copies[:PIECES]:
        copy.wait()
    weights = jnp.concatenate(
        [inproj[pl.ds(0, D, stride=2), :], inproj[pl.ds(1, D, stride=2), :]], axis=1
    )
    both = dot_split(normed, split2(weights))
    message[0:V, :] = both[:, 0:ch]
    message[V : 2 * V, :] = both[:, ch:]
    for copy in copies[PIECES + 8 :]:
        copy.wait()


def top_rows(dims):
    V, D, hl, ch, nh, ns, T, N = dims
    return 2 * V + -(-(T // ch + 1 + hl) // 8) * 8


def head_line(dims, values):
    V, D, hl, ch, nh, ns, T, N = dims
    head_of = iota((1, ch), 1) // (ch // hl)
    line = jnp.zeros((1, ch), f32)
    for head in range(hl):
        line = jnp.where(head_of == head, values[:, head : head + 1], line)
    return line


def prepare_kernel(dims, *refs):
    V, D, hl, ch, nh, ns, T, N = dims
    H, P = nh * hl, ch // hl
    refs = list(refs)

    def take(number):
        taken, refs[:] = refs[:number], refs[number:]
        return taken

    sources = take(14)
    pairs, small, choose_out, own_high, own_low = take(5)
    state_high, state_low, rest_high, rest_low, out_high, out_low = take(6)
    triangles, upto, groups, blocks = take(4)
    places = take(14)
    semaphores = take(1)[0]
    copies = fetch(sources, places, semaphores)
    inproj2, statemap2, statemap, outproj, outproj2, emb, prenorm, complement = places[:8]
    prenorm2, stepmap2, bias2, rates2, skip2, outnorm2 = places[8:]
    row, column = iota((T, 1), 0), iota((1, T), 1)
    triangles[:, 0:T] = (row > column).astype(f32).astype(bf16)
    triangles[:, T : 2 * T] = (row < column).astype(f32).astype(bf16)
    triangles[:, 2 * T :] = jnp.ones((T, 128), bf16)
    upto[...] = (row >= column).astype(f32).astype(bf16)
    size = groups.shape[0]
    groups[...] = (iota((size, 1), 0) // P == iota((1, size), 1) // P).astype(f32).astype(bf16)
    rows, columns = blocks.shape
    blocks[...] = (iota((rows, 1), 0) // V == iota((1, columns), 1) // P).astype(f32).astype(bf16)
    for copy in copies:
        copy.wait()
    normed = split2(rms(emb[...]) * prenorm[...])
    write = dot_split(normed, split2(statemap[pl.ds(0, D, stride=2), :]))
    read = dot_split(normed, split2(statemap[pl.ds(1, D, stride=2), :]))
    pairs[...] = dot3(read, jnp.concatenate([write] * H, axis=0), NT)
    own_high[...], own_low[...] = split2(outproj[...])
    choose = (complement[...] == iota((D, 1), 0)).astype(f32).astype(bf16)
    choose_out[...] = choose
    gain = jnp.transpose(jnp.broadcast_to(prenorm2[...], (128, D)))

    def weights(values):
        return split2(dot_left_exact(choose, values))

    gain_wide = gain[:, 0:1]
    inner = inproj2[pl.ds(1, D, stride=2), :] * gain_wide
    step = jnp.transpose(
        jnp.concatenate(
            [jnp.broadcast_to(stepmap2[head : head + 1, :], (P, D)) for head in range(hl)], axis=0
        )
    )
    write2 = statemap2[pl.ds(0, D, stride=2), :] * gain_wide
    state_high[...], state_low[...] = weights(
        jnp.concatenate([inner, step * gain_wide, write2], axis=1)
    )
    gate = inproj2[pl.ds(0, D, stride=2), :] * gain_wide
    read2 = statemap2[pl.ds(1, D, stride=2), :] * gain_wide
    rest_high[...], rest_low[...] = weights(jnp.concatenate([gate, read2], axis=1))
    small[0:1, :] = head_line(dims, bias2)
    small[1:2, :] = head_line(dims, rates2)
    small[2:3, :] = head_line(dims, skip2)
    out_gain = jnp.transpose(jnp.broadcast_to(outnorm2[...], (128, ch)))
    out_high[...], out_low[...] = split2(outproj2[...] * out_gain[:, 0:1])


def shift_rows(value, amount, fill):
    size = value.shape[0]
    if amount % 8 == 0:
        empty = jnp.full((abs(amount),) + value.shape[1:], fill, value.dtype)
        if amount > 0:
            return jnp.concatenate([empty, value[: size - amount]], axis=0)
        return jnp.concatenate([value[-amount:], empty], axis=0)
    rolled = pltpu.roll(value, amount % size, 0)
    row = iota((8,) + value.shape[1:], 0)
    if amount > 0:
        edge = jnp.where(row >= amount, rolled[0:8], fill)
        return jnp.concatenate([edge, rolled[8:]], axis=0)
    edge = jnp.where(row < 8 + amount, rolled[size - 8 :], fill)
    return jnp.concatenate([rolled[: size - 8], edge], axis=0)


def scan_rows(decay, value, sign):
    size = value.shape[0]
    amount = 1
    while amount < size:
        value = value + decay * shift_rows(value, sign * amount, 0.0)
        decay = decay * shift_rows(decay, sign * amount, 1.0)
        amount *= 2
    return value, decay


def mix_kernel(dims, *refs):
    V, D, hl, ch, nh, ns, T, N = dims
    H, LV, P = nh * hl, nh * hl * V, ch // hl
    C = nh * ch
    refs = list(refs)

    def take(number):
        taken, refs[:] = refs[:number], refs[number:]
        return taken

    count = max(ns, nh)
    packets = dict(zip(in_turn(count)[::-1] + [0], take(count)))
    emb, pairs, triangles, groups, blocks = take(5)
    out_high, out_low, out_embedded = take(3)
    tokens = take(1)[0]
    mine = lax.axis_index("seq")

    for k in range(ns):
        block = ns - 1 - lax.bitwise_xor(mine, partners(ns, nh)[k][0])
        row = 2 * V
        pieces = [packets[k][row + place : row + place + 1, :] for place in range(T // ch)]
        tokens[pl.ds(block, 1), :] = jnp.concatenate(pieces, axis=1)

    first = 2 * V + T // ch + 1
    steps = jnp.concatenate(
        [packets[k][first : first + hl, 0 : 3 * V] for k in range(nh)], axis=0
    )
    log_t = steps[:, V : 2 * V]
    narrow = jnp.concatenate([part.astype(f32) for part in split3(steps)], axis=0).astype(bf16)
    spread_heads = (iota((1, LV), 1) // V == iota((3 * H, 1), 0) % H).astype(f32).astype(bf16)
    wide = dot(narrow, spread_heads, TN)
    own = iota((1, LV), 1) % V == iota((V, 1), 0)
    decay_table = jnp.exp(wide[V : 2 * V])
    step_table = jnp.where(own, wide[0:V], 0.0)
    gain_table = jnp.where(own, wide[2 * V : 3 * V], 0.0)
    gates = jnp.concatenate([packets[k][0:V, :] for k in range(nh)], axis=1)
    inners = jnp.concatenate([packets[k][V : 2 * V, :] for k in range(nh)], axis=1)
    gains = jnp.concatenate([packets[k][first - 1 : first, :] for k in range(nh)], axis=1)

    token_row = (iota((LV, 1), 0) % V).astype(f32)
    log_split = jnp.concatenate(split3(log_t), axis=1)
    onehots, logs = [], []
    for block in range(ns):
        onehot = (tokens[block : block + 1, :] == token_row).astype(f32).astype(bf16)
        onehots.append(onehot)
        logs.append(dot(log_split, onehot[0 : 3 * V, :]))
    logs = jnp.concatenate(logs, axis=0)
    size = ns * H
    sums = dot(jnp.concatenate(split3(logs)[::-1], axis=0), triangles[...])
    sums = (sums[0:size] + sums[size : 2 * size]) + sums[2 * size :]
    blocks_of = [sums[block * H : (block + 1) * H] for block in range(ns)]
    weight_up, weight_down = [None] * ns, [None] * ns
    gap = jnp.zeros((H, 128), f32)
    for block in reversed(range(ns)):
        wide = jnp.concatenate([gap] * (T // 128), axis=1)
        weight_up[block] = jnp.where(
            block < mine, jnp.exp(blocks_of[block][:, 0:T] + wide), 0.0
        )
        gap = jnp.where(block < mine, gap + blocks_of[block][:, 2 * T :], gap)
    gap = jnp.zeros((H, 128), f32)
    for block in range(ns):
        wide = jnp.concatenate([gap] * (T // 128), axis=1)
        weight_down[block] = jnp.where(
            block > mine, jnp.exp(blocks_of[block][:, T : 2 * T] + wide), 0.0
        )
        gap = jnp.where(block > mine, gap + blocks_of[block][:, 2 * T :], gap)
    entering = jnp.zeros((4 * H, LV), f32)
    for block in range(ns):
        both = jnp.concatenate([weight_up[block], weight_down[block]], axis=0)
        entering = entering + dot(
            jnp.concatenate(split2(both), axis=0), onehots[block], NT
        )
    entering = entering[2 * H :] + entering[0 : 2 * H]
    diagonal = iota((1, LV), 1) // V == iota((H, 1), 0)
    step_row = jnp.sum(step_table, axis=0, keepdims=True)
    enter_up = step_row * jnp.sum(
        jnp.where(diagonal, entering[0:H], 0.0), axis=0, keepdims=True
    )
    enter_down = step_row * jnp.sum(
        jnp.where(diagonal, entering[H : 2 * H], 0.0), axis=0, keepdims=True
    )

    looked = jnp.concatenate(
        [decay_table, step_table, pairs[...], gain_table, silu(gates), emb[...]], axis=1
    )
    looked = jnp.concatenate(split3(looked), axis=0)
    token = tokens[pl.ds(mine, 1), :]
    onehot = (token == token_row[0 : 3 * V]).astype(f32).astype(bf16)
    rows = dot(onehot, looked, TN)
    decay, step = rows[:, 0:LV], rows[:, LV : 2 * LV]
    pair, gain = rows[:, 2 * LV : 3 * LV], rows[:, 3 * LV : 4 * LV]
    silu_rows = rows[:, 4 * LV : 4 * LV + C]
    out_embedded[...] = rows[:, 4 * LV + C :]

    up, fade = scan_rows(decay, step, 1)
    up = up + fade * enter_up
    down, fade = scan_rows(decay, step, -1)
    down = down + fade * enter_down

    spread_high, spread_low = [
        jnp.concatenate([part] * H, axis=0) * blocks[...] for part in split2(inners)
    ]
    both = jnp.concatenate([up * pair + gain, down * pair + gain], axis=0)
    high = both.astype(bf16)
    high_wide = high.astype(f32)
    low_turned = pltpu.roll(both - high_wide, LV // 2, 1)
    lower = iota((1, LV), 1) < LV // 2
    value = []
    for side in (0, 1):
        mixed = jnp.where(lower == (side == 0), high_wide, low_turned).astype(bf16)
        rows = slice(side * LV // 2, (side + 1) * LV // 2)
        columns = slice(side * C // 2, (side + 1) * C // 2)
        weight, rest = spread_high[rows, columns], spread_low[:, columns]
        value.append(
            dot(
                jnp.concatenate([mixed, high], axis=1),
                jnp.concatenate([weight, weight, rest], axis=0),
            )
        )
    value = jnp.concatenate(value, axis=1)
    value = value * jnp.concatenate([silu_rows, silu_rows], axis=0)
    wide = groups.shape[0]
    high, low = split2(value * value)
    starts = list(range(0, C, wide))
    rows = 2 * T
    stacked = [half[:, start : start + wide] for start in starts for half in (low, high)]
    squares = dot(jnp.concatenate(stacked, axis=0), groups[...])
    for number, start in enumerate(starts):
        place = 2 * number * rows
        square = squares[place : place + rows] + squares[place + rows : place + 2 * rows]
        stop = start + wide
        normed = value[:, start:stop] * lax.rsqrt(square * (1.0 / P) + epsilon)
        out_high[:, start:stop], out_low[:, start:stop] = split2(
            (normed[0:T] + normed[T : 2 * T]) * gains[:, start:stop]
        )


def project_kernel(dims, *refs):
    V, D, hl, ch, nh, ns, T, N = dims
    P = ch // hl
    refs = list(refs)

    def take(number):
        taken, refs[:] = refs[:number], refs[number:]
        return taken

    high, low, embedded, small, own_high, own_low, state_high, state_low, upto = take(9)
    order = in_turn(nh)[::-1]
    nears = dict(zip(order, take(nh - 1)))
    others = dict(zip(order, take(nh - 1)))
    out_state, out_high, out_low, out_scale = take(4)
    out_write, out_inner, out_stepped, out_total = take(4)
    half = ch // 2
    base = top_rows(dims)
    mine = lax.axis_index("seq")

    pieces = []
    for k in range(1, nh):
        near, other = [
            jnp.concatenate(
                [
                    ref[base + place * half : base + (place + 1) * half, :]
                    for place in range(D // ch)
                ],
                axis=1,
            )
            for ref in (nears[k], others[k])
        ]
        even = lax.rem(lax.bitwise_xor(mine, partners(ns, nh)[k][0]), 2) == 0
        pieces.append(jnp.where(even, near, other))
        pieces.append(jnp.where(even, other, near))
    weights = split2(jnp.concatenate(pieces, axis=0))
    weights = (
        jnp.concatenate([own_high[...], weights[0]], axis=0),
        jnp.concatenate([own_low[...], weights[1]], axis=0),
    )
    hidden = embedded[...] + dot_split((high[...], low[...]), weights)
    split = split2(hidden)
    out_high[...], out_low[...] = split
    scale = lax.rsqrt(jnp.mean(hidden * hidden, axis=-1, keepdims=True) + epsilon)
    out_scale[...] = jnp.broadcast_to(scale, (T, ch))

    rows = dot_split(split, (state_high[...], state_low[...])) * scale
    inner, write = rows[:, 0:ch], rows[:, 2 * ch :]
    step = softplus(rows[:, ch : 2 * ch] + small[0:1, :])
    stepped = inner * step
    log_high, log_middle, log_low = split3(-small[1:2, :] * step)
    total = dot(upto[...], jnp.concatenate([log_low, log_middle], axis=1))
    total = (total[:, 0:ch] + total[:, ch:]) + dot(upto[...], log_high)
    end = total[T - 1 : T, :]
    state = dot3(stepped * jnp.exp(end - total), write, TN)
    out_state[0:ch, :] = state
    for head in range(hl):
        out_state[ch + head : ch + head + 1, :] = jnp.broadcast_to(
            end[:, head * P : head * P + 1], (1, N)
        )
    out_write[...] = write
    out_inner[...] = inner
    out_stepped[...] = stepped
    out_total[...] = total


def block_kernel(dims, *refs):
    V, D, hl, ch, nh, ns, T, N = dims
    P = ch // hl
    refs = list(refs)

    def take(number):
        taken, refs[:] = refs[:number], refs[number:]
        return taken

    high, low, scale, write, inner, stepped, total, choose = take(8)
    rest_high, rest_low, small = take(3)
    base, read_high, read_low, out_fade, out_gate, own, hidden_ref = take(7)
    rows = dot_split((high[...], low[...]), (rest_high[...], rest_low[...]))
    out_gate[...] = silu(rows[:, 0:ch] * scale[...])
    read = rows[:, ch:] * scale[...]
    read = split2(read)
    read_high[...], read_low[...] = read
    out_fade[...] = jnp.exp(total[...])
    products = dot_split(read, split2(write[...]), NT)
    stepped_high, stepped_low = split2(stepped[...])
    select = (iota((8, ch), 1) == iota((8, ch), 0) * P).astype(f32).astype(bf16)
    total_high, total_middle, total_low = split3(total[...])
    total_t = (dot(select, total_low, NT) + dot(select, total_middle, NT)) + dot(
        select, total_high, NT
    )
    allowed = iota((T, 1), 0) >= iota((1, T), 1)
    parts = []
    for head in range(hl):
        start, stop = head * P, (head + 1) * P
        differ = total[:, start : start + 1] - total_t[head : head + 1, :]
        weights = jnp.where(allowed, jnp.exp(jnp.where(allowed, differ, 0.0)), 0.0) * products
        part = dot_split(
            split2(weights), (stepped_high[:, start:stop], stepped_low[:, start:stop])
        )
        parts.append(part + small[2:3, start:stop] * inner[:, start:stop])
    base[...] = jnp.concatenate(parts, axis=1)
    share = T // nh
    hidden_ref[...] = high[...].astype(f32) + low[...].astype(f32)
    place = pl.multiple_of(lax.axis_index("head") * share, 8)
    own[...] = dot_right_exact(hidden_ref[pl.ds(place, share), :], choose[...])


def state_rows(dims, values):
    V, D, hl, ch, nh, ns, T, N = dims
    head_of = iota((ch, N), 0) // (ch // hl)
    result = jnp.broadcast_to(values[0:1, :], (ch, N))
    for head in range(1, hl):
        result = jnp.where(head_of == head, values[head : head + 1, :], result)
    return result


def join_kernel(dims, bit, total, prefix, came, out_total, out_prefix):
    V, D, hl, ch, nh, ns, T, N = dims
    later = lax.rem(lax.div(lax.axis_index("seq"), 2**bit), 2) == 1
    came_state, came_log = came[0:ch, :], came[ch : ch + hl, :]
    state, log = total[0:ch, :], total[ch : ch + hl, :]
    factor = jnp.exp(state_rows(dims, jnp.where(later, log, came_log)))
    out_total[0:ch, :] = jnp.where(
        later, factor * came_state + state, factor * state + came_state
    )
    out_total[ch : ch + hl, :] = log + came_log
    if prefix is None:
        out_prefix[0:ch, :] = jnp.where(later, came_state, 0.0)
        out_prefix[ch : ch + hl, :] = jnp.where(later, came_log, 0.0)
    else:
        joined = prefix_joined(dims, bit, prefix, came)
        out_prefix[0:ch, :] = joined
        out_prefix[ch : ch + hl, :] = prefix[ch : ch + hl, :] + jnp.where(later, came_log, 0.0)


def prefix_joined(dims, bit, prefix, came):
    V, D, hl, ch, nh, ns, T, N = dims
    later = lax.rem(lax.div(lax.axis_index("seq"), 2**bit), 2) == 1
    factor = jnp.exp(state_rows(dims, prefix[ch : ch + hl, :]))
    return prefix[0:ch, :] + jnp.where(later, factor * came[0:ch, :], 0.0)


def output_kernel(dims, bit, *refs):
    V, D, hl, ch, nh, ns, T, N = dims
    P = ch // hl
    prefix, came, read_high, read_low, base, fade, gate, own, proj_high, proj_low = refs[:10]
    groups, outs, partial_ref = refs[10], refs[11 : 11 + nh], refs[11 + nh]
    entering = prefix_joined(dims, bit, prefix, came)
    carried = dot_split((read_high[...], read_low[...]), split2(entering), NT)
    value = (base[...] + carried * fade[...]) * gate[...]
    square = dot(jnp.concatenate(split2(value * value), axis=0), groups[0:ch, 0:ch])
    square = square[T:] + square[0:T]
    value = value * lax.rsqrt(square * (1.0 / P) + epsilon)
    share = T // nh
    partial_ref[...] = dot_split(split2(value), (proj_high[...], proj_low[...]))
    mine = lax.axis_index("head")
    for k in range(nh):
        place = pl.multiple_of(lax.bitwise_xor(mine, k) * share, 8)
        part = partial_ref[pl.ds(place, share), :]
        outs[k][...] = part + own[...] if k == 0 else part


def per_device(
    token_ids,
    embedding,
    complement,
    prenorm_first,
    inproj_first,
    statemap_first,
    stepmap_first,
    stepbias_first,
    rates_first,
    skipgain_first,
    outnorm_first,
    outproj_first,
    prenorm_second,
    inproj_second,
    statemap_second,
    stepmap_second,
    stepbias_second,
    rates_second,
    skipgain_second,
    outnorm_second,
    outproj_second,
):
    nh, ns = lax.axis_size("head"), lax.axis_size("seq")
    V, D = embedding.shape
    ch = inproj_first.shape[2]
    hl = stepmap_first.shape[1]
    N = statemap_first.shape[2]
    T = token_ids.shape[0]
    LV = nh * hl * V
    dims = (V, D, hl, ch, nh, ns, T, N)
    vmem = pl.BlockSpec(memory_space=pltpu.VMEM)
    anywhere = pl.BlockSpec(memory_space=pl.ANY)
    params = pltpu.CompilerParams(vmem_limit_bytes=LIMIT)

    def shape(*sizes, dtype=f32):
        return jax.ShapeDtypeStruct(sizes, dtype)

    def halves(*sizes):
        return [shape(*sizes, dtype=bf16)] * 2

    def room(value):
        return pltpu.VMEM(value.shape, value.dtype)

    def kept(values):
        return [pltpu.with_memory_space_constraint(value, pltpu.HBM) for value in values]

    def line(value):
        return value.reshape(1, -1)

    def flat(value):
        return value.reshape(-1, value.shape[-1])

    heavy = pl.CostEstimate(flops=960 * T * D * D, bytes_accessed=4 * T * D, transcendentals=T * D)

    half = ch // 2
    share = T // nh
    fetched = [
        flat(inproj_first),
        line(token_ids),
        embedding,
        line(prenorm_first),
        stepmap_first.T,
        line(stepbias_first),
        line(rates_first),
        line(skipgain_first),
        line(outnorm_first),
    ]
    message = pl.pallas_call(
        functools.partial(tables_kernel, dims),
        out_shape=pltpu.VMEM((top_rows(dims) + half * (D // ch), ch), f32),
        in_specs=[anywhere] * (len(fetched) + 1),
        out_specs=vmem,
        scratch_shapes=[room(value) for value in fetched]
        + [pltpu.SemaphoreType.DMA((len(fetched) - 1 + PIECES + D // ch,))],
        compiler_params=params,
        name="tables",
    )(*kept([*fetched, outproj_first]))

    prepared = [
        flat(inproj_second),
        flat(statemap_second),
        flat(statemap_first),
        outproj_first,
        outproj_second,
        embedding,
        line(prenorm_first),
        line(complement),
        line(prenorm_second),
        stepmap_second.T,
        line(stepbias_second),
        line(rates_second),
        line(skipgain_second),
        line(outnorm_second),
    ]
    (
        pair_table,
        small,
        choose,
        own_high,
        own_low,
        state_high,
        state_low,
        rest_high,
        rest_low,
        proj_high,
        proj_low,
        triangles,
        upto,
        groups,
        blocks,
    ) = pl.pallas_call(
        functools.partial(prepare_kernel, dims),
        out_shape=(
            shape(V, LV),
            shape(8, ch),
            shape(D, D, dtype=bf16),
            *halves(ch, D),
            *halves(D, 2 * ch + N),
            *halves(D, ch + N),
            *halves(ch, D),
            shape(T, 2 * T + 128, dtype=bf16),
            shape(T, T, dtype=bf16),
            shape(2 * ch, 2 * ch, dtype=bf16),
            shape(LV, nh * ch, dtype=bf16),
        ),
        in_specs=[anywhere] * len(prepared),
        out_specs=(vmem,) * 15,
        scratch_shapes=[room(value) for value in prepared]
        + [pltpu.SemaphoreType.DMA((len(prepared),))],
        compiler_params=params,
        cost_estimate=heavy,
        name="prepare",
    )(*kept(prepared))

    count = max(ns, nh)
    messages = {0: message}
    for k in in_turn(count):
        seq_bits, head_bits = partners(ns, nh)[k]
        pairs = [
            (seq * nh + head, (seq ^ seq_bits) * nh + (head ^ head_bits))
            for seq in range(ns)
            for head in range(nh)
        ]
        sent = message if k < nh else message[0 : top_rows(dims)]
        messages[k] = lax.ppermute(sent, ("seq", "head"), pairs)
    swap = [(seq, seq ^ 1) for seq in range(ns)]
    order = in_turn(nh)[::-1]
    others = [lax.ppermute(messages[k], "seq", swap) for k in order]

    mixed_high, mixed_low, embedded = pl.pallas_call(
        functools.partial(mix_kernel, dims),
        out_shape=(*halves(T, nh * ch), shape(T, D)),
        in_specs=[vmem] * (count + 5),
        out_specs=(vmem,) * 3,
        scratch_shapes=[pltpu.VMEM((max(ns, 8), T), f32)],
        compiler_params=params,
        cost_estimate=heavy,
        name="mix",
    )(
        *[messages[k] for k in in_turn(count)[::-1] + [0]],
        embedding,
        pair_table,
        triangles,
        groups,
        blocks,
    )

    state, hidden_high, hidden_low, scale, write, inner, stepped, total = pl.pallas_call(
        functools.partial(project_kernel, dims),
        out_shape=(
            shape(ch + 8, N),
            *halves(T, D),
            shape(T, ch),
            shape(T, N),
            shape(T, ch),
            shape(T, ch),
            shape(T, ch),
        ),
        in_specs=[vmem] * (9 + 2 * (nh - 1)),
        out_specs=(vmem,) * 8,
        compiler_params=params,
        name="project",
    )(
        mixed_high,
        mixed_low,
        embedded,
        small,
        own_high,
        own_low,
        state_high,
        state_low,
        upto,
        *[messages[k] for k in order],
        *others,
    )

    base, read_high, read_low, fade, gate, own = pl.pallas_call(
        functools.partial(block_kernel, dims),
        out_shape=(
            shape(T, ch),
            *halves(T, N),
            shape(T, ch),
            shape(T, ch),
            shape(share, D),
        ),
        in_specs=[vmem] * 11,
        out_specs=(vmem,) * 6,
        scratch_shapes=[pltpu.VMEM((T, D), f32)],
        compiler_params=params,
        cost_estimate=heavy,
        name="block",
    )(
        hidden_high,
        hidden_low,
        scale,
        write,
        inner,
        stepped,
        total,
        choose,
        rest_high,
        rest_low,
        small,
    )

    prefix = None
    bits = ns.bit_length() - 1
    for bit in range(bits):
        came = lax.ppermute(state, "seq", [(seq, seq ^ 2**bit) for seq in range(ns)])
        if bit == bits - 1:
            break
        given = [state] + ([] if prefix is None else [prefix]) + [came]

        def join(bit, known, *refs):
            if known:
                join_kernel(dims, bit, *refs)
            else:
                join_kernel(dims, bit, refs[0], None, *refs[1:])

        state, prefix = pl.pallas_call(
            functools.partial(join, bit, prefix is not None),
            out_shape=(shape(ch + 8, N),) * 2,
            in_specs=[vmem] * len(given),
            out_specs=(vmem,) * 2,
            compiler_params=params,
            name="join",
        )(*given)
    if prefix is None:
        prefix = jnp.zeros_like(state)

    parts = pl.pallas_call(
        functools.partial(output_kernel, dims, bits - 1),
        out_shape=(shape(share, D),) * nh,
        in_specs=[vmem] * 11,
        out_specs=(vmem,) * nh,
        scratch_shapes=[pltpu.VMEM((T, D), f32)],
        compiler_params=params,
        name="output",
    )(
        prefix,
        came,
        read_high,
        read_low,
        base,
        fade,
        gate,
        own,
        proj_high,
        proj_low,
        groups,
    )
    result = parts[0]
    for k in in_turn(nh):
        pairs = [(source, source ^ k) for source in range(nh)]
        result = result + lax.ppermute(parts[k], "head", pairs)
    return result


def solution(mesh):
    return jax.shard_map(
        per_device,
        mesh=mesh,
        in_specs=(
            P(("rep", "seq")),
            P(),
            P(),
            P(),
            P(None, None, "head"),
            P(),
            P(None, "head"),
            P("head"),
            P("head"),
            P("head"),
            P("head"),
            P("head", None),
            P(),
            P(None, None, "head"),
            P(),
            P(None, "head"),
            P("head"),
            P("head"),
            P("head"),
            P("head"),
            P("head", None),
        ),
        out_specs=P(("rep", "seq", "head"), None),
        check_vma=False,
    )
```

```python
import functools

import jax
import jax.numpy as jnp
from jax import lax
from jax.experimental import pallas as pl
from jax.experimental.pallas import tpu as pltpu
from jax.sharding import PartitionSpec as P

epsilon = 1e-05
f32 = jnp.float32
bf16 = jnp.bfloat16
LIMIT = 48 * 1024 * 1024

MM = (((1,), (0,)), ((), ()))
NT = (((1,), (1,)), ((), ()))
TN = (((0,), (0,)), ((), ()))


def shifts(count):
    found = []
    for step in range(1, count):
        for shift in (step, count - step):
            if shift not in found:
                found.append(shift)
    return found


def moved(place, shift, count):
    half = count // 2
    position = place % half * 2 + place // half
    position = (position + shift) % count
    return position // 2 + position % 2 * half


def partners(ns, nh):
    bits = list(range(1, ns))
    if ns > 2:
        bits[:2] = [2, 1]
    heads = shifts(nh)
    count = max(len(bits), len(heads))
    bits += [0] * (count - len(bits))
    heads += [0] * (count - len(heads))
    return [(0, 0)] + list(zip(bits, heads))


def in_turn(count):
    return list(range(1, count))


def iota(shape, axis):
    return lax.broadcasted_iota(jnp.int32, shape, axis)


def split2(value):
    high = value.astype(bf16)
    return high, (value - high.astype(f32)).astype(bf16)


def split3(value):
    high = value.astype(bf16)
    rest = value - high.astype(f32)
    middle = rest.astype(bf16)
    return high, middle, (rest - middle.astype(f32)).astype(bf16)


def dot(left, right, dims=MM):
    return lax.dot_general(left, right, dims, preferred_element_type=f32)


def dot_split(left, right, dims=MM):
    axis = 1 if dims == TN else 0
    size = left[0].shape[axis]
    if size % 16:
        return (dot(left[0], right[1], dims) + dot(left[1], right[0], dims)) + dot(
            left[0], right[0], dims
        )
    both = dot(jnp.concatenate([left[1], left[0]], axis=axis), right[0], dims)
    return (dot(left[0], right[1], dims) + both[0:size]) + both[size:]


def dot3(left, right, dims=MM):
    return dot_split(split2(left), split2(right), dims)


def dot_left_exact(left, right, dims=MM):
    high, middle, low = split3(right)
    return (dot(left, low, dims) + dot(left, middle, dims)) + dot(left, high, dims)


def dot_right_exact(left, right, dims=MM):
    high, middle, low = split3(left)
    return (dot(low, right, dims) + dot(middle, right, dims)) + dot(high, right, dims)


def softplus(value):
    return jnp.maximum(value, 0.0) + jnp.log1p(jnp.exp(-jnp.abs(value)))


def silu(value):
    return value / (1.0 + jnp.exp(-value))


def rms(value):
    return value * lax.rsqrt(jnp.mean(value * value, axis=-1, keepdims=True) + epsilon)


def fetch(sources, places, semaphores):
    copies = []
    for number, (source, place) in enumerate(zip(sources, places)):
        copies.append(pltpu.make_async_copy(source, place, semaphores.at[number]))
        copies[-1].start()
    return copies


def fetch(sources, places, semaphores):
    copies = []
    for number, (source, place) in enumerate(zip(sources, places)):
        copies.append(pltpu.make_async_copy(source, place, semaphores.at[number]))
        copies[-1].start()
    return copies


PIECES = 1


def tables_kernel(dims, *refs):
    V, D, hl, ch, nh, ns, T, N = dims
    refs = list(refs)

    def take(number):
        taken, refs[:] = refs[:number], refs[number:]
        return taken

    sources = take(9)
    outproj_source, message = take(2)
    places = take(9)
    semaphores = take(1)[0]
    half = ch // 2
    top = top_rows(dims)
    core = lax.rem(lax.axis_index("seq"), 2)
    (inproj, tok, emb, prenorm, stepmap, bias, rates, skip, outnorm) = places
    size = inproj.shape[0] // PIECES
    pieces = [pl.ds(number * size, size) for number in range(PIECES)]
    rows = pl.ds(pl.multiple_of(core * half, 8), half)
    wide = [(place, pl.ds(place * ch, ch)) for place in range(D // ch)]
    copies = fetch(
        [sources[0].at[piece, :] for piece in pieces]
        + sources[1:]
        + [outproj_source.at[rows, columns] for _, columns in wide],
        [inproj.at[piece, :] for piece in pieces]
        + places[1:]
        + [message.at[pl.ds(top + place * half, half), :] for place, _ in wide],
        semaphores,
    )
    flip = (iota((T, 1), 0) + iota((1, T), 1) == T - 1).astype(f32).astype(bf16)
    for copy in copies[PIECES : PIECES + 8]:
        copy.wait()
    normed = split2(rms(emb[...]) * prenorm[...])
    raw_t = dot_split(split2(stepmap[...]), normed, NT)
    tokens = jnp.broadcast_to(tok[...].astype(f32), (8, T)).astype(bf16)
    tokens = dot(tokens, flip)
    for place in range(T // ch):
        message[2 * V + place : 2 * V + place + 1, :] = tokens[0:1, place * ch : (place + 1) * ch]
    row = 2 * V + T // ch
    message[row : row + 1, :] = outnorm[...]
    for head in range(hl):
        line = softplus(raw_t[head : head + 1, :] + bias[:, head : head + 1])
        row = row + 1
        message[row : row + 1, 0:V] = line
        message[row : row + 1, V : 2 * V] = -rates[:, head : head + 1] * line
        message[row : row + 1, 2 * V : 3 * V] = jnp.broadcast_to(skip[:, head : head + 1], (1, V))
    for copy in copies[:PIECES]:
        copy.wait()
    weights = jnp.concatenate(
        [inproj[pl.ds(0, D, stride=2), :], inproj[pl.ds(1, D, stride=2), :]], axis=1
    )
    both = dot_split(normed, split2(weights))
    message[0:V, :] = both[:, 0:ch]
    message[V : 2 * V, :] = both[:, ch:]
    for copy in copies[PIECES + 8 :]:
        copy.wait()


def top_rows(dims):
    V, D, hl, ch, nh, ns, T, N = dims
    return 2 * V + -(-(T // ch + 1 + hl) // 8) * 8


def head_line(dims, values):
    V, D, hl, ch, nh, ns, T, N = dims
    head_of = iota((1, ch), 1) // (ch // hl)
    line = jnp.zeros((1, ch), f32)
    for head in range(hl):
        line = jnp.where(head_of == head, values[:, head : head + 1], line)
    return line


def prepare_kernel(dims, *refs):
    V, D, hl, ch, nh, ns, T, N = dims
    H, P = nh * hl, ch // hl
    refs = list(refs)

    def take(number):
        taken, refs[:] = refs[:number], refs[number:]
        return taken

    sources = take(14)
    pairs, small, choose_out, own_high, own_low = take(5)
    state_high, state_low, rest_high, rest_low, out_high, out_low = take(6)
    triangles, upto, groups, blocks = take(4)
    places = take(14)
    semaphores = take(1)[0]
    copies = fetch(sources, places, semaphores)
    inproj2, statemap2, statemap, outproj, outproj2, emb, prenorm, complement = places[:8]
    prenorm2, stepmap2, bias2, rates2, skip2, outnorm2 = places[8:]
    row, column = iota((T, 1), 0), iota((1, T), 1)
    triangles[:, 0:T] = (row > column).astype(f32).astype(bf16)
    triangles[:, T : 2 * T] = (row < column).astype(f32).astype(bf16)
    triangles[:, 2 * T :] = jnp.ones((T, 128), bf16)
    upto[...] = (row >= column).astype(f32).astype(bf16)
    size = groups.shape[0]
    groups[...] = (iota((size, 1), 0) // P == iota((1, size), 1) // P).astype(f32).astype(bf16)
    rows, columns = blocks.shape
    blocks[...] = (iota((rows, 1), 0) // V == iota((1, columns), 1) // P).astype(f32).astype(bf16)
    for copy in copies:
        copy.wait()
    normed = split2(rms(emb[...]) * prenorm[...])
    write = dot_split(normed, split2(statemap[pl.ds(0, D, stride=2), :]))
    read = dot_split(normed, split2(statemap[pl.ds(1, D, stride=2), :]))
    pairs[...] = dot3(read, jnp.concatenate([write] * H, axis=0), NT)
    own_high[...], own_low[...] = split2(outproj[...])
    choose = (complement[...] == iota((D, 1), 0)).astype(f32).astype(bf16)
    choose_out[...] = choose
    gain = jnp.transpose(jnp.broadcast_to(prenorm2[...], (128, D)))

    def weights(values):
        return split2(dot_left_exact(choose, values))

    gain_wide = gain[:, 0:1]
    inner = inproj2[pl.ds(1, D, stride=2), :] * gain_wide
    step = jnp.transpose(
        jnp.concatenate(
            [jnp.broadcast_to(stepmap2[head : head + 1, :], (P, D)) for head in range(hl)], axis=0
        )
    )
    write2 = statemap2[pl.ds(0, D, stride=2), :] * gain_wide
    state_high[...], state_low[...] = weights(
        jnp.concatenate([inner, step * gain_wide, write2], axis=1)
    )
    gate = inproj2[pl.ds(0, D, stride=2), :] * gain_wide
    read2 = statemap2[pl.ds(1, D, stride=2), :] * gain_wide
    rest_high[...], rest_low[...] = weights(jnp.concatenate([gate, read2], axis=1))
    small[0:1, :] = head_line(dims, bias2)
    small[1:2, :] = head_line(dims, rates2)
    small[2:3, :] = head_line(dims, skip2)
    out_gain = jnp.transpose(jnp.broadcast_to(outnorm2[...], (128, ch)))
    out_high[...], out_low[...] = split2(outproj2[...] * out_gain[:, 0:1])


def shift_rows(value, amount, fill):
    size = value.shape[0]
    if amount % 8 == 0:
        empty = jnp.full((abs(amount),) + value.shape[1:], fill, value.dtype)
        if amount > 0:
            return jnp.concatenate([empty, value[: size - amount]], axis=0)
        return jnp.concatenate([value[-amount:], empty], axis=0)
    rolled = pltpu.roll(value, amount % size, 0)
    row = iota((8,) + value.shape[1:], 0)
    if amount > 0:
        edge = jnp.where(row >= amount, rolled[0:8], fill)
        return jnp.concatenate([edge, rolled[8:]], axis=0)
    edge = jnp.where(row < 8 + amount, rolled[size - 8 :], fill)
    return jnp.concatenate([rolled[: size - 8], edge], axis=0)


def scan_rows(decay, value, sign):
    size = value.shape[0]
    amount = 1
    while amount < size:
        value = value + decay * shift_rows(value, sign * amount, 0.0)
        decay = decay * shift_rows(decay, sign * amount, 1.0)
        amount *= 2
    return value, decay


def mix_kernel(dims, *refs):
    V, D, hl, ch, nh, ns, T, N = dims
    H, LV, P = nh * hl, nh * hl * V, ch // hl
    C = nh * ch
    refs = list(refs)

    def take(number):
        taken, refs[:] = refs[:number], refs[number:]
        return taken

    count = max(ns, nh)
    packets = dict(zip(in_turn(count)[::-1] + [0], take(count)))
    emb, pairs, triangles, groups, blocks = take(5)
    out_high, out_low, out_embedded = take(3)
    tokens = take(1)[0]
    mine = lax.axis_index("seq")

    for k in range(ns):
        block = ns - 1 - lax.bitwise_xor(mine, partners(ns, nh)[k][0])
        row = 2 * V
        pieces = [packets[k][row + place : row + place + 1, :] for place in range(T // ch)]
        tokens[pl.ds(block, 1), :] = jnp.concatenate(pieces, axis=1)

    first = 2 * V + T // ch + 1
    steps = jnp.concatenate(
        [packets[k][first : first + hl, 0 : 3 * V] for k in range(nh)], axis=0
    )
    log_t = steps[:, V : 2 * V]
    narrow = jnp.concatenate([part.astype(f32) for part in split3(steps)], axis=0).astype(bf16)
    spread_heads = (iota((1, LV), 1) // V == iota((3 * H, 1), 0) % H).astype(f32).astype(bf16)
    wide = dot(narrow, spread_heads, TN)
    own = iota((1, LV), 1) % V == iota((V, 1), 0)
    decay_table = jnp.exp(wide[V : 2 * V])
    step_table = jnp.where(own, wide[0:V], 0.0)
    gain_table = jnp.where(own, wide[2 * V : 3 * V], 0.0)
    gates = jnp.concatenate([packets[k][0:V, :] for k in range(nh)], axis=1)
    inners = jnp.concatenate([packets[k][V : 2 * V, :] for k in range(nh)], axis=1)
    gains = jnp.concatenate([packets[k][first - 1 : first, :] for k in range(nh)], axis=1)

    token_row = (iota((LV, 1), 0) % V).astype(f32)
    log_split = jnp.concatenate(split3(log_t), axis=1)
    onehots, logs = [], []
    for block in range(ns):
        onehot = (tokens[block : block + 1, :] == token_row).astype(f32).astype(bf16)
        onehots.append(onehot)
        logs.append(dot(log_split, onehot[0 : 3 * V, :]))
    logs = jnp.concatenate(logs, axis=0)
    size = ns * H
    sums = dot(jnp.concatenate(split3(logs)[::-1], axis=0), triangles[...])
    sums = (sums[0:size] + sums[size : 2 * size]) + sums[2 * size :]
    blocks_of = [sums[block * H : (block + 1) * H] for block in range(ns)]
    weight_up, weight_down = [None] * ns, [None] * ns
    gap = jnp.zeros((H, 128), f32)
    for block in reversed(range(ns)):
        wide = jnp.concatenate([gap] * (T // 128), axis=1)
        weight_up[block] = jnp.where(
            block < mine, jnp.exp(blocks_of[block][:, 0:T] + wide), 0.0
        )
        gap = jnp.where(block < mine, gap + blocks_of[block][:, 2 * T :], gap)
    gap = jnp.zeros((H, 128), f32)
    for block in range(ns):
        wide = jnp.concatenate([gap] * (T // 128), axis=1)
        weight_down[block] = jnp.where(
            block > mine, jnp.exp(blocks_of[block][:, T : 2 * T] + wide), 0.0
        )
        gap = jnp.where(block > mine, gap + blocks_of[block][:, 2 * T :], gap)
    entering = jnp.zeros((4 * H, LV), f32)
    for block in range(ns):
        both = jnp.concatenate([weight_up[block], weight_down[block]], axis=0)
        entering = entering + dot(
            jnp.concatenate(split2(both), axis=0), onehots[block], NT
        )
    entering = entering[2 * H :] + entering[0 : 2 * H]
    diagonal = iota((1, LV), 1) // V == iota((H, 1), 0)
    step_row = jnp.sum(step_table, axis=0, keepdims=True)
    enter_up = step_row * jnp.sum(
        jnp.where(diagonal, entering[0:H], 0.0), axis=0, keepdims=True
    )
    enter_down = step_row * jnp.sum(
        jnp.where(diagonal, entering[H : 2 * H], 0.0), axis=0, keepdims=True
    )

    looked = jnp.concatenate(
        [decay_table, step_table, pairs[...], gain_table, silu(gates), emb[...]], axis=1
    )
    looked = jnp.concatenate(split3(looked), axis=0)
    token = tokens[pl.ds(mine, 1), :]
    onehot = (token == token_row[0 : 3 * V]).astype(f32).astype(bf16)
    rows = dot(onehot, looked, TN)
    decay, step = rows[:, 0:LV], rows[:, LV : 2 * LV]
    pair, gain = rows[:, 2 * LV : 3 * LV], rows[:, 3 * LV : 4 * LV]
    silu_rows = rows[:, 4 * LV : 4 * LV + C]
    out_embedded[...] = rows[:, 4 * LV + C :]

    up, fade = scan_rows(decay, step, 1)
    up = up + fade * enter_up
    down, fade = scan_rows(decay, step, -1)
    down = down + fade * enter_down

    spread_high, spread_low = [
        jnp.concatenate([part] * H, axis=0) * blocks[...] for part in split2(inners)
    ]
    both = jnp.concatenate([up * pair + gain, down * pair + gain], axis=0)
    high = both.astype(bf16)
    high_wide = high.astype(f32)
    low_turned = pltpu.roll(both - high_wide, LV // 2, 1)
    lower = iota((1, LV), 1) < LV // 2
    value = []
    for side in (0, 1):
        mixed = jnp.where(lower == (side == 0), high_wide, low_turned).astype(bf16)
        rows = slice(side * LV // 2, (side + 1) * LV // 2)
        columns = slice(side * C // 2, (side + 1) * C // 2)
        weight, rest = spread_high[rows, columns], spread_low[:, columns]
        value.append(
            dot(
                jnp.concatenate([mixed, high], axis=1),
                jnp.concatenate([weight, weight, rest], axis=0),
            )
        )
    value = jnp.concatenate(value, axis=1)
    value = value * jnp.concatenate([silu_rows, silu_rows], axis=0)
    wide = groups.shape[0]
    high, low = split2(value * value)
    starts = list(range(0, C, wide))
    rows = 2 * T
    stacked = [half[:, start : start + wide] for start in starts for half in (low, high)]
    squares = dot(jnp.concatenate(stacked, axis=0), groups[...])
    for number, start in enumerate(starts):
        place = 2 * number * rows
        square = squares[place : place + rows] + squares[place + rows : place + 2 * rows]
        stop = start + wide
        normed = value[:, start:stop] * lax.rsqrt(square * (1.0 / P) + epsilon)
        out_high[:, start:stop], out_low[:, start:stop] = split2(
            (normed[0:T] + normed[T : 2 * T]) * gains[:, start:stop]
        )


def project_kernel(dims, *refs):
    V, D, hl, ch, nh, ns, T, N = dims
    P = ch // hl
    refs = list(refs)

    def take(number):
        taken, refs[:] = refs[:number], refs[number:]
        return taken

    high, low, embedded, small, own_high, own_low, state_high, state_low, upto = take(9)
    order = in_turn(nh)[::-1]
    nears = dict(zip(order, take(nh - 1)))
    others = dict(zip(order, take(nh - 1)))
    out_state, out_high, out_low, out_scale = take(4)
    out_write, out_inner, out_stepped, out_total = take(4)
    half = ch // 2
    base = top_rows(dims)
    mine = lax.axis_index("seq")

    pieces = []
    for k in range(1, nh):
        near, other = [
            jnp.concatenate(
                [
                    ref[base + place * half : base + (place + 1) * half, :]
                    for place in range(D // ch)
                ],
                axis=1,
            )
            for ref in (nears[k], others[k])
        ]
        even = lax.rem(lax.bitwise_xor(mine, partners(ns, nh)[k][0]), 2) == 0
        pieces.append(jnp.where(even, near, other))
        pieces.append(jnp.where(even, other, near))
    weights = split2(jnp.concatenate(pieces, axis=0))
    weights = (
        jnp.concatenate([own_high[...], weights[0]], axis=0),
        jnp.concatenate([own_low[...], weights[1]], axis=0),
    )
    hidden = embedded[...] + dot_split((high[...], low[...]), weights)
    split = split2(hidden)
    out_high[...], out_low[...] = split
    scale = lax.rsqrt(jnp.mean(hidden * hidden, axis=-1, keepdims=True) + epsilon)
    out_scale[...] = jnp.broadcast_to(scale, (T, ch))

    rows = dot_split(split, (state_high[...], state_low[...])) * scale
    inner, write = rows[:, 0:ch], rows[:, 2 * ch :]
    step = softplus(rows[:, ch : 2 * ch] + small[0:1, :])
    stepped = inner * step
    log_high, log_middle, log_low = split3(-small[1:2, :] * step)
    total = dot(upto[...], jnp.concatenate([log_low, log_middle], axis=1))
    total = (total[:, 0:ch] + total[:, ch:]) + dot(upto[...], log_high)
    end = total[T - 1 : T, :]
    state = dot3(stepped * jnp.exp(end - total), write, TN)
    out_state[0:ch, :] = state
    for head in range(hl):
        out_state[ch + head : ch + head + 1, :] = jnp.broadcast_to(
            end[:, head * P : head * P + 1], (1, N)
        )
    out_write[...] = write
    out_inner[...] = inner
    out_stepped[...] = stepped
    out_total[...] = total


def block_kernel(dims, *refs):
    V, D, hl, ch, nh, ns, T, N = dims
    P = ch // hl
    refs = list(refs)

    def take(number):
        taken, refs[:] = refs[:number], refs[number:]
        return taken

    high, low, scale, write, inner, stepped, total, choose = take(8)
    rest_high, rest_low, small = take(3)
    base, read_high, read_low, out_fade, out_gate, own, hidden_ref = take(7)
    rows = dot_split((high[...], low[...]), (rest_high[...], rest_low[...]))
    out_gate[...] = silu(rows[:, 0:ch] * scale[...])
    read = rows[:, ch:] * scale[...]
    read = split2(read)
    read_high[...], read_low[...] = read
    out_fade[...] = jnp.exp(total[...])
    products = dot_split(read, split2(write[...]), NT)
    stepped_high, stepped_low = split2(stepped[...])
    select = (iota((8, ch), 1) == iota((8, ch), 0) * P).astype(f32).astype(bf16)
    total_high, total_middle, total_low = split3(total[...])
    total_t = (dot(select, total_low, NT) + dot(select, total_middle, NT)) + dot(
        select, total_high, NT
    )
    allowed = iota((T, 1), 0) >= iota((1, T), 1)
    parts = []
    for head in range(hl):
        start, stop = head * P, (head + 1) * P
        differ = total[:, start : start + 1] - total_t[head : head + 1, :]
        weights = jnp.where(allowed, jnp.exp(jnp.where(allowed, differ, 0.0)), 0.0) * products
        part = dot_split(
            split2(weights), (stepped_high[:, start:stop], stepped_low[:, start:stop])
        )
        parts.append(part + small[2:3, start:stop] * inner[:, start:stop])
    base[...] = jnp.concatenate(parts, axis=1)
    share = T // nh
    hidden_ref[...] = high[...].astype(f32) + low[...].astype(f32)
    place = pl.multiple_of(lax.axis_index("head") * share, 8)
    own[...] = dot_right_exact(hidden_ref[pl.ds(place, share), :], choose[...])


def state_rows(dims, values):
    V, D, hl, ch, nh, ns, T, N = dims
    head_of = iota((ch, N), 0) // (ch // hl)
    result = jnp.broadcast_to(values[0:1, :], (ch, N))
    for head in range(1, hl):
        result = jnp.where(head_of == head, values[head : head + 1, :], result)
    return result


def join_kernel(dims, bit, total, prefix, came, out_total, out_prefix):
    V, D, hl, ch, nh, ns, T, N = dims
    later = lax.rem(lax.div(lax.axis_index("seq"), 2**bit), 2) == 1
    came_state, came_log = came[0:ch, :], came[ch : ch + hl, :]
    state, log = total[0:ch, :], total[ch : ch + hl, :]
    factor = jnp.exp(state_rows(dims, jnp.where(later, log, came_log)))
    out_total[0:ch, :] = jnp.where(
        later, factor * came_state + state, factor * state + came_state
    )
    out_total[ch : ch + hl, :] = log + came_log
    if prefix is None:
        out_prefix[0:ch, :] = jnp.where(later, came_state, 0.0)
        out_prefix[ch : ch + hl, :] = jnp.where(later, came_log, 0.0)
    else:
        joined = prefix_joined(dims, bit, prefix, came)
        out_prefix[0:ch, :] = joined
        out_prefix[ch : ch + hl, :] = prefix[ch : ch + hl, :] + jnp.where(later, came_log, 0.0)


def prefix_joined(dims, bit, prefix, came):
    V, D, hl, ch, nh, ns, T, N = dims
    later = lax.rem(lax.div(lax.axis_index("seq"), 2**bit), 2) == 1
    factor = jnp.exp(state_rows(dims, prefix[ch : ch + hl, :]))
    return prefix[0:ch, :] + jnp.where(later, factor * came[0:ch, :], 0.0)


def output_kernel(dims, bit, *refs):
    V, D, hl, ch, nh, ns, T, N = dims
    P = ch // hl
    prefix, came, read_high, read_low, base, fade, gate, own, proj_high, proj_low = refs[:10]
    groups, outs, partial_ref = refs[10], refs[11 : 11 + nh], refs[11 + nh]
    entering = prefix_joined(dims, bit, prefix, came)
    carried = dot_split((read_high[...], read_low[...]), split2(entering), NT)
    value = (base[...] + carried * fade[...]) * gate[...]
    square = dot(jnp.concatenate(split2(value * value), axis=0), groups[0:ch, 0:ch])
    square = square[T:] + square[0:T]
    value = value * lax.rsqrt(square * (1.0 / P) + epsilon)
    share = T // nh
    partial_ref[...] = dot_split(split2(value), (proj_high[...], proj_low[...]))
    mine = lax.axis_index("head")
    for k in range(nh):
        shift = 0 if k == 0 else shifts(nh)[k - 1]
        position = lax.rem(mine, nh // 2) * 2 + lax.div(mine, nh // 2)
        position = lax.rem(position + shift, nh)
        to = lax.div(position, 2) + lax.rem(position, 2) * (nh // 2)
        place = pl.multiple_of(to * share, 8)
        part = partial_ref[pl.ds(place, share), :]
        outs[k][...] = part + own[...] if k == 0 else part


def per_device(
    token_ids,
    embedding,
    complement,
    prenorm_first,
    inproj_first,
    statemap_first,
    stepmap_first,
    stepbias_first,
    rates_first,
    skipgain_first,
    outnorm_first,
    outproj_first,
    prenorm_second,
    inproj_second,
    statemap_second,
    stepmap_second,
    stepbias_second,
    rates_second,
    skipgain_second,
    outnorm_second,
    outproj_second,
):
    nh, ns = lax.axis_size("head"), lax.axis_size("seq")
    V, D = embedding.shape
    ch = inproj_first.shape[2]
    hl = stepmap_first.shape[1]
    N = statemap_first.shape[2]
    T = token_ids.shape[0]
    LV = nh * hl * V
    dims = (V, D, hl, ch, nh, ns, T, N)
    vmem = pl.BlockSpec(memory_space=pltpu.VMEM)
    anywhere = pl.BlockSpec(memory_space=pl.ANY)
    params = pltpu.CompilerParams(vmem_limit_bytes=LIMIT)

    def shape(*sizes, dtype=f32):
        return jax.ShapeDtypeStruct(sizes, dtype)

    def halves(*sizes):
        return [shape(*sizes, dtype=bf16)] * 2

    def room(value):
        return pltpu.VMEM(value.shape, value.dtype)

    def kept(values):
        return [pltpu.with_memory_space_constraint(value, pltpu.HBM) for value in values]

    def line(value):
        return value.reshape(1, -1)

    def flat(value):
        return value.reshape(-1, value.shape[-1])

    heavy = pl.CostEstimate(flops=960 * T * D * D, bytes_accessed=4 * T * D, transcendentals=T * D)

    half = ch // 2
    share = T // nh
    fetched = [
        flat(inproj_first),
        line(token_ids),
        embedding,
        line(prenorm_first),
        stepmap_first.T,
        line(stepbias_first),
        line(rates_first),
        line(skipgain_first),
        line(outnorm_first),
    ]
    message = pl.pallas_call(
        functools.partial(tables_kernel, dims),
        out_shape=pltpu.VMEM((top_rows(dims) + half * (D // ch), ch), f32),
        in_specs=[anywhere] * (len(fetched) + 1),
        out_specs=vmem,
        scratch_shapes=[room(value) for value in fetched]
        + [pltpu.SemaphoreType.DMA((len(fetched) - 1 + PIECES + D // ch,))],
        compiler_params=params,
        name="tables",
    )(*kept([*fetched, outproj_first]))

    prepared = [
        flat(inproj_second),
        flat(statemap_second),
        flat(statemap_first),
        outproj_first,
        outproj_second,
        embedding,
        line(prenorm_first),
        line(complement),
        line(prenorm_second),
        stepmap_second.T,
        line(stepbias_second),
        line(rates_second),
        line(skipgain_second),
        line(outnorm_second),
    ]
    (
        pair_table,
        small,
        choose,
        own_high,
        own_low,
        state_high,
        state_low,
        rest_high,
        rest_low,
        proj_high,
        proj_low,
        triangles,
        upto,
        groups,
        blocks,
    ) = pl.pallas_call(
        functools.partial(prepare_kernel, dims),
        out_shape=(
            shape(V, LV),
            shape(8, ch),
            shape(D, D, dtype=bf16),
            *halves(ch, D),
            *halves(D, 2 * ch + N),
            *halves(D, ch + N),
            *halves(ch, D),
            shape(T, 2 * T + 128, dtype=bf16),
            shape(T, T, dtype=bf16),
            shape(2 * ch, 2 * ch, dtype=bf16),
            shape(LV, nh * ch, dtype=bf16),
        ),
        in_specs=[anywhere] * len(prepared),
        out_specs=(vmem,) * 15,
        scratch_shapes=[room(value) for value in prepared]
        + [pltpu.SemaphoreType.DMA((len(prepared),))],
        compiler_params=params,
        cost_estimate=heavy,
        name="prepare",
    )(*kept(prepared))

    count = max(ns, nh)
    messages = {0: message}
    for k in in_turn(count):
        seq_bits, shift = partners(ns, nh)[k]
        pairs = [
            (seq * nh + head, (seq ^ seq_bits) * nh + moved(head, shift, nh))
            for seq in range(ns)
            for head in range(nh)
        ]
        sent = message if k < nh else message[0 : top_rows(dims)]
        messages[k] = lax.ppermute(sent, ("seq", "head"), pairs)
    swap = [(seq, seq ^ 1) for seq in range(ns)]
    order = in_turn(nh)[::-1]
    others = [lax.ppermute(messages[k], "seq", swap) for k in order]

    mixed_high, mixed_low, embedded = pl.pallas_call(
        functools.partial(mix_kernel, dims),
        out_shape=(*halves(T, nh * ch), shape(T, D)),
        in_specs=[vmem] * (count + 5),
        out_specs=(vmem,) * 3,
        scratch_shapes=[pltpu.VMEM((max(ns, 8), T), f32)],
        compiler_params=params,
        cost_estimate=heavy,
        name="mix",
    )(
        *[messages[k] for k in in_turn(count)[::-1] + [0]],
        embedding,
        pair_table,
        triangles,
        groups,
        blocks,
    )

    state, hidden_high, hidden_low, scale, write, inner, stepped, total = pl.pallas_call(
        functools.partial(project_kernel, dims),
        out_shape=(
            shape(ch + 8, N),
            *halves(T, D),
            shape(T, ch),
            shape(T, N),
            shape(T, ch),
            shape(T, ch),
            shape(T, ch),
        ),
        in_specs=[vmem] * (9 + 2 * (nh - 1)),
        out_specs=(vmem,) * 8,
        compiler_params=params,
        name="project",
    )(
        mixed_high,
        mixed_low,
        embedded,
        small,
        own_high,
        own_low,
        state_high,
        state_low,
        upto,
        *[messages[k] for k in order],
        *others,
    )

    base, read_high, read_low, fade, gate, own = pl.pallas_call(
        functools.partial(block_kernel, dims),
        out_shape=(
            shape(T, ch),
            *halves(T, N),
            shape(T, ch),
            shape(T, ch),
            shape(share, D),
        ),
        in_specs=[vmem] * 11,
        out_specs=(vmem,) * 6,
        scratch_shapes=[pltpu.VMEM((T, D), f32)],
        compiler_params=params,
        cost_estimate=heavy,
        name="block",
    )(
        hidden_high,
        hidden_low,
        scale,
        write,
        inner,
        stepped,
        total,
        choose,
        rest_high,
        rest_low,
        small,
    )

    prefix = None
    bits = ns.bit_length() - 1
    for bit in range(bits):
        came = lax.ppermute(state, "seq", [(seq, seq ^ 2**bit) for seq in range(ns)])
        if bit == bits - 1:
            break
        given = [state] + ([] if prefix is None else [prefix]) + [came]

        def join(bit, known, *refs):
            if known:
                join_kernel(dims, bit, *refs)
            else:
                join_kernel(dims, bit, refs[0], None, *refs[1:])

        state, prefix = pl.pallas_call(
            functools.partial(join, bit, prefix is not None),
            out_shape=(shape(ch + 8, N),) * 2,
            in_specs=[vmem] * len(given),
            out_specs=(vmem,) * 2,
            compiler_params=params,
            name="join",
        )(*given)
    if prefix is None:
        prefix = jnp.zeros_like(state)

    parts = pl.pallas_call(
        functools.partial(output_kernel, dims, bits - 1),
        out_shape=(shape(share, D),) * nh,
        in_specs=[vmem] * 11,
        out_specs=(vmem,) * nh,
        scratch_shapes=[pltpu.VMEM((T, D), f32)],
        compiler_params=params,
        name="output",
    )(
        prefix,
        came,
        read_high,
        read_low,
        base,
        fade,
        gate,
        own,
        proj_high,
        proj_low,
        groups,
    )
    result = parts[0]
    for k in in_turn(nh):
        shift = shifts(nh)[k - 1]
        pairs = [(source, moved(source, shift, nh)) for source in range(nh)]
        result = result + lax.ppermute(parts[k], "head", pairs)
    return result


def solution(mesh):
    return jax.shard_map(
        per_device,
        mesh=mesh,
        in_specs=(
            P(("rep", "seq")),
            P(),
            P(),
            P(),
            P(None, None, "head"),
            P(),
            P(None, "head"),
            P("head"),
            P("head"),
            P("head"),
            P("head"),
            P("head", None),
            P(),
            P(None, None, "head"),
            P(),
            P(None, "head"),
            P("head"),
            P("head"),
            P("head"),
            P("head"),
            P("head", None),
        ),
        out_specs=P(("rep", "seq", "head"), None),
        check_vma=False,
    )
```

```python
import functools

import jax
import jax.numpy as jnp
from jax import lax
from jax.experimental import pallas as pl
from jax.experimental.pallas import tpu as pltpu
from jax.sharding import PartitionSpec as P

epsilon = 1e-05
f32 = jnp.float32
bf16 = jnp.bfloat16
LIMIT = 48 * 1024 * 1024

MM = (((1,), (0,)), ((), ()))
NT = (((1,), (1,)), ((), ()))
TN = (((0,), (0,)), ((), ()))


def shifts(count):
    found = []
    for step in range(1, count):
        for shift in (step, count - step):
            if shift not in found:
                found.append(shift)
    return found


def moved(place, shift, count):
    half = count // 2
    position = place % half * 2 + place // half
    position = (position + shift) % count
    return position // 2 + position % 2 * half


def partners(ns, nh):
    bits = list(range(1, ns))
    if ns > 2:
        bits[:2] = [2, 1]
    heads = shifts(nh)
    count = max(len(bits), len(heads))
    bits += [0] * (count - len(bits))
    heads += [0] * (count - len(heads))
    return [(0, 0)] + list(zip(bits, heads))


def in_turn(count):
    return list(range(1, count))


def iota(shape, axis):
    return lax.broadcasted_iota(jnp.int32, shape, axis)


def split2(value):
    high = value.astype(bf16)
    return high, (value - high.astype(f32)).astype(bf16)


def split3(value):
    high = value.astype(bf16)
    rest = value - high.astype(f32)
    middle = rest.astype(bf16)
    return high, middle, (rest - middle.astype(f32)).astype(bf16)


def dot(left, right, dims=MM):
    return lax.dot_general(left, right, dims, preferred_element_type=f32)


def dot_split(left, right, dims=MM):
    axis = 1 if dims == TN else 0
    size = left[0].shape[axis]
    if size % 16:
        return (dot(left[0], right[1], dims) + dot(left[1], right[0], dims)) + dot(
            left[0], right[0], dims
        )
    both = dot(jnp.concatenate([left[1], left[0]], axis=axis), right[0], dims)
    return (dot(left[0], right[1], dims) + both[0:size]) + both[size:]


def dot3(left, right, dims=MM):
    return dot_split(split2(left), split2(right), dims)


def dot_left_exact(left, right, dims=MM):
    high, middle, low = split3(right)
    return (dot(left, low, dims) + dot(left, middle, dims)) + dot(left, high, dims)


def dot_right_exact(left, right, dims=MM):
    high, middle, low = split3(left)
    return (dot(low, right, dims) + dot(middle, right, dims)) + dot(high, right, dims)


def softplus(value):
    return jnp.maximum(value, 0.0) + jnp.log1p(jnp.exp(-jnp.abs(value)))


def silu(value):
    return value / (1.0 + jnp.exp(-value))


def rms(value):
    return value * lax.rsqrt(jnp.mean(value * value, axis=-1, keepdims=True) + epsilon)


def fetch(sources, places, semaphores):
    copies = []
    for number, (source, place) in enumerate(zip(sources, places)):
        copies.append(pltpu.make_async_copy(source, place, semaphores.at[number]))
        copies[-1].start()
    return copies


def fetch(sources, places, semaphores):
    copies = []
    for number, (source, place) in enumerate(zip(sources, places)):
        copies.append(pltpu.make_async_copy(source, place, semaphores.at[number]))
        copies[-1].start()
    return copies


PIECES = 1


def tables_kernel(dims, *refs):
    V, D, hl, ch, nh, ns, T, N = dims
    refs = list(refs)

    def take(number):
        taken, refs[:] = refs[:number], refs[number:]
        return taken

    sources = take(9)
    outproj_source, message = take(2)
    places = take(9)
    semaphores = take(1)[0]
    half = ch // 2
    top = top_rows(dims)
    core = lax.rem(lax.axis_index("seq"), 2)
    (inproj, tok, emb, prenorm, stepmap, bias, rates, skip, outnorm) = places
    size = inproj.shape[0] // PIECES
    pieces = [pl.ds(number * size, size) for number in range(PIECES)]
    rows = pl.ds(pl.multiple_of(core * half, 8), half)
    wide = [(place, pl.ds(place * ch, ch)) for place in range(D // ch)]
    copies = fetch(
        [sources[0].at[piece, :] for piece in pieces]
        + sources[1:]
        + [outproj_source.at[rows, columns] for _, columns in wide],
        [inproj.at[piece, :] for piece in pieces]
        + places[1:]
        + [message.at[pl.ds(top + place * half, half), :] for place, _ in wide],
        semaphores,
    )
    flip = (iota((T, 1), 0) + iota((1, T), 1) == T - 1).astype(f32).astype(bf16)
    for copy in copies[PIECES : PIECES + 8]:
        copy.wait()
    normed = split2(rms(emb[...]) * prenorm[...])
    raw_t = dot_split(split2(stepmap[...]), normed, NT)
    tokens = jnp.broadcast_to(tok[...].astype(f32), (8, T)).astype(bf16)
    tokens = dot(tokens, flip)
    for place in range(T // ch):
        message[2 * V + place : 2 * V + place + 1, :] = tokens[0:1, place * ch : (place + 1) * ch]
    row = 2 * V + T // ch
    message[row : row + 1, :] = outnorm[...]
    for head in range(hl):
        line = softplus(raw_t[head : head + 1, :] + bias[:, head : head + 1])
        row = row + 1
        message[row : row + 1, 0:V] = line
        message[row : row + 1, V : 2 * V] = -rates[:, head : head + 1] * line
        message[row : row + 1, 2 * V : 3 * V] = jnp.broadcast_to(skip[:, head : head + 1], (1, V))
    for copy in copies[:PIECES]:
        copy.wait()
    weights = jnp.concatenate(
        [inproj[pl.ds(0, D, stride=2), :], inproj[pl.ds(1, D, stride=2), :]], axis=1
    )
    both = dot_split(normed, split2(weights))
    message[0:V, :] = both[:, 0:ch]
    message[V : 2 * V, :] = both[:, ch:]
    for copy in copies[PIECES + 8 :]:
        copy.wait()


def top_rows(dims):
    V, D, hl, ch, nh, ns, T, N = dims
    return 2 * V + -(-(T // ch + 1 + hl) // 8) * 8


def head_line(dims, values):
    V, D, hl, ch, nh, ns, T, N = dims
    head_of = iota((1, ch), 1) // (ch // hl)
    line = jnp.zeros((1, ch), f32)
    for head in range(hl):
        line = jnp.where(head_of == head, values[:, head : head + 1], line)
    return line


def prepare_kernel(dims, *refs):
    V, D, hl, ch, nh, ns, T, N = dims
    H, P = nh * hl, ch // hl
    refs = list(refs)

    def take(number):
        taken, refs[:] = refs[:number], refs[number:]
        return taken

    sources = take(14)
    pairs, small, choose_out, own_high, own_low = take(5)
    state_high, state_low, rest_high, rest_low, out_high, out_low = take(6)
    triangles, upto, groups, blocks = take(4)
    places = take(14)
    semaphores = take(1)[0]
    copies = fetch(sources, places, semaphores)
    inproj2, statemap2, statemap, outproj, outproj2, emb, prenorm, complement = places[:8]
    prenorm2, stepmap2, bias2, rates2, skip2, outnorm2 = places[8:]
    row, column = iota((T, 1), 0), iota((1, T), 1)
    triangles[:, 0:T] = (row > column).astype(f32).astype(bf16)
    triangles[:, T : 2 * T] = (row < column).astype(f32).astype(bf16)
    triangles[:, 2 * T :] = jnp.ones((T, 128), bf16)
    upto[...] = (row >= column).astype(f32).astype(bf16)
    size = groups.shape[0]
    groups[...] = (iota((size, 1), 0) // P == iota((1, size), 1) // P).astype(f32).astype(bf16)
    rows, columns = blocks.shape
    blocks[...] = (iota((rows, 1), 0) // V == iota((1, columns), 1) // P).astype(f32).astype(bf16)
    for copy in copies:
        copy.wait()
    normed = split2(rms(emb[...]) * prenorm[...])
    write = dot_split(normed, split2(statemap[pl.ds(0, D, stride=2), :]))
    read = dot_split(normed, split2(statemap[pl.ds(1, D, stride=2), :]))
    pairs[...] = dot3(read, jnp.concatenate([write] * H, axis=0), NT)
    own_high[...], own_low[...] = split2(outproj[...])
    choose = (complement[...] == iota((D, 1), 0)).astype(f32).astype(bf16)
    choose_out[...] = choose
    gain = jnp.transpose(jnp.broadcast_to(prenorm2[...], (128, D)))

    def weights(values):
        return split2(dot_left_exact(choose, values))

    gain_wide = gain[:, 0:1]
    inner = inproj2[pl.ds(1, D, stride=2), :] * gain_wide
    step = jnp.transpose(
        jnp.concatenate(
            [jnp.broadcast_to(stepmap2[head : head + 1, :], (P, D)) for head in range(hl)], axis=0
        )
    )
    write2 = statemap2[pl.ds(0, D, stride=2), :] * gain_wide
    state_high[...], state_low[...] = weights(
        jnp.concatenate([inner, step * gain_wide, write2], axis=1)
    )
    gate = inproj2[pl.ds(0, D, stride=2), :] * gain_wide
    read2 = statemap2[pl.ds(1, D, stride=2), :] * gain_wide
    rest_high[...], rest_low[...] = weights(jnp.concatenate([gate, read2], axis=1))
    small[0:1, :] = head_line(dims, bias2)
    small[1:2, :] = head_line(dims, rates2)
    small[2:3, :] = head_line(dims, skip2)
    out_gain = jnp.transpose(jnp.broadcast_to(outnorm2[...], (128, ch)))
    out_high[...], out_low[...] = split2(outproj2[...] * out_gain[:, 0:1])


def shift_rows(value, amount, fill):
    size = value.shape[0]
    if amount % 8 == 0:
        empty = jnp.full((abs(amount),) + value.shape[1:], fill, value.dtype)
        if amount > 0:
            return jnp.concatenate([empty, value[: size - amount]], axis=0)
        return jnp.concatenate([value[-amount:], empty], axis=0)
    rolled = pltpu.roll(value, amount % size, 0)
    row = iota((8,) + value.shape[1:], 0)
    if amount > 0:
        edge = jnp.where(row >= amount, rolled[0:8], fill)
        return jnp.concatenate([edge, rolled[8:]], axis=0)
    edge = jnp.where(row < 8 + amount, rolled[size - 8 :], fill)
    return jnp.concatenate([rolled[: size - 8], edge], axis=0)


def scan_rows(decay, value, sign):
    size = value.shape[0]
    amount = 1
    while amount < size:
        value = value + decay * shift_rows(value, sign * amount, 0.0)
        decay = decay * shift_rows(decay, sign * amount, 1.0)
        amount *= 2
    return value, decay


def mix_kernel(dims, *refs):
    V, D, hl, ch, nh, ns, T, N = dims
    H, LV, P = nh * hl, nh * hl * V, ch // hl
    C = nh * ch
    refs = list(refs)

    def take(number):
        taken, refs[:] = refs[:number], refs[number:]
        return taken

    count = max(ns, nh)
    packets = dict(zip(in_turn(count)[::-1] + [0], take(count)))
    emb, pairs, triangles, groups, blocks = take(5)
    out_high, out_low, out_embedded = take(3)
    tokens = take(1)[0]
    mine = lax.axis_index("seq")

    for k in range(ns):
        block = ns - 1 - lax.bitwise_xor(mine, partners(ns, nh)[k][0])
        row = 2 * V
        pieces = [packets[k][row + place : row + place + 1, :] for place in range(T // ch)]
        tokens[pl.ds(block, 1), :] = jnp.concatenate(pieces, axis=1)

    first = 2 * V + T // ch + 1
    steps = jnp.concatenate(
        [packets[k][first : first + hl, 0 : 3 * V] for k in range(nh)], axis=0
    )
    log_t = steps[:, V : 2 * V]
    narrow = jnp.concatenate([part.astype(f32) for part in split3(steps)], axis=0).astype(bf16)
    spread_heads = (iota((1, LV), 1) // V == iota((3 * H, 1), 0) % H).astype(f32).astype(bf16)
    wide = dot(narrow, spread_heads, TN)
    own = iota((1, LV), 1) % V == iota((V, 1), 0)
    decay_table = jnp.exp(wide[V : 2 * V])
    step_table = jnp.where(own, wide[0:V], 0.0)
    gain_table = jnp.where(own, wide[2 * V : 3 * V], 0.0)
    gates = jnp.concatenate([packets[k][0:V, :] for k in range(nh)], axis=1)
    inners = jnp.concatenate([packets[k][V : 2 * V, :] for k in range(nh)], axis=1)
    gains = jnp.concatenate([packets[k][first - 1 : first, :] for k in range(nh)], axis=1)

    token_row = (iota((LV, 1), 0) % V).astype(f32)
    log_split = jnp.concatenate(split3(log_t), axis=1)
    onehots, logs = [], []
    for block in range(ns):
        onehot = (tokens[block : block + 1, :] == token_row).astype(f32).astype(bf16)
        onehots.append(onehot)
        logs.append(dot(log_split, onehot[0 : 3 * V, :]))
    logs = jnp.concatenate(logs, axis=0)
    size = ns * H
    sums = dot(jnp.concatenate(split3(logs)[::-1], axis=0), triangles[...])
    sums = (sums[0:size] + sums[size : 2 * size]) + sums[2 * size :]
    blocks_of = [sums[block * H : (block + 1) * H] for block in range(ns)]
    weight_up, weight_down = [None] * ns, [None] * ns
    gap = jnp.zeros((H, 128), f32)
    for block in reversed(range(ns)):
        wide = jnp.concatenate([gap] * (T // 128), axis=1)
        weight_up[block] = jnp.where(
            block < mine, jnp.exp(blocks_of[block][:, 0:T] + wide), 0.0
        )
        gap = jnp.where(block < mine, gap + blocks_of[block][:, 2 * T :], gap)
    gap = jnp.zeros((H, 128), f32)
    for block in range(ns):
        wide = jnp.concatenate([gap] * (T // 128), axis=1)
        weight_down[block] = jnp.where(
            block > mine, jnp.exp(blocks_of[block][:, T : 2 * T] + wide), 0.0
        )
        gap = jnp.where(block > mine, gap + blocks_of[block][:, 2 * T :], gap)
    entering = jnp.zeros((4 * H, LV), f32)
    for block in range(ns):
        both = jnp.concatenate([weight_up[block], weight_down[block]], axis=0)
        entering = entering + dot(
            jnp.concatenate(split2(both), axis=0), onehots[block], NT
        )
    entering = entering[2 * H :] + entering[0 : 2 * H]
    diagonal = iota((1, LV), 1) // V == iota((H, 1), 0)
    step_row = jnp.sum(step_table, axis=0, keepdims=True)
    enter_up = step_row * jnp.sum(
        jnp.where(diagonal, entering[0:H], 0.0), axis=0, keepdims=True
    )
    enter_down = step_row * jnp.sum(
        jnp.where(diagonal, entering[H : 2 * H], 0.0), axis=0, keepdims=True
    )

    looked = jnp.concatenate(
        [decay_table, step_table, pairs[...], gain_table, silu(gates), emb[...]], axis=1
    )
    looked = jnp.concatenate(split3(looked), axis=0)
    token = tokens[pl.ds(mine, 1), :]
    onehot = (token == token_row[0 : 3 * V]).astype(f32).astype(bf16)
    rows = dot(onehot, looked, TN)
    decay, step = rows[:, 0:LV], rows[:, LV : 2 * LV]
    pair, gain = rows[:, 2 * LV : 3 * LV], rows[:, 3 * LV : 4 * LV]
    silu_rows = rows[:, 4 * LV : 4 * LV + C]
    out_embedded[...] = rows[:, 4 * LV + C :]

    up, fade = scan_rows(decay, step, 1)
    up = up + fade * enter_up
    down, fade = scan_rows(decay, step, -1)
    down = down + fade * enter_down

    spread_high, spread_low = [
        jnp.concatenate([part] * H, axis=0) * blocks[...] for part in split2(inners)
    ]
    both = jnp.concatenate([up * pair + gain, down * pair + gain], axis=0)
    high = both.astype(bf16)
    high_wide = high.astype(f32)
    low_turned = pltpu.roll(both - high_wide, LV // 2, 1)
    lower = iota((1, LV), 1) < LV // 2
    value = []
    for side in (0, 1):
        mixed = jnp.where(lower == (side == 0), high_wide, low_turned).astype(bf16)
        rows = slice(side * LV // 2, (side + 1) * LV // 2)
        columns = slice(side * C // 2, (side + 1) * C // 2)
        weight, rest = spread_high[rows, columns], spread_low[:, columns]
        value.append(
            dot(
                jnp.concatenate([mixed, high], axis=1),
                jnp.concatenate([weight, weight, rest], axis=0),
            )
        )
    value = jnp.concatenate(value, axis=1)
    value = value * jnp.concatenate([silu_rows, silu_rows], axis=0)
    wide = groups.shape[0]
    high, low = split2(value * value)
    starts = list(range(0, C, wide))
    rows = 2 * T
    stacked = [half[:, start : start + wide] for start in starts for half in (low, high)]
    squares = dot(jnp.concatenate(stacked, axis=0), groups[...])
    for number, start in enumerate(starts):
        place = 2 * number * rows
        square = squares[place : place + rows] + squares[place + rows : place + 2 * rows]
        stop = start + wide
        normed = value[:, start:stop] * lax.rsqrt(square * (1.0 / P) + epsilon)
        out_high[:, start:stop], out_low[:, start:stop] = split2(
            (normed[0:T] + normed[T : 2 * T]) * gains[:, start:stop]
        )


def project_kernel(dims, *refs):
    V, D, hl, ch, nh, ns, T, N = dims
    P = ch // hl
    refs = list(refs)

    def take(number):
        taken, refs[:] = refs[:number], refs[number:]
        return taken

    high, low, embedded, small, own_high, own_low, state_high, state_low, upto = take(9)
    order = in_turn(nh)[::-1]
    nears = dict(zip(order, take(nh - 1)))
    others = dict(zip(order, take(nh - 1)))
    out_state, out_high, out_low, out_scale = take(4)
    out_write, out_inner, out_stepped, out_total = take(4)
    half = ch // 2
    base = top_rows(dims)
    mine = lax.axis_index("seq")

    pieces = []
    for k in range(1, nh):
        near, other = [
            jnp.concatenate(
                [
                    ref[base + place * half : base + (place + 1) * half, :]
                    for place in range(D // ch)
                ],
                axis=1,
            )
            for ref in (nears[k], others[k])
        ]
        even = lax.rem(lax.bitwise_xor(mine, partners(ns, nh)[k][0]), 2) == 0
        pieces.append(jnp.where(even, near, other))
        pieces.append(jnp.where(even, other, near))
    weights = split2(jnp.concatenate(pieces, axis=0))
    weights = (
        jnp.concatenate([own_high[...], weights[0]], axis=0),
        jnp.concatenate([own_low[...], weights[1]], axis=0),
    )
    hidden = embedded[...] + dot_split((high[...], low[...]), weights)
    split = split2(hidden)
    out_high[...], out_low[...] = split
    scale = lax.rsqrt(jnp.mean(hidden * hidden, axis=-1, keepdims=True) + epsilon)
    out_scale[...] = jnp.broadcast_to(scale, (T, ch))

    rows = dot_split(split, (state_high[...], state_low[...])) * scale
    inner, write = rows[:, 0:ch], rows[:, 2 * ch :]
    step = softplus(rows[:, ch : 2 * ch] + small[0:1, :])
    stepped = inner * step
    log_high, log_middle, log_low = split3(-small[1:2, :] * step)
    total = dot(upto[...], jnp.concatenate([log_low, log_middle], axis=1))
    total = (total[:, 0:ch] + total[:, ch:]) + dot(upto[...], log_high)
    end = total[T - 1 : T, :]
    state = dot3(stepped * jnp.exp(end - total), write, TN)
    out_state[0:ch, :] = state
    for head in range(hl):
        out_state[ch + head : ch + head + 1, :] = jnp.broadcast_to(
            end[:, head * P : head * P + 1], (1, N)
        )
    out_write[...] = write
    out_inner[...] = inner
    out_stepped[...] = stepped
    out_total[...] = total


def block_kernel(dims, *refs):
    V, D, hl, ch, nh, ns, T, N = dims
    P = ch // hl
    refs = list(refs)

    def take(number):
        taken, refs[:] = refs[:number], refs[number:]
        return taken

    high, low, scale, write, inner, stepped, total, choose = take(8)
    rest_high, rest_low, small = take(3)
    base, read_high, read_low, out_fade, out_gate, own, hidden_ref = take(7)
    rows = dot_split((high[...], low[...]), (rest_high[...], rest_low[...]))
    out_gate[...] = silu(rows[:, 0:ch] * scale[...])
    read = rows[:, ch:] * scale[...]
    read = split2(read)
    read_high[...], read_low[...] = read
    out_fade[...] = jnp.exp(total[...])
    products = dot_split(read, split2(write[...]), NT)
    stepped_high, stepped_low = split2(stepped[...])
    select = (iota((8, ch), 1) == iota((8, ch), 0) * P).astype(f32).astype(bf16)
    total_high, total_middle, total_low = split3(total[...])
    total_t = (dot(select, total_low, NT) + dot(select, total_middle, NT)) + dot(
        select, total_high, NT
    )
    allowed = iota((T, 1), 0) >= iota((1, T), 1)
    parts = []
    for head in range(hl):
        start, stop = head * P, (head + 1) * P
        differ = total[:, start : start + 1] - total_t[head : head + 1, :]
        weights = jnp.where(allowed, jnp.exp(jnp.where(allowed, differ, 0.0)), 0.0) * products
        part = dot_split(
            split2(weights), (stepped_high[:, start:stop], stepped_low[:, start:stop])
        )
        parts.append(part + small[2:3, start:stop] * inner[:, start:stop])
    base[...] = jnp.concatenate(parts, axis=1)
    share = T // nh
    hidden_ref[...] = high[...].astype(f32) + low[...].astype(f32)
    place = pl.multiple_of(lax.axis_index("head") * share, 8)
    own[...] = dot_right_exact(hidden_ref[pl.ds(place, share), :], choose[...])


def state_rows(dims, values):
    V, D, hl, ch, nh, ns, T, N = dims
    head_of = iota((ch, N), 0) // (ch // hl)
    result = jnp.broadcast_to(values[0:1, :], (ch, N))
    for head in range(1, hl):
        result = jnp.where(head_of == head, values[head : head + 1, :], result)
    return result


def join_kernel(dims, bit, total, prefix, came, out_total, out_prefix):
    V, D, hl, ch, nh, ns, T, N = dims
    later = lax.rem(lax.div(lax.axis_index("seq"), 2**bit), 2) == 1
    came_state, came_log = came[0:ch, :], came[ch : ch + hl, :]
    state, log = total[0:ch, :], total[ch : ch + hl, :]
    factor = jnp.exp(state_rows(dims, jnp.where(later, log, came_log)))
    out_total[0:ch, :] = jnp.where(
        later, factor * came_state + state, factor * state + came_state
    )
    out_total[ch : ch + hl, :] = log + came_log
    if prefix is None:
        out_prefix[0:ch, :] = jnp.where(later, came_state, 0.0)
        out_prefix[ch : ch + hl, :] = jnp.where(later, came_log, 0.0)
    else:
        joined = prefix_joined(dims, bit, prefix, came)
        out_prefix[0:ch, :] = joined
        out_prefix[ch : ch + hl, :] = prefix[ch : ch + hl, :] + jnp.where(later, came_log, 0.0)


def prefix_joined(dims, bit, prefix, came):
    V, D, hl, ch, nh, ns, T, N = dims
    later = lax.rem(lax.div(lax.axis_index("seq"), 2**bit), 2) == 1
    factor = jnp.exp(state_rows(dims, prefix[ch : ch + hl, :]))
    return prefix[0:ch, :] + jnp.where(later, factor * came[0:ch, :], 0.0)


def output_kernel(dims, bit, *refs):
    V, D, hl, ch, nh, ns, T, N = dims
    P = ch // hl
    prefix, came, read_high, read_low, base, fade, gate, own, proj_high, proj_low = refs[:10]
    groups, outs, partial_ref = refs[10], refs[11 : 11 + nh], refs[11 + nh]
    entering = prefix_joined(dims, bit, prefix, came)
    carried = dot_split((read_high[...], read_low[...]), split2(entering), NT)
    value = (base[...] + carried * fade[...]) * gate[...]
    square = dot(jnp.concatenate(split2(value * value), axis=0), groups[0:ch, 0:ch])
    square = square[T:] + square[0:T]
    value = value * lax.rsqrt(square * (1.0 / P) + epsilon)
    share = T // nh
    partial_ref[...] = dot_split(split2(value), (proj_high[...], proj_low[...]))
    mine = lax.axis_index("head")
    for k in range(nh):
        shift = 0 if k == 0 else shifts(nh)[k - 1]
        position = lax.rem(mine, nh // 2) * 2 + lax.div(mine, nh // 2)
        position = lax.rem(position + shift, nh)
        to = lax.div(position, 2) + lax.rem(position, 2) * (nh // 2)
        place = pl.multiple_of(to * share, 8)
        part = partial_ref[pl.ds(place, share), :]
        outs[k][...] = part + own[...] if k == 0 else part


def per_device(
    token_ids,
    embedding,
    complement,
    prenorm_first,
    inproj_first,
    statemap_first,
    stepmap_first,
    stepbias_first,
    rates_first,
    skipgain_first,
    outnorm_first,
    outproj_first,
    prenorm_second,
    inproj_second,
    statemap_second,
    stepmap_second,
    stepbias_second,
    rates_second,
    skipgain_second,
    outnorm_second,
    outproj_second,
):
    nh, ns = lax.axis_size("head"), lax.axis_size("seq")
    V, D = embedding.shape
    ch = inproj_first.shape[2]
    hl = stepmap_first.shape[1]
    N = statemap_first.shape[2]
    T = token_ids.shape[0]
    LV = nh * hl * V
    dims = (V, D, hl, ch, nh, ns, T, N)
    vmem = pl.BlockSpec(memory_space=pltpu.VMEM)
    anywhere = pl.BlockSpec(memory_space=pl.ANY)
    params = pltpu.CompilerParams(vmem_limit_bytes=LIMIT)

    def shape(*sizes, dtype=f32):
        return jax.ShapeDtypeStruct(sizes, dtype)

    def halves(*sizes):
        return [shape(*sizes, dtype=bf16)] * 2

    def room(value):
        return pltpu.VMEM(value.shape, value.dtype)

    def kept(values):
        return [pltpu.with_memory_space_constraint(value, pltpu.HBM) for value in values]

    def line(value):
        return value.reshape(1, -1)

    def flat(value):
        return value.reshape(-1, value.shape[-1])

    heavy = pl.CostEstimate(flops=960 * T * D * D, bytes_accessed=4 * T * D, transcendentals=T * D)

    half = ch // 2
    share = T // nh
    fetched = [
        flat(inproj_first),
        line(token_ids),
        embedding,
        line(prenorm_first),
        stepmap_first.T,
        line(stepbias_first),
        line(rates_first),
        line(skipgain_first),
        line(outnorm_first),
    ]
    message = pl.pallas_call(
        functools.partial(tables_kernel, dims),
        out_shape=pltpu.VMEM((top_rows(dims) + half * (D // ch), ch), f32),
        in_specs=[anywhere] * (len(fetched) + 1),
        out_specs=vmem,
        scratch_shapes=[room(value) for value in fetched]
        + [pltpu.SemaphoreType.DMA((len(fetched) - 1 + PIECES + D // ch,))],
        compiler_params=params,
        name="tables",
    )(*kept([*fetched, outproj_first]))

    prepared = [
        flat(inproj_second),
        flat(statemap_second),
        flat(statemap_first),
        outproj_first,
        outproj_second,
        embedding,
        line(prenorm_first),
        line(complement),
        line(prenorm_second),
        stepmap_second.T,
        line(stepbias_second),
        line(rates_second),
        line(skipgain_second),
        line(outnorm_second),
    ]
    (
        pair_table,
        small,
        choose,
        own_high,
        own_low,
        state_high,
        state_low,
        rest_high,
        rest_low,
        proj_high,
        proj_low,
        triangles,
        upto,
        groups,
        blocks,
    ) = pl.pallas_call(
        functools.partial(prepare_kernel, dims),
        out_shape=(
            shape(V, LV),
            shape(8, ch),
            shape(D, D, dtype=bf16),
            *halves(ch, D),
            *halves(D, 2 * ch + N),
            *halves(D, ch + N),
            *halves(ch, D),
            shape(T, 2 * T + 128, dtype=bf16),
            shape(T, T, dtype=bf16),
            shape(2 * ch, 2 * ch, dtype=bf16),
            shape(LV, nh * ch, dtype=bf16),
        ),
        in_specs=[anywhere] * len(prepared),
        out_specs=(vmem,) * 15,
        scratch_shapes=[room(value) for value in prepared]
        + [pltpu.SemaphoreType.DMA((len(prepared),))],
        compiler_params=params,
        cost_estimate=heavy,
        name="prepare",
    )(*kept(prepared))

    count = max(ns, nh)
    messages = {0: message}
    for k in in_turn(count):
        seq_bits, shift = partners(ns, nh)[k]
        pairs = [
            (seq * nh + head, (seq ^ seq_bits) * nh + moved(head, shift, nh))
            for seq in range(ns)
            for head in range(nh)
        ]
        sent = message if k < nh else message[0 : top_rows(dims)]
        messages[k] = lax.ppermute(sent, ("seq", "head"), pairs)
    swap = [(seq, seq ^ 1) for seq in range(ns)]
    order = in_turn(nh)[::-1]
    others = [lax.ppermute(messages[k], "seq", swap) for k in order]

    mixed_high, mixed_low, embedded = pl.pallas_call(
        functools.partial(mix_kernel, dims),
        out_shape=(*halves(T, nh * ch), shape(T, D)),
        in_specs=[vmem] * (count + 5),
        out_specs=(vmem,) * 3,
        scratch_shapes=[pltpu.VMEM((max(ns, 8), T), f32)],
        compiler_params=params,
        cost_estimate=heavy,
        name="mix",
    )(
        *[messages[k] for k in in_turn(count)[::-1] + [0]],
        embedding,
        pair_table,
        triangles,
        groups,
        blocks,
    )

    state, hidden_high, hidden_low, scale, write, inner, stepped, total = pl.pallas_call(
        functools.partial(project_kernel, dims),
        out_shape=(
            shape(ch + 8, N),
            *halves(T, D),
            shape(T, ch),
            shape(T, N),
            shape(T, ch),
            shape(T, ch),
            shape(T, ch),
        ),
        in_specs=[vmem] * (9 + 2 * (nh - 1)),
        out_specs=(vmem,) * 8,
        compiler_params=params,
        name="project",
    )(
        mixed_high,
        mixed_low,
        embedded,
        small,
        own_high,
        own_low,
        state_high,
        state_low,
        upto,
        *[messages[k] for k in order],
        *others,
    )

    base, read_high, read_low, fade, gate, own = pl.pallas_call(
        functools.partial(block_kernel, dims),
        out_shape=(
            shape(T, ch),
            *halves(T, N),
            shape(T, ch),
            shape(T, ch),
            shape(share, D),
        ),
        in_specs=[vmem] * 11,
        out_specs=(vmem,) * 6,
        scratch_shapes=[pltpu.VMEM((T, D), f32)],
        compiler_params=params,
        cost_estimate=heavy,
        name="block",
    )(
        hidden_high,
        hidden_low,
        scale,
        write,
        inner,
        stepped,
        total,
        choose,
        rest_high,
        rest_low,
        small,
    )

    prefix = None
    bits = ns.bit_length() - 1
    for bit in range(bits):
        pairs = [
            (seq, seq ^ 2**bit) for seq in range(ns) if bit < bits - 1 or not seq & 2**bit
        ]
        came = lax.ppermute(state, "seq", pairs)
        if bit == bits - 1:
            break
        given = [state] + ([] if prefix is None else [prefix]) + [came]

        def join(bit, known, *refs):
            if known:
                join_kernel(dims, bit, *refs)
            else:
                join_kernel(dims, bit, refs[0], None, *refs[1:])

        state, prefix = pl.pallas_call(
            functools.partial(join, bit, prefix is not None),
            out_shape=(shape(ch + 8, N),) * 2,
            in_specs=[vmem] * len(given),
            out_specs=(vmem,) * 2,
            compiler_params=params,
            name="join",
        )(*given)
    if prefix is None:
        prefix = jnp.zeros_like(state)

    parts = pl.pallas_call(
        functools.partial(output_kernel, dims, bits - 1),
        out_shape=(shape(share, D),) * nh,
        in_specs=[vmem] * 11,
        out_specs=(vmem,) * nh,
        scratch_shapes=[pltpu.VMEM((T, D), f32)],
        compiler_params=params,
        name="output",
    )(
        prefix,
        came,
        read_high,
        read_low,
        base,
        fade,
        gate,
        own,
        proj_high,
        proj_low,
        groups,
    )
    result = parts[0]
    for k in in_turn(nh):
        shift = shifts(nh)[k - 1]
        pairs = [(source, moved(source, shift, nh)) for source in range(nh)]
        result = result + lax.ppermute(parts[k], "head", pairs)
    return result


def solution(mesh):
    return jax.shard_map(
        per_device,
        mesh=mesh,
        in_specs=(
            P(("rep", "seq")),
            P(),
            P(),
            P(),
            P(None, None, "head"),
            P(),
            P(None, "head"),
            P("head"),
            P("head"),
            P("head"),
            P("head"),
            P("head", None),
            P(),
            P(None, None, "head"),
            P(),
            P(None, "head"),
            P("head"),
            P("head"),
            P("head"),
            P("head"),
            P("head", None),
        ),
        out_specs=P(("rep", "seq", "head"), None),
        check_vma=False,
    )
```

```python
import functools

import jax
import jax.numpy as jnp
from jax import lax
from jax.experimental import pallas as pl
from jax.experimental.pallas import tpu as pltpu
from jax.sharding import PartitionSpec as P

epsilon = 1e-05
f32 = jnp.float32
bf16 = jnp.bfloat16
LIMIT = 48 * 1024 * 1024

MM = (((1,), (0,)), ((), ()))
NT = (((1,), (1,)), ((), ()))
TN = (((0,), (0,)), ((), ()))


def partners(ns, nh):
    count = max(ns, nh)
    return [((ns - k) if 0 < k < ns else 0, k if k < nh else 0) for k in range(count)]


def in_turn(count):
    return sorted(range(1, count), key=lambda k: (-k.bit_length(), k))


def iota(shape, axis):
    return lax.broadcasted_iota(jnp.int32, shape, axis)


def split2(value):
    high = value.astype(bf16)
    return high, (value - high.astype(f32)).astype(bf16)


def split3(value):
    high = value.astype(bf16)
    rest = value - high.astype(f32)
    middle = rest.astype(bf16)
    return high, middle, (rest - middle.astype(f32)).astype(bf16)


def dot(left, right, dims=MM):
    return lax.dot_general(left, right, dims, preferred_element_type=f32)


def dot_split(left, right, dims=MM):
    axis = 1 if dims == TN else 0
    size = left[0].shape[axis]
    if size % 16:
        return (dot(left[0], right[1], dims) + dot(left[1], right[0], dims)) + dot(
            left[0], right[0], dims
        )
    both = dot(jnp.concatenate([left[1], left[0]], axis=axis), right[0], dims)
    return (dot(left[0], right[1], dims) + both[0:size]) + both[size:]


def dot3(left, right, dims=MM):
    return dot_split(split2(left), split2(right), dims)


def dot_left_exact(left, right, dims=MM):
    high, middle, low = split3(right)
    return (dot(left, low, dims) + dot(left, middle, dims)) + dot(left, high, dims)


def dot_right_exact(left, right, dims=MM):
    high, middle, low = split3(left)
    return (dot(low, right, dims) + dot(middle, right, dims)) + dot(high, right, dims)


def softplus(value):
    return jnp.maximum(value, 0.0) + jnp.log1p(jnp.exp(-jnp.abs(value)))


def silu(value):
    return value / (1.0 + jnp.exp(-value))


def rms(value):
    return value * lax.rsqrt(jnp.mean(value * value, axis=-1, keepdims=True) + epsilon)


def fetch(sources, places, semaphores):
    copies = []
    for number, (source, place) in enumerate(zip(sources, places)):
        copies.append(pltpu.make_async_copy(source, place, semaphores.at[number]))
        copies[-1].start()
    return copies


def fetch(sources, places, semaphores):
    copies = []
    for number, (source, place) in enumerate(zip(sources, places)):
        copies.append(pltpu.make_async_copy(source, place, semaphores.at[number]))
        copies[-1].start()
    return copies


PIECES = 1


def tables_kernel(dims, *refs):
    V, D, hl, ch, nh, ns, T, N = dims
    refs = list(refs)

    def take(number):
        taken, refs[:] = refs[:number], refs[number:]
        return taken

    sources = take(9)
    outproj_source, message = take(2)
    places = take(9)
    semaphores = take(1)[0]
    half = ch // 2
    top = top_rows(dims)
    core = lax.rem(lax.axis_index("seq"), 2)
    (inproj, tok, emb, prenorm, stepmap, bias, rates, skip, outnorm) = places
    size = inproj.shape[0] // PIECES
    pieces = [pl.ds(number * size, size) for number in range(PIECES)]
    rows = pl.ds(pl.multiple_of(core * half, 8), half)
    wide = [(place, pl.ds(place * ch, ch)) for place in range(D // ch)]
    copies = fetch(
        [sources[0].at[piece, :] for piece in pieces]
        + sources[1:]
        + [outproj_source.at[rows, columns] for _, columns in wide],
        [inproj.at[piece, :] for piece in pieces]
        + places[1:]
        + [message.at[pl.ds(top + place * half, half), :] for place, _ in wide],
        semaphores,
    )
    flip = (iota((T, 1), 0) + iota((1, T), 1) == T - 1).astype(f32).astype(bf16)
    for copy in copies[PIECES : PIECES + 8]:
        copy.wait()
    normed = split2(rms(emb[...]) * prenorm[...])
    raw_t = dot_split(split2(stepmap[...]), normed, NT)
    tokens = jnp.broadcast_to(tok[...].astype(f32), (8, T)).astype(bf16)
    tokens = dot(tokens, flip)
    for place in range(T // ch):
        message[2 * V + place : 2 * V + place + 1, :] = tokens[0:1, place * ch : (place + 1) * ch]
    row = 2 * V + T // ch
    message[row : row + 1, :] = outnorm[...]
    for head in range(hl):
        line = softplus(raw_t[head : head + 1, :] + bias[:, head : head + 1])
        row = row + 1
        message[row : row + 1, 0:V] = line
        message[row : row + 1, V : 2 * V] = -rates[:, head : head + 1] * line
        message[row : row + 1, 2 * V : 3 * V] = jnp.broadcast_to(skip[:, head : head + 1], (1, V))
    for copy in copies[:PIECES]:
        copy.wait()
    weights = jnp.concatenate(
        [inproj[pl.ds(0, D, stride=2), :], inproj[pl.ds(1, D, stride=2), :]], axis=1
    )
    both = dot_split(normed, split2(weights))
    message[0:V, :] = both[:, 0:ch]
    message[V : 2 * V, :] = both[:, ch:]
    for copy in copies[PIECES + 8 :]:
        copy.wait()


def top_rows(dims):
    V, D, hl, ch, nh, ns, T, N = dims
    return 2 * V + -(-(T // ch + 1 + hl) // 8) * 8


def head_line(dims, values):
    V, D, hl, ch, nh, ns, T, N = dims
    head_of = iota((1, ch), 1) // (ch // hl)
    line = jnp.zeros((1, ch), f32)
    for head in range(hl):
        line = jnp.where(head_of == head, values[:, head : head + 1], line)
    return line


def prepare_kernel(dims, *refs):
    V, D, hl, ch, nh, ns, T, N = dims
    H, P = nh * hl, ch // hl
    refs = list(refs)

    def take(number):
        taken, refs[:] = refs[:number], refs[number:]
        return taken

    sources = take(14)
    pairs, small, choose_out, own_high, own_low = take(5)
    state_high, state_low, rest_high, rest_low, out_high, out_low = take(6)
    triangles, upto, groups, blocks = take(4)
    places = take(14)
    semaphores = take(1)[0]
    copies = fetch(sources, places, semaphores)
    inproj2, statemap2, statemap, outproj, outproj2, emb, prenorm, complement = places[:8]
    prenorm2, stepmap2, bias2, rates2, skip2, outnorm2 = places[8:]
    row, column = iota((T, 1), 0), iota((1, T), 1)
    triangles[:, 0:T] = (row > column).astype(f32).astype(bf16)
    triangles[:, T : 2 * T] = (row < column).astype(f32).astype(bf16)
    triangles[:, 2 * T :] = jnp.ones((T, 128), bf16)
    upto[...] = (row >= column).astype(f32).astype(bf16)
    size = groups.shape[0]
    groups[...] = (iota((size, 1), 0) // P == iota((1, size), 1) // P).astype(f32).astype(bf16)
    rows, columns = blocks.shape
    blocks[...] = (iota((rows, 1), 0) // V == iota((1, columns), 1) // P).astype(f32).astype(bf16)
    for copy in copies:
        copy.wait()
    normed = split2(rms(emb[...]) * prenorm[...])
    write = dot_split(normed, split2(statemap[pl.ds(0, D, stride=2), :]))
    read = dot_split(normed, split2(statemap[pl.ds(1, D, stride=2), :]))
    pairs[...] = dot3(read, jnp.concatenate([write] * H, axis=0), NT)
    own_high[...], own_low[...] = split2(outproj[...])
    choose = (complement[...] == iota((D, 1), 0)).astype(f32).astype(bf16)
    choose_out[...] = choose
    gain = jnp.transpose(jnp.broadcast_to(prenorm2[...], (128, D)))

    def weights(values):
        return split2(dot_left_exact(choose, values))

    gain_wide = gain[:, 0:1]
    inner = inproj2[pl.ds(1, D, stride=2), :] * gain_wide
    step = jnp.transpose(
        jnp.concatenate(
            [jnp.broadcast_to(stepmap2[head : head + 1, :], (P, D)) for head in range(hl)], axis=0
        )
    )
    write2 = statemap2[pl.ds(0, D, stride=2), :] * gain_wide
    state_high[...], state_low[...] = weights(
        jnp.concatenate([inner, step * gain_wide, write2], axis=1)
    )
    gate = inproj2[pl.ds(0, D, stride=2), :] * gain_wide
    read2 = statemap2[pl.ds(1, D, stride=2), :] * gain_wide
    rest_high[...], rest_low[...] = weights(jnp.concatenate([gate, read2], axis=1))
    small[0:1, :] = head_line(dims, bias2)
    small[1:2, :] = head_line(dims, rates2)
    small[2:3, :] = head_line(dims, skip2)
    out_gain = jnp.transpose(jnp.broadcast_to(outnorm2[...], (128, ch)))
    out_high[...], out_low[...] = split2(outproj2[...] * out_gain[:, 0:1])


def shift_rows(value, amount, fill):
    size = value.shape[0]
    if amount % 8 == 0:
        empty = jnp.full((abs(amount),) + value.shape[1:], fill, value.dtype)
        if amount > 0:
            return jnp.concatenate([empty, value[: size - amount]], axis=0)
        return jnp.concatenate([value[-amount:], empty], axis=0)
    rolled = pltpu.roll(value, amount % size, 0)
    row = iota((8,) + value.shape[1:], 0)
    if amount > 0:
        edge = jnp.where(row >= amount, rolled[0:8], fill)
        return jnp.concatenate([edge, rolled[8:]], axis=0)
    edge = jnp.where(row < 8 + amount, rolled[size - 8 :], fill)
    return jnp.concatenate([rolled[: size - 8], edge], axis=0)


def scan_rows(decay, value, sign):
    size = value.shape[0]
    amount = 1
    while amount < size:
        value = value + decay * shift_rows(value, sign * amount, 0.0)
        decay = decay * shift_rows(decay, sign * amount, 1.0)
        amount *= 2
    return value, decay


def mix_kernel(dims, *refs):
    V, D, hl, ch, nh, ns, T, N = dims
    H, LV, P = nh * hl, nh * hl * V, ch // hl
    C = nh * ch
    refs = list(refs)

    def take(number):
        taken, refs[:] = refs[:number], refs[number:]
        return taken

    count = max(ns, nh)
    packets = dict(zip(in_turn(count)[::-1] + [0], take(count)))
    emb, pairs, triangles, groups, blocks = take(5)
    out_high, out_low, out_embedded = take(3)
    tokens = take(1)[0]
    mine = lax.axis_index("seq")

    for k in range(ns):
        block = ns - 1 - lax.bitwise_xor(mine, partners(ns, nh)[k][0])
        row = 2 * V
        pieces = [packets[k][row + place : row + place + 1, :] for place in range(T // ch)]
        tokens[pl.ds(block, 1), :] = jnp.concatenate(pieces, axis=1)

    first = 2 * V + T // ch + 1
    steps = jnp.concatenate(
        [packets[k][first : first + hl, 0 : 3 * V] for k in range(nh)], axis=0
    )
    log_t = steps[:, V : 2 * V]
    narrow = jnp.concatenate([part.astype(f32) for part in split3(steps)], axis=0).astype(bf16)
    spread_heads = (iota((1, LV), 1) // V == iota((3 * H, 1), 0) % H).astype(f32).astype(bf16)
    wide = dot(narrow, spread_heads, TN)
    own = iota((1, LV), 1) % V == iota((V, 1), 0)
    decay_table = jnp.exp(wide[V : 2 * V])
    step_table = jnp.where(own, wide[0:V], 0.0)
    gain_table = jnp.where(own, wide[2 * V : 3 * V], 0.0)
    gates = jnp.concatenate([packets[k][0:V, :] for k in range(nh)], axis=1)
    inners = jnp.concatenate([packets[k][V : 2 * V, :] for k in range(nh)], axis=1)
    gains = jnp.concatenate([packets[k][first - 1 : first, :] for k in range(nh)], axis=1)

    token_row = (iota((LV, 1), 0) % V).astype(f32)
    log_split = jnp.concatenate(split3(log_t), axis=1)
    onehots, logs = [], []
    for block in range(ns):
        onehot = (tokens[block : block + 1, :] == token_row).astype(f32).astype(bf16)
        onehots.append(onehot)
        logs.append(dot(log_split, onehot[0 : 3 * V, :]))
    logs = jnp.concatenate(logs, axis=0)
    size = ns * H
    sums = dot(jnp.concatenate(split3(logs)[::-1], axis=0), triangles[...])
    sums = (sums[0:size] + sums[size : 2 * size]) + sums[2 * size :]
    blocks_of = [sums[block * H : (block + 1) * H] for block in range(ns)]
    weight_up, weight_down = [None] * ns, [None] * ns
    gap = jnp.zeros((H, 128), f32)
    for block in reversed(range(ns)):
        wide = jnp.concatenate([gap] * (T // 128), axis=1)
        weight_up[block] = jnp.where(
            block < mine, jnp.exp(blocks_of[block][:, 0:T] + wide), 0.0
        )
        gap = jnp.where(block < mine, gap + blocks_of[block][:, 2 * T :], gap)
    gap = jnp.zeros((H, 128), f32)
    for block in range(ns):
        wide = jnp.concatenate([gap] * (T // 128), axis=1)
        weight_down[block] = jnp.where(
            block > mine, jnp.exp(blocks_of[block][:, T : 2 * T] + wide), 0.0
        )
        gap = jnp.where(block > mine, gap + blocks_of[block][:, 2 * T :], gap)
    entering = jnp.zeros((4 * H, LV), f32)
    for block in range(ns):
        both = jnp.concatenate([weight_up[block], weight_down[block]], axis=0)
        entering = entering + dot(
            jnp.concatenate(split2(both), axis=0), onehots[block], NT
        )
    entering = entering[2 * H :] + entering[0 : 2 * H]
    diagonal = iota((1, LV), 1) // V == iota((H, 1), 0)
    step_row = jnp.sum(step_table, axis=0, keepdims=True)
    enter_up = step_row * jnp.sum(
        jnp.where(diagonal, entering[0:H], 0.0), axis=0, keepdims=True
    )
    enter_down = step_row * jnp.sum(
        jnp.where(diagonal, entering[H : 2 * H], 0.0), axis=0, keepdims=True
    )

    looked = jnp.concatenate(
        [decay_table, step_table, pairs[...], gain_table, silu(gates), emb[...]], axis=1
    )
    looked = jnp.concatenate(split3(looked), axis=0)
    token = tokens[pl.ds(mine, 1), :]
    onehot = (token == token_row[0 : 3 * V]).astype(f32).astype(bf16)
    rows = dot(onehot, looked, TN)
    decay, step = rows[:, 0:LV], rows[:, LV : 2 * LV]
    pair, gain = rows[:, 2 * LV : 3 * LV], rows[:, 3 * LV : 4 * LV]
    silu_rows = rows[:, 4 * LV : 4 * LV + C]
    out_embedded[...] = rows[:, 4 * LV + C :]

    up, fade = scan_rows(decay, step, 1)
    up = up + fade * enter_up
    down, fade = scan_rows(decay, step, -1)
    down = down + fade * enter_down

    spread_high, spread_low = [
        jnp.concatenate([part] * H, axis=0) * blocks[...] for part in split2(inners)
    ]
    both = jnp.concatenate([up * pair + gain, down * pair + gain], axis=0)
    high = both.astype(bf16)
    high_wide = high.astype(f32)
    low_turned = pltpu.roll(both - high_wide, LV // 2, 1)
    lower = iota((1, LV), 1) < LV // 2
    value = []
    for side in (0, 1):
        mixed = jnp.where(lower == (side == 0), high_wide, low_turned).astype(bf16)
        rows = slice(side * LV // 2, (side + 1) * LV // 2)
        columns = slice(side * C // 2, (side + 1) * C // 2)
        weight, rest = spread_high[rows, columns], spread_low[:, columns]
        value.append(
            dot(
                jnp.concatenate([mixed, high], axis=1),
                jnp.concatenate([weight, weight, rest], axis=0),
            )
        )
    value = jnp.concatenate(value, axis=1)
    value = value * jnp.concatenate([silu_rows, silu_rows], axis=0)
    wide = groups.shape[0]
    high, low = split2(value * value)
    starts = list(range(0, C, wide))
    rows = 2 * T
    stacked = [half[:, start : start + wide] for start in starts for half in (low, high)]
    squares = dot(jnp.concatenate(stacked, axis=0), groups[...])
    for number, start in enumerate(starts):
        place = 2 * number * rows
        square = squares[place : place + rows] + squares[place + rows : place + 2 * rows]
        stop = start + wide
        normed = value[:, start:stop] * lax.rsqrt(square * (1.0 / P) + epsilon)
        out_high[:, start:stop], out_low[:, start:stop] = split2(
            (normed[0:T] + normed[T : 2 * T]) * gains[:, start:stop]
        )


def project_kernel(dims, *refs):
    V, D, hl, ch, nh, ns, T, N = dims
    P = ch // hl
    refs = list(refs)

    def take(number):
        taken, refs[:] = refs[:number], refs[number:]
        return taken

    high, low, embedded, small, own_high, own_low, state_high, state_low, upto = take(9)
    order = in_turn(nh)[::-1]
    nears = dict(zip(order, take(nh - 1)))
    others = dict(zip(order, take(nh - 1)))
    out_state, out_high, out_low, out_scale = take(4)
    out_write, out_inner, out_stepped, out_total = take(4)
    half = ch // 2
    base = top_rows(dims)
    mine = lax.axis_index("seq")

    pieces = []
    for k in range(1, nh):
        near, other = [
            jnp.concatenate(
                [
                    ref[base + place * half : base + (place + 1) * half, :]
                    for place in range(D // ch)
                ],
                axis=1,
            )
            for ref in (nears[k], others[k])
        ]
        even = lax.rem(lax.bitwise_xor(mine, partners(ns, nh)[k][0]), 2) == 0
        pieces.append(jnp.where(even, near, other))
        pieces.append(jnp.where(even, other, near))
    weights = split2(jnp.concatenate(pieces, axis=0))
    weights = (
        jnp.concatenate([own_high[...], weights[0]], axis=0),
        jnp.concatenate([own_low[...], weights[1]], axis=0),
    )
    hidden = embedded[...] + dot_split((high[...], low[...]), weights)
    split = split2(hidden)
    out_high[...], out_low[...] = split
    scale = lax.rsqrt(jnp.mean(hidden * hidden, axis=-1, keepdims=True) + epsilon)
    out_scale[...] = jnp.broadcast_to(scale, (T, ch))

    rows = dot_split(split, (state_high[...], state_low[...])) * scale
    inner, write = rows[:, 0:ch], rows[:, 2 * ch :]
    step = softplus(rows[:, ch : 2 * ch] + small[0:1, :])
    stepped = inner * step
    log_high, log_middle, log_low = split3(-small[1:2, :] * step)
    total = dot(upto[...], jnp.concatenate([log_low, log_middle], axis=1))
    total = (total[:, 0:ch] + total[:, ch:]) + dot(upto[...], log_high)
    end = total[T - 1 : T, :]
    state = dot3(stepped * jnp.exp(end - total), write, TN)
    out_state[0:ch, :] = state
    for head in range(hl):
        out_state[ch + head : ch + head + 1, :] = jnp.broadcast_to(
            end[:, head * P : head * P + 1], (1, N)
        )
    out_write[...] = write
    out_inner[...] = inner
    out_stepped[...] = stepped
    out_total[...] = total


def block_kernel(dims, *refs):
    V, D, hl, ch, nh, ns, T, N = dims
    P = ch // hl
    refs = list(refs)

    def take(number):
        taken, refs[:] = refs[:number], refs[number:]
        return taken

    high, low, scale, write, inner, stepped, total, choose = take(8)
    rest_high, rest_low, small = take(3)
    base, read_high, read_low, out_fade, out_gate, own, hidden_ref = take(7)
    rows = dot_split((high[...], low[...]), (rest_high[...], rest_low[...]))
    out_gate[...] = silu(rows[:, 0:ch] * scale[...])
    read = rows[:, ch:] * scale[...]
    read = split2(read)
    read_high[...], read_low[...] = read
    out_fade[...] = jnp.exp(total[...])
    products = dot_split(read, split2(write[...]), NT)
    stepped_high, stepped_low = split2(stepped[...])
    select = (iota((8, ch), 1) == iota((8, ch), 0) * P).astype(f32).astype(bf16)
    total_high, total_middle, total_low = split3(total[...])
    total_t = (dot(select, total_low, NT) + dot(select, total_middle, NT)) + dot(
        select, total_high, NT
    )
    allowed = iota((T, 1), 0) >= iota((1, T), 1)
    parts = []
    for head in range(hl):
        start, stop = head * P, (head + 1) * P
        differ = total[:, start : start + 1] - total_t[head : head + 1, :]
        weights = jnp.where(allowed, jnp.exp(jnp.where(allowed, differ, 0.0)), 0.0) * products
        part = dot_split(
            split2(weights), (stepped_high[:, start:stop], stepped_low[:, start:stop])
        )
        parts.append(part + small[2:3, start:stop] * inner[:, start:stop])
    base[...] = jnp.concatenate(parts, axis=1)
    share = T // nh
    hidden_ref[...] = high[...].astype(f32) + low[...].astype(f32)
    place = pl.multiple_of(lax.axis_index("head") * share, 8)
    own[...] = dot_right_exact(hidden_ref[pl.ds(place, share), :], choose[...])


def state_rows(dims, values):
    V, D, hl, ch, nh, ns, T, N = dims
    head_of = iota((ch, N), 0) // (ch // hl)
    result = jnp.broadcast_to(values[0:1, :], (ch, N))
    for head in range(1, hl):
        result = jnp.where(head_of == head, values[head : head + 1, :], result)
    return result


def join_kernel(dims, bit, total, prefix, came, out_total, out_prefix):
    V, D, hl, ch, nh, ns, T, N = dims
    later = lax.rem(lax.div(lax.axis_index("seq"), 2**bit), 2) == 1
    came_state, came_log = came[0:ch, :], came[ch : ch + hl, :]
    state, log = total[0:ch, :], total[ch : ch + hl, :]
    factor = jnp.exp(state_rows(dims, jnp.where(later, log, came_log)))
    out_total[0:ch, :] = jnp.where(
        later, factor * came_state + state, factor * state + came_state
    )
    out_total[ch : ch + hl, :] = log + came_log
    if prefix is None:
        out_prefix[0:ch, :] = jnp.where(later, came_state, 0.0)
        out_prefix[ch : ch + hl, :] = jnp.where(later, came_log, 0.0)
    else:
        joined = prefix_joined(dims, bit, prefix, came)
        out_prefix[0:ch, :] = joined
        out_prefix[ch : ch + hl, :] = prefix[ch : ch + hl, :] + jnp.where(later, came_log, 0.0)


def prefix_joined(dims, bit, prefix, came):
    V, D, hl, ch, nh, ns, T, N = dims
    later = lax.rem(lax.div(lax.axis_index("seq"), 2**bit), 2) == 1
    factor = jnp.exp(state_rows(dims, prefix[ch : ch + hl, :]))
    return prefix[0:ch, :] + jnp.where(later, factor * came[0:ch, :], 0.0)


def entering_state(dims, bit, prefix, came):
    V, D, hl, ch, nh, ns, T, N = dims
    place = lax.rem(lax.div(lax.axis_index("seq"), 2**bit), 2 ** (len(came) // 2 + 1))
    odd = lax.rem(place, 2) == 1

    def fade(value):
        return jnp.exp(state_rows(dims, value))

    nearest, log = came[0][0:ch, :], came[0][ch : ch + hl, :]
    if len(came) > 1:
        nearest = jnp.where(odd, nearest, came[2][0:ch, :])
        log = jnp.where(odd, log, came[2][ch : ch + hl, :])
    entering = jnp.where(place > 0, nearest, 0.0)
    if len(came) > 1:
        second = jnp.where(place > 1, came[1][0:ch, :], 0.0)
        third = jnp.where(place > 2, came[2][0:ch, :], 0.0)
        entering = entering + fade(log) * (second + fade(came[1][ch : ch + hl, :]) * third)
    if prefix is not None:
        entering = prefix[0:ch, :] + fade(prefix[ch : ch + hl, :]) * entering
    return entering


def output_kernel(dims, bit, known, number, *refs):
    V, D, hl, ch, nh, ns, T, N = dims
    P = ch // hl
    came, refs = refs[:number], refs[number:]
    prefix, refs = (refs[0], refs[1:]) if known else (None, refs)
    read_high, read_low, base, fade, gate, own, proj_high, proj_low, groups = refs[:9]
    outs, partial_ref = refs[9 : 9 + nh], refs[9 + nh]
    entering = entering_state(dims, bit, prefix, came)
    carried = dot_split((read_high[...], read_low[...]), split2(entering), NT)
    value = (base[...] + carried * fade[...]) * gate[...]
    square = dot(jnp.concatenate(split2(value * value), axis=0), groups[0:ch, 0:ch])
    square = square[T:] + square[0:T]
    value = value * lax.rsqrt(square * (1.0 / P) + epsilon)
    share = T // nh
    partial_ref[...] = dot_split(split2(value), (proj_high[...], proj_low[...]))
    mine = lax.axis_index("head")
    for k in range(nh):
        place = pl.multiple_of(lax.bitwise_xor(mine, k) * share, 8)
        part = partial_ref[pl.ds(place, share), :]
        outs[k][...] = part + own[...] if k == 0 else part


def per_device(
    token_ids,
    embedding,
    complement,
    prenorm_first,
    inproj_first,
    statemap_first,
    stepmap_first,
    stepbias_first,
    rates_first,
    skipgain_first,
    outnorm_first,
    outproj_first,
    prenorm_second,
    inproj_second,
    statemap_second,
    stepmap_second,
    stepbias_second,
    rates_second,
    skipgain_second,
    outnorm_second,
    outproj_second,
):
    nh, ns = lax.axis_size("head"), lax.axis_size("seq")
    V, D = embedding.shape
    ch = inproj_first.shape[2]
    hl = stepmap_first.shape[1]
    N = statemap_first.shape[2]
    T = token_ids.shape[0]
    LV = nh * hl * V
    dims = (V, D, hl, ch, nh, ns, T, N)
    vmem = pl.BlockSpec(memory_space=pltpu.VMEM)
    anywhere = pl.BlockSpec(memory_space=pl.ANY)
    params = pltpu.CompilerParams(vmem_limit_bytes=LIMIT)

    def shape(*sizes, dtype=f32):
        return jax.ShapeDtypeStruct(sizes, dtype)

    def halves(*sizes):
        return [shape(*sizes, dtype=bf16)] * 2

    def room(value):
        return pltpu.VMEM(value.shape, value.dtype)

    def kept(values):
        return [pltpu.with_memory_space_constraint(value, pltpu.HBM) for value in values]

    def line(value):
        return value.reshape(1, -1)

    def flat(value):
        return value.reshape(-1, value.shape[-1])

    heavy = pl.CostEstimate(flops=960 * T * D * D, bytes_accessed=4 * T * D, transcendentals=T * D)

    half = ch // 2
    share = T // nh
    fetched = [
        flat(inproj_first),
        line(token_ids),
        embedding,
        line(prenorm_first),
        stepmap_first.T,
        line(stepbias_first),
        line(rates_first),
        line(skipgain_first),
        line(outnorm_first),
    ]
    message = pl.pallas_call(
        functools.partial(tables_kernel, dims),
        out_shape=pltpu.VMEM((top_rows(dims) + half * (D // ch), ch), f32),
        in_specs=[anywhere] * (len(fetched) + 1),
        out_specs=vmem,
        scratch_shapes=[room(value) for value in fetched]
        + [pltpu.SemaphoreType.DMA((len(fetched) - 1 + PIECES + D // ch,))],
        compiler_params=params,
        name="tables",
    )(*kept([*fetched, outproj_first]))

    prepared = [
        flat(inproj_second),
        flat(statemap_second),
        flat(statemap_first),
        outproj_first,
        outproj_second,
        embedding,
        line(prenorm_first),
        line(complement),
        line(prenorm_second),
        stepmap_second.T,
        line(stepbias_second),
        line(rates_second),
        line(skipgain_second),
        line(outnorm_second),
    ]
    (
        pair_table,
        small,
        choose,
        own_high,
        own_low,
        state_high,
        state_low,
        rest_high,
        rest_low,
        proj_high,
        proj_low,
        triangles,
        upto,
        groups,
        blocks,
    ) = pl.pallas_call(
        functools.partial(prepare_kernel, dims),
        out_shape=(
            shape(V, LV),
            shape(8, ch),
            shape(D, D, dtype=bf16),
            *halves(ch, D),
            *halves(D, 2 * ch + N),
            *halves(D, ch + N),
            *halves(ch, D),
            shape(T, 2 * T + 128, dtype=bf16),
            shape(T, T, dtype=bf16),
            shape(2 * ch, 2 * ch, dtype=bf16),
            shape(LV, nh * ch, dtype=bf16),
        ),
        in_specs=[anywhere] * len(prepared),
        out_specs=(vmem,) * 15,
        scratch_shapes=[room(value) for value in prepared]
        + [pltpu.SemaphoreType.DMA((len(prepared),))],
        compiler_params=params,
        cost_estimate=heavy,
        name="prepare",
    )(*kept(prepared))

    count = max(ns, nh)
    messages = {0: message}
    for k in in_turn(count):
        seq_bits, head_bits = partners(ns, nh)[k]
        pairs = [
            (seq * nh + head, (seq ^ seq_bits) * nh + (head ^ head_bits))
            for seq in range(ns)
            for head in range(nh)
        ]
        sent = message if k < nh else message[0 : top_rows(dims)]
        messages[k] = lax.ppermute(sent, ("seq", "head"), pairs)
    swap = [(seq, seq ^ 1) for seq in range(ns)]
    order = in_turn(nh)[::-1]
    others = [lax.ppermute(messages[k], "seq", swap) for k in order]

    mixed_high, mixed_low, embedded = pl.pallas_call(
        functools.partial(mix_kernel, dims),
        out_shape=(*halves(T, nh * ch), shape(T, D)),
        in_specs=[vmem] * (count + 5),
        out_specs=(vmem,) * 3,
        scratch_shapes=[pltpu.VMEM((max(ns, 8), T), f32)],
        compiler_params=params,
        cost_estimate=heavy,
        name="mix",
    )(
        *[messages[k] for k in in_turn(count)[::-1] + [0]],
        embedding,
        pair_table,
        triangles,
        groups,
        blocks,
    )

    state, hidden_high, hidden_low, scale, write, inner, stepped, total = pl.pallas_call(
        functools.partial(project_kernel, dims),
        out_shape=(
            shape(ch + 8, N),
            *halves(T, D),
            shape(T, ch),
            shape(T, N),
            shape(T, ch),
            shape(T, ch),
            shape(T, ch),
        ),
        in_specs=[vmem] * (9 + 2 * (nh - 1)),
        out_specs=(vmem,) * 8,
        compiler_params=params,
        name="project",
    )(
        mixed_high,
        mixed_low,
        embedded,
        small,
        own_high,
        own_low,
        state_high,
        state_low,
        upto,
        *[messages[k] for k in order],
        *others,
    )

    base, read_high, read_low, fade, gate, own = pl.pallas_call(
        functools.partial(block_kernel, dims),
        out_shape=(
            shape(T, ch),
            *halves(T, N),
            shape(T, ch),
            shape(T, ch),
            shape(share, D),
        ),
        in_specs=[vmem] * 11,
        out_specs=(vmem,) * 6,
        scratch_shapes=[pltpu.VMEM((T, D), f32)],
        compiler_params=params,
        cost_estimate=heavy,
        name="block",
    )(
        hidden_high,
        hidden_low,
        scale,
        write,
        inner,
        stepped,
        total,
        choose,
        rest_high,
        rest_low,
        small,
    )

    prefix = None
    bits = ns.bit_length() - 1
    direct = max(bits - 2, 0)
    for bit in range(direct):
        came = lax.ppermute(state, "seq", [(seq, seq ^ 2**bit) for seq in range(ns)])
        given = [state] + ([] if prefix is None else [prefix]) + [came]

        def join(bit, known, *refs):
            if known:
                join_kernel(dims, bit, *refs)
            else:
                join_kernel(dims, bit, refs[0], None, *refs[1:])

        state, prefix = pl.pallas_call(
            functools.partial(join, bit, prefix is not None),
            out_shape=(shape(ch + 8, N),) * 2,
            in_specs=[vmem] * len(given),
            out_specs=(vmem,) * 2,
            compiler_params=params,
            name="join",
        )(*given)
    came = {
        k: lax.ppermute(state, "seq", [(seq, seq ^ k * 2**direct) for seq in range(ns)])
        for k in range(1, ns // 2**direct)
    }
    came = [came[k] for k in sorted(came)]
    known = [] if prefix is None else [prefix]

    parts = pl.pallas_call(
        functools.partial(output_kernel, dims, direct, bool(known), len(came)),
        out_shape=(shape(share, D),) * nh,
        in_specs=[vmem] * (len(came) + len(known) + 9),
        out_specs=(vmem,) * nh,
        scratch_shapes=[pltpu.VMEM((T, D), f32)],
        compiler_params=params,
        name="output",
    )(
        *came,
        *known,
        read_high,
        read_low,
        base,
        fade,
        gate,
        own,
        proj_high,
        proj_low,
        groups,
    )
    result = parts[0]
    for k in in_turn(nh):
        pairs = [(source, source ^ k) for source in range(nh)]
        result = result + lax.ppermute(parts[k], "head", pairs)
    return result


def solution(mesh):
    return jax.shard_map(
        per_device,
        mesh=mesh,
        in_specs=(
            P(("rep", "seq")),
            P(),
            P(),
            P(),
            P(None, None, "head"),
            P(),
            P(None, "head"),
            P("head"),
            P("head"),
            P("head"),
            P("head"),
            P("head", None),
            P(),
            P(None, None, "head"),
            P(),
            P(None, "head"),
            P("head"),
            P("head"),
            P("head"),
            P("head"),
            P("head", None),
        ),
        out_specs=P(("rep", "seq", "head"), None),
        check_vma=False,
    )
```

```python
import functools

import jax
import jax.numpy as jnp
from jax import lax
from jax.experimental import pallas as pl
from jax.experimental.pallas import tpu as pltpu
from jax.sharding import PartitionSpec as P

epsilon = 1e-05
f32 = jnp.float32
bf16 = jnp.bfloat16
LIMIT = 48 * 1024 * 1024

MM = (((1,), (0,)), ((), ()))
NT = (((1,), (1,)), ((), ()))
TN = (((0,), (0,)), ((), ()))


def partners(ns, nh):
    count = max(ns, nh)
    return [((ns - k) if 0 < k < ns else 0, k if k < nh else 0) for k in range(count)]


def in_turn(count):
    return sorted(range(1, count), key=lambda k: (-k.bit_length(), k))


def iota(shape, axis):
    return lax.broadcasted_iota(jnp.int32, shape, axis)


def split2(value):
    high = value.astype(bf16)
    return high, (value - high.astype(f32)).astype(bf16)


def split3(value):
    high = value.astype(bf16)
    rest = value - high.astype(f32)
    middle = rest.astype(bf16)
    return high, middle, (rest - middle.astype(f32)).astype(bf16)


def dot(left, right, dims=MM):
    return lax.dot_general(left, right, dims, preferred_element_type=f32)


def dot_split(left, right, dims=MM):
    axis = 1 if dims == TN else 0
    size = left[0].shape[axis]
    if size % 16:
        return (dot(left[0], right[1], dims) + dot(left[1], right[0], dims)) + dot(
            left[0], right[0], dims
        )
    both = dot(jnp.concatenate([left[1], left[0]], axis=axis), right[0], dims)
    return (dot(left[0], right[1], dims) + both[0:size]) + both[size:]


def dot3(left, right, dims=MM):
    return dot_split(split2(left), split2(right), dims)


def dot_left_exact(left, right, dims=MM):
    high, middle, low = split3(right)
    return (dot(left, low, dims) + dot(left, middle, dims)) + dot(left, high, dims)


def dot_right_exact(left, right, dims=MM):
    high, middle, low = split3(left)
    return (dot(low, right, dims) + dot(middle, right, dims)) + dot(high, right, dims)


def softplus(value):
    return jnp.maximum(value, 0.0) + jnp.log1p(jnp.exp(-jnp.abs(value)))


def silu(value):
    return value / (1.0 + jnp.exp(-value))


def rms(value):
    return value * lax.rsqrt(jnp.mean(value * value, axis=-1, keepdims=True) + epsilon)


def fetch(sources, places, semaphores):
    copies = []
    for number, (source, place) in enumerate(zip(sources, places)):
        copies.append(pltpu.make_async_copy(source, place, semaphores.at[number]))
        copies[-1].start()
    return copies


def fetch(sources, places, semaphores):
    copies = []
    for number, (source, place) in enumerate(zip(sources, places)):
        copies.append(pltpu.make_async_copy(source, place, semaphores.at[number]))
        copies[-1].start()
    return copies


PIECES = 1


def tables_kernel(dims, *refs):
    V, D, hl, ch, nh, ns, T, N = dims
    refs = list(refs)

    def take(number):
        taken, refs[:] = refs[:number], refs[number:]
        return taken

    sources = take(9)
    outproj_source, message = take(2)
    places = take(9)
    semaphores = take(1)[0]
    half = ch // 2
    top = top_rows(dims)
    core = lax.rem(lax.axis_index("seq"), 2)
    (inproj, tok, emb, prenorm, stepmap, bias, rates, skip, outnorm) = places
    size = inproj.shape[0] // PIECES
    pieces = [pl.ds(number * size, size) for number in range(PIECES)]
    rows = pl.ds(pl.multiple_of(core * half, 8), half)
    wide = [(place, pl.ds(place * ch, ch)) for place in range(D // ch)]
    copies = fetch(
        [sources[0].at[piece, :] for piece in pieces]
        + sources[1:]
        + [outproj_source.at[rows, columns] for _, columns in wide],
        [inproj.at[piece, :] for piece in pieces]
        + places[1:]
        + [message.at[pl.ds(top + place * half, half), :] for place, _ in wide],
        semaphores,
    )
    flip = (iota((T, 1), 0) + iota((1, T), 1) == T - 1).astype(f32).astype(bf16)
    for copy in copies[PIECES : PIECES + 8]:
        copy.wait()
    normed = split2(rms(emb[...]) * prenorm[...])
    raw_t = dot_split(split2(stepmap[...]), normed, NT)
    tokens = jnp.broadcast_to(tok[...].astype(f32), (8, T)).astype(bf16)
    tokens = dot(tokens, flip)
    for place in range(T // ch):
        message[2 * V + place : 2 * V + place + 1, :] = tokens[0:1, place * ch : (place + 1) * ch]
    row = 2 * V + T // ch
    message[row : row + 1, :] = outnorm[...]
    for head in range(hl):
        line = softplus(raw_t[head : head + 1, :] + bias[:, head : head + 1])
        row = row + 1
        message[row : row + 1, 0:V] = line
        message[row : row + 1, V : 2 * V] = -rates[:, head : head + 1] * line
        message[row : row + 1, 2 * V : 3 * V] = jnp.broadcast_to(skip[:, head : head + 1], (1, V))
    for copy in copies[:PIECES]:
        copy.wait()
    weights = jnp.concatenate(
        [inproj[pl.ds(0, D, stride=2), :], inproj[pl.ds(1, D, stride=2), :]], axis=1
    )
    both = dot_split(normed, split2(weights))
    message[0:V, :] = both[:, 0:ch]
    message[V : 2 * V, :] = both[:, ch:]
    for copy in copies[PIECES + 8 :]:
        copy.wait()


def top_rows(dims):
    V, D, hl, ch, nh, ns, T, N = dims
    return 2 * V + -(-(T // ch + 1 + hl) // 8) * 8


def head_line(dims, values):
    V, D, hl, ch, nh, ns, T, N = dims
    head_of = iota((1, ch), 1) // (ch // hl)
    line = jnp.zeros((1, ch), f32)
    for head in range(hl):
        line = jnp.where(head_of == head, values[:, head : head + 1], line)
    return line


def prepare_kernel(dims, *refs):
    V, D, hl, ch, nh, ns, T, N = dims
    H, P = nh * hl, ch // hl
    refs = list(refs)

    def take(number):
        taken, refs[:] = refs[:number], refs[number:]
        return taken

    sources = take(14)
    pairs, small, choose_out, own_high, own_low = take(5)
    state_high, state_low, rest_high, rest_low, out_high, out_low = take(6)
    triangles, upto, groups, blocks = take(4)
    places = take(14)
    semaphores = take(1)[0]
    copies = fetch(sources, places, semaphores)
    inproj2, statemap2, statemap, outproj, outproj2, emb, prenorm, complement = places[:8]
    prenorm2, stepmap2, bias2, rates2, skip2, outnorm2 = places[8:]
    row, column = iota((T, 1), 0), iota((1, T), 1)
    triangles[:, 0:T] = (row > column).astype(f32).astype(bf16)
    triangles[:, T : 2 * T] = (row < column).astype(f32).astype(bf16)
    triangles[:, 2 * T :] = jnp.ones((T, 128), bf16)
    upto[...] = (row >= column).astype(f32).astype(bf16)
    size = groups.shape[0]
    groups[...] = (iota((size, 1), 0) // P == iota((1, size), 1) // P).astype(f32).astype(bf16)
    rows, columns = blocks.shape
    blocks[...] = (iota((rows, 1), 0) // V == iota((1, columns), 1) // P).astype(f32).astype(bf16)
    for copy in copies:
        copy.wait()
    normed = split2(rms(emb[...]) * prenorm[...])
    write = dot_split(normed, split2(statemap[pl.ds(0, D, stride=2), :]))
    read = dot_split(normed, split2(statemap[pl.ds(1, D, stride=2), :]))
    pairs[...] = dot3(read, jnp.concatenate([write] * H, axis=0), NT)
    own_high[...], own_low[...] = split2(outproj[...])
    choose = (complement[...] == iota((D, 1), 0)).astype(f32).astype(bf16)
    choose_out[...] = choose
    gain = jnp.transpose(jnp.broadcast_to(prenorm2[...], (128, D)))

    def weights(values):
        return split2(dot_left_exact(choose, values))

    gain_wide = gain[:, 0:1]
    inner = inproj2[pl.ds(1, D, stride=2), :] * gain_wide
    step = jnp.transpose(
        jnp.concatenate(
            [jnp.broadcast_to(stepmap2[head : head + 1, :], (P, D)) for head in range(hl)], axis=0
        )
    )
    write2 = statemap2[pl.ds(0, D, stride=2), :] * gain_wide
    state_high[...], state_low[...] = weights(
        jnp.concatenate([inner, step * gain_wide, write2], axis=1)
    )
    gate = inproj2[pl.ds(0, D, stride=2), :] * gain_wide
    read2 = statemap2[pl.ds(1, D, stride=2), :] * gain_wide
    rest_high[...], rest_low[...] = weights(jnp.concatenate([gate, read2], axis=1))
    small[0:1, :] = head_line(dims, bias2)
    small[1:2, :] = head_line(dims, rates2)
    small[2:3, :] = head_line(dims, skip2)
    out_gain = jnp.transpose(jnp.broadcast_to(outnorm2[...], (128, ch)))
    out_high[...], out_low[...] = split2(outproj2[...] * out_gain[:, 0:1])


def shift_rows(value, amount, fill):
    size = value.shape[0]
    if amount % 8 == 0:
        empty = jnp.full((abs(amount),) + value.shape[1:], fill, value.dtype)
        if amount > 0:
            return jnp.concatenate([empty, value[: size - amount]], axis=0)
        return jnp.concatenate([value[-amount:], empty], axis=0)
    rolled = pltpu.roll(value, amount % size, 0)
    row = iota((8,) + value.shape[1:], 0)
    if amount > 0:
        edge = jnp.where(row >= amount, rolled[0:8], fill)
        return jnp.concatenate([edge, rolled[8:]], axis=0)
    edge = jnp.where(row < 8 + amount, rolled[size - 8 :], fill)
    return jnp.concatenate([rolled[: size - 8], edge], axis=0)


def scan_rows(decay, value, sign):
    size = value.shape[0]
    amount = 1
    while amount < size:
        value = value + decay * shift_rows(value, sign * amount, 0.0)
        decay = decay * shift_rows(decay, sign * amount, 1.0)
        amount *= 2
    return value, decay


def mix_kernel(dims, *refs):
    V, D, hl, ch, nh, ns, T, N = dims
    H, LV, P = nh * hl, nh * hl * V, ch // hl
    C = nh * ch
    refs = list(refs)

    def take(number):
        taken, refs[:] = refs[:number], refs[number:]
        return taken

    count = max(ns, nh)
    packets = dict(zip(in_turn(count)[::-1] + [0], take(count)))
    emb, pairs, triangles, groups, blocks = take(5)
    out_high, out_low, out_embedded = take(3)
    tokens = take(1)[0]
    mine = lax.axis_index("seq")

    for k in range(ns):
        block = ns - 1 - lax.bitwise_xor(mine, partners(ns, nh)[k][0])
        row = 2 * V
        pieces = [packets[k][row + place : row + place + 1, :] for place in range(T // ch)]
        tokens[pl.ds(block, 1), :] = jnp.concatenate(pieces, axis=1)

    first = 2 * V + T // ch + 1
    steps = jnp.concatenate(
        [packets[k][first : first + hl, 0 : 3 * V] for k in range(nh)], axis=0
    )
    log_t = steps[:, V : 2 * V]
    narrow = jnp.concatenate([part.astype(f32) for part in split3(steps)], axis=0).astype(bf16)
    spread_heads = (iota((1, LV), 1) // V == iota((3 * H, 1), 0) % H).astype(f32).astype(bf16)
    wide = dot(narrow, spread_heads, TN)
    own = iota((1, LV), 1) % V == iota((V, 1), 0)
    decay_table = jnp.exp(wide[V : 2 * V])
    step_table = jnp.where(own, wide[0:V], 0.0)
    gain_table = jnp.where(own, wide[2 * V : 3 * V], 0.0)
    gates = jnp.concatenate([packets[k][0:V, :] for k in range(nh)], axis=1)
    inners = jnp.concatenate([packets[k][V : 2 * V, :] for k in range(nh)], axis=1)
    gains = jnp.concatenate([packets[k][first - 1 : first, :] for k in range(nh)], axis=1)

    token_row = (iota((LV, 1), 0) % V).astype(f32)
    log_split = jnp.concatenate(split3(log_t), axis=1)
    onehots, logs = [], []
    for block in range(ns):
        onehot = (tokens[block : block + 1, :] == token_row).astype(f32).astype(bf16)
        onehots.append(onehot)
        logs.append(dot(log_split, onehot[0 : 3 * V, :]))
    logs = jnp.concatenate(logs, axis=0)
    size = ns * H
    sums = dot(jnp.concatenate(split3(logs)[::-1], axis=0), triangles[...])
    sums = (sums[0:size] + sums[size : 2 * size]) + sums[2 * size :]
    blocks_of = [sums[block * H : (block + 1) * H] for block in range(ns)]
    weight_up, weight_down = [None] * ns, [None] * ns
    gap = jnp.zeros((H, 128), f32)
    for block in reversed(range(ns)):
        wide = jnp.concatenate([gap] * (T // 128), axis=1)
        weight_up[block] = jnp.where(
            block < mine, jnp.exp(blocks_of[block][:, 0:T] + wide), 0.0
        )
        gap = jnp.where(block < mine, gap + blocks_of[block][:, 2 * T :], gap)
    gap = jnp.zeros((H, 128), f32)
    for block in range(ns):
        wide = jnp.concatenate([gap] * (T // 128), axis=1)
        weight_down[block] = jnp.where(
            block > mine, jnp.exp(blocks_of[block][:, T : 2 * T] + wide), 0.0
        )
        gap = jnp.where(block > mine, gap + blocks_of[block][:, 2 * T :], gap)
    entering = jnp.zeros((4 * H, LV), f32)
    for block in range(ns):
        both = jnp.concatenate([weight_up[block], weight_down[block]], axis=0)
        entering = entering + dot(
            jnp.concatenate(split2(both), axis=0), onehots[block], NT
        )
    entering = entering[2 * H :] + entering[0 : 2 * H]
    diagonal = iota((1, LV), 1) // V == iota((H, 1), 0)
    step_row = jnp.sum(step_table, axis=0, keepdims=True)
    enter_up = step_row * jnp.sum(
        jnp.where(diagonal, entering[0:H], 0.0), axis=0, keepdims=True
    )
    enter_down = step_row * jnp.sum(
        jnp.where(diagonal, entering[H : 2 * H], 0.0), axis=0, keepdims=True
    )

    looked = jnp.concatenate(
        [decay_table, step_table, pairs[...], gain_table, silu(gates), emb[...]], axis=1
    )
    looked = jnp.concatenate(split3(looked), axis=0)
    token = tokens[pl.ds(mine, 1), :]
    onehot = (token == token_row[0 : 3 * V]).astype(f32).astype(bf16)
    rows = dot(onehot, looked, TN)
    decay, step = rows[:, 0:LV], rows[:, LV : 2 * LV]
    pair, gain = rows[:, 2 * LV : 3 * LV], rows[:, 3 * LV : 4 * LV]
    silu_rows = rows[:, 4 * LV : 4 * LV + C]
    out_embedded[...] = rows[:, 4 * LV + C :]

    up, fade = scan_rows(decay, step, 1)
    up = up + fade * enter_up
    down, fade = scan_rows(decay, step, -1)
    down = down + fade * enter_down

    spread_high, spread_low = [
        jnp.concatenate([part] * H, axis=0) * blocks[...] for part in split2(inners)
    ]
    both = jnp.concatenate([up * pair + gain, down * pair + gain], axis=0)
    high = both.astype(bf16)
    high_wide = high.astype(f32)
    low_turned = pltpu.roll(both - high_wide, LV // 2, 1)
    lower = iota((1, LV), 1) < LV // 2
    value = []
    for side in (0, 1):
        mixed = jnp.where(lower == (side == 0), high_wide, low_turned).astype(bf16)
        rows = slice(side * LV // 2, (side + 1) * LV // 2)
        columns = slice(side * C // 2, (side + 1) * C // 2)
        weight, rest = spread_high[rows, columns], spread_low[:, columns]
        value.append(
            dot(
                jnp.concatenate([mixed, high], axis=1),
                jnp.concatenate([weight, weight, rest], axis=0),
            )
        )
    value = jnp.concatenate(value, axis=1)
    value = value * jnp.concatenate([silu_rows, silu_rows], axis=0)
    wide = groups.shape[0]
    high, low = split2(value * value)
    starts = list(range(0, C, wide))
    rows = 2 * T
    stacked = [half[:, start : start + wide] for start in starts for half in (low, high)]
    squares = dot(jnp.concatenate(stacked, axis=0), groups[...])
    for number, start in enumerate(starts):
        place = 2 * number * rows
        square = squares[place : place + rows] + squares[place + rows : place + 2 * rows]
        stop = start + wide
        normed = value[:, start:stop] * lax.rsqrt(square * (1.0 / P) + epsilon)
        out_high[:, start:stop], out_low[:, start:stop] = split2(
            (normed[0:T] + normed[T : 2 * T]) * gains[:, start:stop]
        )


def project_kernel(dims, *refs):
    V, D, hl, ch, nh, ns, T, N = dims
    P = ch // hl
    refs = list(refs)

    def take(number):
        taken, refs[:] = refs[:number], refs[number:]
        return taken

    high, low, embedded, small, own_high, own_low, state_high, state_low, upto = take(9)
    order = in_turn(nh)[::-1]
    nears = dict(zip(order, take(nh - 1)))
    others = dict(zip(order, take(nh - 1)))
    out_state, out_high, out_low, out_scale = take(4)
    out_write, out_inner, out_stepped, out_total = take(4)
    half = ch // 2
    base = top_rows(dims)
    mine = lax.axis_index("seq")

    pieces = []
    for k in range(1, nh):
        near, other = [
            jnp.concatenate(
                [
                    ref[base + place * half : base + (place + 1) * half, :]
                    for place in range(D // ch)
                ],
                axis=1,
            )
            for ref in (nears[k], others[k])
        ]
        even = lax.rem(lax.bitwise_xor(mine, partners(ns, nh)[k][0]), 2) == 0
        pieces.append(jnp.where(even, near, other))
        pieces.append(jnp.where(even, other, near))
    weights = split2(jnp.concatenate(pieces, axis=0))
    weights = (
        jnp.concatenate([own_high[...], weights[0]], axis=0),
        jnp.concatenate([own_low[...], weights[1]], axis=0),
    )
    hidden = embedded[...] + dot_split((high[...], low[...]), weights)
    split = split2(hidden)
    out_high[...], out_low[...] = split
    scale = lax.rsqrt(jnp.mean(hidden * hidden, axis=-1, keepdims=True) + epsilon)
    out_scale[...] = jnp.broadcast_to(scale, (T, ch))

    rows = dot_split(split, (state_high[...], state_low[...])) * scale
    inner, write = rows[:, 0:ch], rows[:, 2 * ch :]
    step = softplus(rows[:, ch : 2 * ch] + small[0:1, :])
    stepped = inner * step
    log_high, log_middle, log_low = split3(-small[1:2, :] * step)
    total = dot(upto[...], jnp.concatenate([log_low, log_middle], axis=1))
    total = (total[:, 0:ch] + total[:, ch:]) + dot(upto[...], log_high)
    end = total[T - 1 : T, :]
    state = dot3(stepped * jnp.exp(end - total), write, TN)
    out_state[0:ch, :] = state
    for head in range(hl):
        out_state[ch + head : ch + head + 1, :] = jnp.broadcast_to(
            end[:, head * P : head * P + 1], (1, N)
        )
    out_write[...] = write
    out_inner[...] = inner
    out_stepped[...] = stepped
    out_total[...] = total


def block_kernel(dims, *refs):
    V, D, hl, ch, nh, ns, T, N = dims
    P = ch // hl
    refs = list(refs)

    def take(number):
        taken, refs[:] = refs[:number], refs[number:]
        return taken

    high, low, scale, write, inner, stepped, total, choose = take(8)
    rest_high, rest_low, small = take(3)
    base, read_high, read_low, out_fade, out_gate, own, hidden_ref = take(7)
    rows = dot_split((high[...], low[...]), (rest_high[...], rest_low[...]))
    out_gate[...] = silu(rows[:, 0:ch] * scale[...])
    read = rows[:, ch:] * scale[...]
    read = split2(read)
    read_high[...], read_low[...] = read
    out_fade[...] = jnp.exp(total[...])
    products = dot_split(read, split2(write[...]), NT)
    stepped_high, stepped_low = split2(stepped[...])
    select = (iota((8, ch), 1) == iota((8, ch), 0) * P).astype(f32).astype(bf16)
    total_high, total_middle, total_low = split3(total[...])
    total_t = (dot(select, total_low, NT) + dot(select, total_middle, NT)) + dot(
        select, total_high, NT
    )
    allowed = iota((T, 1), 0) >= iota((1, T), 1)
    parts = []
    for head in range(hl):
        start, stop = head * P, (head + 1) * P
        differ = total[:, start : start + 1] - total_t[head : head + 1, :]
        weights = jnp.where(allowed, jnp.exp(jnp.where(allowed, differ, 0.0)), 0.0) * products
        part = dot_split(
            split2(weights), (stepped_high[:, start:stop], stepped_low[:, start:stop])
        )
        parts.append(part + small[2:3, start:stop] * inner[:, start:stop])
    base[...] = jnp.concatenate(parts, axis=1)
    share = T // nh
    hidden_ref[...] = high[...].astype(f32) + low[...].astype(f32)
    place = pl.multiple_of(lax.axis_index("head") * share, 8)
    own[...] = dot_right_exact(hidden_ref[pl.ds(place, share), :], choose[...])


def state_rows(dims, values):
    V, D, hl, ch, nh, ns, T, N = dims
    head_of = iota((ch, N), 0) // (ch // hl)
    result = jnp.broadcast_to(values[0:1, :], (ch, N))
    for head in range(1, hl):
        result = jnp.where(head_of == head, values[head : head + 1, :], result)
    return result


def join_kernel(dims, bit, total, prefix, came, out_total, out_prefix):
    V, D, hl, ch, nh, ns, T, N = dims
    later = lax.rem(lax.div(lax.axis_index("seq"), 2**bit), 2) == 1
    came_state, came_log = came[0:ch, :], came[ch : ch + hl, :]
    state, log = total[0:ch, :], total[ch : ch + hl, :]
    factor = jnp.exp(state_rows(dims, jnp.where(later, log, came_log)))
    out_total[0:ch, :] = jnp.where(
        later, factor * came_state + state, factor * state + came_state
    )
    out_total[ch : ch + hl, :] = log + came_log
    if prefix is None:
        out_prefix[0:ch, :] = jnp.where(later, came_state, 0.0)
        out_prefix[ch : ch + hl, :] = jnp.where(later, came_log, 0.0)
    else:
        joined = prefix_joined(dims, bit, prefix, came)
        out_prefix[0:ch, :] = joined
        out_prefix[ch : ch + hl, :] = prefix[ch : ch + hl, :] + jnp.where(later, came_log, 0.0)


def prefix_joined(dims, bit, prefix, came):
    V, D, hl, ch, nh, ns, T, N = dims
    later = lax.rem(lax.div(lax.axis_index("seq"), 2**bit), 2) == 1
    factor = jnp.exp(state_rows(dims, prefix[ch : ch + hl, :]))
    return prefix[0:ch, :] + jnp.where(later, factor * came[0:ch, :], 0.0)


def entering_state(dims, bit, prefix, came):
    V, D, hl, ch, nh, ns, T, N = dims
    place = lax.rem(lax.div(lax.axis_index("seq"), 2**bit), 2 ** (len(came) // 2 + 1))
    odd = lax.rem(place, 2) == 1

    def fade(value):
        return jnp.exp(state_rows(dims, value))

    nearest, log = came[0][0:ch, :], came[0][ch : ch + hl, :]
    if len(came) > 1:
        nearest = jnp.where(odd, nearest, came[2][0:ch, :])
        log = jnp.where(odd, log, came[2][ch : ch + hl, :])
    entering = jnp.where(place > 0, nearest, 0.0)
    if len(came) > 1:
        second = jnp.where(place > 1, came[1][0:ch, :], 0.0)
        third = jnp.where(place > 2, came[2][0:ch, :], 0.0)
        entering = entering + fade(log) * (second + fade(came[1][ch : ch + hl, :]) * third)
    if prefix is not None:
        entering = prefix[0:ch, :] + fade(prefix[ch : ch + hl, :]) * entering
    return entering


def output_kernel(dims, bit, known, number, *refs):
    V, D, hl, ch, nh, ns, T, N = dims
    P = ch // hl
    came, refs = refs[:number], refs[number:]
    prefix, refs = (refs[0], refs[1:]) if known else (None, refs)
    read_high, read_low, base, fade, gate, own, proj_high, proj_low, groups = refs[:9]
    outs, partial_ref = refs[9 : 9 + nh], refs[9 + nh]
    entering = entering_state(dims, bit, prefix, came)
    carried = dot_split((read_high[...], read_low[...]), split2(entering), NT)
    value = (base[...] + carried * fade[...]) * gate[...]
    square = dot(jnp.concatenate(split2(value * value), axis=0), groups[0:ch, 0:ch])
    square = square[T:] + square[0:T]
    value = value * lax.rsqrt(square * (1.0 / P) + epsilon)
    share = T // nh
    partial_ref[...] = dot_split(split2(value), (proj_high[...], proj_low[...]))
    mine = lax.axis_index("head")
    for k in range(nh):
        place = pl.multiple_of(lax.bitwise_xor(mine, k) * share, 8)
        part = partial_ref[pl.ds(place, share), :]
        outs[k][...] = part + own[...] if k == 0 else part


def per_device(
    token_ids,
    embedding,
    complement,
    prenorm_first,
    inproj_first,
    statemap_first,
    stepmap_first,
    stepbias_first,
    rates_first,
    skipgain_first,
    outnorm_first,
    outproj_first,
    prenorm_second,
    inproj_second,
    statemap_second,
    stepmap_second,
    stepbias_second,
    rates_second,
    skipgain_second,
    outnorm_second,
    outproj_second,
):
    nh, ns = lax.axis_size("head"), lax.axis_size("seq")
    V, D = embedding.shape
    ch = inproj_first.shape[2]
    hl = stepmap_first.shape[1]
    N = statemap_first.shape[2]
    T = token_ids.shape[0]
    LV = nh * hl * V
    dims = (V, D, hl, ch, nh, ns, T, N)
    vmem = pl.BlockSpec(memory_space=pltpu.VMEM)
    anywhere = pl.BlockSpec(memory_space=pl.ANY)
    params = pltpu.CompilerParams(vmem_limit_bytes=LIMIT)

    def shape(*sizes, dtype=f32):
        return jax.ShapeDtypeStruct(sizes, dtype)

    def halves(*sizes):
        return [shape(*sizes, dtype=bf16)] * 2

    def room(value):
        return pltpu.VMEM(value.shape, value.dtype)

    def kept(values):
        return [pltpu.with_memory_space_constraint(value, pltpu.HBM) for value in values]

    def line(value):
        return value.reshape(1, -1)

    def flat(value):
        return value.reshape(-1, value.shape[-1])

    heavy = pl.CostEstimate(flops=960 * T * D * D, bytes_accessed=4 * T * D, transcendentals=T * D)

    half = ch // 2
    share = T // nh
    fetched = [
        flat(inproj_first),
        line(token_ids),
        embedding,
        line(prenorm_first),
        stepmap_first.T,
        line(stepbias_first),
        line(rates_first),
        line(skipgain_first),
        line(outnorm_first),
    ]
    message = pl.pallas_call(
        functools.partial(tables_kernel, dims),
        out_shape=pltpu.VMEM((top_rows(dims) + half * (D // ch), ch), f32),
        in_specs=[anywhere] * (len(fetched) + 1),
        out_specs=vmem,
        scratch_shapes=[room(value) for value in fetched]
        + [pltpu.SemaphoreType.DMA((len(fetched) - 1 + PIECES + D // ch,))],
        compiler_params=params,
        name="tables",
    )(*kept([*fetched, outproj_first]))

    prepared = [
        flat(inproj_second),
        flat(statemap_second),
        flat(statemap_first),
        outproj_first,
        outproj_second,
        embedding,
        line(prenorm_first),
        line(complement),
        line(prenorm_second),
        stepmap_second.T,
        line(stepbias_second),
        line(rates_second),
        line(skipgain_second),
        line(outnorm_second),
    ]
    (
        pair_table,
        small,
        choose,
        own_high,
        own_low,
        state_high,
        state_low,
        rest_high,
        rest_low,
        proj_high,
        proj_low,
        triangles,
        upto,
        groups,
        blocks,
    ) = pl.pallas_call(
        functools.partial(prepare_kernel, dims),
        out_shape=(
            shape(V, LV),
            shape(8, ch),
            shape(D, D, dtype=bf16),
            *halves(ch, D),
            *halves(D, 2 * ch + N),
            *halves(D, ch + N),
            *halves(ch, D),
            shape(T, 2 * T + 128, dtype=bf16),
            shape(T, T, dtype=bf16),
            shape(2 * ch, 2 * ch, dtype=bf16),
            shape(LV, nh * ch, dtype=bf16),
        ),
        in_specs=[anywhere] * len(prepared),
        out_specs=(vmem,) * 15,
        scratch_shapes=[room(value) for value in prepared]
        + [pltpu.SemaphoreType.DMA((len(prepared),))],
        compiler_params=params,
        cost_estimate=heavy,
        name="prepare",
    )(*kept(prepared))

    count = max(ns, nh)
    messages = {0: message}
    for k in in_turn(count):
        seq_bits, head_bits = partners(ns, nh)[k]
        pairs = [
            (seq * nh + head, (seq ^ seq_bits) * nh + (head ^ head_bits))
            for seq in range(ns)
            for head in range(nh)
        ]
        sent = message if k < nh else message[0 : top_rows(dims)]
        messages[k] = lax.ppermute(sent, ("seq", "head"), pairs)
    swap = [(seq, seq ^ 1) for seq in range(ns)]
    order = in_turn(nh)[::-1]
    others = [lax.ppermute(messages[k], "seq", swap) for k in order]

    mixed_high, mixed_low, embedded = pl.pallas_call(
        functools.partial(mix_kernel, dims),
        out_shape=(*halves(T, nh * ch), shape(T, D)),
        in_specs=[vmem] * (count + 5),
        out_specs=(vmem,) * 3,
        scratch_shapes=[pltpu.VMEM((max(ns, 8), T), f32)],
        compiler_params=params,
        cost_estimate=heavy,
        name="mix",
    )(
        *[messages[k] for k in in_turn(count)[::-1] + [0]],
        embedding,
        pair_table,
        triangles,
        groups,
        blocks,
    )

    state, hidden_high, hidden_low, scale, write, inner, stepped, total = pl.pallas_call(
        functools.partial(project_kernel, dims),
        out_shape=(
            shape(ch + 8, N),
            *halves(T, D),
            shape(T, ch),
            shape(T, N),
            shape(T, ch),
            shape(T, ch),
            shape(T, ch),
        ),
        in_specs=[vmem] * (9 + 2 * (nh - 1)),
        out_specs=(vmem,) * 8,
        compiler_params=params,
        name="project",
    )(
        mixed_high,
        mixed_low,
        embedded,
        small,
        own_high,
        own_low,
        state_high,
        state_low,
        upto,
        *[messages[k] for k in order],
        *others,
    )

    base, read_high, read_low, fade, gate, own = pl.pallas_call(
        functools.partial(block_kernel, dims),
        out_shape=(
            shape(T, ch),
            *halves(T, N),
            shape(T, ch),
            shape(T, ch),
            shape(share, D),
        ),
        in_specs=[vmem] * 11,
        out_specs=(vmem,) * 6,
        scratch_shapes=[pltpu.VMEM((T, D), f32)],
        compiler_params=params,
        cost_estimate=heavy,
        name="block",
    )(
        hidden_high,
        hidden_low,
        scale,
        write,
        inner,
        stepped,
        total,
        choose,
        rest_high,
        rest_low,
        small,
    )

    prefix = None
    bits = ns.bit_length() - 1
    direct = max(bits - 2, 0)
    for bit in range(direct):
        came = lax.ppermute(state, "seq", [(seq, seq ^ 2**bit) for seq in range(ns)])
        given = [state] + ([] if prefix is None else [prefix]) + [came]

        def join(bit, known, *refs):
            if known:
                join_kernel(dims, bit, *refs)
            else:
                join_kernel(dims, bit, refs[0], None, *refs[1:])

        state, prefix = pl.pallas_call(
            functools.partial(join, bit, prefix is not None),
            out_shape=(shape(ch + 8, N),) * 2,
            in_specs=[vmem] * len(given),
            out_specs=(vmem,) * 2,
            compiler_params=params,
            name="join",
        )(*given)

    def across(value, k):
        return lax.ppermute(value, "seq", [(seq, seq ^ k * 2**direct) for seq in range(ns)])

    came = [across(state, 1)]
    if bits > 1:
        base, far = lax.optimization_barrier((base, across(state, 2)))
        came += [far, across(far, 1)]
    known = [] if prefix is None else [prefix]

    parts = pl.pallas_call(
        functools.partial(output_kernel, dims, direct, bool(known), len(came)),
        out_shape=(shape(share, D),) * nh,
        in_specs=[vmem] * (len(came) + len(known) + 9),
        out_specs=(vmem,) * nh,
        scratch_shapes=[pltpu.VMEM((T, D), f32)],
        compiler_params=params,
        name="output",
    )(
        *came,
        *known,
        read_high,
        read_low,
        base,
        fade,
        gate,
        own,
        proj_high,
        proj_low,
        groups,
    )
    result = parts[0]
    for k in in_turn(nh):
        pairs = [(source, source ^ k) for source in range(nh)]
        result = result + lax.ppermute(parts[k], "head", pairs)
    return result


def solution(mesh):
    return jax.shard_map(
        per_device,
        mesh=mesh,
        in_specs=(
            P(("rep", "seq")),
            P(),
            P(),
            P(),
            P(None, None, "head"),
            P(),
            P(None, "head"),
            P("head"),
            P("head"),
            P("head"),
            P("head"),
            P("head", None),
            P(),
            P(None, None, "head"),
            P(),
            P(None, "head"),
            P("head"),
            P("head"),
            P("head"),
            P("head"),
            P("head", None),
        ),
        out_specs=P(("rep", "seq", "head"), None),
        check_vma=False,
    )
```

```python
import functools

import jax
import jax.numpy as jnp
from jax import lax
from jax.experimental import pallas as pl
from jax.experimental.pallas import tpu as pltpu
from jax.sharding import PartitionSpec as P

epsilon = 1e-05
f32 = jnp.float32
bf16 = jnp.bfloat16
LIMIT = 48 * 1024 * 1024

MM = (((1,), (0,)), ((), ()))
NT = (((1,), (1,)), ((), ()))
TN = (((0,), (0,)), ((), ()))


def partners(ns, nh):
    return [(k if k < ns else 0, k if k < nh else 0) for k in range(max(ns, nh))]


def first_turn(count):
    return list(range(1, count))


def in_turn(count):
    return sorted(range(1, count), key=lambda k: (-k.bit_length(), k))


def iota(shape, axis):
    return lax.broadcasted_iota(jnp.int32, shape, axis)


def split2(value):
    high = value.astype(bf16)
    return high, (value - high.astype(f32)).astype(bf16)


def split3(value):
    high = value.astype(bf16)
    rest = value - high.astype(f32)
    middle = rest.astype(bf16)
    return high, middle, (rest - middle.astype(f32)).astype(bf16)


def dot(left, right, dims=MM):
    return lax.dot_general(left, right, dims, preferred_element_type=f32)


def dot_split(left, right, dims=MM):
    axis = 1 if dims == TN else 0
    size = left[0].shape[axis]
    if size % 16:
        return (dot(left[0], right[1], dims) + dot(left[1], right[0], dims)) + dot(
            left[0], right[0], dims
        )
    both = dot(jnp.concatenate([left[1], left[0]], axis=axis), right[0], dims)
    return (dot(left[0], right[1], dims) + both[0:size]) + both[size:]


def dot3(left, right, dims=MM):
    return dot_split(split2(left), split2(right), dims)


def dot_left_exact(left, right, dims=MM):
    high, middle, low = split3(right)
    return (dot(left, low, dims) + dot(left, middle, dims)) + dot(left, high, dims)


def dot_right_exact(left, right, dims=MM):
    high, middle, low = split3(left)
    return (dot(low, right, dims) + dot(middle, right, dims)) + dot(high, right, dims)


def softplus(value):
    return jnp.maximum(value, 0.0) + jnp.log1p(jnp.exp(-jnp.abs(value)))


def silu(value):
    return value / (1.0 + jnp.exp(-value))


def rms(value):
    return value * lax.rsqrt(jnp.mean(value * value, axis=-1, keepdims=True) + epsilon)


def fetch(sources, places, semaphores):
    copies = []
    for number, (source, place) in enumerate(zip(sources, places)):
        copies.append(pltpu.make_async_copy(source, place, semaphores.at[number]))
        copies[-1].start()
    return copies


def fetch(sources, places, semaphores):
    copies = []
    for number, (source, place) in enumerate(zip(sources, places)):
        copies.append(pltpu.make_async_copy(source, place, semaphores.at[number]))
        copies[-1].start()
    return copies


PIECES = 1


def tables_kernel(dims, *refs):
    V, D, hl, ch, nh, ns, T, N = dims
    refs = list(refs)

    def take(number):
        taken, refs[:] = refs[:number], refs[number:]
        return taken

    sources = take(9)
    outproj_source, message = take(2)
    places = take(9)
    semaphores = take(1)[0]
    half = ch // 2
    top = top_rows(dims)
    core = lax.rem(lax.axis_index("seq"), 2)
    (inproj, tok, emb, prenorm, stepmap, bias, rates, skip, outnorm) = places
    size = inproj.shape[0] // PIECES
    pieces = [pl.ds(number * size, size) for number in range(PIECES)]
    rows = pl.ds(pl.multiple_of(core * half, 8), half)
    wide = [(place, pl.ds(place * ch, ch)) for place in range(D // ch)]
    copies = fetch(
        [sources[0].at[piece, :] for piece in pieces]
        + sources[1:]
        + [outproj_source.at[rows, columns] for _, columns in wide],
        [inproj.at[piece, :] for piece in pieces]
        + places[1:]
        + [message.at[pl.ds(top + place * half, half), :] for place, _ in wide],
        semaphores,
    )
    flip = (iota((T, 1), 0) + iota((1, T), 1) == T - 1).astype(f32).astype(bf16)
    for copy in copies[PIECES : PIECES + 8]:
        copy.wait()
    normed = split2(rms(emb[...]) * prenorm[...])
    raw_t = dot_split(split2(stepmap[...]), normed, NT)
    tokens = jnp.broadcast_to(tok[...].astype(f32), (8, T)).astype(bf16)
    tokens = dot(tokens, flip)
    for place in range(T // ch):
        message[2 * V + place : 2 * V + place + 1, :] = tokens[0:1, place * ch : (place + 1) * ch]
    row = 2 * V + T // ch
    message[row : row + 1, :] = outnorm[...]
    for head in range(hl):
        line = softplus(raw_t[head : head + 1, :] + bias[:, head : head + 1])
        row = row + 1
        message[row : row + 1, 0:V] = line
        message[row : row + 1, V : 2 * V] = -rates[:, head : head + 1] * line
        message[row : row + 1, 2 * V : 3 * V] = jnp.broadcast_to(skip[:, head : head + 1], (1, V))
    for copy in copies[:PIECES]:
        copy.wait()
    weights = jnp.concatenate(
        [inproj[pl.ds(0, D, stride=2), :], inproj[pl.ds(1, D, stride=2), :]], axis=1
    )
    both = dot_split(normed, split2(weights))
    message[0:V, :] = both[:, 0:ch]
    message[V : 2 * V, :] = both[:, ch:]
    for copy in copies[PIECES + 8 :]:
        copy.wait()


def top_rows(dims):
    V, D, hl, ch, nh, ns, T, N = dims
    return 2 * V + -(-(T // ch + 1 + hl) // 8) * 8


def head_line(dims, values):
    V, D, hl, ch, nh, ns, T, N = dims
    head_of = iota((1, ch), 1) // (ch // hl)
    line = jnp.zeros((1, ch), f32)
    for head in range(hl):
        line = jnp.where(head_of == head, values[:, head : head + 1], line)
    return line


def prepare_kernel(dims, *refs):
    V, D, hl, ch, nh, ns, T, N = dims
    H, P = nh * hl, ch // hl
    refs = list(refs)

    def take(number):
        taken, refs[:] = refs[:number], refs[number:]
        return taken

    sources = take(14)
    pairs, small, choose_out, own_high, own_low = take(5)
    state_high, state_low, rest_high, rest_low, out_high, out_low = take(6)
    triangles, upto, groups, blocks = take(4)
    places = take(14)
    semaphores = take(1)[0]
    copies = fetch(sources, places, semaphores)
    inproj2, statemap2, statemap, outproj, outproj2, emb, prenorm, complement = places[:8]
    prenorm2, stepmap2, bias2, rates2, skip2, outnorm2 = places[8:]
    row, column = iota((T, 1), 0), iota((1, T), 1)
    triangles[:, 0:T] = (row > column).astype(f32).astype(bf16)
    triangles[:, T : 2 * T] = (row < column).astype(f32).astype(bf16)
    triangles[:, 2 * T :] = jnp.ones((T, 128), bf16)
    upto[...] = (row >= column).astype(f32).astype(bf16)
    size = groups.shape[0]
    groups[...] = (iota((size, 1), 0) // P == iota((1, size), 1) // P).astype(f32).astype(bf16)
    rows, columns = blocks.shape
    blocks[...] = (iota((rows, 1), 0) // V == iota((1, columns), 1) // P).astype(f32).astype(bf16)
    for copy in copies:
        copy.wait()
    normed = split2(rms(emb[...]) * prenorm[...])
    write = dot_split(normed, split2(statemap[pl.ds(0, D, stride=2), :]))
    read = dot_split(normed, split2(statemap[pl.ds(1, D, stride=2), :]))
    pairs[...] = dot3(read, jnp.concatenate([write] * H, axis=0), NT)
    own_high[...], own_low[...] = split2(outproj[...])
    choose = (complement[...] == iota((D, 1), 0)).astype(f32).astype(bf16)
    choose_out[...] = choose
    gain = jnp.transpose(jnp.broadcast_to(prenorm2[...], (128, D)))

    def weights(values):
        return split2(dot_left_exact(choose, values))

    gain_wide = gain[:, 0:1]
    inner = inproj2[pl.ds(1, D, stride=2), :] * gain_wide
    step = jnp.transpose(
        jnp.concatenate(
            [jnp.broadcast_to(stepmap2[head : head + 1, :], (P, D)) for head in range(hl)], axis=0
        )
    )
    write2 = statemap2[pl.ds(0, D, stride=2), :] * gain_wide
    state_high[...], state_low[...] = weights(
        jnp.concatenate([inner, step * gain_wide, write2], axis=1)
    )
    gate = inproj2[pl.ds(0, D, stride=2), :] * gain_wide
    read2 = statemap2[pl.ds(1, D, stride=2), :] * gain_wide
    rest_high[...], rest_low[...] = weights(jnp.concatenate([gate, read2], axis=1))
    small[0:1, :] = head_line(dims, bias2)
    small[1:2, :] = head_line(dims, rates2)
    small[2:3, :] = head_line(dims, skip2)
    out_gain = jnp.transpose(jnp.broadcast_to(outnorm2[...], (128, ch)))
    out_high[...], out_low[...] = split2(outproj2[...] * out_gain[:, 0:1])


def shift_rows(value, amount, fill):
    size = value.shape[0]
    if amount % 8 == 0:
        empty = jnp.full((abs(amount),) + value.shape[1:], fill, value.dtype)
        if amount > 0:
            return jnp.concatenate([empty, value[: size - amount]], axis=0)
        return jnp.concatenate([value[-amount:], empty], axis=0)
    rolled = pltpu.roll(value, amount % size, 0)
    row = iota((8,) + value.shape[1:], 0)
    if amount > 0:
        edge = jnp.where(row >= amount, rolled[0:8], fill)
        return jnp.concatenate([edge, rolled[8:]], axis=0)
    edge = jnp.where(row < 8 + amount, rolled[size - 8 :], fill)
    return jnp.concatenate([rolled[: size - 8], edge], axis=0)


def scan_rows(decay, value, sign):
    size = value.shape[0]
    amount = 1
    while amount < size:
        value = value + decay * shift_rows(value, sign * amount, 0.0)
        decay = decay * shift_rows(decay, sign * amount, 1.0)
        amount *= 2
    return value, decay


def mix_kernel(dims, *refs):
    V, D, hl, ch, nh, ns, T, N = dims
    H, LV, P = nh * hl, nh * hl * V, ch // hl
    C = nh * ch
    refs = list(refs)

    def take(number):
        taken, refs[:] = refs[:number], refs[number:]
        return taken

    count = max(ns, nh)
    packets = dict(zip(first_turn(count)[::-1] + [0], take(count)))
    emb, pairs, triangles, groups, blocks = take(5)
    out_high, out_low, out_embedded = take(3)
    tokens = take(1)[0]
    mine = lax.axis_index("seq")

    for k in range(ns):
        block = ns - 1 - lax.bitwise_xor(mine, partners(ns, nh)[k][0])
        row = 2 * V
        pieces = [packets[k][row + place : row + place + 1, :] for place in range(T // ch)]
        tokens[pl.ds(block, 1), :] = jnp.concatenate(pieces, axis=1)

    first = 2 * V + T // ch + 1
    steps = jnp.concatenate(
        [packets[k][first : first + hl, 0 : 3 * V] for k in range(nh)], axis=0
    )
    log_t = steps[:, V : 2 * V]
    narrow = jnp.concatenate([part.astype(f32) for part in split3(steps)], axis=0).astype(bf16)
    spread_heads = (iota((1, LV), 1) // V == iota((3 * H, 1), 0) % H).astype(f32).astype(bf16)
    wide = dot(narrow, spread_heads, TN)
    own = iota((1, LV), 1) % V == iota((V, 1), 0)
    decay_table = jnp.exp(wide[V : 2 * V])
    step_table = jnp.where(own, wide[0:V], 0.0)
    gain_table = jnp.where(own, wide[2 * V : 3 * V], 0.0)
    gates = jnp.concatenate([packets[k][0:V, :] for k in range(nh)], axis=1)
    inners = jnp.concatenate([packets[k][V : 2 * V, :] for k in range(nh)], axis=1)
    gains = jnp.concatenate([packets[k][first - 1 : first, :] for k in range(nh)], axis=1)

    token_row = (iota((LV, 1), 0) % V).astype(f32)
    log_split = jnp.concatenate(split3(log_t), axis=1)
    onehots, logs = [], []
    for block in range(ns):
        onehot = (tokens[block : block + 1, :] == token_row).astype(f32).astype(bf16)
        onehots.append(onehot)
        logs.append(dot(log_split, onehot[0 : 3 * V, :]))
    logs = jnp.concatenate(logs, axis=0)
    size = ns * H
    sums = dot(jnp.concatenate(split3(logs)[::-1], axis=0), triangles[...])
    sums = (sums[0:size] + sums[size : 2 * size]) + sums[2 * size :]
    blocks_of = [sums[block * H : (block + 1) * H] for block in range(ns)]
    weight_up, weight_down = [None] * ns, [None] * ns
    gap = jnp.zeros((H, 128), f32)
    for block in reversed(range(ns)):
        wide = jnp.concatenate([gap] * (T // 128), axis=1)
        weight_up[block] = jnp.where(
            block < mine, jnp.exp(blocks_of[block][:, 0:T] + wide), 0.0
        )
        gap = jnp.where(block < mine, gap + blocks_of[block][:, 2 * T :], gap)
    gap = jnp.zeros((H, 128), f32)
    for block in range(ns):
        wide = jnp.concatenate([gap] * (T // 128), axis=1)
        weight_down[block] = jnp.where(
            block > mine, jnp.exp(blocks_of[block][:, T : 2 * T] + wide), 0.0
        )
        gap = jnp.where(block > mine, gap + blocks_of[block][:, 2 * T :], gap)
    entering = jnp.zeros((4 * H, LV), f32)
    for block in range(ns):
        both = jnp.concatenate([weight_up[block], weight_down[block]], axis=0)
        entering = entering + dot(
            jnp.concatenate(split2(both), axis=0), onehots[block], NT
        )
    entering = entering[2 * H :] + entering[0 : 2 * H]
    diagonal = iota((1, LV), 1) // V == iota((H, 1), 0)
    step_row = jnp.sum(step_table, axis=0, keepdims=True)
    enter_up = step_row * jnp.sum(
        jnp.where(diagonal, entering[0:H], 0.0), axis=0, keepdims=True
    )
    enter_down = step_row * jnp.sum(
        jnp.where(diagonal, entering[H : 2 * H], 0.0), axis=0, keepdims=True
    )

    looked = jnp.concatenate(
        [decay_table, step_table, pairs[...], gain_table, silu(gates), emb[...]], axis=1
    )
    looked = jnp.concatenate(split3(looked), axis=0)
    token = tokens[pl.ds(mine, 1), :]
    onehot = (token == token_row[0 : 3 * V]).astype(f32).astype(bf16)
    rows = dot(onehot, looked, TN)
    decay, step = rows[:, 0:LV], rows[:, LV : 2 * LV]
    pair, gain = rows[:, 2 * LV : 3 * LV], rows[:, 3 * LV : 4 * LV]
    silu_rows = rows[:, 4 * LV : 4 * LV + C]
    out_embedded[...] = rows[:, 4 * LV + C :]

    up, fade = scan_rows(decay, step, 1)
    up = up + fade * enter_up
    down, fade = scan_rows(decay, step, -1)
    down = down + fade * enter_down

    spread_high, spread_low = [
        jnp.concatenate([part] * H, axis=0) * blocks[...] for part in split2(inners)
    ]
    both = jnp.concatenate([up * pair + gain, down * pair + gain], axis=0)
    high = both.astype(bf16)
    high_wide = high.astype(f32)
    low_turned = pltpu.roll(both - high_wide, LV // 2, 1)
    lower = iota((1, LV), 1) < LV // 2
    value = []
    for side in (0, 1):
        mixed = jnp.where(lower == (side == 0), high_wide, low_turned).astype(bf16)
        rows = slice(side * LV // 2, (side + 1) * LV // 2)
        columns = slice(side * C // 2, (side + 1) * C // 2)
        weight, rest = spread_high[rows, columns], spread_low[:, columns]
        value.append(
            dot(
                jnp.concatenate([mixed, high], axis=1),
                jnp.concatenate([weight, weight, rest], axis=0),
            )
        )
    value = jnp.concatenate(value, axis=1)
    value = value * jnp.concatenate([silu_rows, silu_rows], axis=0)
    wide = groups.shape[0]
    high, low = split2(value * value)
    starts = list(range(0, C, wide))
    rows = 2 * T
    stacked = [half[:, start : start + wide] for start in starts for half in (low, high)]
    squares = dot(jnp.concatenate(stacked, axis=0), groups[...])
    for number, start in enumerate(starts):
        place = 2 * number * rows
        square = squares[place : place + rows] + squares[place + rows : place + 2 * rows]
        stop = start + wide
        normed = value[:, start:stop] * lax.rsqrt(square * (1.0 / P) + epsilon)
        out_high[:, start:stop], out_low[:, start:stop] = split2(
            (normed[0:T] + normed[T : 2 * T]) * gains[:, start:stop]
        )


def project_kernel(dims, *refs):
    V, D, hl, ch, nh, ns, T, N = dims
    P = ch // hl
    refs = list(refs)

    def take(number):
        taken, refs[:] = refs[:number], refs[number:]
        return taken

    high, low, embedded, small, own_high, own_low, state_high, state_low, upto = take(9)
    order = first_turn(nh)[::-1]
    nears = dict(zip(order, take(nh - 1)))
    others = dict(zip(order, take(nh - 1)))
    out_state, out_high, out_low, out_scale = take(4)
    out_write, out_inner, out_stepped, out_total = take(4)
    half = ch // 2
    base = top_rows(dims)
    mine = lax.axis_index("seq")

    pieces = []
    for k in range(1, nh):
        near, other = [
            jnp.concatenate(
                [
                    ref[base + place * half : base + (place + 1) * half, :]
                    for place in range(D // ch)
                ],
                axis=1,
            )
            for ref in (nears[k], others[k])
        ]
        even = lax.rem(lax.bitwise_xor(mine, partners(ns, nh)[k][0]), 2) == 0
        pieces.append(jnp.where(even, near, other))
        pieces.append(jnp.where(even, other, near))
    weights = split2(jnp.concatenate(pieces, axis=0))
    weights = (
        jnp.concatenate([own_high[...], weights[0]], axis=0),
        jnp.concatenate([own_low[...], weights[1]], axis=0),
    )
    hidden = embedded[...] + dot_split((high[...], low[...]), weights)
    split = split2(hidden)
    out_high[...], out_low[...] = split
    scale = lax.rsqrt(jnp.mean(hidden * hidden, axis=-1, keepdims=True) + epsilon)
    out_scale[...] = jnp.broadcast_to(scale, (T, ch))

    rows = dot_split(split, (state_high[...], state_low[...])) * scale
    inner, write = rows[:, 0:ch], rows[:, 2 * ch :]
    step = softplus(rows[:, ch : 2 * ch] + small[0:1, :])
    stepped = inner * step
    log_high, log_middle, log_low = split3(-small[1:2, :] * step)
    total = dot(upto[...], jnp.concatenate([log_low, log_middle], axis=1))
    total = (total[:, 0:ch] + total[:, ch:]) + dot(upto[...], log_high)
    end = total[T - 1 : T, :]
    state = dot3(stepped * jnp.exp(end - total), write, TN)
    out_state[0:ch, :] = state
    for head in range(hl):
        out_state[ch + head : ch + head + 1, :] = jnp.broadcast_to(
            end[:, head * P : head * P + 1], (1, N)
        )
    out_write[...] = write
    out_inner[...] = inner
    out_stepped[...] = stepped
    out_total[...] = total


def block_kernel(dims, *refs):
    V, D, hl, ch, nh, ns, T, N = dims
    P = ch // hl
    refs = list(refs)

    def take(number):
        taken, refs[:] = refs[:number], refs[number:]
        return taken

    high, low, scale, write, inner, stepped, total, choose = take(8)
    rest_high, rest_low, small = take(3)
    base, read_high, read_low, out_fade, out_gate, own, hidden_ref = take(7)
    rows = dot_split((high[...], low[...]), (rest_high[...], rest_low[...]))
    out_gate[...] = silu(rows[:, 0:ch] * scale[...])
    read = rows[:, ch:] * scale[...]
    read = split2(read)
    read_high[...], read_low[...] = read
    out_fade[...] = jnp.exp(total[...])
    products = dot_split(read, split2(write[...]), NT)
    stepped_high, stepped_low = split2(stepped[...])
    select = (iota((8, ch), 1) == iota((8, ch), 0) * P).astype(f32).astype(bf16)
    total_high, total_middle, total_low = split3(total[...])
    total_t = (dot(select, total_low, NT) + dot(select, total_middle, NT)) + dot(
        select, total_high, NT
    )
    allowed = iota((T, 1), 0) >= iota((1, T), 1)
    parts = []
    for head in range(hl):
        start, stop = head * P, (head + 1) * P
        differ = total[:, start : start + 1] - total_t[head : head + 1, :]
        weights = jnp.where(allowed, jnp.exp(jnp.where(allowed, differ, 0.0)), 0.0) * products
        part = dot_split(
            split2(weights), (stepped_high[:, start:stop], stepped_low[:, start:stop])
        )
        parts.append(part + small[2:3, start:stop] * inner[:, start:stop])
    base[...] = jnp.concatenate(parts, axis=1)
    share = T // nh
    hidden_ref[...] = high[...].astype(f32) + low[...].astype(f32)
    place = pl.multiple_of(lax.axis_index("head") * share, 8)
    own[...] = dot_right_exact(hidden_ref[pl.ds(place, share), :], choose[...])


def state_rows(dims, values):
    V, D, hl, ch, nh, ns, T, N = dims
    head_of = iota((ch, N), 0) // (ch // hl)
    result = jnp.broadcast_to(values[0:1, :], (ch, N))
    for head in range(1, hl):
        result = jnp.where(head_of == head, values[head : head + 1, :], result)
    return result


def join_kernel(dims, bit, total, prefix, came, out_total, out_prefix):
    V, D, hl, ch, nh, ns, T, N = dims
    later = lax.rem(lax.div(lax.axis_index("seq"), 2**bit), 2) == 1
    came_state, came_log = came[0:ch, :], came[ch : ch + hl, :]
    state, log = total[0:ch, :], total[ch : ch + hl, :]
    factor = jnp.exp(state_rows(dims, jnp.where(later, log, came_log)))
    out_total[0:ch, :] = jnp.where(
        later, factor * came_state + state, factor * state + came_state
    )
    out_total[ch : ch + hl, :] = log + came_log
    if prefix is None:
        out_prefix[0:ch, :] = jnp.where(later, came_state, 0.0)
        out_prefix[ch : ch + hl, :] = jnp.where(later, came_log, 0.0)
    else:
        joined = prefix_joined(dims, bit, prefix, came)
        out_prefix[0:ch, :] = joined
        out_prefix[ch : ch + hl, :] = prefix[ch : ch + hl, :] + jnp.where(later, came_log, 0.0)


def prefix_joined(dims, bit, prefix, came):
    V, D, hl, ch, nh, ns, T, N = dims
    later = lax.rem(lax.div(lax.axis_index("seq"), 2**bit), 2) == 1
    factor = jnp.exp(state_rows(dims, prefix[ch : ch + hl, :]))
    return prefix[0:ch, :] + jnp.where(later, factor * came[0:ch, :], 0.0)


def output_kernel(dims, bit, *refs):
    V, D, hl, ch, nh, ns, T, N = dims
    P = ch // hl
    prefix, came, read_high, read_low, base, fade, gate, own, proj_high, proj_low = refs[:10]
    groups, outs, partial_ref = refs[10], refs[11 : 11 + nh], refs[11 + nh]
    entering = prefix_joined(dims, bit, prefix, came)
    carried = dot_split((read_high[...], read_low[...]), split2(entering), NT)
    value = (base[...] + carried * fade[...]) * gate[...]
    square = dot(jnp.concatenate(split2(value * value), axis=0), groups[0:ch, 0:ch])
    square = square[T:] + square[0:T]
    value = value * lax.rsqrt(square * (1.0 / P) + epsilon)
    share = T // nh
    partial_ref[...] = dot_split(split2(value), (proj_high[...], proj_low[...]))
    mine = lax.axis_index("head")
    for k in range(nh):
        place = pl.multiple_of(lax.bitwise_xor(mine, k) * share, 8)
        part = partial_ref[pl.ds(place, share), :]
        outs[k][...] = part + own[...] if k == 0 else part


def per_device(
    token_ids,
    embedding,
    complement,
    prenorm_first,
    inproj_first,
    statemap_first,
    stepmap_first,
    stepbias_first,
    rates_first,
    skipgain_first,
    outnorm_first,
    outproj_first,
    prenorm_second,
    inproj_second,
    statemap_second,
    stepmap_second,
    stepbias_second,
    rates_second,
    skipgain_second,
    outnorm_second,
    outproj_second,
):
    nh, ns = lax.axis_size("head"), lax.axis_size("seq")
    V, D = embedding.shape
    ch = inproj_first.shape[2]
    hl = stepmap_first.shape[1]
    N = statemap_first.shape[2]
    T = token_ids.shape[0]
    LV = nh * hl * V
    dims = (V, D, hl, ch, nh, ns, T, N)
    vmem = pl.BlockSpec(memory_space=pltpu.VMEM)
    anywhere = pl.BlockSpec(memory_space=pl.ANY)
    params = pltpu.CompilerParams(vmem_limit_bytes=LIMIT)

    def shape(*sizes, dtype=f32):
        return jax.ShapeDtypeStruct(sizes, dtype)

    def halves(*sizes):
        return [shape(*sizes, dtype=bf16)] * 2

    def room(value):
        return pltpu.VMEM(value.shape, value.dtype)

    def kept(values):
        return [pltpu.with_memory_space_constraint(value, pltpu.HBM) for value in values]

    def line(value):
        return value.reshape(1, -1)

    def flat(value):
        return value.reshape(-1, value.shape[-1])

    heavy = pl.CostEstimate(flops=960 * T * D * D, bytes_accessed=4 * T * D, transcendentals=T * D)

    half = ch // 2
    share = T // nh
    fetched = [
        flat(inproj_first),
        line(token_ids),
        embedding,
        line(prenorm_first),
        stepmap_first.T,
        line(stepbias_first),
        line(rates_first),
        line(skipgain_first),
        line(outnorm_first),
    ]
    message = pl.pallas_call(
        functools.partial(tables_kernel, dims),
        out_shape=pltpu.VMEM((top_rows(dims) + half * (D // ch), ch), f32),
        in_specs=[anywhere] * (len(fetched) + 1),
        out_specs=vmem,
        scratch_shapes=[room(value) for value in fetched]
        + [pltpu.SemaphoreType.DMA((len(fetched) - 1 + PIECES + D // ch,))],
        compiler_params=params,
        name="tables",
    )(*kept([*fetched, outproj_first]))

    prepared = [
        flat(inproj_second),
        flat(statemap_second),
        flat(statemap_first),
        outproj_first,
        outproj_second,
        embedding,
        line(prenorm_first),
        line(complement),
        line(prenorm_second),
        stepmap_second.T,
        line(stepbias_second),
        line(rates_second),
        line(skipgain_second),
        line(outnorm_second),
    ]
    (
        pair_table,
        small,
        choose,
        own_high,
        own_low,
        state_high,
        state_low,
        rest_high,
        rest_low,
        proj_high,
        proj_low,
        triangles,
        upto,
        groups,
        blocks,
    ) = pl.pallas_call(
        functools.partial(prepare_kernel, dims),
        out_shape=(
            shape(V, LV),
            shape(8, ch),
            shape(D, D, dtype=bf16),
            *halves(ch, D),
            *halves(D, 2 * ch + N),
            *halves(D, ch + N),
            *halves(ch, D),
            shape(T, 2 * T + 128, dtype=bf16),
            shape(T, T, dtype=bf16),
            shape(2 * ch, 2 * ch, dtype=bf16),
            shape(LV, nh * ch, dtype=bf16),
        ),
        in_specs=[anywhere] * len(prepared),
        out_specs=(vmem,) * 15,
        scratch_shapes=[room(value) for value in prepared]
        + [pltpu.SemaphoreType.DMA((len(prepared),))],
        compiler_params=params,
        cost_estimate=heavy,
        name="prepare",
    )(*kept(prepared))

    count = max(ns, nh)
    messages = {0: message}
    for k in first_turn(count):
        seq_bits, shift = partners(ns, nh)[k]
        pairs = [
            (seq * nh + head, (seq ^ seq_bits) * nh + (head + shift) % nh)
            for seq in range(ns)
            for head in range(nh)
        ]
        sent = message if k < nh else message[0 : top_rows(dims)]
        messages[k] = lax.ppermute(sent, ("seq", "head"), pairs)
    swap = [(seq, seq ^ 1) for seq in range(ns)]
    order = first_turn(nh)[::-1]
    others = [lax.ppermute(messages[k], "seq", swap) for k in order]

    mixed_high, mixed_low, embedded = pl.pallas_call(
        functools.partial(mix_kernel, dims),
        out_shape=(*halves(T, nh * ch), shape(T, D)),
        in_specs=[vmem] * (count + 5),
        out_specs=(vmem,) * 3,
        scratch_shapes=[pltpu.VMEM((max(ns, 8), T), f32)],
        compiler_params=params,
        cost_estimate=heavy,
        name="mix",
    )(
        *[messages[k] for k in first_turn(count)[::-1] + [0]],
        embedding,
        pair_table,
        triangles,
        groups,
        blocks,
    )

    state, hidden_high, hidden_low, scale, write, inner, stepped, total = pl.pallas_call(
        functools.partial(project_kernel, dims),
        out_shape=(
            shape(ch + 8, N),
            *halves(T, D),
            shape(T, ch),
            shape(T, N),
            shape(T, ch),
            shape(T, ch),
            shape(T, ch),
        ),
        in_specs=[vmem] * (9 + 2 * (nh - 1)),
        out_specs=(vmem,) * 8,
        compiler_params=params,
        name="project",
    )(
        mixed_high,
        mixed_low,
        embedded,
        small,
        own_high,
        own_low,
        state_high,
        state_low,
        upto,
        *[messages[k] for k in order],
        *others,
    )

    base, read_high, read_low, fade, gate, own = pl.pallas_call(
        functools.partial(block_kernel, dims),
        out_shape=(
            shape(T, ch),
            *halves(T, N),
            shape(T, ch),
            shape(T, ch),
            shape(share, D),
        ),
        in_specs=[vmem] * 11,
        out_specs=(vmem,) * 6,
        scratch_shapes=[pltpu.VMEM((T, D), f32)],
        compiler_params=params,
        cost_estimate=heavy,
        name="block",
    )(
        hidden_high,
        hidden_low,
        scale,
        write,
        inner,
        stepped,
        total,
        choose,
        rest_high,
        rest_low,
        small,
    )

    prefix = None
    bits = ns.bit_length() - 1
    for bit in range(bits):
        came = lax.ppermute(state, "seq", [(seq, seq ^ 2**bit) for seq in range(ns)])
        if bit == bits - 1:
            break
        given = [state] + ([] if prefix is None else [prefix]) + [came]

        def join(bit, known, *refs):
            if known:
                join_kernel(dims, bit, *refs)
            else:
                join_kernel(dims, bit, refs[0], None, *refs[1:])

        state, prefix = pl.pallas_call(
            functools.partial(join, bit, prefix is not None),
            out_shape=(shape(ch + 8, N),) * 2,
            in_specs=[vmem] * len(given),
            out_specs=(vmem,) * 2,
            compiler_params=params,
            name="join",
        )(*given)
    if prefix is None:
        prefix = jnp.zeros_like(state)

    parts = pl.pallas_call(
        functools.partial(output_kernel, dims, bits - 1),
        out_shape=(shape(share, D),) * nh,
        in_specs=[vmem] * 11,
        out_specs=(vmem,) * nh,
        scratch_shapes=[pltpu.VMEM((T, D), f32)],
        compiler_params=params,
        name="output",
    )(
        prefix,
        came,
        read_high,
        read_low,
        base,
        fade,
        gate,
        own,
        proj_high,
        proj_low,
        groups,
    )
    result = parts[0]
    for k in in_turn(nh):
        pairs = [(source, source ^ k) for source in range(nh)]
        result = result + lax.ppermute(parts[k], "head", pairs)
    return result


def solution(mesh):
    return jax.shard_map(
        per_device,
        mesh=mesh,
        in_specs=(
            P(("rep", "seq")),
            P(),
            P(),
            P(),
            P(None, None, "head"),
            P(),
            P(None, "head"),
            P("head"),
            P("head"),
            P("head"),
            P("head"),
            P("head", None),
            P(),
            P(None, None, "head"),
            P(),
            P(None, "head"),
            P("head"),
            P("head"),
            P("head"),
            P("head"),
            P("head", None),
        ),
        out_specs=P(("rep", "seq", "head"), None),
        check_vma=False,
    )
```

```python
import functools

import jax
import jax.numpy as jnp
from jax import lax
from jax.experimental import pallas as pl
from jax.experimental.pallas import tpu as pltpu
from jax.sharding import PartitionSpec as P

epsilon = 1e-05
f32 = jnp.float32
bf16 = jnp.bfloat16
LIMIT = 48 * 1024 * 1024

MM = (((1,), (0,)), ((), ()))
NT = (((1,), (1,)), ((), ()))
TN = (((0,), (0,)), ((), ()))


def partners(ns, nh):
    count = max(ns, nh)
    return [((ns - k) if 0 < k < ns else 0, k if k < nh else 0) for k in range(count)]


def in_turn(count):
    return sorted(range(1, count), key=lambda k: (-k.bit_length(), k))


def around(shift, count):
    ring = [place ^ place >> 1 for place in range(count)]
    if sorted(ring) != list(range(count)):
        ring = list(range(count))
    return [ring[(ring.index(plane) + shift) % count] for plane in range(count)]


def iota(shape, axis):
    return lax.broadcasted_iota(jnp.int32, shape, axis)


def split2(value):
    high = value.astype(bf16)
    return high, (value - high.astype(f32)).astype(bf16)


def split3(value):
    high = value.astype(bf16)
    rest = value - high.astype(f32)
    middle = rest.astype(bf16)
    return high, middle, (rest - middle.astype(f32)).astype(bf16)


def dot(left, right, dims=MM):
    return lax.dot_general(left, right, dims, preferred_element_type=f32)


def dot_split(left, right, dims=MM):
    axis = 1 if dims == TN else 0
    size = left[0].shape[axis]
    if size % 16:
        return (dot(left[0], right[1], dims) + dot(left[1], right[0], dims)) + dot(
            left[0], right[0], dims
        )
    both = dot(jnp.concatenate([left[1], left[0]], axis=axis), right[0], dims)
    return (dot(left[0], right[1], dims) + both[0:size]) + both[size:]


def dot3(left, right, dims=MM):
    return dot_split(split2(left), split2(right), dims)


def dot_left_exact(left, right, dims=MM):
    high, middle, low = split3(right)
    return (dot(left, low, dims) + dot(left, middle, dims)) + dot(left, high, dims)


def dot_right_exact(left, right, dims=MM):
    high, middle, low = split3(left)
    return (dot(low, right, dims) + dot(middle, right, dims)) + dot(high, right, dims)


def softplus(value):
    return jnp.maximum(value, 0.0) + jnp.log1p(jnp.exp(-jnp.abs(value)))


def silu(value):
    return value / (1.0 + jnp.exp(-value))


def rms(value):
    return value * lax.rsqrt(jnp.mean(value * value, axis=-1, keepdims=True) + epsilon)


def fetch(sources, places, semaphores):
    copies = []
    for number, (source, place) in enumerate(zip(sources, places)):
        copies.append(pltpu.make_async_copy(source, place, semaphores.at[number]))
        copies[-1].start()
    return copies


def fetch(sources, places, semaphores):
    copies = []
    for number, (source, place) in enumerate(zip(sources, places)):
        copies.append(pltpu.make_async_copy(source, place, semaphores.at[number]))
        copies[-1].start()
    return copies


PIECES = 1


def tables_kernel(dims, *refs):
    V, D, hl, ch, nh, ns, T, N = dims
    refs = list(refs)

    def take(number):
        taken, refs[:] = refs[:number], refs[number:]
        return taken

    sources = take(9)
    outproj_source, message = take(2)
    places = take(9)
    semaphores = take(1)[0]
    half = ch // 2
    top = top_rows(dims)
    core = lax.rem(lax.axis_index("seq"), 2)
    (inproj, tok, emb, prenorm, stepmap, bias, rates, skip, outnorm) = places
    size = inproj.shape[0] // PIECES
    pieces = [pl.ds(number * size, size) for number in range(PIECES)]
    rows = pl.ds(pl.multiple_of(core * half, 8), half)
    wide = [(place, pl.ds(place * ch, ch)) for place in range(D // ch)]
    copies = fetch(
        [sources[0].at[piece, :] for piece in pieces]
        + sources[1:]
        + [outproj_source.at[rows, columns] for _, columns in wide],
        [inproj.at[piece, :] for piece in pieces]
        + places[1:]
        + [message.at[pl.ds(top + place * half, half), :] for place, _ in wide],
        semaphores,
    )
    flip = (iota((T, 1), 0) + iota((1, T), 1) == T - 1).astype(f32).astype(bf16)
    for copy in copies[PIECES : PIECES + 8]:
        copy.wait()
    normed = split2(rms(emb[...]) * prenorm[...])
    raw_t = dot_split(split2(stepmap[...]), normed, NT)
    tokens = jnp.broadcast_to(tok[...].astype(f32), (8, T)).astype(bf16)
    tokens = dot(tokens, flip)
    for place in range(T // ch):
        message[2 * V + place : 2 * V + place + 1, :] = tokens[0:1, place * ch : (place + 1) * ch]
    row = 2 * V + T // ch
    message[row : row + 1, :] = outnorm[...]
    for head in range(hl):
        line = softplus(raw_t[head : head + 1, :] + bias[:, head : head + 1])
        row = row + 1
        message[row : row + 1, 0:V] = line
        message[row : row + 1, V : 2 * V] = -rates[:, head : head + 1] * line
        message[row : row + 1, 2 * V : 3 * V] = jnp.broadcast_to(skip[:, head : head + 1], (1, V))
    for copy in copies[:PIECES]:
        copy.wait()
    weights = jnp.concatenate(
        [inproj[pl.ds(0, D, stride=2), :], inproj[pl.ds(1, D, stride=2), :]], axis=1
    )
    both = dot_split(normed, split2(weights))
    message[0:V, :] = both[:, 0:ch]
    message[V : 2 * V, :] = both[:, ch:]
    for copy in copies[PIECES + 8 :]:
        copy.wait()


def top_rows(dims):
    V, D, hl, ch, nh, ns, T, N = dims
    return 2 * V + -(-(T // ch + 1 + hl) // 8) * 8


def head_line(dims, values):
    V, D, hl, ch, nh, ns, T, N = dims
    head_of = iota((1, ch), 1) // (ch // hl)
    line = jnp.zeros((1, ch), f32)
    for head in range(hl):
        line = jnp.where(head_of == head, values[:, head : head + 1], line)
    return line


def prepare_kernel(dims, *refs):
    V, D, hl, ch, nh, ns, T, N = dims
    H, P = nh * hl, ch // hl
    refs = list(refs)

    def take(number):
        taken, refs[:] = refs[:number], refs[number:]
        return taken

    sources = take(14)
    pairs, small, choose_out, own_high, own_low = take(5)
    state_high, state_low, rest_high, rest_low, out_high, out_low = take(6)
    triangles, upto, groups, blocks = take(4)
    places = take(14)
    semaphores = take(1)[0]
    copies = fetch(sources, places, semaphores)
    inproj2, statemap2, statemap, outproj, outproj2, emb, prenorm, complement = places[:8]
    prenorm2, stepmap2, bias2, rates2, skip2, outnorm2 = places[8:]
    row, column = iota((T, 1), 0), iota((1, T), 1)
    triangles[:, 0:T] = (row > column).astype(f32).astype(bf16)
    triangles[:, T : 2 * T] = (row < column).astype(f32).astype(bf16)
    triangles[:, 2 * T :] = jnp.ones((T, 128), bf16)
    upto[...] = (row >= column).astype(f32).astype(bf16)
    size = groups.shape[0]
    groups[...] = (iota((size, 1), 0) // P == iota((1, size), 1) // P).astype(f32).astype(bf16)
    rows, columns = blocks.shape
    blocks[...] = (iota((rows, 1), 0) // V == iota((1, columns), 1) // P).astype(f32).astype(bf16)
    for copy in copies:
        copy.wait()
    normed = split2(rms(emb[...]) * prenorm[...])
    write = dot_split(normed, split2(statemap[pl.ds(0, D, stride=2), :]))
    read = dot_split(normed, split2(statemap[pl.ds(1, D, stride=2), :]))
    pairs[...] = dot3(read, jnp.concatenate([write] * H, axis=0), NT)
    own_high[...], own_low[...] = split2(outproj[...])
    choose = (complement[...] == iota((D, 1), 0)).astype(f32).astype(bf16)
    choose_out[...] = choose
    gain = jnp.transpose(jnp.broadcast_to(prenorm2[...], (128, D)))

    def weights(values):
        return split2(dot_left_exact(choose, values))

    gain_wide = gain[:, 0:1]
    inner = inproj2[pl.ds(1, D, stride=2), :] * gain_wide
    step = jnp.transpose(
        jnp.concatenate(
            [jnp.broadcast_to(stepmap2[head : head + 1, :], (P, D)) for head in range(hl)], axis=0
        )
    )
    write2 = statemap2[pl.ds(0, D, stride=2), :] * gain_wide
    state_high[...], state_low[...] = weights(
        jnp.concatenate([inner, step * gain_wide, write2], axis=1)
    )
    gate = inproj2[pl.ds(0, D, stride=2), :] * gain_wide
    read2 = statemap2[pl.ds(1, D, stride=2), :] * gain_wide
    rest_high[...], rest_low[...] = weights(jnp.concatenate([gate, read2], axis=1))
    small[0:1, :] = head_line(dims, bias2)
    small[1:2, :] = head_line(dims, rates2)
    small[2:3, :] = head_line(dims, skip2)
    out_gain = jnp.transpose(jnp.broadcast_to(outnorm2[...], (128, ch)))
    out_high[...], out_low[...] = split2(outproj2[...] * out_gain[:, 0:1])


def shift_rows(value, amount, fill):
    size = value.shape[0]
    if amount % 8 == 0:
        empty = jnp.full((abs(amount),) + value.shape[1:], fill, value.dtype)
        if amount > 0:
            return jnp.concatenate([empty, value[: size - amount]], axis=0)
        return jnp.concatenate([value[-amount:], empty], axis=0)
    rolled = pltpu.roll(value, amount % size, 0)
    row = iota((8,) + value.shape[1:], 0)
    if amount > 0:
        edge = jnp.where(row >= amount, rolled[0:8], fill)
        return jnp.concatenate([edge, rolled[8:]], axis=0)
    edge = jnp.where(row < 8 + amount, rolled[size - 8 :], fill)
    return jnp.concatenate([rolled[: size - 8], edge], axis=0)


def scan_rows(decay, value, sign):
    size = value.shape[0]
    amount = 1
    while amount < size:
        value = value + decay * shift_rows(value, sign * amount, 0.0)
        decay = decay * shift_rows(decay, sign * amount, 1.0)
        amount *= 2
    return value, decay


def mix_kernel(dims, *refs):
    V, D, hl, ch, nh, ns, T, N = dims
    H, LV, P = nh * hl, nh * hl * V, ch // hl
    C = nh * ch
    refs = list(refs)

    def take(number):
        taken, refs[:] = refs[:number], refs[number:]
        return taken

    count = max(ns, nh)
    packets = dict(zip(in_turn(count)[::-1] + [0], take(count)))
    emb, pairs, triangles, groups, blocks = take(5)
    out_high, out_low, out_embedded = take(3)
    tokens = take(1)[0]
    mine = lax.axis_index("seq")

    for k in range(ns):
        block = ns - 1 - lax.bitwise_xor(mine, partners(ns, nh)[k][0])
        row = 2 * V
        pieces = [packets[k][row + place : row + place + 1, :] for place in range(T // ch)]
        tokens[pl.ds(block, 1), :] = jnp.concatenate(pieces, axis=1)

    first = 2 * V + T // ch + 1
    steps = jnp.concatenate(
        [packets[k][first : first + hl, 0 : 3 * V] for k in range(nh)], axis=0
    )
    log_t = steps[:, V : 2 * V]
    narrow = jnp.concatenate([part.astype(f32) for part in split3(steps)], axis=0).astype(bf16)
    spread_heads = (iota((1, LV), 1) // V == iota((3 * H, 1), 0) % H).astype(f32).astype(bf16)
    wide = dot(narrow, spread_heads, TN)
    own = iota((1, LV), 1) % V == iota((V, 1), 0)
    decay_table = jnp.exp(wide[V : 2 * V])
    step_table = jnp.where(own, wide[0:V], 0.0)
    gain_table = jnp.where(own, wide[2 * V : 3 * V], 0.0)
    gates = jnp.concatenate([packets[k][0:V, :] for k in range(nh)], axis=1)
    inners = jnp.concatenate([packets[k][V : 2 * V, :] for k in range(nh)], axis=1)
    gains = jnp.concatenate([packets[k][first - 1 : first, :] for k in range(nh)], axis=1)

    token_row = (iota((LV, 1), 0) % V).astype(f32)
    log_split = jnp.concatenate(split3(log_t), axis=1)
    onehots, logs = [], []
    for block in range(ns):
        onehot = (tokens[block : block + 1, :] == token_row).astype(f32).astype(bf16)
        onehots.append(onehot)
        logs.append(dot(log_split, onehot[0 : 3 * V, :]))
    logs = jnp.concatenate(logs, axis=0)
    size = ns * H
    sums = dot(jnp.concatenate(split3(logs)[::-1], axis=0), triangles[...])
    sums = (sums[0:size] + sums[size : 2 * size]) + sums[2 * size :]
    blocks_of = [sums[block * H : (block + 1) * H] for block in range(ns)]
    weight_up, weight_down = [None] * ns, [None] * ns
    gap = jnp.zeros((H, 128), f32)
    for block in reversed(range(ns)):
        wide = jnp.concatenate([gap] * (T // 128), axis=1)
        weight_up[block] = jnp.where(
            block < mine, jnp.exp(blocks_of[block][:, 0:T] + wide), 0.0
        )
        gap = jnp.where(block < mine, gap + blocks_of[block][:, 2 * T :], gap)
    gap = jnp.zeros((H, 128), f32)
    for block in range(ns):
        wide = jnp.concatenate([gap] * (T // 128), axis=1)
        weight_down[block] = jnp.where(
            block > mine, jnp.exp(blocks_of[block][:, T : 2 * T] + wide), 0.0
        )
        gap = jnp.where(block > mine, gap + blocks_of[block][:, 2 * T :], gap)
    entering = jnp.zeros((4 * H, LV), f32)
    for block in range(ns):
        both = jnp.concatenate([weight_up[block], weight_down[block]], axis=0)
        entering = entering + dot(
            jnp.concatenate(split2(both), axis=0), onehots[block], NT
        )
    entering = entering[2 * H :] + entering[0 : 2 * H]
    diagonal = iota((1, LV), 1) // V == iota((H, 1), 0)
    step_row = jnp.sum(step_table, axis=0, keepdims=True)
    enter_up = step_row * jnp.sum(
        jnp.where(diagonal, entering[0:H], 0.0), axis=0, keepdims=True
    )
    enter_down = step_row * jnp.sum(
        jnp.where(diagonal, entering[H : 2 * H], 0.0), axis=0, keepdims=True
    )

    looked = jnp.concatenate(
        [decay_table, step_table, pairs[...], gain_table, silu(gates), emb[...]], axis=1
    )
    looked = jnp.concatenate(split3(looked), axis=0)
    token = tokens[pl.ds(mine, 1), :]
    onehot = (token == token_row[0 : 3 * V]).astype(f32).astype(bf16)
    rows = dot(onehot, looked, TN)
    decay, step = rows[:, 0:LV], rows[:, LV : 2 * LV]
    pair, gain = rows[:, 2 * LV : 3 * LV], rows[:, 3 * LV : 4 * LV]
    silu_rows = rows[:, 4 * LV : 4 * LV + C]
    out_embedded[...] = rows[:, 4 * LV + C :]

    up, fade = scan_rows(decay, step, 1)
    up = up + fade * enter_up
    down, fade = scan_rows(decay, step, -1)
    down = down + fade * enter_down

    spread_high, spread_low = [
        jnp.concatenate([part] * H, axis=0) * blocks[...] for part in split2(inners)
    ]
    both = jnp.concatenate([up * pair + gain, down * pair + gain], axis=0)
    high = both.astype(bf16)
    high_wide = high.astype(f32)
    low_turned = pltpu.roll(both - high_wide, LV // 2, 1)
    lower = iota((1, LV), 1) < LV // 2
    value = []
    for side in (0, 1):
        mixed = jnp.where(lower == (side == 0), high_wide, low_turned).astype(bf16)
        rows = slice(side * LV // 2, (side + 1) * LV // 2)
        columns = slice(side * C // 2, (side + 1) * C // 2)
        weight, rest = spread_high[rows, columns], spread_low[:, columns]
        value.append(
            dot(
                jnp.concatenate([mixed, high], axis=1),
                jnp.concatenate([weight, weight, rest], axis=0),
            )
        )
    value = jnp.concatenate(value, axis=1)
    value = value * jnp.concatenate([silu_rows, silu_rows], axis=0)
    wide = groups.shape[0]
    high, low = split2(value * value)
    starts = list(range(0, C, wide))
    rows = 2 * T
    stacked = [half[:, start : start + wide] for start in starts for half in (low, high)]
    squares = dot(jnp.concatenate(stacked, axis=0), groups[...])
    for number, start in enumerate(starts):
        place = 2 * number * rows
        square = squares[place : place + rows] + squares[place + rows : place + 2 * rows]
        stop = start + wide
        normed = value[:, start:stop] * lax.rsqrt(square * (1.0 / P) + epsilon)
        out_high[:, start:stop], out_low[:, start:stop] = split2(
            (normed[0:T] + normed[T : 2 * T]) * gains[:, start:stop]
        )


def project_kernel(dims, *refs):
    V, D, hl, ch, nh, ns, T, N = dims
    P = ch // hl
    refs = list(refs)

    def take(number):
        taken, refs[:] = refs[:number], refs[number:]
        return taken

    high, low, embedded, small, own_high, own_low, state_high, state_low, upto = take(9)
    order = in_turn(nh)[::-1]
    nears = dict(zip(order, take(nh - 1)))
    others = dict(zip(order, take(nh - 1)))
    out_state, out_high, out_low, out_scale = take(4)
    out_write, out_inner, out_stepped, out_total = take(4)
    half = ch // 2
    base = top_rows(dims)
    mine = lax.axis_index("seq")

    pieces = []
    for k in range(1, nh):
        near, other = [
            jnp.concatenate(
                [
                    ref[base + place * half : base + (place + 1) * half, :]
                    for place in range(D // ch)
                ],
                axis=1,
            )
            for ref in (nears[k], others[k])
        ]
        even = lax.rem(lax.bitwise_xor(mine, partners(ns, nh)[k][0]), 2) == 0
        pieces.append(jnp.where(even, near, other))
        pieces.append(jnp.where(even, other, near))
    weights = split2(jnp.concatenate(pieces, axis=0))
    weights = (
        jnp.concatenate([own_high[...], weights[0]], axis=0),
        jnp.concatenate([own_low[...], weights[1]], axis=0),
    )
    hidden = embedded[...] + dot_split((high[...], low[...]), weights)
    split = split2(hidden)
    out_high[...], out_low[...] = split
    scale = lax.rsqrt(jnp.mean(hidden * hidden, axis=-1, keepdims=True) + epsilon)
    out_scale[...] = jnp.broadcast_to(scale, (T, ch))

    rows = dot_split(split, (state_high[...], state_low[...])) * scale
    inner, write = rows[:, 0:ch], rows[:, 2 * ch :]
    step = softplus(rows[:, ch : 2 * ch] + small[0:1, :])
    stepped = inner * step
    log_high, log_middle, log_low = split3(-small[1:2, :] * step)
    total = dot(upto[...], jnp.concatenate([log_low, log_middle], axis=1))
    total = (total[:, 0:ch] + total[:, ch:]) + dot(upto[...], log_high)
    end = total[T - 1 : T, :]
    state = dot3(stepped * jnp.exp(end - total), write, TN)
    out_state[0:ch, :] = state
    for head in range(hl):
        out_state[ch + head : ch + head + 1, :] = jnp.broadcast_to(
            end[:, head * P : head * P + 1], (1, N)
        )
    out_write[...] = write
    out_inner[...] = inner
    out_stepped[...] = stepped
    out_total[...] = total


def block_kernel(dims, *refs):
    V, D, hl, ch, nh, ns, T, N = dims
    P = ch // hl
    refs = list(refs)

    def take(number):
        taken, refs[:] = refs[:number], refs[number:]
        return taken

    high, low, scale, write, inner, stepped, total, choose = take(8)
    rest_high, rest_low, small = take(3)
    base, read_high, read_low, out_fade, out_gate, own, hidden_ref = take(7)
    rows = dot_split((high[...], low[...]), (rest_high[...], rest_low[...]))
    out_gate[...] = silu(rows[:, 0:ch] * scale[...])
    read = rows[:, ch:] * scale[...]
    read = split2(read)
    read_high[...], read_low[...] = read
    out_fade[...] = jnp.exp(total[...])
    products = dot_split(read, split2(write[...]), NT)
    stepped_high, stepped_low = split2(stepped[...])
    select = (iota((8, ch), 1) == iota((8, ch), 0) * P).astype(f32).astype(bf16)
    total_high, total_middle, total_low = split3(total[...])
    total_t = (dot(select, total_low, NT) + dot(select, total_middle, NT)) + dot(
        select, total_high, NT
    )
    allowed = iota((T, 1), 0) >= iota((1, T), 1)
    parts = []
    for head in range(hl):
        start, stop = head * P, (head + 1) * P
        differ = total[:, start : start + 1] - total_t[head : head + 1, :]
        weights = jnp.where(allowed, jnp.exp(jnp.where(allowed, differ, 0.0)), 0.0) * products
        part = dot_split(
            split2(weights), (stepped_high[:, start:stop], stepped_low[:, start:stop])
        )
        parts.append(part + small[2:3, start:stop] * inner[:, start:stop])
    base[...] = jnp.concatenate(parts, axis=1)
    share = T // nh
    hidden_ref[...] = high[...].astype(f32) + low[...].astype(f32)
    place = pl.multiple_of(lax.axis_index("head") * share, 8)
    own[...] = dot_right_exact(hidden_ref[pl.ds(place, share), :], choose[...])


def state_rows(dims, values):
    V, D, hl, ch, nh, ns, T, N = dims
    head_of = iota((ch, N), 0) // (ch // hl)
    result = jnp.broadcast_to(values[0:1, :], (ch, N))
    for head in range(1, hl):
        result = jnp.where(head_of == head, values[head : head + 1, :], result)
    return result


def join_kernel(dims, bit, total, prefix, came, out_total, out_prefix):
    V, D, hl, ch, nh, ns, T, N = dims
    later = lax.rem(lax.div(lax.axis_index("seq"), 2**bit), 2) == 1
    came_state, came_log = came[0:ch, :], came[ch : ch + hl, :]
    state, log = total[0:ch, :], total[ch : ch + hl, :]
    factor = jnp.exp(state_rows(dims, jnp.where(later, log, came_log)))
    out_total[0:ch, :] = jnp.where(
        later, factor * came_state + state, factor * state + came_state
    )
    out_total[ch : ch + hl, :] = log + came_log
    if prefix is None:
        out_prefix[0:ch, :] = jnp.where(later, came_state, 0.0)
        out_prefix[ch : ch + hl, :] = jnp.where(later, came_log, 0.0)
    else:
        joined = prefix_joined(dims, bit, prefix, came)
        out_prefix[0:ch, :] = joined
        out_prefix[ch : ch + hl, :] = prefix[ch : ch + hl, :] + jnp.where(later, came_log, 0.0)


def prefix_joined(dims, bit, prefix, came):
    V, D, hl, ch, nh, ns, T, N = dims
    later = lax.rem(lax.div(lax.axis_index("seq"), 2**bit), 2) == 1
    factor = jnp.exp(state_rows(dims, prefix[ch : ch + hl, :]))
    return prefix[0:ch, :] + jnp.where(later, factor * came[0:ch, :], 0.0)


def output_kernel(dims, bit, *refs):
    V, D, hl, ch, nh, ns, T, N = dims
    P = ch // hl
    prefix, came, read_high, read_low, base, fade, gate, own, proj_high, proj_low = refs[:10]
    groups, outs, partial_ref = refs[10], refs[11 : 11 + nh], refs[11 + nh]
    entering = prefix_joined(dims, bit, prefix, came)
    carried = dot_split((read_high[...], read_low[...]), split2(entering), NT)
    value = (base[...] + carried * fade[...]) * gate[...]
    square = dot(jnp.concatenate(split2(value * value), axis=0), groups[0:ch, 0:ch])
    square = square[T:] + square[0:T]
    value = value * lax.rsqrt(square * (1.0 / P) + epsilon)
    share = T // nh
    partial_ref[...] = dot_split(split2(value), (proj_high[...], proj_low[...]))
    mine = lax.axis_index("head")
    for k in range(nh):
        to = 0
        for plane, target in enumerate(around(k, nh)):
            to = jnp.where(mine == plane, target, to)
        place = pl.multiple_of(to * share, 8)
        part = partial_ref[pl.ds(place, share), :]
        outs[k][...] = part + own[...] if k == 0 else part


def per_device(
    token_ids,
    embedding,
    complement,
    prenorm_first,
    inproj_first,
    statemap_first,
    stepmap_first,
    stepbias_first,
    rates_first,
    skipgain_first,
    outnorm_first,
    outproj_first,
    prenorm_second,
    inproj_second,
    statemap_second,
    stepmap_second,
    stepbias_second,
    rates_second,
    skipgain_second,
    outnorm_second,
    outproj_second,
):
    nh, ns = lax.axis_size("head"), lax.axis_size("seq")
    V, D = embedding.shape
    ch = inproj_first.shape[2]
    hl = stepmap_first.shape[1]
    N = statemap_first.shape[2]
    T = token_ids.shape[0]
    LV = nh * hl * V
    dims = (V, D, hl, ch, nh, ns, T, N)
    vmem = pl.BlockSpec(memory_space=pltpu.VMEM)
    anywhere = pl.BlockSpec(memory_space=pl.ANY)
    params = pltpu.CompilerParams(vmem_limit_bytes=LIMIT)

    def shape(*sizes, dtype=f32):
        return jax.ShapeDtypeStruct(sizes, dtype)

    def halves(*sizes):
        return [shape(*sizes, dtype=bf16)] * 2

    def room(value):
        return pltpu.VMEM(value.shape, value.dtype)

    def kept(values):
        return [pltpu.with_memory_space_constraint(value, pltpu.HBM) for value in values]

    def line(value):
        return value.reshape(1, -1)

    def flat(value):
        return value.reshape(-1, value.shape[-1])

    heavy = pl.CostEstimate(flops=960 * T * D * D, bytes_accessed=4 * T * D, transcendentals=T * D)

    half = ch // 2
    share = T // nh
    fetched = [
        flat(inproj_first),
        line(token_ids),
        embedding,
        line(prenorm_first),
        stepmap_first.T,
        line(stepbias_first),
        line(rates_first),
        line(skipgain_first),
        line(outnorm_first),
    ]
    message = pl.pallas_call(
        functools.partial(tables_kernel, dims),
        out_shape=pltpu.VMEM((top_rows(dims) + half * (D // ch), ch), f32),
        in_specs=[anywhere] * (len(fetched) + 1),
        out_specs=vmem,
        scratch_shapes=[room(value) for value in fetched]
        + [pltpu.SemaphoreType.DMA((len(fetched) - 1 + PIECES + D // ch,))],
        compiler_params=params,
        name="tables",
    )(*kept([*fetched, outproj_first]))

    prepared = [
        flat(inproj_second),
        flat(statemap_second),
        flat(statemap_first),
        outproj_first,
        outproj_second,
        embedding,
        line(prenorm_first),
        line(complement),
        line(prenorm_second),
        stepmap_second.T,
        line(stepbias_second),
        line(rates_second),
        line(skipgain_second),
        line(outnorm_second),
    ]
    (
        pair_table,
        small,
        choose,
        own_high,
        own_low,
        state_high,
        state_low,
        rest_high,
        rest_low,
        proj_high,
        proj_low,
        triangles,
        upto,
        groups,
        blocks,
    ) = pl.pallas_call(
        functools.partial(prepare_kernel, dims),
        out_shape=(
            shape(V, LV),
            shape(8, ch),
            shape(D, D, dtype=bf16),
            *halves(ch, D),
            *halves(D, 2 * ch + N),
            *halves(D, ch + N),
            *halves(ch, D),
            shape(T, 2 * T + 128, dtype=bf16),
            shape(T, T, dtype=bf16),
            shape(2 * ch, 2 * ch, dtype=bf16),
            shape(LV, nh * ch, dtype=bf16),
        ),
        in_specs=[anywhere] * len(prepared),
        out_specs=(vmem,) * 15,
        scratch_shapes=[room(value) for value in prepared]
        + [pltpu.SemaphoreType.DMA((len(prepared),))],
        compiler_params=params,
        cost_estimate=heavy,
        name="prepare",
    )(*kept(prepared))

    count = max(ns, nh)
    messages = {0: message}
    for k in in_turn(count):
        seq_bits, head_bits = partners(ns, nh)[k]
        pairs = [
            (seq * nh + head, (seq ^ seq_bits) * nh + (head ^ head_bits))
            for seq in range(ns)
            for head in range(nh)
        ]
        sent = message if k < nh else message[0 : top_rows(dims)]
        messages[k] = lax.ppermute(sent, ("seq", "head"), pairs)
    swap = [(seq, seq ^ 1) for seq in range(ns)]
    order = in_turn(nh)[::-1]
    others = [lax.ppermute(messages[k], "seq", swap) for k in order]

    mixed_high, mixed_low, embedded = pl.pallas_call(
        functools.partial(mix_kernel, dims),
        out_shape=(*halves(T, nh * ch), shape(T, D)),
        in_specs=[vmem] * (count + 5),
        out_specs=(vmem,) * 3,
        scratch_shapes=[pltpu.VMEM((max(ns, 8), T), f32)],
        compiler_params=params,
        cost_estimate=heavy,
        name="mix",
    )(
        *[messages[k] for k in in_turn(count)[::-1] + [0]],
        embedding,
        pair_table,
        triangles,
        groups,
        blocks,
    )

    state, hidden_high, hidden_low, scale, write, inner, stepped, total = pl.pallas_call(
        functools.partial(project_kernel, dims),
        out_shape=(
            shape(ch + 8, N),
            *halves(T, D),
            shape(T, ch),
            shape(T, N),
            shape(T, ch),
            shape(T, ch),
            shape(T, ch),
        ),
        in_specs=[vmem] * (9 + 2 * (nh - 1)),
        out_specs=(vmem,) * 8,
        compiler_params=params,
        name="project",
    )(
        mixed_high,
        mixed_low,
        embedded,
        small,
        own_high,
        own_low,
        state_high,
        state_low,
        upto,
        *[messages[k] for k in order],
        *others,
    )

    base, read_high, read_low, fade, gate, own = pl.pallas_call(
        functools.partial(block_kernel, dims),
        out_shape=(
            shape(T, ch),
            *halves(T, N),
            shape(T, ch),
            shape(T, ch),
            shape(share, D),
        ),
        in_specs=[vmem] * 11,
        out_specs=(vmem,) * 6,
        scratch_shapes=[pltpu.VMEM((T, D), f32)],
        compiler_params=params,
        cost_estimate=heavy,
        name="block",
    )(
        hidden_high,
        hidden_low,
        scale,
        write,
        inner,
        stepped,
        total,
        choose,
        rest_high,
        rest_low,
        small,
    )

    prefix = None
    bits = ns.bit_length() - 1
    for bit in range(bits):
        came = lax.ppermute(state, "seq", [(seq, seq ^ 2**bit) for seq in range(ns)])
        if bit == bits - 1:
            break
        given = [state] + ([] if prefix is None else [prefix]) + [came]

        def join(bit, known, *refs):
            if known:
                join_kernel(dims, bit, *refs)
            else:
                join_kernel(dims, bit, refs[0], None, *refs[1:])

        state, prefix = pl.pallas_call(
            functools.partial(join, bit, prefix is not None),
            out_shape=(shape(ch + 8, N),) * 2,
            in_specs=[vmem] * len(given),
            out_specs=(vmem,) * 2,
            compiler_params=params,
            name="join",
        )(*given)
    if prefix is None:
        prefix = jnp.zeros_like(state)

    parts = pl.pallas_call(
        functools.partial(output_kernel, dims, bits - 1),
        out_shape=(shape(share, D),) * nh,
        in_specs=[vmem] * 11,
        out_specs=(vmem,) * nh,
        scratch_shapes=[pltpu.VMEM((T, D), f32)],
        compiler_params=params,
        name="output",
    )(
        prefix,
        came,
        read_high,
        read_low,
        base,
        fade,
        gate,
        own,
        proj_high,
        proj_low,
        groups,
    )
    result = parts[0]
    for k in range(1, nh):
        pairs = list(enumerate(around(k, nh)))
        result = result + lax.ppermute(parts[k], "head", pairs)
    return result


def solution(mesh):
    return jax.shard_map(
        per_device,
        mesh=mesh,
        in_specs=(
            P(("rep", "seq")),
            P(),
            P(),
            P(),
            P(None, None, "head"),
            P(),
            P(None, "head"),
            P("head"),
            P("head"),
            P("head"),
            P("head"),
            P("head", None),
            P(),
            P(None, None, "head"),
            P(),
            P(None, "head"),
            P("head"),
            P("head"),
            P("head"),
            P("head"),
            P("head", None),
        ),
        out_specs=P(("rep", "seq", "head"), None),
        check_vma=False,
    )
```

```python
import functools

import jax
import jax.numpy as jnp
from jax import lax
from jax.experimental import pallas as pl
from jax.experimental.pallas import tpu as pltpu
from jax.sharding import PartitionSpec as P

epsilon = 1e-05
f32 = jnp.float32
bf16 = jnp.bfloat16
LIMIT = 48 * 1024 * 1024

MM = (((1,), (0,)), ((), ()))
NT = (((1,), (1,)), ((), ()))
TN = (((0,), (0,)), ((), ()))


def partners(ns, nh):
    return [(k if k < ns else 0, k if k < nh else 0) for k in range(max(ns, nh))]


def first_turn(count):
    return list(range(1, count))


def around(shift, count):
    ring = [place ^ place >> 1 for place in range(count)]
    if sorted(ring) != list(range(count)):
        ring = list(range(count))
    return [ring[(ring.index(plane) + shift) % count] for plane in range(count)]


def iota(shape, axis):
    return lax.broadcasted_iota(jnp.int32, shape, axis)


def split2(value):
    high = value.astype(bf16)
    return high, (value - high.astype(f32)).astype(bf16)


def split3(value):
    high = value.astype(bf16)
    rest = value - high.astype(f32)
    middle = rest.astype(bf16)
    return high, middle, (rest - middle.astype(f32)).astype(bf16)


def dot(left, right, dims=MM):
    return lax.dot_general(left, right, dims, preferred_element_type=f32)


def dot_split(left, right, dims=MM):
    axis = 1 if dims == TN else 0
    size = left[0].shape[axis]
    if size % 16:
        return (dot(left[0], right[1], dims) + dot(left[1], right[0], dims)) + dot(
            left[0], right[0], dims
        )
    both = dot(jnp.concatenate([left[1], left[0]], axis=axis), right[0], dims)
    return (dot(left[0], right[1], dims) + both[0:size]) + both[size:]


def dot3(left, right, dims=MM):
    return dot_split(split2(left), split2(right), dims)


def dot_left_exact(left, right, dims=MM):
    high, middle, low = split3(right)
    return (dot(left, low, dims) + dot(left, middle, dims)) + dot(left, high, dims)


def dot_right_exact(left, right, dims=MM):
    high, middle, low = split3(left)
    return (dot(low, right, dims) + dot(middle, right, dims)) + dot(high, right, dims)


def softplus(value):
    return jnp.maximum(value, 0.0) + jnp.log1p(jnp.exp(-jnp.abs(value)))


def silu(value):
    return value / (1.0 + jnp.exp(-value))


def rms(value):
    return value * lax.rsqrt(jnp.mean(value * value, axis=-1, keepdims=True) + epsilon)


def fetch(sources, places, semaphores):
    copies = []
    for number, (source, place) in enumerate(zip(sources, places)):
        copies.append(pltpu.make_async_copy(source, place, semaphores.at[number]))
        copies[-1].start()
    return copies


def fetch(sources, places, semaphores):
    copies = []
    for number, (source, place) in enumerate(zip(sources, places)):
        copies.append(pltpu.make_async_copy(source, place, semaphores.at[number]))
        copies[-1].start()
    return copies


PIECES = 1


def tables_kernel(dims, *refs):
    V, D, hl, ch, nh, ns, T, N = dims
    refs = list(refs)

    def take(number):
        taken, refs[:] = refs[:number], refs[number:]
        return taken

    sources = take(9)
    outproj_source, message = take(2)
    places = take(9)
    semaphores = take(1)[0]
    half = ch // 2
    top = top_rows(dims)
    core = lax.rem(lax.axis_index("seq"), 2)
    (inproj, tok, emb, prenorm, stepmap, bias, rates, skip, outnorm) = places
    size = inproj.shape[0] // PIECES
    pieces = [pl.ds(number * size, size) for number in range(PIECES)]
    rows = pl.ds(pl.multiple_of(core * half, 8), half)
    wide = [(place, pl.ds(place * ch, ch)) for place in range(D // ch)]
    copies = fetch(
        [sources[0].at[piece, :] for piece in pieces]
        + sources[1:]
        + [outproj_source.at[rows, columns] for _, columns in wide],
        [inproj.at[piece, :] for piece in pieces]
        + places[1:]
        + [message.at[pl.ds(top + place * half, half), :] for place, _ in wide],
        semaphores,
    )
    flip = (iota((T, 1), 0) + iota((1, T), 1) == T - 1).astype(f32).astype(bf16)
    for copy in copies[PIECES : PIECES + 8]:
        copy.wait()
    normed = split2(rms(emb[...]) * prenorm[...])
    raw_t = dot_split(split2(stepmap[...]), normed, NT)
    tokens = jnp.broadcast_to(tok[...].astype(f32), (8, T)).astype(bf16)
    tokens = dot(tokens, flip)
    for place in range(T // ch):
        message[2 * V + place : 2 * V + place + 1, :] = tokens[0:1, place * ch : (place + 1) * ch]
    row = 2 * V + T // ch
    message[row : row + 1, :] = outnorm[...]
    for head in range(hl):
        line = softplus(raw_t[head : head + 1, :] + bias[:, head : head + 1])
        row = row + 1
        message[row : row + 1, 0:V] = line
        message[row : row + 1, V : 2 * V] = -rates[:, head : head + 1] * line
        message[row : row + 1, 2 * V : 3 * V] = jnp.broadcast_to(skip[:, head : head + 1], (1, V))
    for copy in copies[:PIECES]:
        copy.wait()
    weights = jnp.concatenate(
        [inproj[pl.ds(0, D, stride=2), :], inproj[pl.ds(1, D, stride=2), :]], axis=1
    )
    both = dot_split(normed, split2(weights))
    message[0:V, :] = both[:, 0:ch]
    message[V : 2 * V, :] = both[:, ch:]
    for copy in copies[PIECES + 8 :]:
        copy.wait()


def top_rows(dims):
    V, D, hl, ch, nh, ns, T, N = dims
    return 2 * V + -(-(T // ch + 1 + hl) // 8) * 8


def head_line(dims, values):
    V, D, hl, ch, nh, ns, T, N = dims
    head_of = iota((1, ch), 1) // (ch // hl)
    line = jnp.zeros((1, ch), f32)
    for head in range(hl):
        line = jnp.where(head_of == head, values[:, head : head + 1], line)
    return line


def prepare_kernel(dims, *refs):
    V, D, hl, ch, nh, ns, T, N = dims
    H, P = nh * hl, ch // hl
    refs = list(refs)

    def take(number):
        taken, refs[:] = refs[:number], refs[number:]
        return taken

    sources = take(14)
    pairs, small, choose_out, own_high, own_low = take(5)
    state_high, state_low, rest_high, rest_low, out_high, out_low = take(6)
    triangles, upto, groups, blocks = take(4)
    places = take(14)
    semaphores = take(1)[0]
    copies = fetch(sources, places, semaphores)
    inproj2, statemap2, statemap, outproj, outproj2, emb, prenorm, complement = places[:8]
    prenorm2, stepmap2, bias2, rates2, skip2, outnorm2 = places[8:]
    row, column = iota((T, 1), 0), iota((1, T), 1)
    triangles[:, 0:T] = (row > column).astype(f32).astype(bf16)
    triangles[:, T : 2 * T] = (row < column).astype(f32).astype(bf16)
    triangles[:, 2 * T :] = jnp.ones((T, 128), bf16)
    upto[...] = (row >= column).astype(f32).astype(bf16)
    size = groups.shape[0]
    groups[...] = (iota((size, 1), 0) // P == iota((1, size), 1) // P).astype(f32).astype(bf16)
    rows, columns = blocks.shape
    blocks[...] = (iota((rows, 1), 0) // V == iota((1, columns), 1) // P).astype(f32).astype(bf16)
    for copy in copies:
        copy.wait()
    normed = split2(rms(emb[...]) * prenorm[...])
    write = dot_split(normed, split2(statemap[pl.ds(0, D, stride=2), :]))
    read = dot_split(normed, split2(statemap[pl.ds(1, D, stride=2), :]))
    pairs[...] = dot3(read, jnp.concatenate([write] * H, axis=0), NT)
    own_high[...], own_low[...] = split2(outproj[...])
    choose = (complement[...] == iota((D, 1), 0)).astype(f32).astype(bf16)
    choose_out[...] = choose
    gain = jnp.transpose(jnp.broadcast_to(prenorm2[...], (128, D)))

    def weights(values):
        return split2(dot_left_exact(choose, values))

    gain_wide = gain[:, 0:1]
    inner = inproj2[pl.ds(1, D, stride=2), :] * gain_wide
    step = jnp.transpose(
        jnp.concatenate(
            [jnp.broadcast_to(stepmap2[head : head + 1, :], (P, D)) for head in range(hl)], axis=0
        )
    )
    write2 = statemap2[pl.ds(0, D, stride=2), :] * gain_wide
    state_high[...], state_low[...] = weights(
        jnp.concatenate([inner, step * gain_wide, write2], axis=1)
    )
    gate = inproj2[pl.ds(0, D, stride=2), :] * gain_wide
    read2 = statemap2[pl.ds(1, D, stride=2), :] * gain_wide
    rest_high[...], rest_low[...] = weights(jnp.concatenate([gate, read2], axis=1))
    small[0:1, :] = head_line(dims, bias2)
    small[1:2, :] = head_line(dims, rates2)
    small[2:3, :] = head_line(dims, skip2)
    out_gain = jnp.transpose(jnp.broadcast_to(outnorm2[...], (128, ch)))
    out_high[...], out_low[...] = split2(outproj2[...] * out_gain[:, 0:1])


def shift_rows(value, amount, fill):
    size = value.shape[0]
    if amount % 8 == 0:
        empty = jnp.full((abs(amount),) + value.shape[1:], fill, value.dtype)
        if amount > 0:
            return jnp.concatenate([empty, value[: size - amount]], axis=0)
        return jnp.concatenate([value[-amount:], empty], axis=0)
    rolled = pltpu.roll(value, amount % size, 0)
    row = iota((8,) + value.shape[1:], 0)
    if amount > 0:
        edge = jnp.where(row >= amount, rolled[0:8], fill)
        return jnp.concatenate([edge, rolled[8:]], axis=0)
    edge = jnp.where(row < 8 + amount, rolled[size - 8 :], fill)
    return jnp.concatenate([rolled[: size - 8], edge], axis=0)


def scan_rows(decay, value, sign):
    size = value.shape[0]
    amount = 1
    while amount < size:
        value = value + decay * shift_rows(value, sign * amount, 0.0)
        decay = decay * shift_rows(decay, sign * amount, 1.0)
        amount *= 2
    return value, decay


def mix_kernel(dims, *refs):
    V, D, hl, ch, nh, ns, T, N = dims
    H, LV, P = nh * hl, nh * hl * V, ch // hl
    C = nh * ch
    refs = list(refs)

    def take(number):
        taken, refs[:] = refs[:number], refs[number:]
        return taken

    count = max(ns, nh)
    packets = dict(zip(first_turn(count)[::-1] + [0], take(count)))
    emb, pairs, triangles, groups, blocks = take(5)
    out_high, out_low, out_embedded = take(3)
    tokens = take(1)[0]
    mine = lax.axis_index("seq")

    for k in range(ns):
        block = ns - 1 - lax.bitwise_xor(mine, partners(ns, nh)[k][0])
        row = 2 * V
        pieces = [packets[k][row + place : row + place + 1, :] for place in range(T // ch)]
        tokens[pl.ds(block, 1), :] = jnp.concatenate(pieces, axis=1)

    first = 2 * V + T // ch + 1
    steps = jnp.concatenate(
        [packets[k][first : first + hl, 0 : 3 * V] for k in range(nh)], axis=0
    )
    log_t = steps[:, V : 2 * V]
    narrow = jnp.concatenate([part.astype(f32) for part in split3(steps)], axis=0).astype(bf16)
    spread_heads = (iota((1, LV), 1) // V == iota((3 * H, 1), 0) % H).astype(f32).astype(bf16)
    wide = dot(narrow, spread_heads, TN)
    own = iota((1, LV), 1) % V == iota((V, 1), 0)
    decay_table = jnp.exp(wide[V : 2 * V])
    step_table = jnp.where(own, wide[0:V], 0.0)
    gain_table = jnp.where(own, wide[2 * V : 3 * V], 0.0)
    gates = jnp.concatenate([packets[k][0:V, :] for k in range(nh)], axis=1)
    inners = jnp.concatenate([packets[k][V : 2 * V, :] for k in range(nh)], axis=1)
    gains = jnp.concatenate([packets[k][first - 1 : first, :] for k in range(nh)], axis=1)

    token_row = (iota((LV, 1), 0) % V).astype(f32)
    log_split = jnp.concatenate(split3(log_t), axis=1)
    onehots, logs = [], []
    for block in range(ns):
        onehot = (tokens[block : block + 1, :] == token_row).astype(f32).astype(bf16)
        onehots.append(onehot)
        logs.append(dot(log_split, onehot[0 : 3 * V, :]))
    logs = jnp.concatenate(logs, axis=0)
    size = ns * H
    sums = dot(jnp.concatenate(split3(logs)[::-1], axis=0), triangles[...])
    sums = (sums[0:size] + sums[size : 2 * size]) + sums[2 * size :]
    blocks_of = [sums[block * H : (block + 1) * H] for block in range(ns)]
    weight_up, weight_down = [None] * ns, [None] * ns
    gap = jnp.zeros((H, 128), f32)
    for block in reversed(range(ns)):
        wide = jnp.concatenate([gap] * (T // 128), axis=1)
        weight_up[block] = jnp.where(
            block < mine, jnp.exp(blocks_of[block][:, 0:T] + wide), 0.0
        )
        gap = jnp.where(block < mine, gap + blocks_of[block][:, 2 * T :], gap)
    gap = jnp.zeros((H, 128), f32)
    for block in range(ns):
        wide = jnp.concatenate([gap] * (T // 128), axis=1)
        weight_down[block] = jnp.where(
            block > mine, jnp.exp(blocks_of[block][:, T : 2 * T] + wide), 0.0
        )
        gap = jnp.where(block > mine, gap + blocks_of[block][:, 2 * T :], gap)
    entering = jnp.zeros((4 * H, LV), f32)
    for block in range(ns):
        both = jnp.concatenate([weight_up[block], weight_down[block]], axis=0)
        entering = entering + dot(
            jnp.concatenate(split2(both), axis=0), onehots[block], NT
        )
    entering = entering[2 * H :] + entering[0 : 2 * H]
    diagonal = iota((1, LV), 1) // V == iota((H, 1), 0)
    step_row = jnp.sum(step_table, axis=0, keepdims=True)
    enter_up = step_row * jnp.sum(
        jnp.where(diagonal, entering[0:H], 0.0), axis=0, keepdims=True
    )
    enter_down = step_row * jnp.sum(
        jnp.where(diagonal, entering[H : 2 * H], 0.0), axis=0, keepdims=True
    )

    looked = jnp.concatenate(
        [decay_table, step_table, pairs[...], gain_table, silu(gates), emb[...]], axis=1
    )
    looked = jnp.concatenate(split3(looked), axis=0)
    token = tokens[pl.ds(mine, 1), :]
    onehot = (token == token_row[0 : 3 * V]).astype(f32).astype(bf16)
    rows = dot(onehot, looked, TN)
    decay, step = rows[:, 0:LV], rows[:, LV : 2 * LV]
    pair, gain = rows[:, 2 * LV : 3 * LV], rows[:, 3 * LV : 4 * LV]
    silu_rows = rows[:, 4 * LV : 4 * LV + C]
    out_embedded[...] = rows[:, 4 * LV + C :]

    up, fade = scan_rows(decay, step, 1)
    up = up + fade * enter_up
    down, fade = scan_rows(decay, step, -1)
    down = down + fade * enter_down

    spread_high, spread_low = [
        jnp.concatenate([part] * H, axis=0) * blocks[...] for part in split2(inners)
    ]
    both = jnp.concatenate([up * pair + gain, down * pair + gain], axis=0)
    high = both.astype(bf16)
    high_wide = high.astype(f32)
    low_turned = pltpu.roll(both - high_wide, LV // 2, 1)
    lower = iota((1, LV), 1) < LV // 2
    value = []
    for side in (0, 1):
        mixed = jnp.where(lower == (side == 0), high_wide, low_turned).astype(bf16)
        rows = slice(side * LV // 2, (side + 1) * LV // 2)
        columns = slice(side * C // 2, (side + 1) * C // 2)
        weight, rest = spread_high[rows, columns], spread_low[:, columns]
        value.append(
            dot(
                jnp.concatenate([mixed, high], axis=1),
                jnp.concatenate([weight, weight, rest], axis=0),
            )
        )
    value = jnp.concatenate(value, axis=1)
    value = value * jnp.concatenate([silu_rows, silu_rows], axis=0)
    wide = groups.shape[0]
    high, low = split2(value * value)
    starts = list(range(0, C, wide))
    rows = 2 * T
    stacked = [half[:, start : start + wide] for start in starts for half in (low, high)]
    squares = dot(jnp.concatenate(stacked, axis=0), groups[...])
    for number, start in enumerate(starts):
        place = 2 * number * rows
        square = squares[place : place + rows] + squares[place + rows : place + 2 * rows]
        stop = start + wide
        normed = value[:, start:stop] * lax.rsqrt(square * (1.0 / P) + epsilon)
        out_high[:, start:stop], out_low[:, start:stop] = split2(
            (normed[0:T] + normed[T : 2 * T]) * gains[:, start:stop]
        )


def project_kernel(dims, *refs):
    V, D, hl, ch, nh, ns, T, N = dims
    P = ch // hl
    refs = list(refs)

    def take(number):
        taken, refs[:] = refs[:number], refs[number:]
        return taken

    high, low, embedded, small, own_high, own_low, state_high, state_low, upto = take(9)
    order = first_turn(nh)[::-1]
    nears = dict(zip(order, take(nh - 1)))
    others = dict(zip(order, take(nh - 1)))
    out_state, out_high, out_low, out_scale = take(4)
    out_write, out_inner, out_stepped, out_total = take(4)
    half = ch // 2
    base = top_rows(dims)
    mine = lax.axis_index("seq")

    pieces = []
    for k in range(1, nh):
        near, other = [
            jnp.concatenate(
                [
                    ref[base + place * half : base + (place + 1) * half, :]
                    for place in range(D // ch)
                ],
                axis=1,
            )
            for ref in (nears[k], others[k])
        ]
        even = lax.rem(lax.bitwise_xor(mine, partners(ns, nh)[k][0]), 2) == 0
        pieces.append(jnp.where(even, near, other))
        pieces.append(jnp.where(even, other, near))
    weights = split2(jnp.concatenate(pieces, axis=0))
    weights = (
        jnp.concatenate([own_high[...], weights[0]], axis=0),
        jnp.concatenate([own_low[...], weights[1]], axis=0),
    )
    hidden = embedded[...] + dot_split((high[...], low[...]), weights)
    split = split2(hidden)
    out_high[...], out_low[...] = split
    scale = lax.rsqrt(jnp.mean(hidden * hidden, axis=-1, keepdims=True) + epsilon)
    out_scale[...] = jnp.broadcast_to(scale, (T, ch))

    rows = dot_split(split, (state_high[...], state_low[...])) * scale
    inner, write = rows[:, 0:ch], rows[:, 2 * ch :]
    step = softplus(rows[:, ch : 2 * ch] + small[0:1, :])
    stepped = inner * step
    log_high, log_middle, log_low = split3(-small[1:2, :] * step)
    total = dot(upto[...], jnp.concatenate([log_low, log_middle], axis=1))
    total = (total[:, 0:ch] + total[:, ch:]) + dot(upto[...], log_high)
    end = total[T - 1 : T, :]
    state = dot3(stepped * jnp.exp(end - total), write, TN)
    out_state[0:ch, :] = state
    for head in range(hl):
        out_state[ch + head : ch + head + 1, :] = jnp.broadcast_to(
            end[:, head * P : head * P + 1], (1, N)
        )
    out_write[...] = write
    out_inner[...] = inner
    out_stepped[...] = stepped
    out_total[...] = total


def block_kernel(dims, *refs):
    V, D, hl, ch, nh, ns, T, N = dims
    P = ch // hl
    refs = list(refs)

    def take(number):
        taken, refs[:] = refs[:number], refs[number:]
        return taken

    high, low, scale, write, inner, stepped, total, choose = take(8)
    rest_high, rest_low, small = take(3)
    base, read_high, read_low, out_fade, out_gate, own, hidden_ref = take(7)
    rows = dot_split((high[...], low[...]), (rest_high[...], rest_low[...]))
    out_gate[...] = silu(rows[:, 0:ch] * scale[...])
    read = rows[:, ch:] * scale[...]
    read = split2(read)
    read_high[...], read_low[...] = read
    out_fade[...] = jnp.exp(total[...])
    products = dot_split(read, split2(write[...]), NT)
    stepped_high, stepped_low = split2(stepped[...])
    select = (iota((8, ch), 1) == iota((8, ch), 0) * P).astype(f32).astype(bf16)
    total_high, total_middle, total_low = split3(total[...])
    total_t = (dot(select, total_low, NT) + dot(select, total_middle, NT)) + dot(
        select, total_high, NT
    )
    allowed = iota((T, 1), 0) >= iota((1, T), 1)
    parts = []
    for head in range(hl):
        start, stop = head * P, (head + 1) * P
        differ = total[:, start : start + 1] - total_t[head : head + 1, :]
        weights = jnp.where(allowed, jnp.exp(jnp.where(allowed, differ, 0.0)), 0.0) * products
        part = dot_split(
            split2(weights), (stepped_high[:, start:stop], stepped_low[:, start:stop])
        )
        parts.append(part + small[2:3, start:stop] * inner[:, start:stop])
    base[...] = jnp.concatenate(parts, axis=1)
    share = T // nh
    hidden_ref[...] = high[...].astype(f32) + low[...].astype(f32)
    place = pl.multiple_of(lax.axis_index("head") * share, 8)
    own[...] = dot_right_exact(hidden_ref[pl.ds(place, share), :], choose[...])


def state_rows(dims, values):
    V, D, hl, ch, nh, ns, T, N = dims
    head_of = iota((ch, N), 0) // (ch // hl)
    result = jnp.broadcast_to(values[0:1, :], (ch, N))
    for head in range(1, hl):
        result = jnp.where(head_of == head, values[head : head + 1, :], result)
    return result


def join_kernel(dims, bit, total, prefix, came, out_total, out_prefix):
    V, D, hl, ch, nh, ns, T, N = dims
    later = lax.rem(lax.div(lax.axis_index("seq"), 2**bit), 2) == 1
    came_state, came_log = came[0:ch, :], came[ch : ch + hl, :]
    state, log = total[0:ch, :], total[ch : ch + hl, :]
    factor = jnp.exp(state_rows(dims, jnp.where(later, log, came_log)))
    out_total[0:ch, :] = jnp.where(
        later, factor * came_state + state, factor * state + came_state
    )
    out_total[ch : ch + hl, :] = log + came_log
    if prefix is None:
        out_prefix[0:ch, :] = jnp.where(later, came_state, 0.0)
        out_prefix[ch : ch + hl, :] = jnp.where(later, came_log, 0.0)
    else:
        joined = prefix_joined(dims, bit, prefix, came)
        out_prefix[0:ch, :] = joined
        out_prefix[ch : ch + hl, :] = prefix[ch : ch + hl, :] + jnp.where(later, came_log, 0.0)


def prefix_joined(dims, bit, prefix, came):
    V, D, hl, ch, nh, ns, T, N = dims
    later = lax.rem(lax.div(lax.axis_index("seq"), 2**bit), 2) == 1
    factor = jnp.exp(state_rows(dims, prefix[ch : ch + hl, :]))
    return prefix[0:ch, :] + jnp.where(later, factor * came[0:ch, :], 0.0)


def output_kernel(dims, bit, *refs):
    V, D, hl, ch, nh, ns, T, N = dims
    P = ch // hl
    prefix, came, read_high, read_low, base, fade, gate, own, proj_high, proj_low = refs[:10]
    groups, outs, partial_ref = refs[10], refs[11 : 11 + nh], refs[11 + nh]
    entering = prefix_joined(dims, bit, prefix, came)
    carried = dot_split((read_high[...], read_low[...]), split2(entering), NT)
    value = (base[...] + carried * fade[...]) * gate[...]
    square = dot(jnp.concatenate(split2(value * value), axis=0), groups[0:ch, 0:ch])
    square = square[T:] + square[0:T]
    value = value * lax.rsqrt(square * (1.0 / P) + epsilon)
    share = T // nh
    partial_ref[...] = dot_split(split2(value), (proj_high[...], proj_low[...]))
    mine = lax.axis_index("head")
    for k in range(nh):
        to = 0
        for plane, target in enumerate(around(k, nh)):
            to = jnp.where(mine == plane, target, to)
        place = pl.multiple_of(to * share, 8)
        part = partial_ref[pl.ds(place, share), :]
        outs[k][...] = part + own[...] if k == 0 else part


def per_device(
    token_ids,
    embedding,
    complement,
    prenorm_first,
    inproj_first,
    statemap_first,
    stepmap_first,
    stepbias_first,
    rates_first,
    skipgain_first,
    outnorm_first,
    outproj_first,
    prenorm_second,
    inproj_second,
    statemap_second,
    stepmap_second,
    stepbias_second,
    rates_second,
    skipgain_second,
    outnorm_second,
    outproj_second,
):
    nh, ns = lax.axis_size("head"), lax.axis_size("seq")
    V, D = embedding.shape
    ch = inproj_first.shape[2]
    hl = stepmap_first.shape[1]
    N = statemap_first.shape[2]
    T = token_ids.shape[0]
    LV = nh * hl * V
    dims = (V, D, hl, ch, nh, ns, T, N)
    vmem = pl.BlockSpec(memory_space=pltpu.VMEM)
    anywhere = pl.BlockSpec(memory_space=pl.ANY)
    params = pltpu.CompilerParams(vmem_limit_bytes=LIMIT)

    def shape(*sizes, dtype=f32):
        return jax.ShapeDtypeStruct(sizes, dtype)

    def halves(*sizes):
        return [shape(*sizes, dtype=bf16)] * 2

    def room(value):
        return pltpu.VMEM(value.shape, value.dtype)

    def kept(values):
        return [pltpu.with_memory_space_constraint(value, pltpu.HBM) for value in values]

    def line(value):
        return value.reshape(1, -1)

    def flat(value):
        return value.reshape(-1, value.shape[-1])

    heavy = pl.CostEstimate(flops=960 * T * D * D, bytes_accessed=4 * T * D, transcendentals=T * D)

    half = ch // 2
    share = T // nh
    fetched = [
        flat(inproj_first),
        line(token_ids),
        embedding,
        line(prenorm_first),
        stepmap_first.T,
        line(stepbias_first),
        line(rates_first),
        line(skipgain_first),
        line(outnorm_first),
    ]
    message = pl.pallas_call(
        functools.partial(tables_kernel, dims),
        out_shape=pltpu.VMEM((top_rows(dims) + half * (D // ch), ch), f32),
        in_specs=[anywhere] * (len(fetched) + 1),
        out_specs=vmem,
        scratch_shapes=[room(value) for value in fetched]
        + [pltpu.SemaphoreType.DMA((len(fetched) - 1 + PIECES + D // ch,))],
        compiler_params=params,
        name="tables",
    )(*kept([*fetched, outproj_first]))

    prepared = [
        flat(inproj_second),
        flat(statemap_second),
        flat(statemap_first),
        outproj_first,
        outproj_second,
        embedding,
        line(prenorm_first),
        line(complement),
        line(prenorm_second),
        stepmap_second.T,
        line(stepbias_second),
        line(rates_second),
        line(skipgain_second),
        line(outnorm_second),
    ]
    (
        pair_table,
        small,
        choose,
        own_high,
        own_low,
        state_high,
        state_low,
        rest_high,
        rest_low,
        proj_high,
        proj_low,
        triangles,
        upto,
        groups,
        blocks,
    ) = pl.pallas_call(
        functools.partial(prepare_kernel, dims),
        out_shape=(
            shape(V, LV),
            shape(8, ch),
            shape(D, D, dtype=bf16),
            *halves(ch, D),
            *halves(D, 2 * ch + N),
            *halves(D, ch + N),
            *halves(ch, D),
            shape(T, 2 * T + 128, dtype=bf16),
            shape(T, T, dtype=bf16),
            shape(2 * ch, 2 * ch, dtype=bf16),
            shape(LV, nh * ch, dtype=bf16),
        ),
        in_specs=[anywhere] * len(prepared),
        out_specs=(vmem,) * 15,
        scratch_shapes=[room(value) for value in prepared]
        + [pltpu.SemaphoreType.DMA((len(prepared),))],
        compiler_params=params,
        cost_estimate=heavy,
        name="prepare",
    )(*kept(prepared))

    count = max(ns, nh)
    messages = {0: message}
    for k in first_turn(count):
        seq_bits, shift = partners(ns, nh)[k]
        pairs = [
            (seq * nh + head, (seq ^ seq_bits) * nh + (head + shift) % nh)
            for seq in range(ns)
            for head in range(nh)
        ]
        sent = message if k < nh else message[0 : top_rows(dims)]
        messages[k] = lax.ppermute(sent, ("seq", "head"), pairs)
    swap = [(seq, seq ^ 1) for seq in range(ns)]
    order = first_turn(nh)[::-1]
    others = [lax.ppermute(messages[k], "seq", swap) for k in order]

    mixed_high, mixed_low, embedded = pl.pallas_call(
        functools.partial(mix_kernel, dims),
        out_shape=(*halves(T, nh * ch), shape(T, D)),
        in_specs=[vmem] * (count + 5),
        out_specs=(vmem,) * 3,
        scratch_shapes=[pltpu.VMEM((max(ns, 8), T), f32)],
        compiler_params=params,
        cost_estimate=heavy,
        name="mix",
    )(
        *[messages[k] for k in first_turn(count)[::-1] + [0]],
        embedding,
        pair_table,
        triangles,
        groups,
        blocks,
    )

    state, hidden_high, hidden_low, scale, write, inner, stepped, total = pl.pallas_call(
        functools.partial(project_kernel, dims),
        out_shape=(
            shape(ch + 8, N),
            *halves(T, D),
            shape(T, ch),
            shape(T, N),
            shape(T, ch),
            shape(T, ch),
            shape(T, ch),
        ),
        in_specs=[vmem] * (9 + 2 * (nh - 1)),
        out_specs=(vmem,) * 8,
        compiler_params=params,
        name="project",
    )(
        mixed_high,
        mixed_low,
        embedded,
        small,
        own_high,
        own_low,
        state_high,
        state_low,
        upto,
        *[messages[k] for k in order],
        *others,
    )

    base, read_high, read_low, fade, gate, own = pl.pallas_call(
        functools.partial(block_kernel, dims),
        out_shape=(
            shape(T, ch),
            *halves(T, N),
            shape(T, ch),
            shape(T, ch),
            shape(share, D),
        ),
        in_specs=[vmem] * 11,
        out_specs=(vmem,) * 6,
        scratch_shapes=[pltpu.VMEM((T, D), f32)],
        compiler_params=params,
        cost_estimate=heavy,
        name="block",
    )(
        hidden_high,
        hidden_low,
        scale,
        write,
        inner,
        stepped,
        total,
        choose,
        rest_high,
        rest_low,
        small,
    )

    prefix = None
    bits = ns.bit_length() - 1
    for bit in range(bits):
        came = lax.ppermute(state, "seq", [(seq, seq ^ 2**bit) for seq in range(ns)])
        if bit == bits - 1:
            break
        given = [state] + ([] if prefix is None else [prefix]) + [came]

        def join(bit, known, *refs):
            if known:
                join_kernel(dims, bit, *refs)
            else:
                join_kernel(dims, bit, refs[0], None, *refs[1:])

        state, prefix = pl.pallas_call(
            functools.partial(join, bit, prefix is not None),
            out_shape=(shape(ch + 8, N),) * 2,
            in_specs=[vmem] * len(given),
            out_specs=(vmem,) * 2,
            compiler_params=params,
            name="join",
        )(*given)
    if prefix is None:
        prefix = jnp.zeros_like(state)

    parts = pl.pallas_call(
        functools.partial(output_kernel, dims, bits - 1),
        out_shape=(shape(share, D),) * nh,
        in_specs=[vmem] * 11,
        out_specs=(vmem,) * nh,
        scratch_shapes=[pltpu.VMEM((T, D), f32)],
        compiler_params=params,
        name="output",
    )(
        prefix,
        came,
        read_high,
        read_low,
        base,
        fade,
        gate,
        own,
        proj_high,
        proj_low,
        groups,
    )
    result = parts[0]
    for k in range(1, nh):
        pairs = list(enumerate(around(k, nh)))
        result = result + lax.ppermute(parts[k], "head", pairs)
    return result


def solution(mesh):
    return jax.shard_map(
        per_device,
        mesh=mesh,
        in_specs=(
            P(("rep", "seq")),
            P(),
            P(),
            P(),
            P(None, None, "head"),
            P(),
            P(None, "head"),
            P("head"),
            P("head"),
            P("head"),
            P("head"),
            P("head", None),
            P(),
            P(None, None, "head"),
            P(),
            P(None, "head"),
            P("head"),
            P("head"),
            P("head"),
            P("head"),
            P("head", None),
        ),
        out_specs=P(("rep", "seq", "head"), None),
        check_vma=False,
    )
```

```python
import functools

import jax
import jax.numpy as jnp
from jax import lax
from jax.experimental import pallas as pl
from jax.experimental.pallas import tpu as pltpu
from jax.sharding import PartitionSpec as P

epsilon = 1e-05
f32 = jnp.float32
bf16 = jnp.bfloat16
LIMIT = 48 * 1024 * 1024

MM = (((1,), (0,)), ((), ()))
NT = (((1,), (1,)), ((), ()))
TN = (((0,), (0,)), ((), ()))


def partners(ns, nh):
    return [
        ((k + 1) % (ns - 1) + 1 if 0 < k < ns else 0, k if k < nh else 0)
        for k in range(max(ns, nh))
    ]


def first_turn(count):
    return list(range(1, count))


def around(shift, count):
    ring = [place ^ place >> 1 for place in range(count)]
    if sorted(ring) != list(range(count)):
        ring = list(range(count))
    return [ring[(ring.index(plane) + shift) % count] for plane in range(count)]


def iota(shape, axis):
    return lax.broadcasted_iota(jnp.int32, shape, axis)


def split2(value):
    high = value.astype(bf16)
    return high, (value - high.astype(f32)).astype(bf16)


def split3(value):
    high = value.astype(bf16)
    rest = value - high.astype(f32)
    middle = rest.astype(bf16)
    return high, middle, (rest - middle.astype(f32)).astype(bf16)


def dot(left, right, dims=MM):
    return lax.dot_general(left, right, dims, preferred_element_type=f32)


def dot_split(left, right, dims=MM):
    axis = 1 if dims == TN else 0
    size = left[0].shape[axis]
    if size % 16:
        return (dot(left[0], right[1], dims) + dot(left[1], right[0], dims)) + dot(
            left[0], right[0], dims
        )
    both = dot(jnp.concatenate([left[1], left[0]], axis=axis), right[0], dims)
    return (dot(left[0], right[1], dims) + both[0:size]) + both[size:]


def dot3(left, right, dims=MM):
    return dot_split(split2(left), split2(right), dims)


def dot_left_exact(left, right, dims=MM):
    high, middle, low = split3(right)
    return (dot(left, low, dims) + dot(left, middle, dims)) + dot(left, high, dims)


def dot_right_exact(left, right, dims=MM):
    high, middle, low = split3(left)
    return (dot(low, right, dims) + dot(middle, right, dims)) + dot(high, right, dims)


def softplus(value):
    return jnp.maximum(value, 0.0) + jnp.log1p(jnp.exp(-jnp.abs(value)))


def silu(value):
    return value / (1.0 + jnp.exp(-value))


def rms(value):
    return value * lax.rsqrt(jnp.mean(value * value, axis=-1, keepdims=True) + epsilon)


def fetch(sources, places, semaphores):
    copies = []
    for number, (source, place) in enumerate(zip(sources, places)):
        copies.append(pltpu.make_async_copy(source, place, semaphores.at[number]))
        copies[-1].start()
    return copies


def fetch(sources, places, semaphores):
    copies = []
    for number, (source, place) in enumerate(zip(sources, places)):
        copies.append(pltpu.make_async_copy(source, place, semaphores.at[number]))
        copies[-1].start()
    return copies


PIECES = 1


def tables_kernel(dims, *refs):
    V, D, hl, ch, nh, ns, T, N = dims
    refs = list(refs)

    def take(number):
        taken, refs[:] = refs[:number], refs[number:]
        return taken

    sources = take(9)
    outproj_source, message = take(2)
    places = take(9)
    semaphores = take(1)[0]
    half = ch // 2
    top = top_rows(dims)
    core = lax.rem(lax.axis_index("seq"), 2)
    (inproj, tok, emb, prenorm, stepmap, bias, rates, skip, outnorm) = places
    size = inproj.shape[0] // PIECES
    pieces = [pl.ds(number * size, size) for number in range(PIECES)]
    rows = pl.ds(pl.multiple_of(core * half, 8), half)
    wide = [(place, pl.ds(place * ch, ch)) for place in range(D // ch)]
    copies = fetch(
        [sources[0].at[piece, :] for piece in pieces]
        + sources[1:]
        + [outproj_source.at[rows, columns] for _, columns in wide],
        [inproj.at[piece, :] for piece in pieces]
        + places[1:]
        + [message.at[pl.ds(top + place * half, half), :] for place, _ in wide],
        semaphores,
    )
    flip = (iota((T, 1), 0) + iota((1, T), 1) == T - 1).astype(f32).astype(bf16)
    for copy in copies[PIECES : PIECES + 8]:
        copy.wait()
    normed = split2(rms(emb[...]) * prenorm[...])
    raw_t = dot_split(split2(stepmap[...]), normed, NT)
    tokens = jnp.broadcast_to(tok[...].astype(f32), (8, T)).astype(bf16)
    tokens = dot(tokens, flip)
    for place in range(T // ch):
        message[2 * V + place : 2 * V + place + 1, :] = tokens[0:1, place * ch : (place + 1) * ch]
    row = 2 * V + T // ch
    message[row : row + 1, :] = outnorm[...]
    for head in range(hl):
        line = softplus(raw_t[head : head + 1, :] + bias[:, head : head + 1])
        row = row + 1
        message[row : row + 1, 0:V] = line
        message[row : row + 1, V : 2 * V] = -rates[:, head : head + 1] * line
        message[row : row + 1, 2 * V : 3 * V] = jnp.broadcast_to(skip[:, head : head + 1], (1, V))
    for copy in copies[:PIECES]:
        copy.wait()
    weights = jnp.concatenate(
        [inproj[pl.ds(0, D, stride=2), :], inproj[pl.ds(1, D, stride=2), :]], axis=1
    )
    both = dot_split(normed, split2(weights))
    message[0:V, :] = both[:, 0:ch]
    message[V : 2 * V, :] = both[:, ch:]
    for copy in copies[PIECES + 8 :]:
        copy.wait()


def top_rows(dims):
    V, D, hl, ch, nh, ns, T, N = dims
    return 2 * V + -(-(T // ch + 1 + hl) // 8) * 8


def head_line(dims, values):
    V, D, hl, ch, nh, ns, T, N = dims
    head_of = iota((1, ch), 1) // (ch // hl)
    line = jnp.zeros((1, ch), f32)
    for head in range(hl):
        line = jnp.where(head_of == head, values[:, head : head + 1], line)
    return line


def prepare_kernel(dims, *refs):
    V, D, hl, ch, nh, ns, T, N = dims
    H, P = nh * hl, ch // hl
    refs = list(refs)

    def take(number):
        taken, refs[:] = refs[:number], refs[number:]
        return taken

    sources = take(14)
    pairs, small, choose_out, own_high, own_low = take(5)
    state_high, state_low, rest_high, rest_low, out_high, out_low = take(6)
    triangles, upto, groups, blocks = take(4)
    places = take(14)
    semaphores = take(1)[0]
    copies = fetch(sources, places, semaphores)
    inproj2, statemap2, statemap, outproj, outproj2, emb, prenorm, complement = places[:8]
    prenorm2, stepmap2, bias2, rates2, skip2, outnorm2 = places[8:]
    row, column = iota((T, 1), 0), iota((1, T), 1)
    triangles[:, 0:T] = (row > column).astype(f32).astype(bf16)
    triangles[:, T : 2 * T] = (row < column).astype(f32).astype(bf16)
    triangles[:, 2 * T :] = jnp.ones((T, 128), bf16)
    upto[...] = (row >= column).astype(f32).astype(bf16)
    size = groups.shape[0]
    groups[...] = (iota((size, 1), 0) // P == iota((1, size), 1) // P).astype(f32).astype(bf16)
    rows, columns = blocks.shape
    blocks[...] = (iota((rows, 1), 0) // V == iota((1, columns), 1) // P).astype(f32).astype(bf16)
    for copy in copies:
        copy.wait()
    normed = split2(rms(emb[...]) * prenorm[...])
    write = dot_split(normed, split2(statemap[pl.ds(0, D, stride=2), :]))
    read = dot_split(normed, split2(statemap[pl.ds(1, D, stride=2), :]))
    pairs[...] = dot3(read, jnp.concatenate([write] * H, axis=0), NT)
    own_high[...], own_low[...] = split2(outproj[...])
    choose = (complement[...] == iota((D, 1), 0)).astype(f32).astype(bf16)
    choose_out[...] = choose
    gain = jnp.transpose(jnp.broadcast_to(prenorm2[...], (128, D)))

    def weights(values):
        return split2(dot_left_exact(choose, values))

    gain_wide = gain[:, 0:1]
    inner = inproj2[pl.ds(1, D, stride=2), :] * gain_wide
    step = jnp.transpose(
        jnp.concatenate(
            [jnp.broadcast_to(stepmap2[head : head + 1, :], (P, D)) for head in range(hl)], axis=0
        )
    )
    write2 = statemap2[pl.ds(0, D, stride=2), :] * gain_wide
    state_high[...], state_low[...] = weights(
        jnp.concatenate([inner, step * gain_wide, write2], axis=1)
    )
    gate = inproj2[pl.ds(0, D, stride=2), :] * gain_wide
    read2 = statemap2[pl.ds(1, D, stride=2), :] * gain_wide
    rest_high[...], rest_low[...] = weights(jnp.concatenate([gate, read2], axis=1))
    small[0:1, :] = head_line(dims, bias2)
    small[1:2, :] = head_line(dims, rates2)
    small[2:3, :] = head_line(dims, skip2)
    out_gain = jnp.transpose(jnp.broadcast_to(outnorm2[...], (128, ch)))
    out_high[...], out_low[...] = split2(outproj2[...] * out_gain[:, 0:1])


def shift_rows(value, amount, fill):
    size = value.shape[0]
    if amount % 8 == 0:
        empty = jnp.full((abs(amount),) + value.shape[1:], fill, value.dtype)
        if amount > 0:
            return jnp.concatenate([empty, value[: size - amount]], axis=0)
        return jnp.concatenate([value[-amount:], empty], axis=0)
    rolled = pltpu.roll(value, amount % size, 0)
    row = iota((8,) + value.shape[1:], 0)
    if amount > 0:
        edge = jnp.where(row >= amount, rolled[0:8], fill)
        return jnp.concatenate([edge, rolled[8:]], axis=0)
    edge = jnp.where(row < 8 + amount, rolled[size - 8 :], fill)
    return jnp.concatenate([rolled[: size - 8], edge], axis=0)


def scan_rows(decay, value, sign):
    size = value.shape[0]
    amount = 1
    while amount < size:
        value = value + decay * shift_rows(value, sign * amount, 0.0)
        decay = decay * shift_rows(decay, sign * amount, 1.0)
        amount *= 2
    return value, decay


def mix_kernel(dims, *refs):
    V, D, hl, ch, nh, ns, T, N = dims
    H, LV, P = nh * hl, nh * hl * V, ch // hl
    C = nh * ch
    refs = list(refs)

    def take(number):
        taken, refs[:] = refs[:number], refs[number:]
        return taken

    count = max(ns, nh)
    packets = dict(zip(first_turn(count)[::-1] + [0], take(count)))
    emb, pairs, triangles, groups, blocks = take(5)
    out_high, out_low, out_embedded = take(3)
    tokens = take(1)[0]
    mine = lax.axis_index("seq")

    for k in range(ns):
        block = ns - 1 - lax.bitwise_xor(mine, partners(ns, nh)[k][0])
        row = 2 * V
        pieces = [packets[k][row + place : row + place + 1, :] for place in range(T // ch)]
        tokens[pl.ds(block, 1), :] = jnp.concatenate(pieces, axis=1)

    first = 2 * V + T // ch + 1
    steps = jnp.concatenate(
        [packets[k][first : first + hl, 0 : 3 * V] for k in range(nh)], axis=0
    )
    log_t = steps[:, V : 2 * V]
    narrow = jnp.concatenate([part.astype(f32) for part in split3(steps)], axis=0).astype(bf16)
    spread_heads = (iota((1, LV), 1) // V == iota((3 * H, 1), 0) % H).astype(f32).astype(bf16)
    wide = dot(narrow, spread_heads, TN)
    own = iota((1, LV), 1) % V == iota((V, 1), 0)
    decay_table = jnp.exp(wide[V : 2 * V])
    step_table = jnp.where(own, wide[0:V], 0.0)
    gain_table = jnp.where(own, wide[2 * V : 3 * V], 0.0)
    gates = jnp.concatenate([packets[k][0:V, :] for k in range(nh)], axis=1)
    inners = jnp.concatenate([packets[k][V : 2 * V, :] for k in range(nh)], axis=1)
    gains = jnp.concatenate([packets[k][first - 1 : first, :] for k in range(nh)], axis=1)

    token_row = (iota((LV, 1), 0) % V).astype(f32)
    log_split = jnp.concatenate(split3(log_t), axis=1)
    onehots, logs = [], []
    for block in range(ns):
        onehot = (tokens[block : block + 1, :] == token_row).astype(f32).astype(bf16)
        onehots.append(onehot)
        logs.append(dot(log_split, onehot[0 : 3 * V, :]))
    logs = jnp.concatenate(logs, axis=0)
    size = ns * H
    sums = dot(jnp.concatenate(split3(logs)[::-1], axis=0), triangles[...])
    sums = (sums[0:size] + sums[size : 2 * size]) + sums[2 * size :]
    blocks_of = [sums[block * H : (block + 1) * H] for block in range(ns)]
    weight_up, weight_down = [None] * ns, [None] * ns
    gap = jnp.zeros((H, 128), f32)
    for block in reversed(range(ns)):
        wide = jnp.concatenate([gap] * (T // 128), axis=1)
        weight_up[block] = jnp.where(
            block < mine, jnp.exp(blocks_of[block][:, 0:T] + wide), 0.0
        )
        gap = jnp.where(block < mine, gap + blocks_of[block][:, 2 * T :], gap)
    gap = jnp.zeros((H, 128), f32)
    for block in range(ns):
        wide = jnp.concatenate([gap] * (T // 128), axis=1)
        weight_down[block] = jnp.where(
            block > mine, jnp.exp(blocks_of[block][:, T : 2 * T] + wide), 0.0
        )
        gap = jnp.where(block > mine, gap + blocks_of[block][:, 2 * T :], gap)
    entering = jnp.zeros((4 * H, LV), f32)
    for block in range(ns):
        both = jnp.concatenate([weight_up[block], weight_down[block]], axis=0)
        entering = entering + dot(
            jnp.concatenate(split2(both), axis=0), onehots[block], NT
        )
    entering = entering[2 * H :] + entering[0 : 2 * H]
    diagonal = iota((1, LV), 1) // V == iota((H, 1), 0)
    step_row = jnp.sum(step_table, axis=0, keepdims=True)
    enter_up = step_row * jnp.sum(
        jnp.where(diagonal, entering[0:H], 0.0), axis=0, keepdims=True
    )
    enter_down = step_row * jnp.sum(
        jnp.where(diagonal, entering[H : 2 * H], 0.0), axis=0, keepdims=True
    )

    looked = jnp.concatenate(
        [decay_table, step_table, pairs[...], gain_table, silu(gates), emb[...]], axis=1
    )
    looked = jnp.concatenate(split3(looked), axis=0)
    token = tokens[pl.ds(mine, 1), :]
    onehot = (token == token_row[0 : 3 * V]).astype(f32).astype(bf16)
    rows = dot(onehot, looked, TN)
    decay, step = rows[:, 0:LV], rows[:, LV : 2 * LV]
    pair, gain = rows[:, 2 * LV : 3 * LV], rows[:, 3 * LV : 4 * LV]
    silu_rows = rows[:, 4 * LV : 4 * LV + C]
    out_embedded[...] = rows[:, 4 * LV + C :]

    up, fade = scan_rows(decay, step, 1)
    up = up + fade * enter_up
    down, fade = scan_rows(decay, step, -1)
    down = down + fade * enter_down

    spread_high, spread_low = [
        jnp.concatenate([part] * H, axis=0) * blocks[...] for part in split2(inners)
    ]
    both = jnp.concatenate([up * pair + gain, down * pair + gain], axis=0)
    high = both.astype(bf16)
    high_wide = high.astype(f32)
    low_turned = pltpu.roll(both - high_wide, LV // 2, 1)
    lower = iota((1, LV), 1) < LV // 2
    value = []
    for side in (0, 1):
        mixed = jnp.where(lower == (side == 0), high_wide, low_turned).astype(bf16)
        rows = slice(side * LV // 2, (side + 1) * LV // 2)
        columns = slice(side * C // 2, (side + 1) * C // 2)
        weight, rest = spread_high[rows, columns], spread_low[:, columns]
        value.append(
            dot(
                jnp.concatenate([mixed, high], axis=1),
                jnp.concatenate([weight, weight, rest], axis=0),
            )
        )
    value = jnp.concatenate(value, axis=1)
    value = value * jnp.concatenate([silu_rows, silu_rows], axis=0)
    wide = groups.shape[0]
    high, low = split2(value * value)
    starts = list(range(0, C, wide))
    rows = 2 * T
    stacked = [half[:, start : start + wide] for start in starts for half in (low, high)]
    squares = dot(jnp.concatenate(stacked, axis=0), groups[...])
    for number, start in enumerate(starts):
        place = 2 * number * rows
        square = squares[place : place + rows] + squares[place + rows : place + 2 * rows]
        stop = start + wide
        normed = value[:, start:stop] * lax.rsqrt(square * (1.0 / P) + epsilon)
        out_high[:, start:stop], out_low[:, start:stop] = split2(
            (normed[0:T] + normed[T : 2 * T]) * gains[:, start:stop]
        )


def project_kernel(dims, *refs):
    V, D, hl, ch, nh, ns, T, N = dims
    P = ch // hl
    refs = list(refs)

    def take(number):
        taken, refs[:] = refs[:number], refs[number:]
        return taken

    high, low, embedded, small, own_high, own_low, state_high, state_low, upto = take(9)
    order = first_turn(nh)[::-1]
    nears = dict(zip(order, take(nh - 1)))
    others = dict(zip(order, take(nh - 1)))
    out_state, out_high, out_low, out_scale = take(4)
    out_write, out_inner, out_stepped, out_total = take(4)
    half = ch // 2
    base = top_rows(dims)
    mine = lax.axis_index("seq")

    pieces = []
    for k in range(1, nh):
        near, other = [
            jnp.concatenate(
                [
                    ref[base + place * half : base + (place + 1) * half, :]
                    for place in range(D // ch)
                ],
                axis=1,
            )
            for ref in (nears[k], others[k])
        ]
        even = lax.rem(lax.bitwise_xor(mine, partners(ns, nh)[k][0]), 2) == 0
        pieces.append(jnp.where(even, near, other))
        pieces.append(jnp.where(even, other, near))
    weights = split2(jnp.concatenate(pieces, axis=0))
    weights = (
        jnp.concatenate([own_high[...], weights[0]], axis=0),
        jnp.concatenate([own_low[...], weights[1]], axis=0),
    )
    hidden = embedded[...] + dot_split((high[...], low[...]), weights)
    split = split2(hidden)
    out_high[...], out_low[...] = split
    scale = lax.rsqrt(jnp.mean(hidden * hidden, axis=-1, keepdims=True) + epsilon)
    out_scale[...] = jnp.broadcast_to(scale, (T, ch))

    rows = dot_split(split, (state_high[...], state_low[...])) * scale
    inner, write = rows[:, 0:ch], rows[:, 2 * ch :]
    step = softplus(rows[:, ch : 2 * ch] + small[0:1, :])
    stepped = inner * step
    log_high, log_middle, log_low = split3(-small[1:2, :] * step)
    total = dot(upto[...], jnp.concatenate([log_low, log_middle], axis=1))
    total = (total[:, 0:ch] + total[:, ch:]) + dot(upto[...], log_high)
    end = total[T - 1 : T, :]
    state = dot3(stepped * jnp.exp(end - total), write, TN)
    out_state[0:ch, :] = state
    for head in range(hl):
        out_state[ch + head : ch + head + 1, :] = jnp.broadcast_to(
            end[:, head * P : head * P + 1], (1, N)
        )
    out_write[...] = write
    out_inner[...] = inner
    out_stepped[...] = stepped
    out_total[...] = total


def block_kernel(dims, *refs):
    V, D, hl, ch, nh, ns, T, N = dims
    P = ch // hl
    refs = list(refs)

    def take(number):
        taken, refs[:] = refs[:number], refs[number:]
        return taken

    high, low, scale, write, inner, stepped, total, choose = take(8)
    rest_high, rest_low, small = take(3)
    base, read_high, read_low, out_fade, out_gate, own, hidden_ref = take(7)
    rows = dot_split((high[...], low[...]), (rest_high[...], rest_low[...]))
    out_gate[...] = silu(rows[:, 0:ch] * scale[...])
    read = rows[:, ch:] * scale[...]
    read = split2(read)
    read_high[...], read_low[...] = read
    out_fade[...] = jnp.exp(total[...])
    products = dot_split(read, split2(write[...]), NT)
    stepped_high, stepped_low = split2(stepped[...])
    select = (iota((8, ch), 1) == iota((8, ch), 0) * P).astype(f32).astype(bf16)
    total_high, total_middle, total_low = split3(total[...])
    total_t = (dot(select, total_low, NT) + dot(select, total_middle, NT)) + dot(
        select, total_high, NT
    )
    allowed = iota((T, 1), 0) >= iota((1, T), 1)
    parts = []
    for head in range(hl):
        start, stop = head * P, (head + 1) * P
        differ = total[:, start : start + 1] - total_t[head : head + 1, :]
        weights = jnp.where(allowed, jnp.exp(jnp.where(allowed, differ, 0.0)), 0.0) * products
        part = dot_split(
            split2(weights), (stepped_high[:, start:stop], stepped_low[:, start:stop])
        )
        parts.append(part + small[2:3, start:stop] * inner[:, start:stop])
    base[...] = jnp.concatenate(parts, axis=1)
    share = T // nh
    hidden_ref[...] = high[...].astype(f32) + low[...].astype(f32)
    place = pl.multiple_of(lax.axis_index("head") * share, 8)
    own[...] = dot_right_exact(hidden_ref[pl.ds(place, share), :], choose[...])


def state_rows(dims, values):
    V, D, hl, ch, nh, ns, T, N = dims
    head_of = iota((ch, N), 0) // (ch // hl)
    result = jnp.broadcast_to(values[0:1, :], (ch, N))
    for head in range(1, hl):
        result = jnp.where(head_of == head, values[head : head + 1, :], result)
    return result


def join_kernel(dims, bit, total, prefix, came, out_total, out_prefix):
    V, D, hl, ch, nh, ns, T, N = dims
    later = lax.rem(lax.div(lax.axis_index("seq"), 2**bit), 2) == 1
    came_state, came_log = came[0:ch, :], came[ch : ch + hl, :]
    state, log = total[0:ch, :], total[ch : ch + hl, :]
    factor = jnp.exp(state_rows(dims, jnp.where(later, log, came_log)))
    out_total[0:ch, :] = jnp.where(
        later, factor * came_state + state, factor * state + came_state
    )
    out_total[ch : ch + hl, :] = log + came_log
    if prefix is None:
        out_prefix[0:ch, :] = jnp.where(later, came_state, 0.0)
        out_prefix[ch : ch + hl, :] = jnp.where(later, came_log, 0.0)
    else:
        joined = prefix_joined(dims, bit, prefix, came)
        out_prefix[0:ch, :] = joined
        out_prefix[ch : ch + hl, :] = prefix[ch : ch + hl, :] + jnp.where(later, came_log, 0.0)


def prefix_joined(dims, bit, prefix, came):
    V, D, hl, ch, nh, ns, T, N = dims
    later = lax.rem(lax.div(lax.axis_index("seq"), 2**bit), 2) == 1
    factor = jnp.exp(state_rows(dims, prefix[ch : ch + hl, :]))
    return prefix[0:ch, :] + jnp.where(later, factor * came[0:ch, :], 0.0)


def output_kernel(dims, bit, *refs):
    V, D, hl, ch, nh, ns, T, N = dims
    P = ch // hl
    prefix, came, read_high, read_low, base, fade, gate, own, proj_high, proj_low = refs[:10]
    groups, outs, partial_ref = refs[10], refs[11 : 11 + nh], refs[11 + nh]
    entering = prefix_joined(dims, bit, prefix, came)
    carried = dot_split((read_high[...], read_low[...]), split2(entering), NT)
    value = (base[...] + carried * fade[...]) * gate[...]
    square = dot(jnp.concatenate(split2(value * value), axis=0), groups[0:ch, 0:ch])
    square = square[T:] + square[0:T]
    value = value * lax.rsqrt(square * (1.0 / P) + epsilon)
    share = T // nh
    partial_ref[...] = dot_split(split2(value), (proj_high[...], proj_low[...]))
    mine = lax.axis_index("head")
    for k in range(nh):
        to = 0
        for plane, target in enumerate(around(k, nh)):
            to = jnp.where(mine == plane, target, to)
        place = pl.multiple_of(to * share, 8)
        part = partial_ref[pl.ds(place, share), :]
        outs[k][...] = part + own[...] if k == 0 else part


def per_device(
    token_ids,
    embedding,
    complement,
    prenorm_first,
    inproj_first,
    statemap_first,
    stepmap_first,
    stepbias_first,
    rates_first,
    skipgain_first,
    outnorm_first,
    outproj_first,
    prenorm_second,
    inproj_second,
    statemap_second,
    stepmap_second,
    stepbias_second,
    rates_second,
    skipgain_second,
    outnorm_second,
    outproj_second,
):
    nh, ns = lax.axis_size("head"), lax.axis_size("seq")
    V, D = embedding.shape
    ch = inproj_first.shape[2]
    hl = stepmap_first.shape[1]
    N = statemap_first.shape[2]
    T = token_ids.shape[0]
    LV = nh * hl * V
    dims = (V, D, hl, ch, nh, ns, T, N)
    vmem = pl.BlockSpec(memory_space=pltpu.VMEM)
    anywhere = pl.BlockSpec(memory_space=pl.ANY)
    params = pltpu.CompilerParams(vmem_limit_bytes=LIMIT)

    def shape(*sizes, dtype=f32):
        return jax.ShapeDtypeStruct(sizes, dtype)

    def halves(*sizes):
        return [shape(*sizes, dtype=bf16)] * 2

    def room(value):
        return pltpu.VMEM(value.shape, value.dtype)

    def kept(values):
        return [pltpu.with_memory_space_constraint(value, pltpu.HBM) for value in values]

    def line(value):
        return value.reshape(1, -1)

    def flat(value):
        return value.reshape(-1, value.shape[-1])

    heavy = pl.CostEstimate(flops=960 * T * D * D, bytes_accessed=4 * T * D, transcendentals=T * D)

    half = ch // 2
    share = T // nh
    fetched = [
        flat(inproj_first),
        line(token_ids),
        embedding,
        line(prenorm_first),
        stepmap_first.T,
        line(stepbias_first),
        line(rates_first),
        line(skipgain_first),
        line(outnorm_first),
    ]
    message = pl.pallas_call(
        functools.partial(tables_kernel, dims),
        out_shape=pltpu.VMEM((top_rows(dims) + half * (D // ch), ch), f32),
        in_specs=[anywhere] * (len(fetched) + 1),
        out_specs=vmem,
        scratch_shapes=[room(value) for value in fetched]
        + [pltpu.SemaphoreType.DMA((len(fetched) - 1 + PIECES + D // ch,))],
        compiler_params=params,
        name="tables",
    )(*kept([*fetched, outproj_first]))

    prepared = [
        flat(inproj_second),
        flat(statemap_second),
        flat(statemap_first),
        outproj_first,
        outproj_second,
        embedding,
        line(prenorm_first),
        line(complement),
        line(prenorm_second),
        stepmap_second.T,
        line(stepbias_second),
        line(rates_second),
        line(skipgain_second),
        line(outnorm_second),
    ]
    (
        pair_table,
        small,
        choose,
        own_high,
        own_low,
        state_high,
        state_low,
        rest_high,
        rest_low,
        proj_high,
        proj_low,
        triangles,
        upto,
        groups,
        blocks,
    ) = pl.pallas_call(
        functools.partial(prepare_kernel, dims),
        out_shape=(
            shape(V, LV),
            shape(8, ch),
            shape(D, D, dtype=bf16),
            *halves(ch, D),
            *halves(D, 2 * ch + N),
            *halves(D, ch + N),
            *halves(ch, D),
            shape(T, 2 * T + 128, dtype=bf16),
            shape(T, T, dtype=bf16),
            shape(2 * ch, 2 * ch, dtype=bf16),
            shape(LV, nh * ch, dtype=bf16),
        ),
        in_specs=[anywhere] * len(prepared),
        out_specs=(vmem,) * 15,
        scratch_shapes=[room(value) for value in prepared]
        + [pltpu.SemaphoreType.DMA((len(prepared),))],
        compiler_params=params,
        cost_estimate=heavy,
        name="prepare",
    )(*kept(prepared))

    count = max(ns, nh)
    messages = {0: message}
    for k in first_turn(count):
        seq_bits, shift = partners(ns, nh)[k]
        pairs = [
            (seq * nh + head, (seq ^ seq_bits) * nh + (head + shift) % nh)
            for seq in range(ns)
            for head in range(nh)
        ]
        sent = message if k < nh else message[0 : top_rows(dims)]
        messages[k] = lax.ppermute(sent, ("seq", "head"), pairs)
    swap = [(seq, seq ^ 1) for seq in range(ns)]
    order = first_turn(nh)[::-1]
    others = [lax.ppermute(messages[k], "seq", swap) for k in order]

    mixed_high, mixed_low, embedded = pl.pallas_call(
        functools.partial(mix_kernel, dims),
        out_shape=(*halves(T, nh * ch), shape(T, D)),
        in_specs=[vmem] * (count + 5),
        out_specs=(vmem,) * 3,
        scratch_shapes=[pltpu.VMEM((max(ns, 8), T), f32)],
        compiler_params=params,
        cost_estimate=heavy,
        name="mix",
    )(
        *[messages[k] for k in first_turn(count)[::-1] + [0]],
        embedding,
        pair_table,
        triangles,
        groups,
        blocks,
    )

    state, hidden_high, hidden_low, scale, write, inner, stepped, total = pl.pallas_call(
        functools.partial(project_kernel, dims),
        out_shape=(
            shape(ch + 8, N),
            *halves(T, D),
            shape(T, ch),
            shape(T, N),
            shape(T, ch),
            shape(T, ch),
            shape(T, ch),
        ),
        in_specs=[vmem] * (9 + 2 * (nh - 1)),
        out_specs=(vmem,) * 8,
        compiler_params=params,
        name="project",
    )(
        mixed_high,
        mixed_low,
        embedded,
        small,
        own_high,
        own_low,
        state_high,
        state_low,
        upto,
        *[messages[k] for k in order],
        *others,
    )

    base, read_high, read_low, fade, gate, own = pl.pallas_call(
        functools.partial(block_kernel, dims),
        out_shape=(
            shape(T, ch),
            *halves(T, N),
            shape(T, ch),
            shape(T, ch),
            shape(share, D),
        ),
        in_specs=[vmem] * 11,
        out_specs=(vmem,) * 6,
        scratch_shapes=[pltpu.VMEM((T, D), f32)],
        compiler_params=params,
        cost_estimate=heavy,
        name="block",
    )(
        hidden_high,
        hidden_low,
        scale,
        write,
        inner,
        stepped,
        total,
        choose,
        rest_high,
        rest_low,
        small,
    )

    prefix = None
    bits = ns.bit_length() - 1
    for bit in range(bits):
        came = lax.ppermute(state, "seq", [(seq, seq ^ 2**bit) for seq in range(ns)])
        if bit == bits - 1:
            break
        given = [state] + ([] if prefix is None else [prefix]) + [came]

        def join(bit, known, *refs):
            if known:
                join_kernel(dims, bit, *refs)
            else:
                join_kernel(dims, bit, refs[0], None, *refs[1:])

        state, prefix = pl.pallas_call(
            functools.partial(join, bit, prefix is not None),
            out_shape=(shape(ch + 8, N),) * 2,
            in_specs=[vmem] * len(given),
            out_specs=(vmem,) * 2,
            compiler_params=params,
            name="join",
        )(*given)
    if prefix is None:
        prefix = jnp.zeros_like(state)

    parts = pl.pallas_call(
        functools.partial(output_kernel, dims, bits - 1),
        out_shape=(shape(share, D),) * nh,
        in_specs=[vmem] * 11,
        out_specs=(vmem,) * nh,
        scratch_shapes=[pltpu.VMEM((T, D), f32)],
        compiler_params=params,
        name="output",
    )(
        prefix,
        came,
        read_high,
        read_low,
        base,
        fade,
        gate,
        own,
        proj_high,
        proj_low,
        groups,
    )
    result = parts[0]
    for k in range(1, nh):
        pairs = list(enumerate(around(k, nh)))
        result = result + lax.ppermute(parts[k], "head", pairs)
    return result


def solution(mesh):
    return jax.shard_map(
        per_device,
        mesh=mesh,
        in_specs=(
            P(("rep", "seq")),
            P(),
            P(),
            P(),
            P(None, None, "head"),
            P(),
            P(None, "head"),
            P("head"),
            P("head"),
            P("head"),
            P("head"),
            P("head", None),
            P(),
            P(None, None, "head"),
            P(),
            P(None, "head"),
            P("head"),
            P("head"),
            P("head"),
            P("head"),
            P("head", None),
        ),
        out_specs=P(("rep", "seq", "head"), None),
        check_vma=False,
    )
```

```python
import functools

import jax
import jax.numpy as jnp
from jax import lax
from jax.experimental import pallas as pl
from jax.experimental.pallas import tpu as pltpu
from jax.sharding import PartitionSpec as P

epsilon = 1e-05
f32 = jnp.float32
bf16 = jnp.bfloat16
LIMIT = 48 * 1024 * 1024

MM = (((1,), (0,)), ((), ()))
NT = (((1,), (1,)), ((), ()))
TN = (((0,), (0,)), ((), ()))


def partners(ns, nh):
    return [(k if k < ns else 0, k if k < nh else 0) for k in range(max(ns, nh))]


def first_turn(count):
    return list(range(1, count))


def around(shift, count):
    ring = [place ^ place >> 1 for place in range(count)]
    if sorted(ring) != list(range(count)):
        ring = list(range(count))
    return [ring[(ring.index(plane) + shift) % count] for plane in range(count)]


def iota(shape, axis):
    return lax.broadcasted_iota(jnp.int32, shape, axis)


def split2(value):
    high = value.astype(bf16)
    return high, (value - high.astype(f32)).astype(bf16)


def split3(value):
    high = value.astype(bf16)
    rest = value - high.astype(f32)
    middle = rest.astype(bf16)
    return high, middle, (rest - middle.astype(f32)).astype(bf16)


def dot(left, right, dims=MM):
    return lax.dot_general(left, right, dims, preferred_element_type=f32)


def dot_split(left, right, dims=MM):
    axis = 1 if dims == TN else 0
    size = left[0].shape[axis]
    if size % 16:
        return (dot(left[0], right[1], dims) + dot(left[1], right[0], dims)) + dot(
            left[0], right[0], dims
        )
    both = dot(jnp.concatenate([left[1], left[0]], axis=axis), right[0], dims)
    return (dot(left[0], right[1], dims) + both[0:size]) + both[size:]


def dot3(left, right, dims=MM):
    return dot_split(split2(left), split2(right), dims)


def dot_left_exact(left, right, dims=MM):
    high, middle, low = split3(right)
    return (dot(left, low, dims) + dot(left, middle, dims)) + dot(left, high, dims)


def dot_right_exact(left, right, dims=MM):
    high, middle, low = split3(left)
    return (dot(low, right, dims) + dot(middle, right, dims)) + dot(high, right, dims)


def softplus(value):
    return jnp.maximum(value, 0.0) + jnp.log1p(jnp.exp(-jnp.abs(value)))


def silu(value):
    return value / (1.0 + jnp.exp(-value))


def rms(value):
    return value * lax.rsqrt(jnp.mean(value * value, axis=-1, keepdims=True) + epsilon)


def fetch(sources, places, semaphores):
    copies = []
    for number, (source, place) in enumerate(zip(sources, places)):
        copies.append(pltpu.make_async_copy(source, place, semaphores.at[number]))
        copies[-1].start()
    return copies


def fetch(sources, places, semaphores):
    copies = []
    for number, (source, place) in enumerate(zip(sources, places)):
        copies.append(pltpu.make_async_copy(source, place, semaphores.at[number]))
        copies[-1].start()
    return copies


PIECES = 1


def tables_kernel(dims, *refs):
    V, D, hl, ch, nh, ns, T, N = dims
    refs = list(refs)

    def take(number):
        taken, refs[:] = refs[:number], refs[number:]
        return taken

    sources = take(9)
    outproj_source, message = take(2)
    places = take(9)
    semaphores = take(1)[0]
    half = ch // 2
    top = top_rows(dims)
    core = lax.rem(lax.axis_index("seq"), 2)
    (inproj, tok, emb, prenorm, stepmap, bias, rates, skip, outnorm) = places
    size = inproj.shape[0] // PIECES
    pieces = [pl.ds(number * size, size) for number in range(PIECES)]
    rows = pl.ds(pl.multiple_of(core * half, 8), half)
    wide = [(place, pl.ds(place * ch, ch)) for place in range(D // ch)]
    copies = fetch(
        [sources[0].at[piece, :] for piece in pieces]
        + sources[1:]
        + [outproj_source.at[rows, columns] for _, columns in wide],
        [inproj.at[piece, :] for piece in pieces]
        + places[1:]
        + [message.at[pl.ds(top + place * half, half), :] for place, _ in wide],
        semaphores,
    )
    flip = (iota((T, 1), 0) + iota((1, T), 1) == T - 1).astype(f32).astype(bf16)
    for copy in copies[PIECES : PIECES + 8]:
        copy.wait()
    normed = split2(rms(emb[...]) * prenorm[...])
    raw_t = dot_split(split2(stepmap[...]), normed, NT)
    tokens = jnp.broadcast_to(tok[...].astype(f32), (8, T)).astype(bf16)
    tokens = dot(tokens, flip)
    for place in range(T // ch):
        message[2 * V + place : 2 * V + place + 1, :] = tokens[0:1, place * ch : (place + 1) * ch]
    row = 2 * V + T // ch
    message[row : row + 1, :] = outnorm[...]
    for head in range(hl):
        line = softplus(raw_t[head : head + 1, :] + bias[:, head : head + 1])
        row = row + 1
        message[row : row + 1, 0:V] = line
        message[row : row + 1, V : 2 * V] = -rates[:, head : head + 1] * line
        message[row : row + 1, 2 * V : 3 * V] = jnp.broadcast_to(skip[:, head : head + 1], (1, V))
    for copy in copies[:PIECES]:
        copy.wait()
    weights = jnp.concatenate(
        [inproj[pl.ds(0, D, stride=2), :], inproj[pl.ds(1, D, stride=2), :]], axis=1
    )
    both = dot_split(normed, split2(weights))
    message[0:V, :] = both[:, 0:ch]
    message[V : 2 * V, :] = both[:, ch:]
    for copy in copies[PIECES + 8 :]:
        copy.wait()


def top_rows(dims):
    V, D, hl, ch, nh, ns, T, N = dims
    return 2 * V + -(-(T // ch + 1 + hl) // 8) * 8


def head_line(dims, values):
    V, D, hl, ch, nh, ns, T, N = dims
    head_of = iota((1, ch), 1) // (ch // hl)
    line = jnp.zeros((1, ch), f32)
    for head in range(hl):
        line = jnp.where(head_of == head, values[:, head : head + 1], line)
    return line


def prepare_kernel(dims, *refs):
    V, D, hl, ch, nh, ns, T, N = dims
    H, P = nh * hl, ch // hl
    refs = list(refs)

    def take(number):
        taken, refs[:] = refs[:number], refs[number:]
        return taken

    sources = take(14)
    pairs, small, choose_out, own_high, own_low = take(5)
    state_high, state_low, rest_high, rest_low, out_high, out_low = take(6)
    triangles, upto, groups, blocks = take(4)
    places = take(14)
    semaphores = take(1)[0]
    copies = fetch(sources, places, semaphores)
    inproj2, statemap2, statemap, outproj, outproj2, emb, prenorm, complement = places[:8]
    prenorm2, stepmap2, bias2, rates2, skip2, outnorm2 = places[8:]
    row, column = iota((T, 1), 0), iota((1, T), 1)
    triangles[:, 0:T] = (row > column).astype(f32).astype(bf16)
    triangles[:, T : 2 * T] = (row < column).astype(f32).astype(bf16)
    triangles[:, 2 * T :] = jnp.ones((T, 128), bf16)
    upto[...] = (row >= column).astype(f32).astype(bf16)
    size = groups.shape[0]
    groups[...] = (iota((size, 1), 0) // P == iota((1, size), 1) // P).astype(f32).astype(bf16)
    rows, columns = blocks.shape
    blocks[...] = (iota((rows, 1), 0) // V == iota((1, columns), 1) // P).astype(f32).astype(bf16)
    for copy in copies:
        copy.wait()
    normed = split2(rms(emb[...]) * prenorm[...])
    write = dot_split(normed, split2(statemap[pl.ds(0, D, stride=2), :]))
    read = dot_split(normed, split2(statemap[pl.ds(1, D, stride=2), :]))
    pairs[...] = dot3(read, jnp.concatenate([write] * H, axis=0), NT)
    own_high[...], own_low[...] = split2(outproj[...])
    choose = (complement[...] == iota((D, 1), 0)).astype(f32).astype(bf16)
    choose_out[...] = choose
    gain = jnp.transpose(jnp.broadcast_to(prenorm2[...], (128, D)))

    def weights(values):
        return split2(dot_left_exact(choose, values))

    gain_wide = gain[:, 0:1]
    inner = inproj2[pl.ds(1, D, stride=2), :] * gain_wide
    step = jnp.transpose(
        jnp.concatenate(
            [jnp.broadcast_to(stepmap2[head : head + 1, :], (P, D)) for head in range(hl)], axis=0
        )
    )
    write2 = statemap2[pl.ds(0, D, stride=2), :] * gain_wide
    state_high[...], state_low[...] = weights(
        jnp.concatenate([inner, step * gain_wide, write2], axis=1)
    )
    gate = inproj2[pl.ds(0, D, stride=2), :] * gain_wide
    read2 = statemap2[pl.ds(1, D, stride=2), :] * gain_wide
    rest_high[...], rest_low[...] = weights(jnp.concatenate([gate, read2], axis=1))
    small[0:1, :] = head_line(dims, bias2)
    small[1:2, :] = head_line(dims, rates2)
    small[2:3, :] = head_line(dims, skip2)
    out_gain = jnp.transpose(jnp.broadcast_to(outnorm2[...], (128, ch)))
    out_high[...], out_low[...] = split2(outproj2[...] * out_gain[:, 0:1])


def shift_rows(value, amount, fill):
    size = value.shape[0]
    if amount % 8 == 0:
        empty = jnp.full((abs(amount),) + value.shape[1:], fill, value.dtype)
        if amount > 0:
            return jnp.concatenate([empty, value[: size - amount]], axis=0)
        return jnp.concatenate([value[-amount:], empty], axis=0)
    rolled = pltpu.roll(value, amount % size, 0)
    row = iota((8,) + value.shape[1:], 0)
    if amount > 0:
        edge = jnp.where(row >= amount, rolled[0:8], fill)
        return jnp.concatenate([edge, rolled[8:]], axis=0)
    edge = jnp.where(row < 8 + amount, rolled[size - 8 :], fill)
    return jnp.concatenate([rolled[: size - 8], edge], axis=0)


def scan_rows(decay, value, sign):
    size = value.shape[0]
    amount = 1
    while amount < size:
        value = value + decay * shift_rows(value, sign * amount, 0.0)
        decay = decay * shift_rows(decay, sign * amount, 1.0)
        amount *= 2
    return value, decay


def mix_kernel(dims, *refs):
    V, D, hl, ch, nh, ns, T, N = dims
    H, LV, P = nh * hl, nh * hl * V, ch // hl
    C = nh * ch
    refs = list(refs)

    def take(number):
        taken, refs[:] = refs[:number], refs[number:]
        return taken

    count = max(ns, nh)
    packets = dict(zip(first_turn(count)[::-1] + [0], take(count)))
    emb, pairs, triangles, groups, blocks = take(5)
    out_high, out_low, out_embedded = take(3)
    tokens = take(1)[0]
    mine = lax.axis_index("seq")

    for k in range(ns):
        block = ns - 1 - lax.bitwise_xor(mine, partners(ns, nh)[k][0])
        row = 2 * V
        pieces = [packets[k][row + place : row + place + 1, :] for place in range(T // ch)]
        tokens[pl.ds(block, 1), :] = jnp.concatenate(pieces, axis=1)

    first = 2 * V + T // ch + 1
    steps = jnp.concatenate(
        [packets[k][first : first + hl, 0 : 3 * V] for k in range(nh)], axis=0
    )
    log_t = steps[:, V : 2 * V]
    narrow = jnp.concatenate([part.astype(f32) for part in split3(steps)], axis=0).astype(bf16)
    spread_heads = (iota((1, LV), 1) // V == iota((3 * H, 1), 0) % H).astype(f32).astype(bf16)
    wide = dot(narrow, spread_heads, TN)
    own = iota((1, LV), 1) % V == iota((V, 1), 0)
    decay_table = jnp.exp(wide[V : 2 * V])
    step_table = jnp.where(own, wide[0:V], 0.0)
    gain_table = jnp.where(own, wide[2 * V : 3 * V], 0.0)
    gates = jnp.concatenate([packets[k][0:V, :] for k in range(nh)], axis=1)
    inners = jnp.concatenate([packets[k][V : 2 * V, :] for k in range(nh)], axis=1)
    gains = jnp.concatenate([packets[k][first - 1 : first, :] for k in range(nh)], axis=1)

    token_row = (iota((LV, 1), 0) % V).astype(f32)
    log_split = jnp.concatenate(split3(log_t), axis=1)
    onehots, logs = [], []
    for block in range(ns):
        onehot = (tokens[block : block + 1, :] == token_row).astype(f32).astype(bf16)
        onehots.append(onehot)
        logs.append(dot(log_split, onehot[0 : 3 * V, :]))
    logs = jnp.concatenate(logs, axis=0)
    size = ns * H
    sums = dot(jnp.concatenate(split3(logs)[::-1], axis=0), triangles[...])
    sums = (sums[0:size] + sums[size : 2 * size]) + sums[2 * size :]
    blocks_of = [sums[block * H : (block + 1) * H] for block in range(ns)]
    weight_up, weight_down = [None] * ns, [None] * ns
    gap = jnp.zeros((H, 128), f32)
    for block in reversed(range(ns)):
        wide = jnp.concatenate([gap] * (T // 128), axis=1)
        weight_up[block] = jnp.where(
            block < mine, jnp.exp(blocks_of[block][:, 0:T] + wide), 0.0
        )
        gap = jnp.where(block < mine, gap + blocks_of[block][:, 2 * T :], gap)
    gap = jnp.zeros((H, 128), f32)
    for block in range(ns):
        wide = jnp.concatenate([gap] * (T // 128), axis=1)
        weight_down[block] = jnp.where(
            block > mine, jnp.exp(blocks_of[block][:, T : 2 * T] + wide), 0.0
        )
        gap = jnp.where(block > mine, gap + blocks_of[block][:, 2 * T :], gap)
    entering = jnp.zeros((4 * H, LV), f32)
    for block in range(ns):
        both = jnp.concatenate([weight_up[block], weight_down[block]], axis=0)
        entering = entering + dot(
            jnp.concatenate(split2(both), axis=0), onehots[block], NT
        )
    entering = entering[2 * H :] + entering[0 : 2 * H]
    diagonal = iota((1, LV), 1) // V == iota((H, 1), 0)
    step_row = jnp.sum(step_table, axis=0, keepdims=True)
    enter_up = step_row * jnp.sum(
        jnp.where(diagonal, entering[0:H], 0.0), axis=0, keepdims=True
    )
    enter_down = step_row * jnp.sum(
        jnp.where(diagonal, entering[H : 2 * H], 0.0), axis=0, keepdims=True
    )

    looked = jnp.concatenate(
        [decay_table, step_table, pairs[...], gain_table, silu(gates), emb[...]], axis=1
    )
    looked = jnp.concatenate(split3(looked), axis=0)
    token = tokens[pl.ds(mine, 1), :]
    onehot = (token == token_row[0 : 3 * V]).astype(f32).astype(bf16)
    rows = dot(onehot, looked, TN)
    decay, step = rows[:, 0:LV], rows[:, LV : 2 * LV]
    pair, gain = rows[:, 2 * LV : 3 * LV], rows[:, 3 * LV : 4 * LV]
    silu_rows = rows[:, 4 * LV : 4 * LV + C]
    out_embedded[...] = rows[:, 4 * LV + C :]

    up, fade = scan_rows(decay, step, 1)
    up = up + fade * enter_up
    down, fade = scan_rows(decay, step, -1)
    down = down + fade * enter_down

    spread_high, spread_low = [
        jnp.concatenate([part] * H, axis=0) * blocks[...] for part in split2(inners)
    ]
    both = jnp.concatenate([up * pair + gain, down * pair + gain], axis=0)
    high = both.astype(bf16)
    high_wide = high.astype(f32)
    low_turned = pltpu.roll(both - high_wide, LV // 2, 1)
    lower = iota((1, LV), 1) < LV // 2
    value = []
    for side in (0, 1):
        mixed = jnp.where(lower == (side == 0), high_wide, low_turned).astype(bf16)
        rows = slice(side * LV // 2, (side + 1) * LV // 2)
        columns = slice(side * C // 2, (side + 1) * C // 2)
        weight, rest = spread_high[rows, columns], spread_low[:, columns]
        value.append(
            dot(
                jnp.concatenate([mixed, high], axis=1),
                jnp.concatenate([weight, weight, rest], axis=0),
            )
        )
    value = jnp.concatenate(value, axis=1)
    value = value * jnp.concatenate([silu_rows, silu_rows], axis=0)
    wide = groups.shape[0]
    high, low = split2(value * value)
    starts = list(range(0, C, wide))
    rows = 2 * T
    stacked = [half[:, start : start + wide] for start in starts for half in (low, high)]
    squares = dot(jnp.concatenate(stacked, axis=0), groups[...])
    for number, start in enumerate(starts):
        place = 2 * number * rows
        square = squares[place : place + rows] + squares[place + rows : place + 2 * rows]
        stop = start + wide
        normed = value[:, start:stop] * lax.rsqrt(square * (1.0 / P) + epsilon)
        out_high[:, start:stop], out_low[:, start:stop] = split2(
            (normed[0:T] + normed[T : 2 * T]) * gains[:, start:stop]
        )


def project_kernel(dims, *refs):
    V, D, hl, ch, nh, ns, T, N = dims
    P = ch // hl
    refs = list(refs)

    def take(number):
        taken, refs[:] = refs[:number], refs[number:]
        return taken

    high, low, embedded, small, own_high, own_low, state_high, state_low, upto = take(9)
    order = first_turn(nh)[::-1]
    nears = dict(zip(order, take(nh - 1)))
    others = dict(zip(order, take(nh - 1)))
    out_state, out_high, out_low, out_scale = take(4)
    out_write, out_inner, out_stepped, out_total = take(4)
    half = ch // 2
    base = top_rows(dims)
    mine = lax.axis_index("seq")

    pieces = []
    for k in range(1, nh):
        near, other = [
            jnp.concatenate(
                [
                    ref[base + place * half : base + (place + 1) * half, :]
                    for place in range(D // ch)
                ],
                axis=1,
            )
            for ref in (nears[k], others[k])
        ]
        even = lax.rem(lax.bitwise_xor(mine, partners(ns, nh)[k][0]), 2) == 0
        pieces.append(jnp.where(even, near, other))
        pieces.append(jnp.where(even, other, near))
    weights = split2(jnp.concatenate(pieces, axis=0))
    weights = (
        jnp.concatenate([own_high[...], weights[0]], axis=0),
        jnp.concatenate([own_low[...], weights[1]], axis=0),
    )
    hidden = embedded[...] + dot_split((high[...], low[...]), weights)
    split = split2(hidden)
    out_high[...], out_low[...] = split
    scale = lax.rsqrt(jnp.mean(hidden * hidden, axis=-1, keepdims=True) + epsilon)
    out_scale[...] = jnp.broadcast_to(scale, (T, ch))

    rows = dot_split(split, (state_high[...], state_low[...])) * scale
    inner, write = rows[:, 0:ch], rows[:, 2 * ch :]
    step = softplus(rows[:, ch : 2 * ch] + small[0:1, :])
    stepped = inner * step
    log_high, log_middle, log_low = split3(-small[1:2, :] * step)
    total = dot(upto[...], jnp.concatenate([log_low, log_middle], axis=1))
    total = (total[:, 0:ch] + total[:, ch:]) + dot(upto[...], log_high)
    end = total[T - 1 : T, :]
    state = dot3(stepped * jnp.exp(end - total), write, TN)
    out_state[0:ch, :] = state
    for head in range(hl):
        out_state[ch + head : ch + head + 1, :] = jnp.broadcast_to(
            end[:, head * P : head * P + 1], (1, N)
        )
    out_write[...] = write
    out_inner[...] = inner
    out_stepped[...] = stepped
    out_total[...] = total


def block_kernel(dims, *refs):
    V, D, hl, ch, nh, ns, T, N = dims
    P = ch // hl
    refs = list(refs)

    def take(number):
        taken, refs[:] = refs[:number], refs[number:]
        return taken

    high, low, scale, write, inner, stepped, total, choose = take(8)
    rest_high, rest_low, small = take(3)
    base, read_high, read_low, out_fade, own, hidden_ref = take(6)
    rows = dot_split((high[...], low[...]), (rest_high[...], rest_low[...]))
    gate = silu(rows[:, 0:ch] * scale[...])
    read = rows[:, ch:] * scale[...]
    read = split2(read)
    read_high[...], read_low[...] = read
    out_fade[...] = jnp.exp(total[...]) * gate
    products = dot_split(read, split2(write[...]), NT)
    stepped_high, stepped_low = split2(stepped[...])
    select = (iota((8, ch), 1) == iota((8, ch), 0) * P).astype(f32).astype(bf16)
    total_high, total_middle, total_low = split3(total[...])
    total_t = (dot(select, total_low, NT) + dot(select, total_middle, NT)) + dot(
        select, total_high, NT
    )
    allowed = iota((T, 1), 0) >= iota((1, T), 1)
    parts = []
    for head in range(hl):
        start, stop = head * P, (head + 1) * P
        differ = total[:, start : start + 1] - total_t[head : head + 1, :]
        weights = jnp.where(allowed, jnp.exp(jnp.where(allowed, differ, 0.0)), 0.0) * products
        part = dot_split(
            split2(weights), (stepped_high[:, start:stop], stepped_low[:, start:stop])
        )
        parts.append(part + small[2:3, start:stop] * inner[:, start:stop])
    base[...] = jnp.concatenate(parts, axis=1) * gate
    share = T // nh
    hidden_ref[...] = high[...].astype(f32) + low[...].astype(f32)
    place = pl.multiple_of(lax.axis_index("head") * share, 8)
    own[...] = dot_right_exact(hidden_ref[pl.ds(place, share), :], choose[...])


def state_rows(dims, values):
    V, D, hl, ch, nh, ns, T, N = dims
    head_of = iota((ch, N), 0) // (ch // hl)
    result = jnp.broadcast_to(values[0:1, :], (ch, N))
    for head in range(1, hl):
        result = jnp.where(head_of == head, values[head : head + 1, :], result)
    return result


def join_kernel(dims, bit, total, prefix, came, out_total, out_prefix):
    V, D, hl, ch, nh, ns, T, N = dims
    later = lax.rem(lax.div(lax.axis_index("seq"), 2**bit), 2) == 1
    came_state, came_log = came[0:ch, :], came[ch : ch + hl, :]
    state, log = total[0:ch, :], total[ch : ch + hl, :]
    factor = jnp.exp(state_rows(dims, jnp.where(later, log, came_log)))
    out_total[0:ch, :] = jnp.where(
        later, factor * came_state + state, factor * state + came_state
    )
    if out_total.shape[0] > ch:
        out_total[ch : ch + hl, :] = log + came_log
    if prefix is None:
        out_prefix[0:ch, :] = jnp.where(later, came_state, 0.0)
        out_prefix[ch : ch + hl, :] = jnp.where(later, came_log, 0.0)
    else:
        joined = prefix_joined(dims, bit, prefix, came)
        out_prefix[0:ch, :] = joined
        out_prefix[ch : ch + hl, :] = prefix[ch : ch + hl, :] + jnp.where(later, came_log, 0.0)


def prefix_joined(dims, bit, prefix, came):
    V, D, hl, ch, nh, ns, T, N = dims
    later = lax.rem(lax.div(lax.axis_index("seq"), 2**bit), 2) == 1
    factor = jnp.exp(state_rows(dims, prefix[ch : ch + hl, :]))
    return prefix[0:ch, :] + jnp.where(later, factor * came[0:ch, :], 0.0)


def output_kernel(dims, bit, *refs):
    V, D, hl, ch, nh, ns, T, N = dims
    P = ch // hl
    prefix, came, read_high, read_low, base, fade, own, proj_high, proj_low, groups = refs[:10]
    outs, partial_ref = refs[10 : 10 + nh], refs[10 + nh]
    entering = prefix_joined(dims, bit, prefix, came)
    carried = dot_split((read_high[...], read_low[...]), split2(entering), NT)
    value = base[...] + carried * fade[...]
    square = dot(jnp.concatenate(split2(value * value), axis=0), groups[0:ch, 0:ch])
    square = square[T:] + square[0:T]
    value = value * lax.rsqrt(square * (1.0 / P) + epsilon)
    share = T // nh
    partial_ref[...] = dot_split(split2(value), (proj_high[...], proj_low[...]))
    mine = lax.axis_index("head")
    for k in range(nh):
        to = 0
        for plane, target in enumerate(around(k, nh)):
            to = jnp.where(mine == plane, target, to)
        place = pl.multiple_of(to * share, 8)
        part = partial_ref[pl.ds(place, share), :]
        outs[k][...] = part + own[...] if k == 0 else part


def per_device(
    token_ids,
    embedding,
    complement,
    prenorm_first,
    inproj_first,
    statemap_first,
    stepmap_first,
    stepbias_first,
    rates_first,
    skipgain_first,
    outnorm_first,
    outproj_first,
    prenorm_second,
    inproj_second,
    statemap_second,
    stepmap_second,
    stepbias_second,
    rates_second,
    skipgain_second,
    outnorm_second,
    outproj_second,
):
    nh, ns = lax.axis_size("head"), lax.axis_size("seq")
    V, D = embedding.shape
    ch = inproj_first.shape[2]
    hl = stepmap_first.shape[1]
    N = statemap_first.shape[2]
    T = token_ids.shape[0]
    LV = nh * hl * V
    dims = (V, D, hl, ch, nh, ns, T, N)
    vmem = pl.BlockSpec(memory_space=pltpu.VMEM)
    anywhere = pl.BlockSpec(memory_space=pl.ANY)
    params = pltpu.CompilerParams(vmem_limit_bytes=LIMIT)

    def shape(*sizes, dtype=f32):
        return jax.ShapeDtypeStruct(sizes, dtype)

    def halves(*sizes):
        return [shape(*sizes, dtype=bf16)] * 2

    def room(value):
        return pltpu.VMEM(value.shape, value.dtype)

    def kept(values):
        return [pltpu.with_memory_space_constraint(value, pltpu.HBM) for value in values]

    def line(value):
        return value.reshape(1, -1)

    def flat(value):
        return value.reshape(-1, value.shape[-1])

    heavy = pl.CostEstimate(flops=960 * T * D * D, bytes_accessed=4 * T * D, transcendentals=T * D)

    half = ch // 2
    share = T // nh
    fetched = [
        flat(inproj_first),
        line(token_ids),
        embedding,
        line(prenorm_first),
        stepmap_first.T,
        line(stepbias_first),
        line(rates_first),
        line(skipgain_first),
        line(outnorm_first),
    ]
    message = pl.pallas_call(
        functools.partial(tables_kernel, dims),
        out_shape=pltpu.VMEM((top_rows(dims) + half * (D // ch), ch), f32),
        in_specs=[anywhere] * (len(fetched) + 1),
        out_specs=vmem,
        scratch_shapes=[room(value) for value in fetched]
        + [pltpu.SemaphoreType.DMA((len(fetched) - 1 + PIECES + D // ch,))],
        compiler_params=params,
        name="tables",
    )(*kept([*fetched, outproj_first]))

    prepared = [
        flat(inproj_second),
        flat(statemap_second),
        flat(statemap_first),
        outproj_first,
        outproj_second,
        embedding,
        line(prenorm_first),
        line(complement),
        line(prenorm_second),
        stepmap_second.T,
        line(stepbias_second),
        line(rates_second),
        line(skipgain_second),
        line(outnorm_second),
    ]
    (
        pair_table,
        small,
        choose,
        own_high,
        own_low,
        state_high,
        state_low,
        rest_high,
        rest_low,
        proj_high,
        proj_low,
        triangles,
        upto,
        groups,
        blocks,
    ) = pl.pallas_call(
        functools.partial(prepare_kernel, dims),
        out_shape=(
            shape(V, LV),
            shape(8, ch),
            shape(D, D, dtype=bf16),
            *halves(ch, D),
            *halves(D, 2 * ch + N),
            *halves(D, ch + N),
            *halves(ch, D),
            shape(T, 2 * T + 128, dtype=bf16),
            shape(T, T, dtype=bf16),
            shape(2 * ch, 2 * ch, dtype=bf16),
            shape(LV, nh * ch, dtype=bf16),
        ),
        in_specs=[anywhere] * len(prepared),
        out_specs=(vmem,) * 15,
        scratch_shapes=[room(value) for value in prepared]
        + [pltpu.SemaphoreType.DMA((len(prepared),))],
        compiler_params=params,
        cost_estimate=heavy,
        name="prepare",
    )(*kept(prepared))

    count = max(ns, nh)
    messages = {0: message}
    for k in first_turn(count):
        seq_bits, shift = partners(ns, nh)[k]
        pairs = [
            (seq * nh + head, (seq ^ seq_bits) * nh + (head + shift) % nh)
            for seq in range(ns)
            for head in range(nh)
        ]
        sent = message if k < nh else message[0 : top_rows(dims)]
        messages[k] = lax.ppermute(sent, ("seq", "head"), pairs)
    swap = [(seq, seq ^ 1) for seq in range(ns)]
    order = first_turn(nh)[::-1]
    others = [lax.ppermute(messages[k], "seq", swap) for k in order]

    mixed_high, mixed_low, embedded = pl.pallas_call(
        functools.partial(mix_kernel, dims),
        out_shape=(*halves(T, nh * ch), shape(T, D)),
        in_specs=[vmem] * (count + 5),
        out_specs=(vmem,) * 3,
        scratch_shapes=[pltpu.VMEM((max(ns, 8), T), f32)],
        compiler_params=params,
        cost_estimate=heavy,
        name="mix",
    )(
        *[messages[k] for k in first_turn(count)[::-1] + [0]],
        embedding,
        pair_table,
        triangles,
        groups,
        blocks,
    )

    state, hidden_high, hidden_low, scale, write, inner, stepped, total = pl.pallas_call(
        functools.partial(project_kernel, dims),
        out_shape=(
            shape(ch + 8, N),
            *halves(T, D),
            shape(T, ch),
            shape(T, N),
            shape(T, ch),
            shape(T, ch),
            shape(T, ch),
        ),
        in_specs=[vmem] * (9 + 2 * (nh - 1)),
        out_specs=(vmem,) * 8,
        compiler_params=params,
        name="project",
    )(
        mixed_high,
        mixed_low,
        embedded,
        small,
        own_high,
        own_low,
        state_high,
        state_low,
        upto,
        *[messages[k] for k in order],
        *others,
    )

    base, read_high, read_low, fade, own = pl.pallas_call(
        functools.partial(block_kernel, dims),
        out_shape=(
            shape(T, ch),
            *halves(T, N),
            shape(T, ch),
            shape(share, D),
        ),
        in_specs=[vmem] * 11,
        out_specs=(vmem,) * 5,
        scratch_shapes=[pltpu.VMEM((T, D), f32)],
        compiler_params=params,
        cost_estimate=heavy,
        name="block",
    )(
        hidden_high,
        hidden_low,
        scale,
        write,
        inner,
        stepped,
        total,
        choose,
        rest_high,
        rest_low,
        small,
    )

    prefix = None
    bits = ns.bit_length() - 1
    for bit in range(bits):
        came = lax.ppermute(state, "seq", [(seq, seq ^ 2**bit) for seq in range(ns)])
        if bit == bits - 1:
            break
        given = [state] + ([] if prefix is None else [prefix]) + [came]

        def join(bit, known, *refs):
            if known:
                join_kernel(dims, bit, *refs)
            else:
                join_kernel(dims, bit, refs[0], None, *refs[1:])

        state, prefix = pl.pallas_call(
            functools.partial(join, bit, prefix is not None),
            out_shape=(shape(ch if bit == bits - 2 else ch + 8, N), shape(ch + 8, N)),
            in_specs=[vmem] * len(given),
            out_specs=(vmem,) * 2,
            compiler_params=params,
            name="join",
        )(*given)
    if prefix is None:
        prefix = jnp.zeros_like(state)

    parts = pl.pallas_call(
        functools.partial(output_kernel, dims, bits - 1),
        out_shape=(shape(share, D),) * nh,
        in_specs=[vmem] * 10,
        out_specs=(vmem,) * nh,
        scratch_shapes=[pltpu.VMEM((T, D), f32)],
        compiler_params=params,
        name="output",
    )(
        prefix,
        came,
        read_high,
        read_low,
        base,
        fade,
        own,
        proj_high,
        proj_low,
        groups,
    )
    result = parts[0]
    for k in range(1, nh):
        pairs = list(enumerate(around(k, nh)))
        result = result + lax.ppermute(parts[k], "head", pairs)
    return result


def solution(mesh):
    return jax.shard_map(
        per_device,
        mesh=mesh,
        in_specs=(
            P(("rep", "seq")),
            P(),
            P(),
            P(),
            P(None, None, "head"),
            P(),
            P(None, "head"),
            P("head"),
            P("head"),
            P("head"),
            P("head"),
            P("head", None),
            P(),
            P(None, None, "head"),
            P(),
            P(None, "head"),
            P("head"),
            P("head"),
            P("head"),
            P("head"),
            P("head", None),
        ),
        out_specs=P(("rep", "seq", "head"), None),
        check_vma=False,
    )
```
